32 devices in a mesh: seq: 4 (over z), fsdp: 8 (over y, x, core).
Axes of the slice: x: 2, y: 2, z: 4, core: 2. Of those that a mesh axis runs over, the one named last changes fastest.
Arguments:
- tokens: bfloat16 [8, 512, 1024], P('fsdp', 'seq'), may hold values from -6 to 6
- scene_ids: int32 [8, 512], P('fsdp', 'seq'), may hold values from 0 to 1, as said below
- token_kind: int32 [8, 512], P('fsdp', 'seq'), may hold values from 0 to 1, as said below
- out_grad: bfloat16 [8, 512, 1024], P('fsdp', 'seq'), may hold values from -6 to 6
- first_gain: bfloat16 [2, 1024], P(None, 'fsdp'), may hold values from 0.5 to 1.5
- first_shift: bfloat16 [2, 1024], P(None, 'fsdp'), may hold values from -1.796875 to 1.796875
- qkv_weight: bfloat16 [2, 1024, 3072], P(None, 'fsdp'), may hold values from -0.1875 to 0.1875
- qv_bias: bfloat16 [2, 2048], P(None, 'fsdp'), may hold values from -3 to 3
- proj_weight: bfloat16 [2, 1024, 1024], P(None, 'fsdp'), may hold values from -1.5 to 1.5
- proj_bias: bfloat16 [2, 1024], P(None, 'fsdp'), may hold values from -3 to 3
- second_gain: bfloat16 [2, 1024], P(None, 'fsdp'), may hold values from 0.5 to 1.5
- second_shift: bfloat16 [2, 1024], P(None, 'fsdp'), may hold values from -1.796875 to 1.796875
- up_weight: bfloat16 [2, 1024, 4096], P(None, 'fsdp'), may hold values from -0.1875 to 0.1875
- up_bias: bfloat16 [2, 4096], P(None, 'fsdp'), may hold values from -3 to 3
- down_weight: bfloat16 [2, 4096, 1024], P(None, 'fsdp'), may hold values from -0.09375 to 0.09375
- down_bias: bfloat16 [2, 1024], P(None, 'fsdp'), may hold values from -3 to 3
Outputs:
- block_out: float32 [8, 512, 1024], P('fsdp', 'seq')
- input_grad: float32 [8, 512, 1024], P('fsdp', 'seq')
- first_gain_grad: float32 [2, 1024], P(None, 'fsdp')
- first_shift_grad: float32 [2, 1024], P(None, 'fsdp')
- qkv_weight_grad: float32 [2, 1024, 3072], P(None, 'fsdp')
- qv_bias_grad: float32 [2, 2048], P(None, 'fsdp')
- proj_weight_grad: float32 [2, 1024, 1024], P(None, 'fsdp')
- proj_bias_grad: float32 [2, 1024], P(None, 'fsdp')
- second_gain_grad: float32 [2, 1024], P(None, 'fsdp')
- second_shift_grad: float32 [2, 1024], P(None, 'fsdp')
- up_weight_grad: float32 [2, 1024, 4096], P(None, 'fsdp')
- up_bias_grad: float32 [2, 4096], P(None, 'fsdp')
- down_weight_grad: float32 [2, 4096, 1024], P(None, 'fsdp')
- down_bias_grad: float32 [2, 1024], P(None, 'fsdp')
The draws below stay inside these ranges and needn't reach their ends.
Inputs may be any that keep to these rules, and one draw needn't show every extreme that they name: `scene_ids`: within each group the positions hold in order: image tokens of one scene, image tokens of the other, triplane tokens of the other, triplane tokens of the first; all four runs are nonempty. `token_kind`: the image tokens of a group come before its triplane tokens, as described for scene_ids.
All inputs are finite; a program needn't handle non-finite values.
Results may differ from the reference program's by a relative error of at most 0.015.
Values may be sent and summed in bfloat16 or wider, within the bound.
No kernel may reach another device: no remote copies, remote signals or barrier semaphores. Data moves between devices by JAX's collectives and lax.ppermute only.
A program may use at most 256 MiB of HBM per device.

```python
import jax
import jax.numpy as jnp
from jax import lax

D = 1024
HEADS = 16
FF = 4096
HEAD_DIM = 64
LAYERS = 2
TOK_DEV = 128
GROUPS = 8
SEQ_TOK = 512
N_SEQ = 4


def scene_layout(key):
    quarter = SEQ_TOK // 32
    eighth = SEQ_TOK // 8
    streams = jax.random.split(key, 4)
    first_move = jax.random.randint(streams[0], (GROUPS, 1), -quarter, quarter)
    image_move = jax.random.randint(streams[1], (GROUPS, 1), -quarter, quarter)
    second_move = jax.random.randint(streams[2], (GROUPS, 1), -quarter, quarter)
    spanning = jax.random.randint(streams[3], (GROUPS, 1), 0, 2)
    place = jnp.arange(SEQ_TOK, dtype=jnp.int32)[None, :]
    end_first = eighth + first_move
    end_images = 2 * eighth + image_move
    end_second = end_images + eighth + second_move
    outside = (place < end_first) | (place >= end_second)
    scenes = jnp.where(outside, spanning, 1 - spanning).astype(jnp.int32)
    kinds = (place >= end_images).astype(jnp.int32) + jnp.zeros((GROUPS, 1), jnp.int32)
    return (scenes, kinds)


def draw_scene_ids(key, part):
    shared = scene_layout(key)
    return shared[0]


def draw_token_kind(key, part):
    shared = scene_layout(key)
    return shared[1]


def block_levels(rng, dims, cuts, least, high):
    def one(dim, parts):
        draws = jax.random.uniform(jax.random.fold_in(jax.random.fold_in(rng, 6), dim), (parts,), jnp.float32, least / len(cuts), high / len(cuts))
        return jnp.repeat(jnp.exp(draws), dims[dim] // parts).reshape((-1,) + (1,) * (len(dims) - dim - 1))

    loudness = one(*cuts[0])
    for cut in cuts[1:]:
        loudness = loudness * one(*cut)
    return loudness


def bell_draw(key, shape, scale, bound, pieces=(), kind=jnp.bfloat16):
    values = jax.random.normal(key, shape, jnp.float32) * scale
    if len(pieces) > 0:
        values = block_levels(key, shape, pieces, -0.22, 0.18) * values
    return jnp.clip(values, min=-bound, max=bound).astype(kind)


def setup_inputs(seed: int = 0) -> dict:
    key_of = jax.random.split(jax.random.key(seed), 17)
    return {
        "tokens": bell_draw(key_of[0], (GROUPS, SEQ_TOK, D), 1.0, 6.0, ((0, 8), (1, 4))),
        "scene_ids": draw_scene_ids(jax.random.fold_in(key_of[16], 71), 0),
        "token_kind": draw_token_kind(jax.random.fold_in(key_of[16], 71), 0),
        "out_grad": bell_draw(key_of[3], (GROUPS, SEQ_TOK, D), 1.0, 6.0, ((0, 8), (1, 4))),
        "first_gain": jnp.clip(1.0 + 0.1 * jax.random.normal(key_of[4], (LAYERS, D), jnp.float32), 0.5, 1.5).astype(jnp.bfloat16),
        "first_shift": bell_draw(key_of[5], (LAYERS, D), 0.3, 1.796875, ((1, 8),)),
        "qkv_weight": bell_draw(key_of[6], (LAYERS, D, 3 * D), D ** -0.5, 0.1875, ((1, 8),)),
        "qv_bias": bell_draw(key_of[7], (LAYERS, 2 * D), 0.5, 3.0, ((1, 8),)),
        "proj_weight": bell_draw(key_of[8], (LAYERS, D, D), (D // 64) ** -0.5, 1.5, ((1, 8),)),
        "proj_bias": bell_draw(key_of[9], (LAYERS, D), 0.5, 3.0, ((1, 8),)),
        "second_gain": jnp.clip(1.0 + 0.1 * jax.random.normal(key_of[10], (LAYERS, D), jnp.float32), 0.5, 1.5).astype(jnp.bfloat16),
        "second_shift": bell_draw(key_of[11], (LAYERS, D), 0.3, 1.796875, ((1, 8),)),
        "up_weight": bell_draw(key_of[12], (LAYERS, D, FF), D ** -0.5, 0.1875, ((1, 8),)),
        "up_bias": bell_draw(key_of[13], (LAYERS, FF), 0.5, 3.0, ((1, 8),)),
        "down_weight": bell_draw(key_of[14], (LAYERS, FF, D), FF ** -0.5, 0.09375, ((1, 8),)),
        "down_bias": bell_draw(key_of[15], (LAYERS, D), 0.5, 3.0, ((1, 8),)),
    }


@jax.custom_vjp
def low(v):
    return lax.optimization_barrier(v.astype(jnp.bfloat16)).astype(jnp.float32)

@jax.custom_vjp
def low_back(v):
    return v

def low_keep(v):
    return (low(v), None)

def low_pass(kept, grad):
    return (grad,)

def back_keep(v):
    return (v, None)

def back_low(kept, grad):
    return (low(grad),)
low.defvjp(low_keep, low_pass)
low_back.defvjp(back_keep, back_low)
EPS = 1e-05
NEG = -1e+30
SCALE = 0.125

def product(left_side, right_side):
    return jnp.dot(left_side, right_side, precision=lax.Precision.HIGHEST, preferred_element_type=jnp.float32)

def layer_norm(hidden, norm_gain, norm_shift):
    centred = hidden - lax.optimization_barrier(jnp.mean(hidden, axis=-1, keepdims=True))
    spread = lax.optimization_barrier(jnp.mean(centred * centred, axis=-1, keepdims=True))
    return centred * lax.rsqrt(spread + EPS) * norm_gain + norm_shift

def attention(queries, keys, values, scene_row, kind_row):

    def block(inputs):
        query_block, scene_block, kind_block = inputs
        raw_scores = jnp.einsum('the,she->hts', query_block, keys, precision=lax.Precision.HIGHEST) * SCALE
        raw_scores = low_back(raw_scores)
        allowed = (scene_block[:, None] == scene_row[None, :]) & ((kind_row[None, :] == 0) | (kind_block[:, None] == 1))
        masked = jnp.where(allowed[None], raw_scores, NEG)
        probabilities = jax.nn.softmax(masked, axis=-1)
        return jnp.einsum('hts,she->the', low(probabilities), values, precision=lax.Precision.HIGHEST)
    blocks = (queries.reshape(N_SEQ, TOK_DEV, HEADS, HEAD_DIM), scene_row.reshape(N_SEQ, TOK_DEV), kind_row.reshape(N_SEQ, TOK_DEV))
    result = lax.map(jax.checkpoint(block), blocks)
    return result.reshape(SEQ_TOK, D)

def layer_forward(hidden, scene_row, kind_row, params):
    gain_one, shift_one, qkv_full, qv_full, proj_full, proj_add, gain_two, shift_two, up_full, up_add, down_full, down_add = params
    input_one = low(layer_norm(hidden, gain_one, shift_one))
    qkv_add = jnp.concatenate([qv_full[:D], jnp.zeros((D,), jnp.float32), qv_full[D:]])
    projected = low_back(low(product(input_one, qkv_full) + qkv_add))
    queries = projected[:, :D].reshape(SEQ_TOK, HEADS, HEAD_DIM)
    keys = projected[:, D:2 * D].reshape(SEQ_TOK, HEADS, HEAD_DIM)
    values = projected[:, 2 * D:].reshape(SEQ_TOK, HEADS, HEAD_DIM)
    attended = low_back(low(attention(queries, keys, values, scene_row, kind_row)))
    middle = hidden + low_back(product(attended, proj_full) + proj_add)
    input_two = low(layer_norm(middle, gain_two, shift_two))
    pre_act = low_back(product(input_two, up_full) + up_add)
    activated = low(jax.nn.gelu(pre_act, approximate=False))
    return middle + low_back(product(activated, down_full) + down_add)

def reference(tokens, scene_ids, token_kind, out_grad, first_gain, first_shift, qkv_weight, qv_bias, proj_weight, proj_bias, second_gain, second_shift, up_weight, up_bias, down_weight, down_bias):
    params = tuple((member.astype(jnp.float32) for member in (first_gain, first_shift, qkv_weight, qv_bias, proj_weight, proj_bias, second_gain, second_shift, up_weight, up_bias, down_weight, down_bias)))

    def whole(inputs, weights):

        def per_group(group):
            hidden, scene_row, kind_row = group
            for layer_index in range(LAYERS):
                hidden = layer_forward(hidden, scene_row, kind_row, tuple((member[layer_index] for member in weights)))
            return hidden
        return lax.map(jax.checkpoint(per_group), (inputs, scene_ids, token_kind))
    block_out, pull_back = jax.vjp(whole, tokens.astype(jnp.float32), params)
    input_grad, grads = pull_back(out_grad.astype(jnp.float32))
    return (block_out, input_grad, grads[0], grads[1], grads[2], grads[3], grads[4], grads[5], grads[6], grads[7], grads[8], grads[9], grads[10], grads[11])
```

```python
from functools import partial

import jax
import jax.numpy as jnp
from jax import lax
from jax.sharding import PartitionSpec as P

D = 1024
HEADS = 16
HEAD_DIM = 64
FF = 4096
EPS = 1e-05
NEG = -1e30
SCALE = 0.125
BF = jnp.bfloat16
F32 = jnp.float32


def xor_pairs(count, mask):
    return [(i, i ^ mask) for i in range(count)]


class Net:
    def __init__(self):
        self.n_s = lax.axis_size("seq")
        self.n_f = lax.axis_size("fsdp")
        self.n_p = self.n_f // 2
        self.s = lax.axis_index("seq")
        self.f = lax.axis_index("fsdp")
        self.p = self.f // 2
        self.c = self.f % 2

    def transpose(self, v):
        pairs = []
        for s in range(self.n_s):
            for f in range(self.n_f):
                pairs.append((s * self.n_f + f, (f // 2) * self.n_f + 2 * s + f % 2))
        return lax.ppermute(v, ("seq", "fsdp"), pairs)

    def chip(self, v, j):
        return lax.ppermute(v, "fsdp", xor_pairs(self.n_f, 2 * j))

    def core(self, v):
        return lax.ppermute(v, "fsdp", xor_pairs(self.n_f, 1))

    def gather(self, v):
        return [v] + [self.chip(v, j) for j in range(1, self.n_p)]

    def exchange(self, blocks):
        return [blocks[0]] + [self.chip(blocks[j], j) for j in range(1, self.n_p)]

    def scatter(self, blocks):
        parts = self.exchange(blocks)
        total = parts[0].astype(F32)
        for part in parts[1:]:
            total = total + part.astype(F32)
        return total

    def natural(self, blocks):
        bit = 1
        while bit < self.n_p:
            on = (self.p & bit) != 0
            blocks = [jnp.where(on, blocks[i ^ bit], blocks[i]) for i in range(self.n_p)]
            bit *= 2
        return blocks

    def by_core(self, own, other):
        on = self.c == 0
        return jnp.where(on, own, other), jnp.where(on, other, own)

    def z_sum(self, v):
        n = self.n_s
        half = n // 2
        total = v
        for k in range(1, half):
            got = lax.ppermute(total, "seq", [(k - 1, k), (n - k, n - k - 1)])
            here = (self.s == k) | (self.s == n - 1 - k)
            total = jnp.where(here, (v.astype(F32) + got.astype(F32)).astype(BF), total)
        got = lax.ppermute(total, "seq", [(half - 1, half), (half, half - 1)])
        total = (total.astype(F32) + got.astype(F32)).astype(BF)
        for k in range(half - 1, 0, -1):
            got = lax.ppermute(total, "seq", [(k, k - 1), (n - 1 - k, n - k)])
            here = (self.s == k - 1) | (self.s == n - k)
            total = jnp.where(here, got, total)
        return total


def normalize(hidden):
    centred = hidden - jnp.mean(hidden, axis=-1, keepdims=True)
    spread = jnp.mean(centred * centred, axis=-1, keepdims=True)
    inverse = lax.rsqrt(spread + EPS)
    return (centred * inverse, inverse)


def norm_back(gradient, normed, inverse, norm_gain):
    scaled = gradient * norm_gain
    mean_one = jnp.mean(scaled, axis=-1, keepdims=True)
    mean_two = jnp.mean(scaled * normed, axis=-1, keepdims=True)
    input_part = inverse * (scaled - mean_one - normed * mean_two)
    return (input_part, jnp.sum(gradient * normed, axis=0), jnp.sum(gradient, axis=0))


def dot(a, b):
    return jnp.dot(a, b, preferred_element_type=F32)


def dot_tn(a, b):
    return lax.dot_general(a, b, (((0,), (0,)), ((), ())), preferred_element_type=F32)


def dot_nt(a, b):
    return lax.dot_general(a, b, (((1,), (1,)), ((), ())), preferred_element_type=F32)


def scores_of(q, k, allowed):
    raw = jnp.einsum("the,she->hts", q, k, preferred_element_type=F32) * SCALE
    return jnp.where(allowed[None], raw, NEG)


def attend(qkv, allowed, width):
    rows = qkv.shape[0]
    q, k, v = [qkv[:, i * width : (i + 1) * width].reshape(rows, -1, HEAD_DIM) for i in range(3)]
    scores = scores_of(q, k, allowed)
    largest = jnp.max(scores, axis=-1, keepdims=True)
    powers = jnp.exp(scores - largest)
    total = jnp.sum(powers, axis=-1, keepdims=True)
    probs = (powers / total).astype(BF)
    out = jnp.einsum("hts,she->the", probs, v, preferred_element_type=F32)
    return out.reshape(rows, width).astype(BF), largest + jnp.log(total)


def attend_back(qkv, allowed, log_total, do, width):
    rows = qkv.shape[0]
    q, k, v = [qkv[:, i * width : (i + 1) * width].reshape(rows, -1, HEAD_DIM) for i in range(3)]
    do = do.reshape(rows, -1, HEAD_DIM)
    probs = jnp.exp(scores_of(q, k, allowed) - log_total)
    dv = jnp.einsum("hts,the->she", probs.astype(BF), do, preferred_element_type=F32)
    dp = jnp.einsum("the,she->hts", do, v, preferred_element_type=F32)
    ds = (probs * (dp - jnp.sum(probs * dp, axis=-1, keepdims=True))).astype(BF)
    dq = jnp.einsum("hts,she->the", ds, k, preferred_element_type=F32) * SCALE
    dk = jnp.einsum("hts,the->she", ds, q, preferred_element_type=F32) * SCALE
    return jnp.concatenate([t.reshape(rows, width) for t in (dq, dk, dv)], axis=1).astype(BF)


def quarter(v, index, width):
    return lax.dynamic_slice_in_dim(v, index * width, width, axis=1)


def fetch_rows(net, payload_of):
    got = net.exchange([payload_of(net.p ^ j) for j in range(net.n_p)])
    own = jnp.stack(net.natural(got))
    other = net.core(own)
    first, second = net.by_core(own, other)
    return jnp.stack([first, second], axis=1).reshape(-1, own.shape[-1])


def return_rows(net, partial_rows):
    n = partial_rows.shape[1]
    by_owner = partial_rows.astype(BF).reshape(net.n_p, 2, -1, n)
    keep = lax.dynamic_index_in_dim(by_owner, net.c, axis=1, keepdims=False)
    send = lax.dynamic_index_in_dim(by_owner, 1 - net.c, axis=1, keepdims=False)
    summed = (keep.astype(F32) + net.core(send).astype(F32)).astype(BF)
    blocks = [
        lax.dynamic_index_in_dim(summed, net.p ^ j, axis=0, keepdims=False) for j in range(net.n_p)
    ]
    return net.exchange(blocks)


def on_device(
    tokens,
    scene_ids,
    token_kind,
    out_grad,
    first_gain,
    first_shift,
    qkv_weight,
    qv_bias,
    proj_weight,
    proj_bias,
    second_gain,
    second_shift,
    up_weight,
    up_bias,
    down_weight,
    down_bias,
):
    net = Net()
    n_p = net.n_p
    layers = qkv_weight.shape[0]
    cw = D // n_p
    fw = FF // n_p
    rows = tokens.shape[1]

    small = jnp.concatenate(
        [first_gain, first_shift, qv_bias, proj_bias, second_gain, second_shift, up_bias, down_bias],
        axis=1,
    )
    small = lax.all_gather(small, "fsdp", axis=0).astype(F32)
    d8 = first_gain.shape[1]
    widths = [d8, d8, 2 * d8, d8, d8, d8, 4 * d8, d8]
    starts = [sum(widths[:i]) for i in range(8)]

    def vector(layer, which):
        return small[:, layer, starts[which] : starts[which] + widths[which]].reshape(-1)

    hidden = net.transpose(tokens[0]).astype(F32)
    code = net.transpose((scene_ids[0] * 2 + token_kind[0]).reshape(1, -1))
    codes = jnp.concatenate(net.gather(code), axis=1)
    same = codes.reshape(-1, 1) // 2 == codes.reshape(1, -1) // 2
    seen = (codes.reshape(1, -1) % 2 == 0) | (codes.reshape(-1, 1) % 2 == 1)
    allowed = same & seen
    dm_first = net.transpose(out_grad[0])

    def qkv_payload(layer):
        w = qkv_weight[layer].reshape(-1, 3, D)

        def of(i):
            return lax.dynamic_slice_in_dim(w, i * cw, cw, axis=2).reshape(-1, 3 * cw)

        return of

    weights = []
    for layer in range(layers):
        qkv_w = fetch_rows(net, qkv_payload(layer))
        rest = fetch_rows(
            net,
            lambda i, layer=layer: jnp.concatenate(
                [proj_weight[layer], quarter(up_weight[layer], i, fw)], axis=1
            ),
        )
        first, second = net.by_core(down_weight[layer], net.core(down_weight[layer]))
        down_w = jnp.concatenate([first, second], axis=0)
        qv = vector(layer, 2)
        qkv_b = jnp.concatenate(
            [
                lax.dynamic_slice_in_dim(qv, net.p * cw, cw),
                jnp.zeros((cw,), F32),
                lax.dynamic_slice_in_dim(qv, D + net.p * cw, cw),
            ]
        )
        up_b = lax.dynamic_slice_in_dim(vector(layer, 6), net.p * fw, fw)
        weights.append((qkv_w, qkv_b, rest[:, :D], rest[:, D:], up_b, down_w))

    kept = []
    for layer in range(layers):
        qkv_w, qkv_b, proj_w, up_w, up_b, down_w = weights[layer]
        n1, r1 = normalize(hidden)
        a1 = (n1 * vector(layer, 0) + vector(layer, 1)).astype(BF)
        a1g = jnp.concatenate(net.gather(a1), axis=0)
        qkv = (dot(a1g, qkv_w) + qkv_b).astype(BF)
        og, log_total = attend(qkv, allowed, cw)
        o = net.exchange([og[j * rows : (j + 1) * rows] for j in range(n_p)])
        o = jnp.concatenate(net.natural(o), axis=1)
        h2 = hidden + dot(o, proj_w) + vector(layer, 3)
        n2, r2 = normalize(h2)
        a2 = (n2 * vector(layer, 4) + vector(layer, 5)).astype(BF)
        a2g = jnp.concatenate(net.gather(a2), axis=0)
        u = dot(a2g, up_w) + up_b
        z = jax.nn.gelu(u, approximate=False).astype(BF)
        y = dot(z, down_w).astype(BF)
        h3 = h2 + net.scatter([y[j * rows : (j + 1) * rows] for j in range(n_p)]) + vector(layer, 7)
        kept.append((n1, r1, a1g, qkv, log_total, o, n2, r2, a2g, u, z))
        hidden = h3
    block_out = net.transpose(hidden.astype(BF)).astype(F32)

    grads = [None] * layers
    grad = None
    dm = dm_first
    for layer in reversed(range(layers)):
        qkv_w, qkv_b, proj_w, up_w, up_b, down_w = weights[layer]
        n1, r1, a1g, qkv, log_total, o, n2, r2, a2g, u, z = kept[layer]
        if grad is None:
            grad = dm.astype(F32)
        else:
            dm = grad.astype(BF)
        dmg = jnp.concatenate(net.gather(dm), axis=0)
        down_b_grad = jnp.sum(dm.astype(F32), axis=0)
        down_q = dot_tn(z, dmg).astype(BF).reshape(2, -1, D)
        keep = lax.dynamic_index_in_dim(down_q, net.c, axis=0, keepdims=False)
        send = lax.dynamic_index_in_dim(down_q, 1 - net.c, axis=0, keepdims=False)
        down_g = (keep.astype(F32) + net.core(send).astype(F32)).astype(BF)
        dz = dot_nt(dmg, down_w)
        du = jax.vjp(partial(jax.nn.gelu, approximate=False), u)[1](dz)[0].astype(BF)
        up_b_grad = jnp.sum(du.astype(F32), axis=0)
        up_g = jnp.concatenate(net.natural(return_rows(net, dot_tn(a2g, du))), axis=1)
        da2 = dot_nt(du, up_w).astype(BF)
        da2 = net.scatter([da2[j * rows : (j + 1) * rows] for j in range(n_p)])
        part, gain2_grad, shift2_grad = norm_back(da2, n2, r2, vector(layer, 4))
        dh2 = grad + part
        dy = dh2.astype(BF)
        proj_b_grad = jnp.sum(dy.astype(F32), axis=0)
        proj_parts = return_rows(net, dot_tn(o, dy))
        proj_g = sum(t.astype(F32) for t in proj_parts).astype(BF)
        do = dot_nt(dy, proj_w).astype(BF)
        dog = net.exchange([quarter(do, net.p ^ j, cw) for j in range(n_p)])
        dog = jnp.concatenate(dog, axis=0)
        dqkv = attend_back(qkv, allowed, log_total, dog, cw)
        qkv_b_grad = jnp.sum(dqkv.astype(F32), axis=0)
        da1 = dot_nt(dqkv, qkv_w).astype(BF)
        da1 = net.scatter([da1[j * rows : (j + 1) * rows] for j in range(n_p)])
        part, gain1_grad, shift1_grad = norm_back(da1, n1, r1, vector(layer, 0))
        grad = dh2 + part
        qkv_parts = net.natural(return_rows(net, dot_tn(a1g, dqkv)))
        qkv_g = jnp.stack([t.reshape(-1, 3, cw) for t in qkv_parts], axis=2).reshape(-1, 3 * D)
        qv_grad = jnp.zeros((2 * D,), F32)
        qv_grad = lax.dynamic_update_slice(qv_grad, qkv_b_grad[:cw], (net.p * cw,))
        qv_grad = lax.dynamic_update_slice(qv_grad, qkv_b_grad[2 * cw :], (D + net.p * cw,))
        up_b_grad = lax.dynamic_update_slice(jnp.zeros((FF,), F32), up_b_grad, (net.p * fw,))
        vectors = (
            gain1_grad,
            shift1_grad,
            qv_grad,
            proj_b_grad,
            gain2_grad,
            shift2_grad,
            up_b_grad,
            down_b_grad,
        )
        grads[layer] = (
            net.z_sum(qkv_g),
            net.z_sum(proj_g),
            net.z_sum(up_g),
            net.z_sum(down_g),
            jnp.concatenate([t.reshape(net.n_f, -1) for t in vectors], axis=1),
        )
    input_grad = net.transpose(grad.astype(BF)).astype(F32)

    small_g = jnp.stack([g[4] for g in grads], axis=1).astype(BF)
    small_g = lax.psum_scatter(small_g, "fsdp", scatter_dimension=0, tiled=True)[0]
    small_g = lax.psum(small_g, "seq").astype(F32)
    small_out = [small_g[:, starts[i] : starts[i] + widths[i]] for i in range(8)]
    big = [jnp.stack([g[i] for g in grads]).astype(F32) for i in range(4)]
    return (
        block_out[None],
        input_grad[None],
        small_out[0],
        small_out[1],
        big[0],
        small_out[2],
        big[1],
        small_out[3],
        small_out[4],
        small_out[5],
        big[2],
        small_out[6],
        big[3],
        small_out[7],
    )


def solution(mesh):
    tok = P("fsdp", "seq", None)
    lab = P("fsdp", "seq")
    vec = P(None, "fsdp")
    mat = P(None, "fsdp", None)
    return jax.shard_map(
        on_device,
        mesh=mesh,
        in_specs=(tok, lab, lab, tok, vec, vec, mat, vec, mat, vec, vec, vec, mat, vec, mat, vec),
        out_specs=(tok, tok, vec, vec, mat, vec, mat, vec, vec, vec, mat, vec, mat, vec),
        check_vma=False,
    )
```

```python
import jax
import jax.numpy as jnp
from jax import lax
from jax.experimental import pallas as pl
from jax.experimental.pallas import tpu as pltpu
from jax.sharding import PartitionSpec as P

D = 1024
HEAD_DIM = 64
FF = 4096
EPS = 1e-05
NEG = -1e30
SCALE = 0.125
BF = jnp.bfloat16
F32 = jnp.float32
LANES = 128


def xor_pairs(count, mask):
    return [(i, i ^ mask) for i in range(count)]


class Net:
    def __init__(self):
        self.n_s = lax.axis_size("seq")
        self.n_f = lax.axis_size("fsdp")
        self.n_p = self.n_f // 2
        self.s = lax.axis_index("seq")
        self.f = lax.axis_index("fsdp")
        self.p = self.f // 2
        self.c = self.f % 2
        self.place = jnp.stack([self.p, self.c]).astype(jnp.int32)

    def pairs(self):
        n = self.n_f
        return [
            (s * n + f, (f // 2) * n + 2 * ((f // 2) ^ s) + f % 2) for s in range(self.n_s) for f in range(n)
        ]

    def to_planes(self, v):
        return lax.ppermute(v, ("seq", "fsdp"), self.pairs())

    def from_planes(self, v):
        return lax.ppermute(v, ("seq", "fsdp"), [(b, a) for a, b in self.pairs()])

    def chip(self, v, j):
        return lax.ppermute(v, "fsdp", xor_pairs(self.n_f, 2 * j))

    def core(self, v):
        return lax.ppermute(v, "fsdp", xor_pairs(self.n_f, 1))

    def gather(self, v):
        return [v] + [self.chip(v, j) for j in range(1, self.n_p)]

    def exchange(self, blocks):
        return [blocks[0]] + [self.chip(blocks[j], j) for j in range(1, self.n_p)]


def fence(values):
    return lax.optimization_barrier(values)


def block(v, index, size, axis):
    return lax.dynamic_slice_in_dim(v, index * size, size, axis=axis)


IN_VMEM = pl.BlockSpec(memory_space=pltpu.VMEM)
IN_SMEM = pl.BlockSpec(memory_space=pltpu.SMEM)
IN_ANY = pl.BlockSpec(memory_space=pl.ANY)


def run(name, body, outs, ins, place=None, scratch=(), flops=0, ins_at=IN_VMEM):
    specs = [ins_at] * len(ins)
    if place is not None:
        specs = [IN_SMEM] + specs
        ins = [place, *ins]
    moved = sum(v.size * v.dtype.itemsize for v in ins)
    return pl.pallas_call(
        body,
        out_shape=[jax.ShapeDtypeStruct(shape, dtype) for shape, dtype in outs],
        in_specs=specs,
        out_specs=[IN_VMEM] * len(outs),
        scratch_shapes=list(scratch),
        compiler_params=pltpu.CompilerParams(vmem_limit_bytes=16 << 20),
        cost_estimate=pl.CostEstimate(flops=flops, bytes_accessed=moved, transcendentals=0),
        name=name,
    )(*ins)


def dot(a, b):
    return jnp.dot(a, b, preferred_element_type=F32)


def dot_nt(a, b):
    return lax.dot_general(a, b, (((1,), (1,)), ((), ())), preferred_element_type=F32)


def dot_tn(a, b):
    return lax.dot_general(a, b, (((0,), (0,)), ((), ())), preferred_element_type=F32)


def tile(i, size):
    return pl.ds(pl.multiple_of(i * size, size), size)


def join_weights(net, own, other, own_pair, other_pair):
    n_p = net.n_p
    rows, width = D // net.n_f, own[0].shape[1]
    half, depth = own_pair.shape
    count = 2 * n_p + 2

    def body(place, *refs):
        p, c = place[0], place[1]
        whole, pair, sems = refs[count:]
        copies = []
        for j in range(n_p):
            at = (p ^ j) * 2
            copies.append((refs[j].at[0:rows], whole.at[tile(at + c, rows)]))
            copies.append((refs[n_p + j].at[0:rows], whole.at[tile(at + 1 - c, rows)]))
        copies.append((refs[2 * n_p], pair.at[tile(c, half)]))
        copies.append((refs[2 * n_p + 1], pair.at[tile(1 - c, half)]))
        copies = [pltpu.make_async_copy(src, dst, sems.at[k]) for k, (src, dst) in enumerate(copies)]
        for copy in copies:
            copy.start()
        for copy in copies:
            copy.wait()

    outs = [((2 * n_p * rows, width), BF), ((2 * half, depth), BF)]
    ins = [*own, *other, own_pair, other_pair]
    return run("join_weights", body, outs, ins, net.place, [pltpu.SemaphoreType.DMA((count,))], ins_at=IN_ANY)


def cut_columns(net, weight, layer, more):
    n_p = net.n_p
    cw = D // n_p
    rows = weight.shape[1]
    extra = 0 if more is None else more.shape[0]
    count = n_p * (3 + (extra > 0))

    def body(place, weight_ref, *refs):
        p = place[0]
        outs, sems = refs[-n_p - 1 : -1], refs[-1]
        copies = []
        for j in range(n_p):
            for i in range(3):
                cols = tile(i * n_p + (p ^ j), cw)
                to = outs[j].at[0:rows, i * cw : (i + 1) * cw]
                copies.append((weight_ref.at[layer, :, cols], to))
            if extra:
                copies.append((refs[0], outs[j].at[rows : rows + extra]))
        copies = [pltpu.make_async_copy(src, dst, sems.at[k]) for k, (src, dst) in enumerate(copies)]
        for copy in copies:
            copy.start()
        for copy in copies:
            copy.wait()

    outs = [((rows + extra, 3 * cw), BF)] * n_p
    ins = [weight] + ([more] if extra else [])
    scratch = [pltpu.SemaphoreType.DMA((count,))]
    return run("cut_columns", body, outs, ins, net.place, scratch, ins_at=IN_ANY)


def join_vectors(net, layers, pieces, sizes):
    n_p = net.n_p
    width = pieces[0].shape[1]
    starts = [sum(sizes[:i]) for i in range(len(sizes))]
    first_row = D // net.n_f

    def body(place, *refs):
        p, c = place[0], place[1]
        ins, outs = refs[:n_p], refs[n_p:]
        for j in range(n_p):
            low = ins[j][first_row : first_row + 16, :].astype(F32)
            for layer in range(layers):
                for half in range(2):
                    row = layer * 2 + half
                    own = low[row : row + 1, :]
                    other = low[2 * layers + row : 2 * layers + row + 1, :]
                    first = jnp.where(c == 0, own, other)
                    second = jnp.where(c == 0, other, own)
                    for k, (at, size) in enumerate(zip(starts, sizes)):
                        if at // width != half:
                            continue
                        cols = slice(at - half * width, at - half * width + size)
                        both = jnp.concatenate([first[:, cols], second[:, cols]], axis=1)
                        outs[k][layer : layer + 1, tile(p ^ j, 2 * size)] = both

    outs = [((layers, 2 * n_p * size), F32) for size in sizes]
    return run("join_vectors", body, outs, pieces, net.place)


def first_norm(tokens, more, gain, shift):
    rows = tokens.shape[0] - more

    def body(token_ref, gain_ref, shift_ref, out, low):
        hidden = token_ref[0:rows, :].astype(F32)
        normed, _ = norm_rows(hidden)
        out[...] = hidden
        low[0:rows, :] = (normed * gain_ref[0:1, :] + shift_ref[0:1, :]).astype(BF)
        low[rows:, :] = token_ref[rows:, :]

    outs = [((rows, D), F32), (tokens.shape, BF)]
    return run("first_norm", body, outs, [tokens, gain, shift])


def norm_rows(hidden):
    centred = hidden - jnp.mean(hidden, axis=-1, keepdims=True)
    spread = jnp.mean(centred * centred, axis=-1, keepdims=True)
    inverse = lax.rsqrt(spread + EPS)
    return centred * inverse, inverse


def add_and_norm(layer, hidden, parts, bias, norm):
    rows = hidden.shape[0]
    count = len(parts)

    def body(*refs):
        total = refs[0][...].astype(F32)
        for part in refs[1 : 1 + count]:
            total = total + part[...].astype(F32)
        at = 1 + count
        if bias is not None:
            total = total + refs[at][layer : layer + 1, :]
            at += 1
        if norm is None:
            refs[at][...] = total.astype(BF)
            return
        gain, shift, out, low = refs[at : at + 4]
        normed, _ = norm_rows(total)
        row = slice(norm[0], norm[0] + 1)
        out[...] = total
        low[...] = (normed * gain[row, :] + shift[row, :]).astype(BF)

    ins = [hidden, *parts] + ([] if bias is None else [bias]) + ([] if norm is None else list(norm[1:]))
    outs = [((rows, D), BF)] if norm is None else [((rows, D), F32), ((rows, D), BF)]
    return run("add_and_norm", body, outs, ins)


def norm_back(layer, grad, hidden, parts, gain):
    rows = hidden.shape[0]
    count = len(parts)

    def body(grad_ref, hidden_ref, gain_ref, *refs):
        total = refs[0][...].astype(F32)
        for part in refs[1:count]:
            total = total + part[...].astype(F32)
        out, low, sums = refs[count:]
        normed, inverse = norm_rows(hidden_ref[...])
        scaled = total * gain_ref[layer : layer + 1, :]
        one = jnp.mean(scaled, axis=-1, keepdims=True)
        two = jnp.mean(scaled * normed, axis=-1, keepdims=True)
        result = grad_ref[...].astype(F32) + inverse * (scaled - one - normed * two)
        rounded = result.astype(BF)
        out[...] = result
        low[...] = rounded
        sums[0:1, :] = jnp.sum(total * normed, axis=0, keepdims=True)
        sums[1:2, :] = jnp.sum(total, axis=0, keepdims=True)
        sums[2:3, :] = jnp.sum(rounded.astype(F32), axis=0, keepdims=True)

    outs = [((rows, D), F32), ((rows, D), BF), ((3, D), F32)]
    return run("norm_back", body, outs, [grad, hidden, gain, *parts])


def gather_rows(blocks, scratch):
    rows = scratch.shape[0] // len(blocks)
    for j, ref in enumerate(blocks):
        scratch[j * rows : (j + 1) * rows, :] = ref[0:rows, :]


def allowed_pairs(code_col, code_row):
    same = (code_col >> 1) == (code_row >> 1)
    return same & (((code_col & 1) == 0) | ((code_row & 1) == 1))


def head_lanes(shape, head, axis):
    lane = lax.broadcasted_iota(jnp.int32, shape, axis)
    return (lane < HEAD_DIM) if head == 0 else (lane >= HEAD_DIM)


def keep_head(v, head, axis):
    return jnp.where(head_lanes(v.shape, head, axis), v, jnp.zeros_like(v))


def probs_by_key(k2, q2, allowed, head):
    scores = dot_nt(keep_head(k2, head, 1), q2) * SCALE
    scores = jnp.where(allowed, scores, NEG)
    powers = jnp.exp(scores - jnp.max(scores, axis=0, keepdims=True))
    return powers * (1.0 / jnp.sum(powers, axis=0, keepdims=True))


Q_TILE = 256


def attend(net, layer, rows, blocks, weight, bias, codes, proj):
    n_p = net.n_p
    tokens = n_p * rows
    cw = D // n_p
    n_codes = 0 if codes is None else 2

    def body(place, *refs):
        weight_ref, bias_ref, proj_ref = refs[n_p : n_p + 3]
        row_ref, col_ref = refs[n_p + 3 : n_p + 5]
        outs = refs[n_p + 5 : 2 * n_p + 5]
        qkv, attended, a, vt = refs[2 * n_p + 5 :]
        p = place[0]
        gather_rows(refs[:n_p], a)
        if codes is None:
            eye = lax.broadcasted_iota(jnp.int32, (rows, rows), 0) == lax.broadcasted_iota(
                jnp.int32, (rows, rows), 1
            )
            for j in range(n_p):
                line = refs[j][rows : rows + 1, 0:rows].astype(F32)
                row_ref[:, j * rows : (j + 1) * rows] = line.astype(jnp.int32)
                column = jnp.sum(jnp.where(eye, line, 0.0), axis=1, keepdims=True)
                col_ref[j * rows : (j + 1) * rows, :] = column.astype(jnp.int32)
        for i in range(3):
            out = dot(a[...], weight_ref[:, i * cw : (i + 1) * cw])
            if i == 0:
                out = out + bias_ref[layer : layer + 1, tile(p, cw)]
            if i == 2:
                out = out + bias_ref[layer : layer + 1, tile(p + n_p, cw)]
            qkv[:, i * cw : (i + 1) * cw] = out.astype(BF)
        vt[...] = jnp.transpose(qkv[:, 2 * cw : 3 * cw].astype(F32)).astype(BF)

        @pl.loop(0, tokens // Q_TILE)
        def _(t):
            here = tile(t, Q_TILE)
            allowed = allowed_pairs(col_ref[...], row_ref[:, here])
            for pair in range(cw // LANES):
                lanes = slice(pair * LANES, (pair + 1) * LANES)
                q2 = qkv[here, lanes]
                k2 = qkv[:, cw + pair * LANES : cw + (pair + 1) * LANES]
                total = None
                for head in range(2):
                    probs = probs_by_key(k2, q2, allowed, head).astype(BF)
                    part = dot(keep_head(vt[lanes, :], head, 0), probs)
                    total = part if total is None else total + part
                attended[here, lanes] = jnp.transpose(total).astype(BF)

        for j in range(n_p):
            outs[j][...] = dot(attended[j * rows : (j + 1) * rows, :], proj_ref[...]).astype(BF)

    outs = [((rows, D), BF)] * n_p + [((tokens, 3 * cw), BF), ((tokens, cw), BF)]
    scratch = [pltpu.VMEM((tokens, D), BF), pltpu.VMEM((cw, tokens), BF)]
    ins = [*blocks, weight, bias, proj] + ([] if codes is None else list(codes))
    if codes is None:
        outs = [((1, tokens), jnp.int32), ((tokens, 1), jnp.int32)] + outs
    got = run("attend", body, outs, ins, net.place, scratch, flops=2 * tokens * D * 4 * cw)
    if codes is None:
        codes, got = got[:2], got[2:]
    return got[:n_p], got[n_p], got[n_p + 1], codes


def attend_back(net, blocks, proj, qkv, codes, weight):
    n_p = net.n_p
    rows = blocks[0].shape[0]
    tokens = n_p * rows
    cw = D // n_p

    def body(*refs):
        proj_ref, qkv_ref, row_ref, col_ref, weight_ref = refs[n_p : n_p + 5]
        outs = refs[n_p + 5 : 2 * n_p + 5]
        dqkv, sums, do, kt, dk, dv = refs[2 * n_p + 5 :]
        for j in range(n_p):
            do[j * rows : (j + 1) * rows, :] = dot_nt(refs[j][...], proj_ref[...]).astype(BF)
        kt[...] = jnp.transpose(qkv_ref[:, cw : 2 * cw].astype(F32)).astype(BF)
        dk[...] = jnp.zeros_like(dk)
        dv[...] = jnp.zeros_like(dv)

        @pl.loop(0, tokens // Q_TILE)
        def _(t):
            here = tile(t, Q_TILE)
            allowed = allowed_pairs(col_ref[...], row_ref[:, here])
            for pair in range(cw // LANES):
                lanes = slice(pair * LANES, (pair + 1) * LANES)
                q2 = qkv_ref[here, lanes]
                k2 = qkv_ref[:, cw + pair * LANES : cw + (pair + 1) * LANES]
                v2 = qkv_ref[:, 2 * cw + pair * LANES : 2 * cw + (pair + 1) * LANES]
                do2 = do[here, lanes]
                total = None
                for head in range(2):
                    probs = probs_by_key(k2, q2, allowed, head)
                    dp = dot_nt(keep_head(v2, head, 1), do2)
                    mean = jnp.sum(probs * dp, axis=0, keepdims=True)
                    ds = (probs * (dp - mean)).astype(BF)
                    dv[:, lanes] += dot(probs.astype(BF), keep_head(do2, head, 1))
                    dk[:, lanes] += dot(ds, keep_head(q2, head, 1))
                    part = dot(keep_head(kt[lanes, :], head, 0), ds)
                    total = part if total is None else total + part
                dqkv[here, lanes] = (jnp.transpose(total) * SCALE).astype(BF)

        dqkv[:, cw : 2 * cw] = (dk[...] * SCALE).astype(BF)
        dqkv[:, 2 * cw :] = dv[...].astype(BF)
        sums[...] = jnp.sum(dqkv[...].astype(F32), axis=0, keepdims=True)
        for j in range(n_p):
            outs[j][...] = dot_nt(dqkv[j * rows : (j + 1) * rows, :], weight_ref[...]).astype(BF)

    outs = [((rows, D), BF)] * n_p + [((tokens, 3 * cw), BF), ((1, 3 * cw), F32)]
    scratch = [
        pltpu.VMEM((tokens, cw), BF),
        pltpu.VMEM((cw, tokens), BF),
        pltpu.VMEM((tokens, cw), F32),
        pltpu.VMEM((tokens, cw), F32),
    ]
    ins = [*blocks, proj, qkv, *codes, weight]
    got = run("attend_back", body, outs, ins, None, scratch, flops=2 * tokens * D * 8 * cw)
    return got[:n_p], got[n_p], got[n_p + 1]


F_TILE = 256


def feed_forward(net, layer, blocks, up, bias, down):
    n_p = net.n_p
    rows = blocks[0].shape[0]
    tokens = n_p * rows
    fw = FF // n_p

    def body(place, *refs):
        up_ref, bias_ref, down_ref = refs[n_p : n_p + 3]
        outs = refs[n_p + 3 : 2 * n_p + 3]
        z_ref, slope_ref, a_ref = refs[2 * n_p + 3 :]
        p = place[0]
        gather_rows(refs[:n_p], a_ref)

        @pl.loop(0, fw // F_TILE)
        def _(t):
            cols = tile(t, F_TILE)
            there = pl.ds(pl.multiple_of(p * fw + t * F_TILE, F_TILE), F_TILE)
            u = dot(a_ref[...], up_ref[:, cols]) + bias_ref[layer : layer + 1, there]
            phi = 0.5 * (1.0 + lax.erf(u * 0.7071067811865476))
            z_ref[:, cols] = (u * phi).astype(BF)
            slope_ref[:, cols] = phi + u * (jnp.exp(-0.5 * u * u) * 0.3989422804014327)

        for j in range(n_p):
            outs[j][...] = dot(z_ref[j * rows : (j + 1) * rows, :], down_ref[...]).astype(BF)

    outs = [((rows, D), BF)] * n_p + [((tokens, fw), BF), ((tokens, fw), F32)]
    scratch = [pltpu.VMEM((tokens, D), BF)]
    ins = [*blocks, up, bias, down]
    got = run("feed_forward", body, outs, ins, net.place, scratch, flops=4 * tokens * D * fw)
    return got[:n_p], got[n_p], got[n_p + 1]


def feed_back(net, blocks, down, slope, up):
    n_p = net.n_p
    rows = blocks[0].shape[0]
    tokens = n_p * rows
    fw = FF // n_p

    def body(*refs):
        down_ref, slope_ref, up_ref = refs[n_p : n_p + 3]
        outs = refs[n_p + 3 : 2 * n_p + 3]
        du_ref, sums, dm = refs[2 * n_p + 3 :]
        gather_rows(refs[:n_p], dm)

        @pl.loop(0, fw // F_TILE)
        def _(t):
            cols = tile(t, F_TILE)
            dz = dot_nt(dm[...], down_ref[cols, :])
            du = (dz * slope_ref[:, cols]).astype(BF)
            du_ref[:, cols] = du
            sums[:, cols] = jnp.sum(du.astype(F32), axis=0, keepdims=True)

        for j in range(n_p):
            outs[j][...] = dot_nt(du_ref[j * rows : (j + 1) * rows, :], up_ref[...]).astype(BF)

    outs = [((rows, D), BF)] * n_p + [((tokens, fw), BF), ((1, fw), F32)]
    scratch = [pltpu.VMEM((tokens, D), BF)]
    ins = [*blocks, down, slope, up]
    got = run("feed_back", body, outs, ins, None, scratch, flops=4 * tokens * D * fw)
    return got[:n_p], got[n_p], got[n_p + 1]


def by_turns(a, b, parts, c, keep, send, cols):
    rows = a.shape[1] // (2 * parts)
    for i in range(parts):
        both = dot_tn(a[:, i * 2 * rows : (i + 1) * 2 * rows], b).astype(BF)
        first, second = both[:rows], both[rows:]
        here = slice(i * rows, (i + 1) * rows)
        keep[here, cols] = jnp.where(c == 0, first, second)
        send[here, cols] = jnp.where(c == 0, second, first)


def weight_grad(net, left, right, parts):
    n_l, n_r = len(left), len(right)
    tokens = sum(v.shape[0] for v in right)
    m, n = left[0].shape[1], right[0].shape[1]

    def body(place, *refs):
        keep, send, a, b = refs[n_l + n_r :]
        gather_rows(refs[:n_l], a)
        gather_rows(refs[n_l : n_l + n_r], b)
        by_turns(a[...], b[...], parts, place[1], keep, send, slice(0, n))

    outs = [((m // 2, n), BF)] * 2
    scratch = [pltpu.VMEM((tokens, m), BF), pltpu.VMEM((tokens, n), BF)]
    return run("weight_grad", body, outs, [*left, *right], net.place, scratch, flops=2 * tokens * m * n)


def attend_weight_grad(net, a1, dqkv, attended, dy):
    n_p = net.n_p
    tokens, width = dqkv.shape
    cw = D // n_p
    rows = D // net.n_f

    def body(place, *refs):
        dqkv_ref, attended_ref = refs[n_p : n_p + 2]
        keep, send, a, b, low = refs[2 * n_p + 2 :]
        c = place[1]
        gather_rows(refs[:n_p], a)
        by_turns(a[...], dqkv_ref[...], n_p, c, keep, send, slice(0, width))
        gather_rows(refs[n_p + 2 : 2 * n_p + 2], b)
        low[...] = dot_tn(attended_ref[...], b[...]).astype(BF)
        for i in range(n_p):
            first = low[0:rows, i * cw : (i + 1) * cw]
            second = low[rows : 2 * rows, i * cw : (i + 1) * cw]
            keep[i * rows : (i + 1) * rows, width:] = jnp.where(c == 0, first, second)
            send[i * rows : (i + 1) * rows, width:] = jnp.where(c == 0, second, first)

    outs = [((D // 2, width + cw), BF)] * 2
    scratch = [pltpu.VMEM((tokens, D), BF), pltpu.VMEM((tokens, D), BF), pltpu.VMEM((cw, D), BF)]
    flops = 2 * tokens * D * (width + cw)
    ins = [*a1, dqkv, attended, *dy]
    return run("attend_weight_grad", body, outs, ins, net.place, scratch, flops=flops)


def add_low(a, b):
    def body(a_ref, b_ref, out):
        out[...] = (a_ref[...].astype(F32) + b_ref[...].astype(F32)).astype(BF)

    return run("add_low", body, [(a.shape, BF)], [a, b])[0]


def take_if(here, a, b):
    def body(flag, a_ref, b_ref, out):
        @pl.when(flag[0] != 0)
        def _():
            out[...] = a_ref[...]

        @pl.when(flag[0] == 0)
        def _():
            out[...] = b_ref[...]

    return run("take_if", body, [(a.shape, BF)], [a, b], here.astype(jnp.int32).reshape(1))[0]


class Chunk:
    def __init__(self, net, value):
        self.net = net
        self.value = value
        self.got = None
        self.step = 0

    @property
    def done(self):
        return self.step == self.net.n_s - 1

    def start(self):
        if self.done:
            return
        n, k = self.net.n_s, self.step + 1
        half = n // 2
        if k < half:
            pairs = [(k - 1, k), (n - k, n - k - 1)]
        elif k == half:
            pairs = [(half - 1, half), (half, half - 1)]
        else:
            k = n - 1 - k
            pairs = [(k + 1, k), (n - 2 - k, n - 1 - k)]
        self.got = lax.ppermute(self.value, "seq", pairs)

    def finish(self):
        if self.done:
            return
        n, k = self.net.n_s, self.step + 1
        if k <= n // 2:
            self.value = add_low(self.value, self.got)
        else:
            k = n - 1 - k
            here = (self.net.s == k) | (self.net.s == n - 1 - k)
            self.value = take_if(here, self.got, self.value)
        self.got = None
        self.step += 1


def start(*chunks):
    for chunk in chunks:
        chunk.start()


def finish(values, *chunks):
    values, side = fence((values, [(c.value, c.got) for c in chunks]))
    for c, (value, got) in zip(chunks, side):
        c.value, c.got = value, got
        c.finish()
    return values


def pack_vectors(net, layers, vectors, sizes, singles):
    n_p = net.n_p
    starts = [sum(sizes[:i]) for i in range(len(sizes))]
    flat = [v for of_layer in vectors for v in of_layer]
    count = len(sizes)

    def body(place, *refs):
        p, c = place[0], place[1]
        keep, send = refs[-2], refs[-1]
        keep[...] = jnp.zeros_like(keep)
        send[...] = jnp.zeros_like(send)
        for layer in range(layers):
            for k, (at, size) in enumerate(zip(starts, sizes)):
                ref = refs[layer * count + k]
                cols = slice(at, at + size)
                if singles[k] == "chip":
                    first, second = ref[:, :size], ref[:, size:]
                    keep[p, layer : layer + 1, cols] = jnp.where(c == 0, first, second)
                    send[p, layer : layer + 1, cols] = jnp.where(c == 0, second, first)
                elif singles[k] == "heads":
                    mine = (p % 2) == c
                    for turn, value in enumerate((ref[:, :size], ref[:, 2 * size :])):
                        to = p // 2 + turn * (n_p // 2)
                        keep[to, layer : layer + 1, cols] = jnp.where(mine, value, 0.0)
                        send[to, layer : layer + 1, cols] = jnp.where(mine, 0.0, value)
                else:
                    for i in range(n_p):
                        first = ref[:, 2 * i * size : (2 * i + 1) * size]
                        second = ref[:, (2 * i + 1) * size : (2 * i + 2) * size]
                        keep[i, layer : layer + 1, cols] = jnp.where(c == 0, first, second)
                        send[i, layer : layer + 1, cols] = jnp.where(c == 0, second, first)

    outs = [((n_p, layers, sum(sizes)), F32)] * 2
    return run("pack_vectors", body, outs, flat, net.place)


def write_layer(net, layer, layers, before, down, proj, up, qkv):
    n_p = net.n_p
    rows = up[0].shape[0]
    cw, fw = D // n_p, FF // n_p
    n_in = 1 + 3 * n_p
    skip = 0 if before is None else 4
    steps = rows // 16
    while steps > 4:
        steps //= 2
    part = rows // steps
    down_part = down.shape[0] // steps

    def body(place, *refs):
        p = place[0]
        down_ref = refs[0]
        projs, ups, qkvs = refs[1 : 1 + n_p], refs[1 + n_p : 1 + 2 * n_p], refs[1 + 2 * n_p : n_in]
        qkv_out, proj_out, up_out, down_out = refs[n_in + skip :]
        down_out[0] = down_ref[...].astype(F32)
        for j in range(n_p):
            proj_out[0, :, j * cw : (j + 1) * cw] = projs[j][...].astype(F32)
            up_out[0, :, tile(p ^ j, fw)] = ups[j][...].astype(F32)
            for i in range(3):
                to = i * n_p + (p ^ j)
                qkv_out[0, :, tile(to, cw)] = qkvs[j][:, i * cw : (i + 1) * cw].astype(F32)

    def of_rows(v, size):
        return pl.BlockSpec((size, v.shape[1]), lambda i: (i, 0))

    def of_piece(j):
        return pl.BlockSpec((part, cw), lambda i: (j * steps + i, 0))

    ins = [down, *[proj] * n_p, *up, *qkv]
    specs = [IN_SMEM, of_rows(down, down_part)] + [of_piece(j) for j in range(n_p)]
    specs += [of_rows(v, part) for v in [*up, *qkv]]
    aliases = {}
    if before is not None:
        aliases = {1 + n_in + k: k for k in range(4)}
        specs += [IN_ANY] * 4
        ins = ins + list(before)
    shapes = [(rows, 3 * D), (rows, D), (rows, FF), down.shape]
    sizes = [part, part, part, down_part]
    return pl.pallas_call(
        body,
        grid=(steps,),
        out_shape=[jax.ShapeDtypeStruct((layers, *shape), F32) for shape in shapes],
        in_specs=specs,
        out_specs=[
            pl.BlockSpec((1, size, shape[1]), lambda i: (layer, i, 0)) for size, shape in zip(sizes, shapes)
        ],
        input_output_aliases=aliases,
        compiler_params=pltpu.CompilerParams(vmem_limit_bytes=16 << 20),
        name="write_layer",
    )(net.place, *ins)


def on_device(
    tokens,
    scene_ids,
    token_kind,
    out_grad,
    first_gain,
    first_shift,
    qkv_weight,
    qv_bias,
    proj_weight,
    proj_bias,
    second_gain,
    second_shift,
    up_weight,
    up_bias,
    down_weight,
    down_bias,
):
    net = Net()
    n_p = net.n_p
    layers = qkv_weight.shape[0]
    rows = tokens.shape[1]
    cw = D // n_p
    fw = FF // n_p

    def up_send(weight, layer):
        shape = (1, weight.shape[1], fw)
        return net.exchange(
            [lax.dynamic_slice(weight, (layer, 0, (net.p ^ j) * fw), shape)[0] for j in range(n_p)]
        )

    def core_all(values):
        return [net.core(v) for v in values]

    def by_chip(v, size):
        return [block(v, net.p ^ j, size, 0) for j in range(n_p)]

    code = (scene_ids[0] * 2 + token_kind[0]).astype(BF).reshape(1, -1)
    code = jnp.pad(code, ((0, 15), (0, D - code.shape[1])))
    tok = net.to_planes(jnp.concatenate([tokens[0], code], axis=0))
    small_in = [first_gain, first_shift, qv_bias, proj_bias, second_gain, second_shift, up_bias, down_bias]
    sizes = [v.shape[1] for v in small_in]
    small = jnp.concatenate(small_in, axis=1)
    small = jnp.concatenate([small, net.core(small)], axis=0).reshape(-1, 3 * cw)
    small = jnp.pad(small, ((0, 16 - small.shape[0]), (0, 0)))
    qkv_own = net.exchange(cut_columns(net, qkv_weight, 0, small))
    tok, qkv_own, later = fence((tok, qkv_own, (qkv_weight, proj_weight, up_weight, down_weight, out_grad)))
    qkv_weight, proj_weight, up_weight, down_weight, out_grad = later
    vectors = join_vectors(net, layers, qkv_own, sizes)
    gain1, shift1, qv_b, proj_b, gain2, shift2, up_b, down_b = vectors

    weights = []
    kept = []
    dm = None
    codes = None
    proj_own = proj_weight[0]
    hidden, a1 = first_norm(tok, 16, gain1, shift1)
    qkv_other, proj_other = core_all(qkv_own), net.core(proj_own)
    for layer in range(layers):
        last = layer == layers - 1
        a1g = net.gather(a1)
        qkv_w, proj_w = join_weights(net, qkv_own, qkv_other, proj_own, proj_other)
        a1g, qkv_w, proj_w = fence((a1g, qkv_w, proj_w))
        y, qkv, og, codes = attend(net, layer, rows, a1g, qkv_w, qv_b, codes, proj_w)
        up_own = up_send(up_weight, layer)
        y, up_own = fence((y, up_own))
        parts = net.exchange(y)
        down_own = down_weight[layer]
        up_other, down_other = core_all(up_own), net.core(down_own)
        parts, up_other, down_other = fence((parts, up_other, down_other))
        h2, a2 = add_and_norm(layer, hidden, parts, proj_b, (layer, gain2, shift2))
        a2g = net.gather(a2)
        up_w, down_w = join_weights(net, up_own, up_other, down_own, down_other)
        if last:
            dmg = net.gather(dm)
            a2g, up_w, down_w, dmg = fence((a2g, up_w, down_w, dmg))
        else:
            a2g, up_w, down_w = fence((a2g, up_w, down_w))
        y, z, slope = feed_forward(net, layer, a2g, up_w, up_b, down_w)
        kept.append((hidden, a1g, qkv, og, h2, a2g, z, slope))
        weights.append((qkv_w, proj_w, up_w, down_w))
        if last:
            last_y = y
            break
        qkv_own = net.exchange(cut_columns(net, qkv_weight, layer + 1, None))
        y, qkv_own = fence((y, qkv_own))
        parts = net.exchange(y)
        proj_own = proj_weight[layer + 1]
        qkv_other, proj_other = core_all(qkv_own), net.core(proj_own)
        if layer == layers - 2:
            dm = net.to_planes(out_grad[0])
            parts, qkv_other, proj_other, dm = fence((parts, qkv_other, proj_other, dm))
        else:
            parts, qkv_other, proj_other = fence((parts, qkv_other, proj_other))
        hidden, a1 = add_and_norm(layer, h2, parts, down_b, (layer + 1, gain1, shift1))

    sums = [None] * layers
    small_grads = [None] * layers
    grad = dm
    down_b_grad = jnp.sum(dm.astype(F32), axis=0, keepdims=True)
    running = []
    waiting = []

    def run_on():
        running.extend(waiting)
        waiting.clear()
        running[:] = [c for c in running if not c.done]
        start(*running)
        return list(running)

    for layer in reversed(range(layers)):
        last = layer == layers - 1
        qkv_w, proj_w, up_w, down_w = weights[layer]
        h1, a1g, qkv, og, h2, a2g, z, slope = kept[layer]
        down_k, down_s = weight_grad(net, [z], dmg, 1)
        da2, du, up_b_grad = feed_back(net, dmg, down_w, slope, up_w)
        down_s = net.core(down_s)
        da2, du, down_k, down_s = finish((da2, du, down_k, down_s), *([] if last else moved))
        down_g = Chunk(net, add_low(down_k, down_s))
        waiting.append(down_g)
        moved = run_on()
        parts = net.exchange(da2)
        up_k, up_s = weight_grad(net, a2g, [du], n_p)
        up_s = net.core(up_s)
        parts, up_k, up_s = fence((parts, up_k, up_s))
        dh2, dy, sums2 = norm_back(layer, grad, h2, parts, gain2)
        dyg = net.gather(dy)
        up_g = Chunk(net, add_low(up_k, up_s))
        dyg = finish(dyg, *moved)
        waiting.append(up_g)
        moved = run_on()
        da1, dqkv, qkv_b_grad = attend_back(net, dyg, proj_w, qkv, codes, qkv_w)
        if last:
            da1, dqkv = fence((da1, dqkv))
        else:
            last_parts = net.exchange(last_y)
            da1, dqkv, last_parts = fence((da1, dqkv, last_parts))
        parts = net.exchange(da1)
        qkv_k, qkv_s = attend_weight_grad(net, a1g, dqkv, og, dyg)
        qkv_s = net.core(qkv_s)
        parts, qkv_k, qkv_s = finish((parts, qkv_k, qkv_s), *moved)
        grad, dm, sums1 = norm_back(layer, dh2, h1, parts, gain1)
        qkv_g = add_low(qkv_k, qkv_s)
        small_grads[layer] = [
            sums1[0:1],
            sums1[1:2],
            qkv_b_grad,
            sums2[2:3],
            sums2[0:1],
            sums2[1:2],
            up_b_grad,
            down_b_grad,
        ]
        sums[layer] = (down_g, up_g)
        if not last:
            break
        attend_g = Chunk(net, qkv_g)
        sums[layer] += (attend_g,)
        waiting.append(attend_g)
        moved = run_on()
        dmg = net.gather(dm)
        down_b_grad = sums1[2:3]
        dmg, grad = fence((dmg, grad))

    moved = run_on()
    (sent_out,) = add_and_norm(layers - 1, kept[-1][4], last_parts, down_b, None)
    input_grad = net.from_planes(dm)
    kinds = [None, None, "heads", None, None, None, "chip", None]
    keep, send = pack_vectors(net, layers, small_grads, sizes, kinds)
    small = keep + net.core(send)
    pieces = net.exchange(by_chip(qkv_g[:, : 3 * cw], D // net.n_f))
    pieces.append(qkv_g[:, 3 * cw :])
    input_grad, small, pieces, sent_out = finish((input_grad, small, pieces, sent_out), *moved)
    pieces = [Chunk(net, v) for v in pieces]
    sent_out = net.from_planes(sent_out)
    got = net.exchange([v[0] for v in by_chip(small, 1)])
    small = got[0]
    for part in got[1:]:
        small = small + part

    queue = [c for c in running if not c.done] + [pieces[0], pieces[-1], *pieces[1:-1]]
    bit = 1
    while not all(c.done for c in queue):
        moved = []
        for c in queue:
            if not c.done and c.step not in [m.step for m in moved]:
                moved.append(c)
        start(*moved)
        if bit < net.n_s:
            small = small + lax.ppermute(small, "seq", xor_pairs(net.n_s, bit))
            bit *= 2
        sent_out, small = finish((sent_out, small), *moved)

    out = None
    for layer in reversed(range(layers)):
        down_g, up_g = sums[layer][:2]
        up_pieces = net.exchange(by_chip(up_g.value, D // net.n_f))
        if len(sums[layer]) > 2:
            whole = sums[layer][2].value
            qkv_pieces = net.exchange(by_chip(whole[:, : 3 * cw], D // net.n_f))
            proj_g = whole[:, 3 * cw :]
        else:
            qkv_pieces = [c.value for c in pieces[:-1]]
            proj_g = pieces[-1].value
        out = write_layer(net, layer, layers, out, down_g.value, proj_g, up_pieces, qkv_pieces)
    small_out = []
    at = 0
    for size in sizes:
        small_out.append(small[:, at : at + size])
        at += size
    return (
        sent_out.astype(F32)[None],
        input_grad.astype(F32)[None],
        small_out[0],
        small_out[1],
        out[0],
        small_out[2],
        out[1],
        small_out[3],
        small_out[4],
        small_out[5],
        out[2],
        small_out[6],
        out[3],
        small_out[7],
    )


def solution(mesh):
    tok = P("fsdp", "seq", None)
    lab = P("fsdp", "seq")
    vec = P(None, "fsdp")
    mat = P(None, "fsdp", None)
    return jax.shard_map(
        on_device,
        mesh=mesh,
        in_specs=(tok, lab, lab, tok, vec, vec, mat, vec, mat, vec, vec, vec, mat, vec, mat, vec),
        out_specs=(tok, tok, vec, vec, mat, vec, mat, vec, vec, vec, mat, vec, mat, vec),
        check_vma=False,
    )
```

```python
import jax
import jax.numpy as jnp
from jax import lax
from jax.experimental import pallas as pl
from jax.experimental.pallas import tpu as pltpu
from jax.sharding import PartitionSpec as P

D = 1024
HEAD_DIM = 64
FF = 4096
EPS = 1e-05
NEG = -1e30
SCALE = 0.125
BF = jnp.bfloat16
F32 = jnp.float32
LANES = 128


def xor_pairs(count, mask):
    return [(i, i ^ mask) for i in range(count)]


class Net:
    def __init__(self):
        self.n_s = lax.axis_size("seq")
        self.n_f = lax.axis_size("fsdp")
        self.n_p = self.n_f // 2
        self.s = lax.axis_index("seq")
        self.f = lax.axis_index("fsdp")
        self.p = self.f // 2
        self.c = self.f % 2
        self.place = jnp.stack([self.p, self.c]).astype(jnp.int32)

    def moves(self):
        n, n_p = self.n_f, self.n_p
        square = [[s ^ q for s in range(self.n_s)] for q in range(n_p)]
        if n_p == 4:
            square = [[0, 2, 1, 3], [1, 3, 2, 0], [2, 0, 3, 1], [3, 1, 0, 2]]
        pairs = []
        for s in range(self.n_s):
            for q in range(n_p):
                p = square[q][s]
                pairs += [(s * n + 2 * p + c, p * n + 2 * q + c) for c in range(2)]
        return pairs

    def to_planes(self, v):
        return lax.ppermute(v, ("seq", "fsdp"), self.moves())

    def from_planes(self, v):
        return lax.ppermute(v, ("seq", "fsdp"), [(b, a) for a, b in self.moves()])

    def chip(self, v, j):
        return lax.ppermute(v, "fsdp", xor_pairs(self.n_f, 2 * j))

    def core(self, v):
        return lax.ppermute(v, "fsdp", xor_pairs(self.n_f, 1))

    def gather(self, v):
        return [v] + [self.chip(v, j) for j in range(1, self.n_p)]

    def exchange(self, blocks):
        return [blocks[0]] + [self.chip(blocks[j], j) for j in range(1, self.n_p)]


def fence(values):
    return lax.optimization_barrier(values)


def block(v, index, size, axis):
    return lax.dynamic_slice_in_dim(v, index * size, size, axis=axis)


IN_VMEM = pl.BlockSpec(memory_space=pltpu.VMEM)
IN_SMEM = pl.BlockSpec(memory_space=pltpu.SMEM)
IN_ANY = pl.BlockSpec(memory_space=pl.ANY)
IN_HBM = pl.BlockSpec(memory_space=pltpu.HBM)


def run(name, body, outs, ins, place=None, scratch=(), flops=0, ins_at=None):
    specs = [IN_VMEM] * len(ins) if ins_at is None else ins_at
    if place is not None:
        specs = [IN_SMEM] + specs
        ins = [place, *ins]
    moved = sum(v.size * v.dtype.itemsize for v in ins)
    return pl.pallas_call(
        body,
        out_shape=[jax.ShapeDtypeStruct(shape, dtype) for shape, dtype in outs],
        in_specs=specs,
        out_specs=[IN_VMEM] * len(outs),
        scratch_shapes=list(scratch),
        compiler_params=pltpu.CompilerParams(vmem_limit_bytes=16 << 20),
        cost_estimate=pl.CostEstimate(flops=flops, bytes_accessed=moved, transcendentals=0),
        name=name,
    )(*ins)


def dot(a, b):
    return jnp.dot(a, b, preferred_element_type=F32)


def dot_nt(a, b):
    return lax.dot_general(a, b, (((1,), (1,)), ((), ())), preferred_element_type=F32)


def dot_tn(a, b):
    return lax.dot_general(a, b, (((0,), (0,)), ((), ())), preferred_element_type=F32)


def tile(i, size):
    return pl.ds(pl.multiple_of(i * size, size), size)


def copy_all(pairs, sems):
    copies = [pltpu.make_async_copy(src, dst, sems.at[k]) for k, (src, dst) in enumerate(pairs)]
    for copy in copies:
        copy.start()
    return copies


def own_first(v, parts, c):
    rows = v.shape[-1] // (2 * parts)
    own, other = [], []
    for i in range(parts):
        even = v[:, 2 * i * rows : (2 * i + 1) * rows]
        odd = v[:, (2 * i + 1) * rows : (2 * i + 2) * rows]
        own.append(jnp.where(c == 0, even, odd))
        other.append(jnp.where(c == 0, odd, even))
    return jnp.concatenate(own, axis=1), jnp.concatenate(other, axis=1)


def model_order(v, parts, c):
    half = v.shape[-1] // 2
    rows = half // parts
    out = []
    for i in range(parts):
        own = v[:, i * rows : (i + 1) * rows]
        other = v[:, half + i * rows : half + (i + 1) * rows]
        out += [jnp.where(c == 0, own, other), jnp.where(c == 0, other, own)]
    return jnp.concatenate(out, axis=1)


def stack_rows(net, pieces, weight, layer):
    n_p = net.n_p
    rows, width = D // net.n_f, pieces[0].shape[1]
    more, depth = weight.shape[1:]

    def body(place, *refs):
        p = place[0]
        own, rest, sems = refs[n_p + 1 :]
        pairs = [(refs[j].at[0:rows], own.at[tile(p ^ j, rows)]) for j in range(n_p)]
        for copy in copy_all([*pairs, (refs[n_p].at[layer], rest)], sems):
            copy.wait()

    outs = [((n_p * rows, width), BF), ((more, depth), BF)]
    specs = [IN_ANY] * n_p + [IN_HBM]
    scratch = [pltpu.SemaphoreType.DMA((n_p + 1,))]
    return run("stack_rows", body, outs, [*pieces, weight], net.place, scratch, ins_at=specs)


def pack_tokens(tokens, scene_ids, token_kind):
    rows = tokens.shape[1]
    code = (scene_ids * 2 + token_kind).astype(BF)
    return jnp.pad(tokens[0], ((0, 16), (0, 0))) + jnp.pad(code, ((rows, 15), (0, D - rows)))


def pack_small(vectors):
    sizes = [v.shape[1] for v in vectors]
    total = None
    for k, v in enumerate(vectors):
        at = sum(sizes[:k])
        put = jnp.pad(v, ((0, 0), (at, sum(sizes) - at - sizes[k])))
        total = put if total is None else total + put
    return total


def cut_columns(net, weight, layer, groups, small):
    n_p = net.n_p
    rows = weight.shape[1]
    width = weight.shape[2] // (groups * n_p)
    extra = 16 if small else 0

    def body(place, weight_ref, *refs):
        p = place[0]
        outs, sems = refs[len(small) : len(small) + n_p], refs[-1]
        pairs = []
        for j in range(n_p):
            for i in range(groups):
                cols = tile(i * n_p + (p ^ j), width)
                to = outs[j].at[0:rows, i * width : (i + 1) * width]
                pairs.append((weight_ref.at[layer, :, cols], to))
        copies = copy_all(pairs, sems)
        if extra:
            lines = refs[2 + n_p]
            lines[...] = jnp.zeros_like(lines)
            row = 0
            for ref in refs[:2]:
                low = ref[...].astype(F32)
                for k in range(ref.shape[0]):
                    for half in range(2):
                        cols = slice(half * groups * width, (half + 1) * groups * width)
                        lines[row : row + 1, :] = low[k : k + 1, cols]
                        row += 1
            for j in range(n_p):
                outs[j][rows : rows + extra, :] = lines[...].astype(BF)
        for copy in copies:
            copy.wait()

    outs = [((rows + extra, groups * width), BF)] * n_p
    specs = [IN_HBM] + [IN_VMEM] * len(small)
    scratch = [pltpu.VMEM((16, groups * width), F32)] if extra else []
    scratch.append(pltpu.SemaphoreType.DMA((groups * n_p,)))
    return list(run("cut_columns", body, outs, [weight, *small], net.place, scratch, ins_at=specs))


def join_vectors(net, layers, pieces, sizes):
    n_p = net.n_p
    width = pieces[0].shape[1]
    starts = [sum(sizes[:i]) for i in range(len(sizes))]
    first_row = D // net.n_f

    def body(place, *refs):
        p, c = place[0], place[1]
        ins, outs = refs[:n_p], refs[n_p:]
        for j in range(n_p):
            low = ins[j][first_row : first_row + 16, :].astype(F32)
            for layer in range(layers):
                for half in range(2):
                    row = layer * 2 + half
                    own = low[row : row + 1, :]
                    other = low[2 * layers + row : 2 * layers + row + 1, :]
                    first = jnp.where(c == 0, own, other)
                    second = jnp.where(c == 0, other, own)
                    for k, (at, size) in enumerate(zip(starts, sizes)):
                        if at // width != half:
                            continue
                        cols = slice(at - half * width, at - half * width + size)
                        both = jnp.concatenate([first[:, cols], second[:, cols]], axis=1)
                        outs[k][layer : layer + 1, tile(p ^ j, 2 * size)] = both

    outs = [((layers, 2 * n_p * size), F32) for size in sizes]
    return run("join_vectors", body, outs, pieces, net.place)


def norm_rows(hidden):
    centred = hidden - jnp.mean(hidden, axis=-1, keepdims=True)
    spread = jnp.mean(centred * centred, axis=-1, keepdims=True)
    inverse = lax.rsqrt(spread + EPS)
    return centred * inverse, inverse


def add_and_norm(net, layer, hidden, parts, bias, norm):
    rows = parts[0].shape[0]
    count = len(parts)

    def body(place, *refs):
        total = refs[0][0:rows, :].astype(F32) + refs[1 + count][layer : layer + 1, :]
        for part in refs[1 : 1 + count]:
            total = total + part[...].astype(F32)
        if norm is None:
            refs[2 + count][...] = total.astype(BF)
            return
        gain, shift, out, low = refs[2 + count : 6 + count]
        normed, _ = norm_rows(total)
        row = slice(norm[0], norm[0] + 1)
        out[...] = total
        own, other = own_first(normed * gain[row, :] + shift[row, :], net.n_p, place[1])
        low[:, : D // 2] = own.astype(BF)
        low[:, D // 2 :] = other.astype(BF)

    ins = [hidden, *parts, bias] + ([] if norm is None else list(norm[1:]))
    outs = [((rows, D), BF)] if norm is None else [((rows, D), F32), ((rows, D), BF)]
    return run("add_and_norm", body, outs, ins, net.place)


def norm_back(net, layer, grad, hidden, parts, gain):
    rows = parts[0].shape[0]
    count = len(parts)

    def body(place, grad_ref, hidden_ref, gain_ref, *refs):
        total = refs[0][...].astype(F32)
        for part in refs[1:count]:
            total = total + part[...].astype(F32)
        total = model_order(total, net.n_p, place[1])
        out, low, sums = refs[count:]
        normed, inverse = norm_rows(hidden_ref[0:rows, :].astype(F32))
        scaled = total * gain_ref[layer : layer + 1, :]
        one = jnp.mean(scaled, axis=-1, keepdims=True)
        two = jnp.mean(scaled * normed, axis=-1, keepdims=True)
        result = grad_ref[...].astype(F32) + inverse * (scaled - one - normed * two)
        rounded = result.astype(BF)
        out[...] = result
        low[...] = rounded
        sums[0:1, :] = jnp.sum(total * normed, axis=0, keepdims=True)
        sums[1:2, :] = jnp.sum(total, axis=0, keepdims=True)
        sums[2:3, :] = jnp.sum(rounded.astype(F32), axis=0, keepdims=True)

    outs = [((rows, D), F32), ((rows, D), BF), ((3, D), F32)]
    return run("norm_back", body, outs, [grad, hidden, gain, *parts], net.place)


def column_sums(v):
    def body(ref, out):
        out[...] = jnp.sum(ref[...].astype(F32), axis=0, keepdims=True)

    return run("column_sums", body, [((1, v.shape[1]), F32)], [v])[0]


def gather_rows(blocks, scratch):
    rows = scratch.shape[0] // len(blocks)
    for j, ref in enumerate(blocks):
        scratch[j * rows : (j + 1) * rows, :] = ref[0:rows, :]


def allowed_pairs(code_col, code_row):
    same = (code_col >> 1) == (code_row >> 1)
    return same & (((code_col & 1) == 0) | ((code_row & 1) == 1))


def head_lanes(shape, head, axis):
    lane = lax.broadcasted_iota(jnp.int32, shape, axis)
    return (lane < HEAD_DIM) if head == 0 else (lane >= HEAD_DIM)


def keep_head(v, head, axis):
    return jnp.where(head_lanes(v.shape, head, axis), v, jnp.zeros_like(v))


def probs_by_key(k2, q2, allowed, head):
    scores = dot_nt(keep_head(k2, head, 1), q2) * SCALE
    scores = jnp.where(allowed, scores, NEG)
    powers = jnp.exp(scores - jnp.max(scores, axis=0, keepdims=True))
    return powers * (1.0 / jnp.sum(powers, axis=0, keepdims=True))


Q_TILE = 256


def attend(net, layer, rows, blocks, norm, weight, bias, codes, proj):
    n_p = net.n_p
    tokens = n_p * rows
    cw = D // n_p
    first = norm is not None

    def body(place, *refs):
        bias_ref, w_own, w_other, p_own, p_other = refs[n_p : n_p + 5]
        if first:
            gain_ref, shift_ref = refs[n_p + 5 : n_p + 7]
            row_ref, col_ref, a = refs[n_p + 7 : n_p + 10]
            outs = refs[n_p + 10 : 2 * n_p + 10]
            qkv, attended, vt = refs[2 * n_p + 10 :]
        else:
            row_ref, col_ref = refs[n_p + 5 : n_p + 7]
            outs = refs[n_p + 7 : 2 * n_p + 7]
            qkv, attended, vt, a = refs[2 * n_p + 7 :]
        p, c = place[0], place[1]
        if first:
            eye = lax.broadcasted_iota(jnp.int32, (rows, rows), 0) == lax.broadcasted_iota(
                jnp.int32, (rows, rows), 1
            )
            for j in range(n_p):
                here = slice(j * rows, (j + 1) * rows)
                line = refs[j][rows : rows + 1, 0:rows].astype(F32)
                row_ref[:, here] = line.astype(jnp.int32)
                column = jnp.sum(jnp.where(eye, line, 0.0), axis=1, keepdims=True)
                col_ref[here, :] = column.astype(jnp.int32)
                normed, _ = norm_rows(refs[j][0:rows, :].astype(F32))
                own, other = own_first(normed * gain_ref[0:1, :] + shift_ref[0:1, :], n_p, c)
                a[here, : D // 2] = own.astype(BF)
                a[here, D // 2 :] = other.astype(BF)
        else:
            gather_rows(refs[:n_p], a)
        for i in range(3):
            cols = slice(i * cw, (i + 1) * cw)
            out = dot(a[:, : D // 2], w_own[:, cols]) + dot(a[:, D // 2 :], w_other[:, cols])
            if i == 0:
                out = out + bias_ref[layer : layer + 1, tile(p, cw)]
            if i == 2:
                out = out + bias_ref[layer : layer + 1, tile(p + n_p, cw)]
            qkv[:, cols] = out.astype(BF)
        vt[...] = jnp.transpose(qkv[:, 2 * cw : 3 * cw].astype(F32)).astype(BF)

        @pl.loop(0, tokens // Q_TILE)
        def _(t):
            here = tile(t, Q_TILE)
            allowed = allowed_pairs(col_ref[...], row_ref[:, here])
            for pair in range(cw // LANES):
                lanes = slice(pair * LANES, (pair + 1) * LANES)
                q2 = qkv[here, lanes]
                k2 = qkv[:, cw + pair * LANES : cw + (pair + 1) * LANES]
                total = None
                for head in range(2):
                    probs = probs_by_key(k2, q2, allowed, head).astype(BF)
                    part = dot(keep_head(vt[lanes, :], head, 0), probs)
                    total = part if total is None else total + part
                attended[here, lanes] = jnp.transpose(total).astype(BF)

        for j in range(n_p):
            o = attended[j * rows : (j + 1) * rows, :]
            low, high = o[:, : cw // 2], o[:, cw // 2 :]
            own, other = jnp.where(c == 0, low, high), jnp.where(c == 0, high, low)
            outs[j][...] = (dot(own, p_own[...]) + dot(other, p_other[...])).astype(BF)

    outs = [((rows, D), BF)] * n_p + [((tokens, 3 * cw), BF), ((tokens, cw), BF)]
    scratch = [pltpu.VMEM((cw, tokens), BF)]
    ins = [*blocks, bias, *weight, *proj]
    if first:
        ins += list(norm)
        outs = [((1, tokens), jnp.int32), ((tokens, 1), jnp.int32), ((tokens, D), BF)] + outs
    else:
        ins += list(codes)
        scratch.append(pltpu.VMEM((tokens, D), BF))
    got = run("attend", body, outs, ins, net.place, scratch, flops=2 * tokens * D * 4 * cw)
    normed = blocks
    if first:
        codes, normed, got = got[:2], [got[2]], got[3:]
    return got[:n_p], got[n_p], got[n_p + 1], codes, normed


def attend_back(net, blocks, proj, qkv, codes, weight, tokens_in):
    n_p = net.n_p
    rows = blocks[0].shape[0]
    tokens = n_p * rows
    cw = D // n_p
    n_t = len(tokens_in)

    def body(place, *refs):
        p_own, p_other, qkv_ref, row_ref, col_ref, w_own, w_other = refs[n_p : n_p + 7]
        token_refs = refs[n_p + 7 : n_p + 7 + n_t]
        refs_out = refs[n_p + 7 + n_t :]
        outs = refs_out[:n_p]
        dqkv, sums, norm_sums, do, kt, dk, dv = refs_out[n_p:]
        c = place[1]
        for j in range(n_p):
            here = slice(j * rows, (j + 1) * rows)
            own, other = dot_nt(refs[j][...], p_own[...]), dot_nt(refs[j][...], p_other[...])
            do[here, : cw // 2] = jnp.where(c == 0, own, other).astype(BF)
            do[here, cw // 2 :] = jnp.where(c == 0, other, own).astype(BF)
        kt[...] = jnp.transpose(qkv_ref[:, cw : 2 * cw].astype(F32)).astype(BF)
        dk[...] = jnp.zeros_like(dk)
        dv[...] = jnp.zeros_like(dv)

        @pl.loop(0, tokens // Q_TILE)
        def _(t):
            here = tile(t, Q_TILE)
            allowed = allowed_pairs(col_ref[...], row_ref[:, here])
            for pair in range(cw // LANES):
                lanes = slice(pair * LANES, (pair + 1) * LANES)
                q2 = qkv_ref[here, lanes]
                k2 = qkv_ref[:, cw + pair * LANES : cw + (pair + 1) * LANES]
                v2 = qkv_ref[:, 2 * cw + pair * LANES : 2 * cw + (pair + 1) * LANES]
                do2 = do[here, lanes]
                total = None
                for head in range(2):
                    probs = probs_by_key(k2, q2, allowed, head)
                    dp = dot_nt(keep_head(v2, head, 1), do2)
                    mean = jnp.sum(probs * dp, axis=0, keepdims=True)
                    ds = (probs * (dp - mean)).astype(BF)
                    dv[:, lanes] += dot(probs.astype(BF), keep_head(do2, head, 1))
                    dk[:, lanes] += dot(ds, keep_head(q2, head, 1))
                    part = dot(keep_head(kt[lanes, :], head, 0), ds)
                    total = part if total is None else total + part
                dqkv[here, lanes] = (jnp.transpose(total) * SCALE).astype(BF)

        dqkv[:, cw : 2 * cw] = (dk[...] * SCALE).astype(BF)
        dqkv[:, 2 * cw :] = dv[...].astype(BF)
        sums[...] = jnp.sum(dqkv[...].astype(F32), axis=0, keepdims=True)
        norm_sums[...] = jnp.zeros_like(norm_sums)
        for j in range(n_p):
            normed = None
            if n_t:
                normed = own_first(norm_rows(token_refs[j][0:rows, :].astype(F32))[0], n_p, c)
            for k, w in enumerate((w_own, w_other)):
                cols = slice(k * (D // 2), (k + 1) * (D // 2))
                da1 = dot_nt(dqkv[j * rows : (j + 1) * rows, :], w[...])
                outs[j][:, cols] = da1.astype(BF)
                if n_t:
                    norm_sums[0:1, cols] += jnp.sum(da1 * normed[k], axis=0, keepdims=True)
                    norm_sums[1:2, cols] += jnp.sum(da1, axis=0, keepdims=True)

    outs = [((rows, D), BF)] * n_p + [((tokens, 3 * cw), BF), ((1, 3 * cw), F32), ((2, D), F32)]
    scratch = [
        pltpu.VMEM((tokens, cw), BF),
        pltpu.VMEM((cw, tokens), BF),
        pltpu.VMEM((tokens, cw), F32),
        pltpu.VMEM((tokens, cw), F32),
    ]
    ins = [*blocks, *proj, qkv, *codes, *weight, *tokens_in]
    got = run("attend_back", body, outs, ins, net.place, scratch, flops=2 * tokens * D * 8 * cw)
    return got[:n_p], got[n_p], got[n_p + 1], got[n_p + 2]


F_TILE = 256


def feed_forward(net, layer, blocks, up, bias, down):
    n_p = net.n_p
    rows = blocks[0].shape[0]
    tokens = n_p * rows
    fw = FF // n_p

    def body(place, *refs):
        up_own, up_other, bias_ref, d_own, d_other = refs[n_p : n_p + 5]
        outs = refs[n_p + 5 : 2 * n_p + 5]
        z_ref, slope_ref, a_ref = refs[2 * n_p + 5 :]
        p, c = place[0], place[1]
        gather_rows(refs[:n_p], a_ref)

        @pl.loop(0, fw // F_TILE)
        def _(t):
            cols = tile(t, F_TILE)
            there = pl.ds(pl.multiple_of(p * fw + t * F_TILE, F_TILE), F_TILE)
            u = dot(a_ref[:, : D // 2], up_own[:, cols]) + dot(a_ref[:, D // 2 :], up_other[:, cols])
            u = u + bias_ref[layer : layer + 1, there]
            phi = 0.5 * (1.0 + lax.erf(u * 0.7071067811865476))
            z_ref[:, cols] = (u * phi).astype(BF)
            slope_ref[:, cols] = phi + u * (jnp.exp(-0.5 * u * u) * 0.3989422804014327)

        for j in range(n_p):
            here = slice(j * rows, (j + 1) * rows)
            own, other = z_ref[here, tile(c, fw // 2)], z_ref[here, tile(1 - c, fw // 2)]
            outs[j][...] = (dot(own, d_own[...]) + dot(other, d_other[...])).astype(BF)

    outs = [((rows, D), BF)] * n_p + [((tokens, fw), BF), ((tokens, fw), F32)]
    scratch = [pltpu.VMEM((tokens, D), BF)]
    ins = [*blocks, *up, bias, *down]
    got = run("feed_forward", body, outs, ins, net.place, scratch, flops=4 * tokens * D * fw)
    return got[:n_p], got[n_p], got[n_p + 1]


def feed_back(net, blocks, down, slope, up):
    n_p = net.n_p
    rows = blocks[0].shape[0]
    tokens = n_p * rows
    fw = FF // n_p

    def body(place, *refs):
        d_own, d_other, slope_ref, up_own, up_other = refs[n_p : n_p + 5]
        outs = refs[n_p + 5 : 2 * n_p + 5]
        du_ref, sums, dm = refs[2 * n_p + 5 :]
        c = place[1]
        gather_rows(refs[:n_p], dm)
        for w, core in ((d_own, c), (d_other, 1 - c)):

            @pl.loop(0, fw // (2 * F_TILE))
            def _(t):
                start = core * (fw // 2) + t * F_TILE
                cols = pl.ds(pl.multiple_of(start, F_TILE), F_TILE)
                dz = dot_nt(dm[...], w[tile(t, F_TILE), :])
                du = (dz * slope_ref[:, cols]).astype(BF)
                du_ref[:, cols] = du
                sums[:, cols] = jnp.sum(du.astype(F32), axis=0, keepdims=True)

        for j in range(n_p):
            du = du_ref[j * rows : (j + 1) * rows, :]
            outs[j][:, : D // 2] = dot_nt(du, up_own[...]).astype(BF)
            outs[j][:, D // 2 :] = dot_nt(du, up_other[...]).astype(BF)

    outs = [((rows, D), BF)] * n_p + [((tokens, fw), BF), ((1, fw), F32)]
    scratch = [pltpu.VMEM((tokens, D), BF)]
    ins = [*blocks, *down, slope, *up]
    got = run("feed_back", body, outs, ins, net.place, scratch, flops=4 * tokens * D * fw)
    return got[:n_p], got[n_p], got[n_p + 1]


def down_weight_grad(net, z, dm):
    n_r = len(dm)
    tokens, m = z.shape
    half = m // 2

    def body(place, z_ref, *refs):
        keep, send, b = refs[n_r:]
        c = place[1]
        gather_rows(refs[:n_r], b)
        keep[...] = dot_tn(z_ref[:, tile(c, half)], b[...]).astype(BF)
        send[...] = dot_tn(z_ref[:, tile(1 - c, half)], b[...]).astype(BF)

    outs = [((half, D), BF)] * 2
    scratch = [pltpu.VMEM((tokens, D), BF)]
    return run("down_weight_grad", body, outs, [z, *dm], net.place, scratch, flops=2 * tokens * m * D)


def up_weight_grad(net, a2, du):
    n_l = len(a2)
    tokens, n = du.shape

    def body(place, *refs):
        du_ref, out, a = refs[n_l:]
        c = place[1]
        gather_rows(refs[:n_l], a)
        out[c] = dot_tn(a[:, : D // 2], du_ref[...]).astype(BF)
        out[1 - c] = dot_tn(a[:, D // 2 :], du_ref[...]).astype(BF)

    scratch = [pltpu.VMEM((tokens, D), BF)]
    outs = [((2, D // 2, n), BF)]
    return run("up_weight_grad", body, outs, [*a2, du], net.place, scratch, flops=2 * tokens * D * n)[0]


def attend_weight_grad(net, a1, dqkv, attended, dy, small):
    n_p = net.n_p
    n_a = len(a1)
    tokens, width = dqkv.shape
    cw = D // n_p
    rows = D // net.n_f
    extra = 16 if small else 0
    flat = [v for of_layer in small[1] for v in of_layer] if small else []
    sizes = small[0] if small else []
    starts = [sum(sizes[:i]) for i in range(len(sizes))]

    def put_small(place, refs, low):
        p, c = place[0], place[1]
        low[...] = jnp.zeros_like(low)
        for k, (ref, (_, kind)) in enumerate(zip(refs, flat)):
            layer, which = divmod(k, len(sizes))
            at, size = starts[which], sizes[which]
            half = at // width
            row = slice(2 * layer + half, 2 * layer + half + 1)
            cols = slice(at - half * width, at - half * width + size)
            if kind == "chip":
                low[0, p, row, cols] = ref[:, :size]
                low[1, p, row, cols] = ref[:, size:]
            elif kind == "heads":
                low[p % 2, p // 2, row, cols] = ref[:, :size]
                low[p % 2, p // 2 + n_p // 2, row, cols] = ref[:, 2 * size :]
            elif kind == "own":
                for i in range(n_p):
                    low[c, i, row, cols] = ref[:, i * size : (i + 1) * size]
                    low[1 - c, i, row, cols] = ref[:, D // 2 + i * size : D // 2 + (i + 1) * size]
            else:
                for i in range(n_p):
                    for core in range(2):
                        to = (2 * i + core) * size
                        low[core, i, row, cols] = ref[:, to : to + size]

    def body(place, *refs):
        dqkv_ref, attended_ref = refs[n_a : n_a + 2]
        smalls = refs[n_a + 2 + n_p : n_a + 2 + n_p + len(flat)]
        out, a, b, low, lines = refs[n_a + 2 + n_p + len(flat) :]
        c = place[1]
        gather_rows(refs[:n_a], a)
        for k, core in ((0, c), (1, 1 - c)):
            both = dot_tn(a[:, k * (D // 2) : (k + 1) * (D // 2)], dqkv_ref[...]).astype(BF)
            for i in range(n_p):
                out[core, i * (rows + extra) : i * (rows + extra) + rows, :width] = both[i * rows : (i + 1) * rows]
        gather_rows(refs[n_a + 2 : n_a + 2 + n_p], b)
        low[...] = dot_tn(attended_ref[...], b[...]).astype(BF)
        for core in range(2):
            for i in range(n_p):
                here = slice(i * (rows + extra), i * (rows + extra) + rows)
                out[core, here, width:] = low[core * rows : (core + 1) * rows, i * cw : (i + 1) * cw]
        if extra:
            put_small(place, smalls, lines)
            for core in range(2):
                for i in range(n_p):
                    here = slice(i * (rows + extra) + rows, (i + 1) * (rows + extra))
                    out[core, here, :width] = lines[core, i].astype(BF)
                    out[core, here, width:] = jnp.zeros((extra, cw), BF)

    outs = [((2, n_p * (rows + extra), width + cw), BF)]
    scratch = [pltpu.VMEM((tokens, D), BF), pltpu.VMEM((tokens, D), BF), pltpu.VMEM((cw, D), BF)]
    scratch.append(pltpu.VMEM((2, n_p, 16, width), F32))
    flops = 2 * tokens * D * (width + cw)
    ins = [*a1, dqkv, attended, *dy, *[v for v, _ in flat]]
    return run("attend_weight_grad", body, outs, ins, net.place, scratch, flops=flops)[0]


def add_halves(a, b):
    rows, width = a.shape
    half = width // 2

    def body(a_ref, b_ref, *outs):
        for k in range(2):
            cols = slice(k * half, (k + 1) * half)
            outs[k][...] = (a_ref[:, cols].astype(F32) + b_ref[:, cols].astype(F32)).astype(BF)

    return run("add_halves", body, [((rows, half), BF)] * 2, [a, b])


def add_pair(both):
    _, rows, width = both.shape
    half = width // 2

    def body(ref, *outs):
        for k in range(2):
            cols = slice(k * half, (k + 1) * half)
            outs[k][...] = (ref[0, :, cols].astype(F32) + ref[1, :, cols].astype(F32)).astype(BF)

    return run("add_pair", body, [((rows, half), BF)] * 2, [both])


def cut_rows(net, first, second, extra):
    n_p = net.n_p
    rows = first.shape[0] // n_p
    width, more = first.shape[1], second.shape[1]
    split = extra is not None
    taken = more // 2 if split else more

    def body(place, a, b, *outs):
        p = place[0]
        for j in range(n_p):
            here = tile(p ^ j, rows)
            outs[j][:, :width] = a[here, :]
            outs[j][:, width:] = b[here, :taken]
        if split:
            for i in range(n_p):
                outs[n_p][:, i * taken : (i + 1) * taken] = b[i * rows : (i + 1) * rows - extra, taken:]

    outs = [((rows, width + taken), BF)] * n_p
    if split:
        outs.append(((rows - extra, n_p * taken), BF))
    return run("cut_rows", body, outs, [first, second], net.place)


def sum_small(layers, pieces, sizes, rows):
    width = pieces[0].shape[1]
    starts = [sum(sizes[:i]) for i in range(len(sizes))]

    def body(*refs):
        total = refs[0][rows:, :].astype(F32)
        for ref in refs[1 : len(pieces)]:
            total = total + ref[rows:, :].astype(F32)
        for out, at, size in zip(refs[len(pieces) :], starts, sizes):
            half = at // width
            for layer in range(layers):
                row = 2 * layer + half
                out[layer : layer + 1, :] = total[row : row + 1, at - half * width : at - half * width + size]

    return run("sum_small", body, [((layers, size), F32) for size in sizes], pieces)


def take_if(here, a, b, rows):
    def body(flag, a_ref, b_ref, out):
        @pl.when(flag[0] != 0)
        def _():
            count = min(rows, a.shape[0])
            out[0:count, :] = a_ref[0:count, :]

        @pl.when(flag[0] == 0)
        def _():
            count = min(rows, b.shape[0])
            out[0:count, :] = b_ref[0:count, :]

    return run("take_if", body, [((rows, a.shape[1]), BF)], [a, b], here.astype(jnp.int32).reshape(1))[0]


def turn(net, wanted):
    flat, flags, outs = [], [], []
    for one, two, outer in wanted:
        flat += one + (two or [])
        rows = max(one[0].shape[0], two[0].shape[0] if two else 0)
        outs.append(((rows, one[0].shape[1]), BF))
        flags.append(jnp.zeros((), jnp.int32) if outer is None else outer.astype(jnp.int32))

    def put(refs, out):
        rows = refs[0].shape[0]
        if len(refs) == 1:
            out[0:rows, :] = refs[0][...]
            return
        total = refs[0][...].astype(F32)
        for ref in refs[1:]:
            total = total + ref[0:rows, :].astype(F32)
        out[0:rows, :] = total.astype(BF)

    def body(flag, *refs):
        at = 0
        for k, (one, two, outer) in enumerate(wanted):
            out = refs[len(flat) + k]
            first = refs[at : at + len(one)]
            at += len(one)
            if outer is None:
                put(first, out)
                continue
            second = refs[at : at + len(two)]
            at += len(two)
            pl.when(flag[k] != 0)(lambda first=first, out=out: put(first, out))
            pl.when(flag[k] == 0)(lambda second=second, out=out: put(second, out))

    return run("turn", body, outs, flat, jnp.stack(flags))


class Chunk:
    def __init__(self, value):
        self.terms = [value]
        self.step = 0

    @property
    def value(self):
        return self.terms[0]


class Flow:
    def __init__(self, net):
        self.net = net
        self.queue = []
        self.moving = []

    def first(self, step):
        for chunk in self.queue:
            if chunk.step == step:
                return chunk
        return None

    def start(self):
        net = self.net
        n = net.n_s
        half = n // 2
        moves, wanted = [], []
        for k in range(half):
            inward = self.first(k)
            outward = None if k == half - 1 else self.first(n - 2 - k)
            into = [(k, k + 1), (n - 1 - k, n - 2 - k)]
            out = [(k + 1, k), (n - 2 - k, n - 1 - k)]
            outer = (net.s == k) | (net.s == n - 1 - k)
            both = inward is not None and outward is not None
            if both and inward.value.shape[1] == outward.value.shape[1]:
                moves.append((inward, outward, outer, into + out))
                wanted.append((inward.terms, outward.terms, outer))
                continue
            if inward is not None:
                moves.append((inward, None, outer, into))
                wanted.append((inward.terms, None, None))
            if outward is not None:
                moves.append((None, outward, outer, out))
                wanted.append((outward.terms, None, None))
        sent = [w[0][0] for w in wanted]
        work = [k for k, w in enumerate(wanted) if len(w[0]) > 1 or w[1] is not None]
        if work:
            for k, value in zip(work, turn(net, [wanted[k] for k in work])):
                sent[k] = value
        self.moving = [(*m[:3], v, lax.ppermute(v, "seq", m[3])) for m, v in zip(moves, sent)]

    def collect(self, values, *new):
        values, news, got = fence((values, [c.value for c in new], [(m[3], m[4]) for m in self.moving]))
        for c, value in zip(new, news):
            c.terms = [value]
        n = self.net.n_s
        for (inward, outward, outer, _, _), (sent, arrived) in zip(self.moving, got):
            if inward is not None:
                middle = inward.step == n // 2 - 1
                inward.terms = [sent, arrived] if middle else [*inward.terms, arrived]
                inward.step += 1
            if outward is not None:
                outward.terms = [take_if(outer, arrived, sent, outward.value.shape[0])]
                outward.step += 1
        self.queue = [c for c in self.queue if c.step < n - 1] + list(new)
        self.start()
        return values


def write_layer(net, layer, layers, before, down, proj, up, qkv):
    n_p = net.n_p
    rows = up[0].shape[0]
    cw, fw = D // n_p, FF // n_p
    n_in = 3 + 2 * n_p
    skip = 0 if before is None else 4
    steps = min(4, rows // 16)
    part = rows // steps
    down_rows = down[0].shape[0]
    down_part = down_rows // steps

    def body(place, *refs):
        p = place[0]
        downs, proj_ref = refs[:2], refs[2]
        ups, qkvs = refs[3 : 3 + n_p], refs[3 + n_p : n_in]
        qkv_out, proj_out, up_out, down_out = refs[n_in + skip :]
        proj_out[0] = proj_ref[...].astype(F32)
        for k in range(2):
            down_out[0, :, k * (D // 2) : (k + 1) * (D // 2)] = downs[k][...].astype(F32)
        for j in range(n_p):
            up_out[0, :, tile(p ^ j, fw)] = ups[j][...].astype(F32)
            for i in range(3):
                to = tile(i * n_p + (p ^ j), cw)
                qkv_out[0, :, to] = qkvs[j][:, i * cw : (i + 1) * cw].astype(F32)

    def of_rows(v, size):
        return pl.BlockSpec((size, v.shape[1]), lambda i: (i, 0))

    ins = [*down, proj, *up, *qkv]
    specs = [IN_SMEM] + [of_rows(v, down_part) for v in down] + [of_rows(v, part) for v in [proj, *up, *qkv]]
    aliases = {}
    if before is not None:
        aliases = {1 + n_in + k: k for k in range(4)}
        specs += [IN_ANY] * 4
        ins = ins + list(before)
    shapes = [(rows, 3 * D), (rows, D), (rows, FF), (down_rows, D)]
    sizes = [part, part, part, down_part]
    return pl.pallas_call(
        body,
        grid=(steps,),
        out_shape=[jax.ShapeDtypeStruct((layers, *shape), F32) for shape in shapes],
        in_specs=specs,
        out_specs=[
            pl.BlockSpec((1, size, shape[1]), lambda i: (layer, i, 0)) for size, shape in zip(sizes, shapes)
        ],
        input_output_aliases=aliases,
        compiler_params=pltpu.CompilerParams(vmem_limit_bytes=16 << 20),
        name="write_layer",
    )(net.place, *ins)


def on_device(
    tokens,
    scene_ids,
    token_kind,
    out_grad,
    first_gain,
    first_shift,
    qkv_weight,
    qv_bias,
    proj_weight,
    proj_bias,
    second_gain,
    second_shift,
    up_weight,
    up_bias,
    down_weight,
    down_bias,
):
    net = Net()
    n_p = net.n_p
    layers = qkv_weight.shape[0]
    rows = tokens.shape[1]
    pair_groups = [[2 * i, 2 * i + 1] for i in range(n_p)]

    def swap_cores(both):
        return lax.all_to_all(both, "fsdp", 0, 0, axis_index_groups=pair_groups)

    small_in = [first_gain, first_shift, qv_bias, proj_bias, second_gain, second_shift, up_bias, down_bias]
    sizes = [v.shape[1] for v in small_in]
    tok = net.to_planes(pack_tokens(tokens, scene_ids, token_kind))
    small = pack_small(small_in)
    small = [small, net.core(small)]
    qkv_got = net.exchange(cut_columns(net, qkv_weight, 0, 3, small))
    tok, qkv_got, later = fence((tok, qkv_got, (proj_weight, up_weight, down_weight, out_grad)))
    proj_weight, up_weight, down_weight, out_grad = later
    tokg = net.gather(tok)
    qkv_own, proj_own = stack_rows(net, qkv_got, proj_weight, 0)
    qkv_w, proj_w = (qkv_own, net.core(qkv_own)), (proj_own, net.core(proj_own))
    vectors = join_vectors(net, layers, qkv_got, sizes)
    gain1, shift1, qv_b, proj_b, gain2, shift2, up_b, down_b = vectors

    weights = []
    kept = []
    dm = None
    codes = None
    hidden = None
    for layer in range(layers):
        last = layer == layers - 1
        a1g = tokg if layer == 0 else net.gather(a1)
        a1g, qkv_w, proj_w, up_weight = fence((a1g, qkv_w, proj_w, up_weight))
        if layer == 0:
            tokg = a1g
            hidden = tokg[0]
        norm = (gain1, shift1) if layer == 0 else None
        y, qkv, og, codes, a1g = attend(net, layer, rows, a1g, norm, qkv_w, qv_b, codes, proj_w)
        up_got = net.exchange(cut_columns(net, up_weight, layer, 1, []))
        y, up_got, down_weight = fence((y, up_got, down_weight))
        parts = net.exchange(y)
        up_own, down_own = stack_rows(net, up_got, down_weight, layer)
        up_w, down_w = (up_own, net.core(up_own)), (down_own, net.core(down_own))
        parts, up_w, down_w = fence((parts, up_w, down_w))
        h2, a2 = add_and_norm(net, layer, hidden, parts, proj_b, (layer, gain2, shift2))
        a2g = net.gather(a2)
        a2g, qkv_weight, out_grad = fence((a2g, qkv_weight, out_grad))
        y, z, slope = feed_forward(net, layer, a2g, up_w, up_b, down_w)
        kept.append((hidden, a1g, qkv, og, h2, a2g, z, slope))
        weights.append((qkv_w, proj_w, up_w, down_w))
        if last:
            dmg = net.gather(dm)
            last_y, z, slope, dmg = fence((y, z, slope, dmg))
            break
        qkv_got = net.exchange(cut_columns(net, qkv_weight, layer + 1, 3, []))
        if layer == layers - 2:
            dm = net.to_planes(out_grad[0])
        y, qkv_got, proj_weight, dm = fence((y, qkv_got, proj_weight, dm))
        parts = net.exchange(y)
        qkv_own, proj_own = stack_rows(net, qkv_got, proj_weight, layer + 1)
        qkv_w, proj_w = (qkv_own, net.core(qkv_own)), (proj_own, net.core(proj_own))
        parts, qkv_w, proj_w = fence((parts, qkv_w, proj_w))
        hidden, a1 = add_and_norm(net, layer, h2, parts, down_b, (layer + 1, gain1, shift1))

    flow = Flow(net)
    small_grads = [None] * layers
    sums = [None] * layers
    out = None
    grad = dm
    down_b_grad = column_sums(dm)

    def chunks(halves):
        return [Chunk(v) for v in halves]

    for layer in reversed(range(layers)):
        last = layer == layers - 1
        qkv_w, proj_w, up_w, down_w = weights[layer]
        h1, a1g, qkv, og, h2, a2g, z, slope = kept[layer]
        keep, send = down_weight_grad(net, z, dmg)
        da2, du, up_b_grad = feed_back(net, dmg, down_w, slope, up_w)
        send = net.core(send)
        if layer == layers - 2:
            sent_out = net.from_planes(sent_out)
            da2, du, keep, send, sent_out = fence((da2, du, keep, send, sent_out))
        else:
            da2, du, keep, send = fence((da2, du, keep, send))
        down_g = chunks(add_halves(keep, send))
        da2 = flow.collect(da2, down_g[0])
        parts = net.exchange(da2)
        both = swap_cores(up_weight_grad(net, a2g, du))
        parts, both = flow.collect((parts, both), down_g[1])
        up_g = chunks(add_pair(both))
        dh2, dy, sums2 = norm_back(net, layer, grad, h2, parts, gain2)
        dyg = net.gather(dy)
        dyg = flow.collect(dyg, up_g[0])
        tokens_in = tokg if layer == 0 else []
        da1, dqkv, qkv_b_grad, norm_sums = attend_back(net, dyg, proj_w, qkv, codes, qkv_w, tokens_in)
        if last:
            last_parts = net.exchange(last_y)
            da1, dqkv, last_parts = flow.collect((da1, dqkv, last_parts), up_g[1])
            (sent_out,) = add_and_norm(net, layer, h2, last_parts, down_b, None)
        else:
            up_pieces = net.exchange(cut_rows(net, *[c.value for c in sums[layer + 1][1]], None))
            da1, dqkv, up_pieces = flow.collect((da1, dqkv, up_pieces), up_g[1])
        parts = net.exchange(da1)
        names = [None, None, "heads", None, None, None, "chip", None]
        of_layer = [None, None, qkv_b_grad, sums2[2:3], sums2[0:1], sums2[1:2], up_b_grad, down_b_grad]
        small = None
        if layer == 0:
            of_layer[0], of_layer[1] = norm_sums[0:1], norm_sums[1:2]
            names[0] = names[1] = "own"
            small_grads[layer] = list(zip(of_layer, names))
            small = (sizes, small_grads)
        both = swap_cores(attend_weight_grad(net, a1g, dqkv, og, dyg, small))
        parts, both = fence((parts, both))
        attend_g = chunks(add_pair(both))
        grad, dm, sums1 = norm_back(net, layer, dh2, h1, parts, gain1)
        sums[layer] = (down_g, up_g, attend_g)
        dm = flow.collect(dm, attend_g[0])
        if layer > 0:
            of_layer[0], of_layer[1] = sums1[0:1], sums1[1:2]
            small_grads[layer] = list(zip(of_layer, names))
            dmg = net.gather(dm)
            down_b_grad = sums1[2:3]
            dmg, grad = flow.collect((dmg, grad), attend_g[1])

    input_grad = net.from_planes(dm)
    input_grad = flow.collect(input_grad, attend_g[1])
    flow.collect(())
    up_last = None
    pieces = None
    while flow.queue:
        if up_last is None and not [c for c in flow.queue if c in sums[0][1]]:
            up_last = net.exchange(cut_rows(net, *[c.value for c in sums[0][1]], None))
            up_last = flow.collect(up_last)
        elif up_last is not None and pieces is None:
            *pieces, proj_g = cut_rows(net, *[c.value for c in sums[1][2]], 0)
            pieces = net.exchange(pieces)
            pieces, proj_g = flow.collect((pieces, proj_g))
        else:
            flow.collect(())
    if pieces is None:
        *pieces, proj_g = cut_rows(net, *[c.value for c in sums[1][2]], 0)
        pieces = net.exchange(pieces)
    out = write_layer(net, 1, layers, None, [c.value for c in sums[1][0]], proj_g, up_pieces, pieces)
    if up_last is None:
        up_last = net.exchange(cut_rows(net, *[c.value for c in sums[0][1]], None))
    *pieces, proj_g = cut_rows(net, *[c.value for c in sums[0][2]], 16)
    pieces = net.exchange(pieces)
    small_out = sum_small(layers, pieces, sizes, D // net.n_f)
    out = write_layer(net, 0, layers, out, [c.value for c in sums[0][0]], proj_g, up_last, pieces)
    return (
        sent_out.astype(F32)[None],
        input_grad.astype(F32)[None],
        small_out[0],
        small_out[1],
        out[0],
        small_out[2],
        out[1],
        small_out[3],
        small_out[4],
        small_out[5],
        out[2],
        small_out[6],
        out[3],
        small_out[7],
    )


def solution(mesh):
    tok = P("fsdp", "seq", None)
    lab = P("fsdp", "seq")
    vec = P(None, "fsdp")
    mat = P(None, "fsdp", None)
    return jax.shard_map(
        on_device,
        mesh=mesh,
        in_specs=(tok, lab, lab, tok, vec, vec, mat, vec, mat, vec, vec, vec, mat, vec, mat, vec),
        out_specs=(tok, tok, vec, vec, mat, vec, mat, vec, vec, vec, mat, vec, mat, vec),
        check_vma=False,
    )
```

```python
import jax
import jax.numpy as jnp
from jax import lax
from jax.experimental import pallas as pl
from jax.experimental.pallas import tpu as pltpu
from jax.sharding import PartitionSpec as P

D = 1024
HEAD_DIM = 64
FF = 4096
EPS = 1e-05
NEG = -1e30
SCALE = 0.125
BF = jnp.bfloat16
F32 = jnp.float32
LANES = 128


def xor_pairs(count, mask):
    return [(i, i ^ mask) for i in range(count)]


class Net:
    def __init__(self):
        self.n_s = lax.axis_size("seq")
        self.n_f = lax.axis_size("fsdp")
        self.n_p = self.n_f // 2
        self.s = lax.axis_index("seq")
        self.f = lax.axis_index("fsdp")
        self.p = self.f // 2
        self.c = self.f % 2
        self.place = jnp.stack([self.p, self.c, self.s % 2]).astype(jnp.int32)

    def moves(self):
        square = [[s ^ q for s in range(self.n_s)] for q in range(self.n_p)]
        if self.n_p == 4:
            square = [[0, 2, 1, 3], [1, 3, 2, 0], [2, 0, 3, 1], [3, 1, 0, 2]]
        return [(s, square[q][s], q) for s in range(self.n_s) for q in range(self.n_p)]

    def send(self, v, moves):
        n = self.n_f
        pairs = [(s * n + 2 * p + c, t * n + 2 * q + c) for s, p, t, q in moves for c in range(2)]
        return lax.ppermute(v, ("seq", "fsdp"), pairs)

    def to_place(self, v):
        return self.send(v, [(s, p, p, q) for s, p, q in self.moves()])

    def from_place(self, v):
        return self.send(v, [(p, q, s, p) for s, p, q in self.moves()])

    def to_chip(self, v):
        return self.send(v, [(s, p, s, q) for s, p, q in self.moves()])

    def to_plane(self, v):
        return self.send(v, [(s, q, p, q) for s, p, q in self.moves()])

    def from_plane(self, v):
        return self.send(v, [(p, q, s, q) for s, p, q in self.moves()])

    def from_chip(self, v):
        return self.send(v, [(s, q, s, p) for s, p, q in self.moves()])

    def chip(self, v, j):
        return lax.ppermute(v, "fsdp", xor_pairs(self.n_f, 2 * j))

    def core(self, v):
        return lax.ppermute(v, "fsdp", xor_pairs(self.n_f, 1))

    def next_plane(self, v):
        return lax.ppermute(v, "seq", xor_pairs(self.n_s, 1))

    def gather(self, v):
        return [v] + [self.chip(v, j) for j in range(1, self.n_p)]

    def exchange(self, blocks):
        return [blocks[0]] + [self.chip(blocks[j], j) for j in range(1, self.n_p)]


def fence(values):
    return lax.optimization_barrier(values)


def block(v, index, size, axis):
    return lax.dynamic_slice_in_dim(v, index * size, size, axis=axis)


IN_VMEM = pl.BlockSpec(memory_space=pltpu.VMEM)
IN_SMEM = pl.BlockSpec(memory_space=pltpu.SMEM)
IN_ANY = pl.BlockSpec(memory_space=pl.ANY)
IN_HBM = pl.BlockSpec(memory_space=pltpu.HBM)


def run(name, body, outs, ins, place=None, scratch=(), flops=0, ins_at=None):
    specs = [IN_VMEM] * len(ins) if ins_at is None else ins_at
    if place is not None:
        specs = [IN_SMEM] + specs
        ins = [place, *ins]
    moved = sum(v.size * v.dtype.itemsize for v in ins)
    return pl.pallas_call(
        body,
        out_shape=[jax.ShapeDtypeStruct(shape, dtype) for shape, dtype in outs],
        in_specs=specs,
        out_specs=[IN_VMEM] * len(outs),
        scratch_shapes=list(scratch),
        compiler_params=pltpu.CompilerParams(vmem_limit_bytes=16 << 20),
        cost_estimate=pl.CostEstimate(flops=flops, bytes_accessed=moved, transcendentals=0),
        name=name,
    )(*ins)


def dot(a, b):
    return jnp.dot(a, b, preferred_element_type=F32)


def dot_nt(a, b):
    return lax.dot_general(a, b, (((1,), (1,)), ((), ())), preferred_element_type=F32)


def dot_tn(a, b):
    return lax.dot_general(a, b, (((0,), (0,)), ((), ())), preferred_element_type=F32)


def tile(i, size):
    return pl.ds(pl.multiple_of(i * size, size), size)


def copy_all(pairs, sems):
    copies = [pltpu.make_async_copy(src, dst, sems.at[k]) for k, (src, dst) in enumerate(pairs)]
    for copy in copies:
        copy.start()
    return copies


def own_first(v, parts, c):
    rows = v.shape[-1] // (2 * parts)
    own, other = [], []
    for i in range(parts):
        even = v[:, 2 * i * rows : (2 * i + 1) * rows]
        odd = v[:, (2 * i + 1) * rows : (2 * i + 2) * rows]
        own.append(jnp.where(c == 0, even, odd))
        other.append(jnp.where(c == 0, odd, even))
    return jnp.concatenate(own, axis=1), jnp.concatenate(other, axis=1)


def model_order(v, parts, c):
    half = v.shape[-1] // 2
    rows = half // parts
    out = []
    for i in range(parts):
        own = v[:, i * rows : (i + 1) * rows]
        other = v[:, half + i * rows : half + (i + 1) * rows]
        out += [jnp.where(c == 0, own, other), jnp.where(c == 0, other, own)]
    return jnp.concatenate(out, axis=1)


def cut_columns(net, weight, layer, groups):
    n_p = net.n_p
    rows = weight.shape[1] // 2
    width = weight.shape[2] // (groups * n_p)

    def body(place, weight_ref, *refs):
        p, half = place[0], place[2]
        outs, sems = refs[: n_p - 1], refs[-1]
        pairs = []
        for j in range(1, n_p):
            for i in range(groups):
                cols = tile(i * n_p + (p ^ j), width)
                to = outs[j - 1].at[:, i * width : (i + 1) * width]
                pairs.append((weight_ref.at[layer, tile(half, rows), cols], to))
        for copy in copy_all(pairs, sems):
            copy.wait()

    outs = [((rows, groups * width), BF)] * (n_p - 1)
    scratch = [pltpu.SemaphoreType.DMA((groups * (n_p - 1),))]
    return run("cut_columns", body, outs, [weight], net.place, scratch, ins_at=[IN_HBM])


def stack_halves(pieces):
    rows, width = pieces[0].shape
    count = len(pieces)

    def body(*refs):
        out, sems = refs[count:]
        pairs = [(refs[j], out.at[j * rows : (j + 1) * rows]) for j in range(count)]
        for copy in copy_all(pairs, sems):
            copy.wait()

    outs = [((count * rows, width), BF)]
    scratch = [pltpu.SemaphoreType.DMA((count,))]
    return run("stack_halves", body, outs, pieces, None, scratch, ins_at=[IN_ANY] * count)[0]


def stack_rows(net, mine, theirs, weight, groups, more, layer):
    n_p = net.n_p
    half_rows = weight.shape[1] // 2
    rows = 2 * half_rows
    width = weight.shape[2] // (groups * n_p)

    def body(place, mine_ref, their_ref, weight_ref, more_ref, own, rest, sems):
        p, half = place[0], place[2]
        pairs = [(more_ref.at[layer], rest)]
        for i in range(groups):
            to = own.at[tile(p, rows), i * width : (i + 1) * width]
            pairs.append((weight_ref.at[layer, :, tile(i * n_p + p, width)], to))
        for j in range(1, n_p):
            here = slice((j - 1) * half_rows, j * half_rows)
            at = (p ^ j) * 2
            pairs.append((mine_ref.at[here], own.at[tile(at + half, half_rows)]))
            pairs.append((their_ref.at[here], own.at[tile(at + 1 - half, half_rows)]))
        for copy in copy_all(pairs, sems):
            copy.wait()

    outs = [((n_p * rows, groups * width), BF), (more.shape[1:], BF)]
    scratch = [pltpu.SemaphoreType.DMA((1 + groups + 2 * (n_p - 1),))]
    specs = [IN_ANY] * 2 + [IN_HBM] * 2
    return run("stack_rows", body, outs, [mine, theirs, weight, more], net.place, scratch, ins_at=specs)


def pack_tokens(tokens, scene_ids, token_kind):
    rows = tokens.shape[1]
    code = (scene_ids * 2 + token_kind).astype(BF)
    return jnp.pad(tokens[0], ((0, 16), (0, 0))) + jnp.pad(code, ((rows, 15), (0, D - rows)))


def pack_small(vectors):
    sizes = [v.shape[1] for v in vectors]
    total = None
    for k, v in enumerate(vectors):
        at = sum(sizes[:k])
        put = jnp.pad(v, ((0, 0), (at, sum(sizes) - at - sizes[k])))
        total = put if total is None else total + put
    return total


def put_small(tokens, own, other):
    rows = tokens.shape[0] - 16
    width = own.shape[1] // 2

    def body(token_ref, own_ref, other_ref, out, lines):
        out[0:rows, :] = token_ref[0:rows, :]
        lines[...] = token_ref[rows:, :].astype(F32)
        row = 1
        for ref in (own_ref, other_ref):
            low = ref[...].astype(F32)
            for layer in range(own.shape[0]):
                for half in range(2):
                    lines[row : row + 1, 0:width] = low[layer : layer + 1, half * width : (half + 1) * width]
                    row += 1
        out[rows:, :] = lines[...].astype(BF)

    scratch = [pltpu.VMEM((16, D), F32)]
    return run("put_small", body, [(tokens.shape, BF)], [tokens, own, other], None, scratch)[0]


def join_vectors(net, layers, blocks, sizes, rows):
    n_p = net.n_p
    width = sum(sizes) // 2
    starts = [sum(sizes[:i]) for i in range(len(sizes))]

    def body(place, *refs):
        p, c = place[0], place[1]
        ins, outs = refs[:n_p], refs[n_p:]
        for j in range(n_p):
            low = ins[j][rows : rows + 16, 0:width].astype(F32)
            for layer in range(layers):
                for half in range(2):
                    row = 1 + layer * 2 + half
                    own = low[row : row + 1, :]
                    other = low[2 * layers + row : 2 * layers + row + 1, :]
                    first = jnp.where(c == 0, own, other)
                    second = jnp.where(c == 0, other, own)
                    for k, (at, size) in enumerate(zip(starts, sizes)):
                        if at // width != half:
                            continue
                        cols = slice(at - half * width, at - half * width + size)
                        both = jnp.concatenate([first[:, cols], second[:, cols]], axis=1)
                        outs[k][layer : layer + 1, tile(p ^ j, 2 * size)] = both

    outs = [((layers, 2 * n_p * size), F32) for size in sizes]
    return run("join_vectors", body, outs, blocks, net.place)


def norm_rows(hidden):
    centred = hidden - jnp.mean(hidden, axis=-1, keepdims=True)
    spread = jnp.mean(centred * centred, axis=-1, keepdims=True)
    inverse = lax.rsqrt(spread + EPS)
    return centred * inverse, inverse


def add_and_norm(net, layer, hidden, parts, bias, norm):
    rows = parts[0].shape[0]
    count = len(parts)

    def body(place, *refs):
        total = refs[0][0:rows, :].astype(F32) + refs[1 + count][layer : layer + 1, :]
        for part in refs[1 : 1 + count]:
            total = total + part[...].astype(F32)
        if norm is None:
            refs[2 + count][...] = total.astype(BF)
            return
        gain, shift, out, low = refs[2 + count : 6 + count]
        normed, _ = norm_rows(total)
        row = slice(norm[0], norm[0] + 1)
        out[...] = total
        own, other = own_first(normed * gain[row, :] + shift[row, :], net.n_p, place[1])
        low[:, : D // 2] = own.astype(BF)
        low[:, D // 2 :] = other.astype(BF)

    ins = [hidden, *parts, bias] + ([] if norm is None else list(norm[1:]))
    outs = [((rows, D), BF)] if norm is None else [((rows, D), F32), ((rows, D), BF)]
    return run("add_and_norm", body, outs, ins, net.place)


def norm_back(net, layer, grad, hidden, parts, gain):
    rows = parts[0].shape[0]
    count = len(parts)

    def body(place, grad_ref, hidden_ref, gain_ref, *refs):
        total = refs[0][...].astype(F32)
        for part in refs[1:count]:
            total = total + part[...].astype(F32)
        total = model_order(total, net.n_p, place[1])
        out, low, sums = refs[count:]
        normed, inverse = norm_rows(hidden_ref[0:rows, :].astype(F32))
        scaled = total * gain_ref[layer : layer + 1, :]
        one = jnp.mean(scaled, axis=-1, keepdims=True)
        two = jnp.mean(scaled * normed, axis=-1, keepdims=True)
        result = grad_ref[...].astype(F32) + inverse * (scaled - one - normed * two)
        rounded = result.astype(BF)
        out[...] = result
        low[...] = rounded
        sums[0:1, :] = jnp.sum(total * normed, axis=0, keepdims=True)
        sums[1:2, :] = jnp.sum(total, axis=0, keepdims=True)
        sums[2:3, :] = jnp.sum(rounded.astype(F32), axis=0, keepdims=True)

    outs = [((rows, D), F32), ((rows, D), BF), ((3, D), F32)]
    return run("norm_back", body, outs, [grad, hidden, gain, *parts], net.place)


def column_sums(v):
    def body(ref, out):
        out[...] = jnp.sum(ref[...].astype(F32), axis=0, keepdims=True)

    return run("column_sums", body, [((1, v.shape[1]), F32)], [v])[0]


def gather_rows(blocks, scratch):
    rows = scratch.shape[0] // len(blocks)
    for j, ref in enumerate(blocks):
        scratch[j * rows : (j + 1) * rows, :] = ref[0:rows, :]


def allowed_pairs(code_col, code_row):
    same = (code_col >> 1) == (code_row >> 1)
    return same & (((code_col & 1) == 0) | ((code_row & 1) == 1))


def head_lanes(shape, head, axis):
    lane = lax.broadcasted_iota(jnp.int32, shape, axis)
    return (lane < HEAD_DIM) if head == 0 else (lane >= HEAD_DIM)


def keep_head(v, head, axis):
    return jnp.where(head_lanes(v.shape, head, axis), v, jnp.zeros_like(v))


def probs_by_key(k2, q2, allowed, head):
    scores = jnp.where(allowed, dot_nt(keep_head(k2, head, 1), q2), NEG)
    powers = jnp.exp(scores - jnp.max(scores, axis=0, keepdims=True))
    return powers * (1.0 / jnp.sum(powers, axis=0, keepdims=True))


Q_TILE = 256


def attend(net, layer, rows, blocks, norm, weight, bias, codes, proj):
    n_p = net.n_p
    tokens = n_p * rows
    cw = D // n_p
    first = norm is not None

    def body(place, *refs):
        bias_ref, w_own, w_other, p_own, p_other = refs[n_p : n_p + 5]
        if first:
            gain_ref, shift_ref = refs[n_p + 5 : n_p + 7]
            row_ref, col_ref, a = refs[n_p + 7 : n_p + 10]
            outs = refs[n_p + 10 : 2 * n_p + 10]
            qkv, attended, vt = refs[2 * n_p + 10 :]
        else:
            row_ref, col_ref = refs[n_p + 5 : n_p + 7]
            outs = refs[n_p + 7 : 2 * n_p + 7]
            qkv, attended, vt, a = refs[2 * n_p + 7 :]
        p, c = place[0], place[1]
        if first:
            eye = lax.broadcasted_iota(jnp.int32, (rows, rows), 0) == lax.broadcasted_iota(
                jnp.int32, (rows, rows), 1
            )
            for j in range(n_p):
                here = slice(j * rows, (j + 1) * rows)
                line = refs[j][rows : rows + 1, 0:rows].astype(F32)
                row_ref[:, here] = line.astype(jnp.int32)
                column = jnp.sum(jnp.where(eye, line, 0.0), axis=1, keepdims=True)
                col_ref[here, :] = column.astype(jnp.int32)
                normed, _ = norm_rows(refs[j][0:rows, :].astype(F32))
                own, other = own_first(normed * gain_ref[0:1, :] + shift_ref[0:1, :], n_p, c)
                a[here, : D // 2] = own.astype(BF)
                a[here, D // 2 :] = other.astype(BF)
        else:
            gather_rows(refs[:n_p], a)
        for i in range(3):
            cols = slice(i * cw, (i + 1) * cw)
            out = dot(a[:, : D // 2], w_own[:, cols]) + dot(a[:, D // 2 :], w_other[:, cols])
            if i == 0:
                out = out + bias_ref[layer : layer + 1, tile(p, cw)]
            if i == 2:
                out = out + bias_ref[layer : layer + 1, tile(p + n_p, cw)]
            qkv[:, cols] = out.astype(BF)
        vt[...] = jnp.transpose(qkv[:, 2 * cw : 3 * cw].astype(F32)).astype(BF)

        @pl.loop(0, tokens // Q_TILE)
        def _(t):
            here = tile(t, Q_TILE)
            allowed = allowed_pairs(col_ref[...], row_ref[:, here])
            for pair in range(cw // LANES):
                lanes = slice(pair * LANES, (pair + 1) * LANES)
                q2 = qkv[here, lanes]
                k2 = qkv[:, cw + pair * LANES : cw + (pair + 1) * LANES]
                total = None
                for head in range(2):
                    probs = probs_by_key(k2, q2 * BF(SCALE), allowed, head).astype(BF)
                    part = dot(keep_head(vt[lanes, :], head, 0), probs)
                    total = part if total is None else total + part
                attended[here, lanes] = jnp.transpose(total).astype(BF)

        for j in range(n_p):
            o = attended[j * rows : (j + 1) * rows, :]
            low, high = o[:, : cw // 2], o[:, cw // 2 :]
            own, other = jnp.where(c == 0, low, high), jnp.where(c == 0, high, low)
            outs[j][...] = (dot(own, p_own[...]) + dot(other, p_other[...])).astype(BF)

    outs = [((rows, D), BF)] * n_p + [((tokens, 3 * cw), BF), ((tokens, cw), BF)]
    scratch = [pltpu.VMEM((cw, tokens), BF)]
    ins = [*blocks, bias, *weight, *proj]
    if first:
        ins += list(norm)
        outs = [((1, tokens), jnp.int32), ((tokens, 1), jnp.int32), ((tokens, D), BF)] + outs
    else:
        ins += list(codes)
        scratch.append(pltpu.VMEM((tokens, D), BF))
    got = run("attend", body, outs, ins, net.place, scratch, flops=2 * tokens * D * 4 * cw)
    normed = blocks
    if first:
        codes, normed, got = got[:2], [got[2]], got[3:]
    return got[:n_p], got[n_p], got[n_p + 1], codes, normed


def attend_back(net, blocks, proj, qkv, codes, weight, tokens_in):
    n_p = net.n_p
    rows = blocks[0].shape[0]
    tokens = n_p * rows
    cw = D // n_p
    n_t = len(tokens_in)

    def body(place, *refs):
        p_own, p_other, qkv_ref, row_ref, col_ref, w_own, w_other = refs[n_p : n_p + 7]
        token_refs = refs[n_p + 7 : n_p + 7 + n_t]
        refs_out = refs[n_p + 7 + n_t :]
        outs = refs_out[:n_p]
        dqkv, sums, norm_sums, do, kt, dk, dv = refs_out[n_p:]
        c = place[1]
        for j in range(n_p):
            here = slice(j * rows, (j + 1) * rows)
            own, other = dot_nt(refs[j][...], p_own[...]), dot_nt(refs[j][...], p_other[...])
            do[here, : cw // 2] = jnp.where(c == 0, own, other).astype(BF)
            do[here, cw // 2 :] = jnp.where(c == 0, other, own).astype(BF)
        kt[...] = jnp.transpose(qkv_ref[:, cw : 2 * cw].astype(F32)).astype(BF)
        dk[...] = jnp.zeros_like(dk)
        dv[...] = jnp.zeros_like(dv)

        @pl.loop(0, tokens // Q_TILE)
        def _(t):
            here = tile(t, Q_TILE)
            allowed = allowed_pairs(col_ref[...], row_ref[:, here])
            for pair in range(cw // LANES):
                lanes = slice(pair * LANES, (pair + 1) * LANES)
                q2 = qkv_ref[here, lanes]
                k2 = qkv_ref[:, cw + pair * LANES : cw + (pair + 1) * LANES]
                v2 = qkv_ref[:, 2 * cw + pair * LANES : 2 * cw + (pair + 1) * LANES]
                do2 = do[here, lanes]
                total = None
                for head in range(2):
                    probs = probs_by_key(k2, q2 * BF(SCALE), allowed, head)
                    dp = dot_nt(keep_head(v2, head, 1), do2)
                    mean = jnp.sum(probs * dp, axis=0, keepdims=True)
                    ds = (probs * (dp - mean)).astype(BF)
                    dv[:, lanes] += dot(probs.astype(BF), keep_head(do2, head, 1))
                    dk[:, lanes] += dot(ds, keep_head(q2, head, 1))
                    part = dot(keep_head(kt[lanes, :], head, 0), ds)
                    total = part if total is None else total + part
                dqkv[here, lanes] = (jnp.transpose(total) * SCALE).astype(BF)

        dqkv[:, cw : 2 * cw] = (dk[...] * SCALE).astype(BF)
        dqkv[:, 2 * cw :] = dv[...].astype(BF)
        sums[...] = jnp.sum(dqkv[...].astype(F32), axis=0, keepdims=True)
        norm_sums[...] = jnp.zeros_like(norm_sums)
        for j in range(n_p):
            normed = None
            if n_t:
                normed = own_first(norm_rows(token_refs[j][0:rows, :].astype(F32))[0], n_p, c)
            for k, w in enumerate((w_own, w_other)):
                cols = slice(k * (D // 2), (k + 1) * (D // 2))
                da1 = dot_nt(dqkv[j * rows : (j + 1) * rows, :], w[...])
                outs[j][:, cols] = da1.astype(BF)
                if n_t:
                    norm_sums[0:1, cols] += jnp.sum(da1 * normed[k], axis=0, keepdims=True)
                    norm_sums[1:2, cols] += jnp.sum(da1, axis=0, keepdims=True)

    outs = [((rows, D), BF)] * n_p + [((tokens, 3 * cw), BF), ((1, 3 * cw), F32), ((2, D), F32)]
    scratch = [
        pltpu.VMEM((tokens, cw), BF),
        pltpu.VMEM((cw, tokens), BF),
        pltpu.VMEM((tokens, cw), F32),
        pltpu.VMEM((tokens, cw), F32),
    ]
    ins = [*blocks, *proj, qkv, *codes, *weight, *tokens_in]
    got = run("attend_back", body, outs, ins, net.place, scratch, flops=2 * tokens * D * 8 * cw)
    return got[:n_p], got[n_p], got[n_p + 1], got[n_p + 2]


F_TILE = 256


def feed_forward(net, layer, blocks, up, bias, down):
    n_p = net.n_p
    rows = blocks[0].shape[0]
    tokens = n_p * rows
    fw = FF // n_p

    def body(place, *refs):
        up_own, up_other, bias_ref, d_own, d_other = refs[n_p : n_p + 5]
        outs = refs[n_p + 5 : 2 * n_p + 5]
        z_ref, slope_ref, a_ref = refs[2 * n_p + 5 :]
        p, c = place[0], place[1]
        gather_rows(refs[:n_p], a_ref)

        @pl.loop(0, fw // F_TILE)
        def _(t):
            cols = tile(t, F_TILE)
            there = pl.ds(pl.multiple_of(p * fw + t * F_TILE, F_TILE), F_TILE)
            u = dot(a_ref[:, : D // 2], up_own[:, cols]) + dot(a_ref[:, D // 2 :], up_other[:, cols])
            u = u + bias_ref[layer : layer + 1, there]
            phi = 0.5 * (1.0 + lax.erf(u * 0.7071067811865476))
            z_ref[:, cols] = (u * phi).astype(BF)
            slope_ref[:, cols] = phi + u * (jnp.exp(-0.5 * u * u) * 0.3989422804014327)

        for j in range(n_p):
            here = slice(j * rows, (j + 1) * rows)
            own, other = z_ref[here, tile(c, fw // 2)], z_ref[here, tile(1 - c, fw // 2)]
            outs[j][...] = (dot(own, d_own[...]) + dot(other, d_other[...])).astype(BF)

    outs = [((rows, D), BF)] * n_p + [((tokens, fw), BF), ((tokens, fw), F32)]
    scratch = [pltpu.VMEM((tokens, D), BF)]
    ins = [*blocks, *up, bias, *down]
    got = run("feed_forward", body, outs, ins, net.place, scratch, flops=4 * tokens * D * fw)
    return got[:n_p], got[n_p], got[n_p + 1]


def feed_back(net, blocks, down, slope, up):
    n_p = net.n_p
    rows = blocks[0].shape[0]
    tokens = n_p * rows
    fw = FF // n_p

    def body(place, *refs):
        d_own, d_other, slope_ref, up_own, up_other = refs[n_p : n_p + 5]
        outs = refs[n_p + 5 : 2 * n_p + 5]
        du_ref, sums, dm = refs[2 * n_p + 5 :]
        c = place[1]
        gather_rows(refs[:n_p], dm)
        for w, core in ((d_own, c), (d_other, 1 - c)):

            @pl.loop(0, fw // (2 * F_TILE))
            def _(t):
                start = core * (fw // 2) + t * F_TILE
                cols = pl.ds(pl.multiple_of(start, F_TILE), F_TILE)
                dz = dot_nt(dm[...], w[tile(t, F_TILE), :])
                du = (dz * slope_ref[:, cols]).astype(BF)
                du_ref[:, cols] = du
                sums[:, cols] = jnp.sum(du.astype(F32), axis=0, keepdims=True)

        for j in range(n_p):
            du = du_ref[j * rows : (j + 1) * rows, :]
            outs[j][:, : D // 2] = dot_nt(du, up_own[...]).astype(BF)
            outs[j][:, D // 2 :] = dot_nt(du, up_other[...]).astype(BF)

    outs = [((rows, D), BF)] * n_p + [((tokens, fw), BF), ((1, fw), F32)]
    scratch = [pltpu.VMEM((tokens, D), BF)]
    ins = [*blocks, *down, slope, *up]
    got = run("feed_back", body, outs, ins, net.place, scratch, flops=4 * tokens * D * fw)
    return got[:n_p], got[n_p], got[n_p + 1]


def down_weight_grad(net, z, dm):
    n_r = len(dm)
    tokens, m = z.shape
    half = m // 2

    def body(place, z_ref, *refs):
        keep, send, b = refs[n_r:]
        c = place[1]
        gather_rows(refs[:n_r], b)
        keep[...] = dot_tn(z_ref[:, tile(c, half)], b[...]).astype(BF)
        send[...] = dot_tn(z_ref[:, tile(1 - c, half)], b[...]).astype(BF)

    outs = [((half, D), BF)] * 2
    scratch = [pltpu.VMEM((tokens, D), BF)]
    return run("down_weight_grad", body, outs, [z, *dm], net.place, scratch, flops=2 * tokens * m * D)


def up_weight_grad(net, a2, du):
    n_l = len(a2)
    tokens, n = du.shape

    def body(place, *refs):
        du_ref, out, a = refs[n_l:]
        c = place[1]
        gather_rows(refs[:n_l], a)
        out[c] = dot_tn(a[:, : D // 2], du_ref[...]).astype(BF)
        out[1 - c] = dot_tn(a[:, D // 2 :], du_ref[...]).astype(BF)

    scratch = [pltpu.VMEM((tokens, D), BF)]
    outs = [((2, D // 2, n), BF)]
    return run("up_weight_grad", body, outs, [*a2, du], net.place, scratch, flops=2 * tokens * D * n)[0]


def attend_weight_grad(net, a1, dqkv, attended, dy, small):
    n_p = net.n_p
    n_a = len(a1)
    tokens, width = dqkv.shape
    cw = D // n_p
    rows = D // net.n_f
    extra = 16 if small else 0
    flat = [v for of_layer in small[1] for v in of_layer] if small else []
    sizes = small[0] if small else []
    starts = [sum(sizes[:i]) for i in range(len(sizes))]

    def put_small(place, refs, low):
        p, c = place[0], place[1]
        low[...] = jnp.zeros_like(low)
        for k, (ref, (_, kind)) in enumerate(zip(refs, flat)):
            layer, which = divmod(k, len(sizes))
            at, size = starts[which], sizes[which]
            half = at // width
            row = slice(2 * layer + half, 2 * layer + half + 1)
            cols = slice(at - half * width, at - half * width + size)
            if kind == "chip":
                low[0, p, row, cols] = ref[:, :size]
                low[1, p, row, cols] = ref[:, size:]
            elif kind == "heads":
                low[p % 2, p // 2, row, cols] = ref[:, :size]
                low[p % 2, p // 2 + n_p // 2, row, cols] = ref[:, 2 * size :]
            elif kind == "own":
                for i in range(n_p):
                    low[c, i, row, cols] = ref[:, i * size : (i + 1) * size]
                    low[1 - c, i, row, cols] = ref[:, D // 2 + i * size : D // 2 + (i + 1) * size]
            else:
                for i in range(n_p):
                    for core in range(2):
                        to = (2 * i + core) * size
                        low[core, i, row, cols] = ref[:, to : to + size]

    def body(place, *refs):
        dqkv_ref, attended_ref = refs[n_a : n_a + 2]
        smalls = refs[n_a + 2 + n_p : n_a + 2 + n_p + len(flat)]
        out, a, b, low, lines = refs[n_a + 2 + n_p + len(flat) :]
        c = place[1]
        gather_rows(refs[:n_a], a)
        for k, core in ((0, c), (1, 1 - c)):
            both = dot_tn(a[:, k * (D // 2) : (k + 1) * (D // 2)], dqkv_ref[...]).astype(BF)
            for i in range(n_p):
                out[core, i * (rows + extra) : i * (rows + extra) + rows, :width] = both[i * rows : (i + 1) * rows]
        gather_rows(refs[n_a + 2 : n_a + 2 + n_p], b)
        low[...] = dot_tn(attended_ref[...], b[...]).astype(BF)
        for core in range(2):
            for i in range(n_p):
                here = slice(i * (rows + extra), i * (rows + extra) + rows)
                out[core, here, width:] = low[core * rows : (core + 1) * rows, i * cw : (i + 1) * cw]
        if extra:
            put_small(place, smalls, lines)
            for core in range(2):
                for i in range(n_p):
                    here = slice(i * (rows + extra) + rows, (i + 1) * (rows + extra))
                    out[core, here, :width] = lines[core, i].astype(BF)
                    out[core, here, width:] = jnp.zeros((extra, cw), BF)

    outs = [((2, n_p * (rows + extra), width + cw), BF)]
    scratch = [pltpu.VMEM((tokens, D), BF), pltpu.VMEM((tokens, D), BF), pltpu.VMEM((cw, D), BF)]
    scratch.append(pltpu.VMEM((2, n_p, 16, width), F32))
    flops = 2 * tokens * D * (width + cw)
    ins = [*a1, dqkv, attended, *dy, *[v for v, _ in flat]]
    return run("attend_weight_grad", body, outs, ins, net.place, scratch, flops=flops)[0]


def add_halves(a, b):
    rows, width = a.shape
    half = width // 2

    def body(a_ref, b_ref, *outs):
        for k in range(2):
            cols = slice(k * half, (k + 1) * half)
            outs[k][...] = (a_ref[:, cols].astype(F32) + b_ref[:, cols].astype(F32)).astype(BF)

    return run("add_halves", body, [((rows, half), BF)] * 2, [a, b])


def add_pair(both):
    _, rows, width = both.shape
    half = width // 2

    def body(ref, *outs):
        for k in range(2):
            cols = slice(k * half, (k + 1) * half)
            outs[k][...] = (ref[0, :, cols].astype(F32) + ref[1, :, cols].astype(F32)).astype(BF)

    return run("add_pair", body, [((rows, half), BF)] * 2, [both])


def cut_rows(net, first, second, extra):
    n_p = net.n_p
    rows = first.shape[0] // n_p
    width, more = first.shape[1], second.shape[1]
    split = extra is not None
    taken = more // 2 if split else more

    def body(place, a, b, *outs):
        p = place[0]
        for j in range(n_p):
            here = tile(p ^ j, rows)
            outs[j][:, :width] = a[here, :]
            outs[j][:, width:] = b[here, :taken]
        if split:
            for i in range(n_p):
                outs[n_p][:, i * taken : (i + 1) * taken] = b[i * rows : (i + 1) * rows - extra, taken:]

    outs = [((rows, width + taken), BF)] * n_p
    if split:
        outs.append(((rows - extra, n_p * taken), BF))
    return run("cut_rows", body, outs, [first, second], net.place)


def cut_part(net, v, groups, extra=None):
    n_p = net.n_p
    rows = v.shape[0] // n_p
    taken = groups * (D // n_p)
    rest = v.shape[1] - taken

    def body(place, ref, *outs):
        p = place[0]
        for j in range(n_p):
            outs[j][...] = ref[tile(p ^ j, rows), :taken]
        if extra is not None:
            for i in range(n_p):
                outs[n_p][:, i * rest : (i + 1) * rest] = ref[i * rows : (i + 1) * rows - extra, taken:]

    outs = [((rows, taken), BF)] * n_p
    if extra is not None:
        outs.append(((rows - extra, n_p * rest), BF))
    return run("cut_part", body, outs, [v], net.place)


def sum_small(layers, first, second, sizes, rows):
    count = len(first)
    split = first[0].shape[1]
    width = split + second[0].shape[1]
    starts = [sum(sizes[:i]) for i in range(len(sizes))]

    def body(*refs):
        parts = []
        for group in (refs[:count], refs[count : 2 * count]):
            total = group[0][rows:, :].astype(F32)
            for ref in group[1:]:
                total = total + ref[rows:, :].astype(F32)
            parts.append(total)
        total = jnp.concatenate(parts, axis=1)
        for out, at, size in zip(refs[2 * count :], starts, sizes):
            half = at // width
            for layer in range(layers):
                row = 2 * layer + half
                out[layer : layer + 1, :] = total[row : row + 1, at - half * width : at - half * width + size]

    return run("sum_small", body, [((layers, size), F32) for size in sizes], [*first, *second])


def take_if(here, a, b, rows):
    def body(flag, a_ref, b_ref, out):
        @pl.when(flag[0] != 0)
        def _():
            count = min(rows, a.shape[0])
            out[0:count, :] = a_ref[0:count, :]

        @pl.when(flag[0] == 0)
        def _():
            count = min(rows, b.shape[0])
            out[0:count, :] = b_ref[0:count, :]

    return run("take_if", body, [((rows, a.shape[1]), BF)], [a, b], here.astype(jnp.int32).reshape(1))[0]


def turn(net, wanted):
    flat, flags, outs = [], [], []
    for one, two, outer in wanted:
        flat += one + (two or [])
        rows = max(one[0].shape[0], two[0].shape[0] if two else 0)
        outs.append(((rows, one[0].shape[1]), BF))
        flags.append(jnp.zeros((), jnp.int32) if outer is None else outer.astype(jnp.int32))

    def put(refs, out):
        rows = refs[0].shape[0]
        if len(refs) == 1:
            out[0:rows, :] = refs[0][...]
            return
        total = refs[0][...].astype(F32)
        for ref in refs[1:]:
            total = total + ref[0:rows, :].astype(F32)
        out[0:rows, :] = total.astype(BF)

    def body(flag, *refs):
        at = 0
        for k, (one, two, outer) in enumerate(wanted):
            out = refs[len(flat) + k]
            first = refs[at : at + len(one)]
            at += len(one)
            if outer is None:
                put(first, out)
                continue
            second = refs[at : at + len(two)]
            at += len(two)
            pl.when(flag[k] != 0)(lambda first=first, out=out: put(first, out))
            pl.when(flag[k] == 0)(lambda second=second, out=out: put(second, out))

    return run("turn", body, outs, flat, jnp.stack(flags))


class Chunk:
    def __init__(self, value):
        self.terms = [value]
        self.step = 0

    @property
    def value(self):
        return self.terms[0]


class Flow:
    def __init__(self, net):
        self.net = net
        self.queue = []
        self.moving = []

    def first(self, step):
        for chunk in self.queue:
            if chunk.step == step:
                return chunk
        return None

    def start(self):
        net = self.net
        n = net.n_s
        half = n // 2
        moves, wanted = [], []
        for k in range(half):
            inward = self.first(k)
            outward = None if k == half - 1 else self.first(n - 2 - k)
            into = [(k, k + 1), (n - 1 - k, n - 2 - k)]
            out = [(k + 1, k), (n - 2 - k, n - 1 - k)]
            outer = (net.s == k) | (net.s == n - 1 - k)
            both = inward is not None and outward is not None
            if both and inward.value.shape[1] == outward.value.shape[1]:
                moves.append((inward, outward, outer, into + out))
                wanted.append((inward.terms, outward.terms, outer))
                continue
            if inward is not None:
                moves.append((inward, None, outer, into))
                wanted.append((inward.terms, None, None))
            if outward is not None:
                moves.append((None, outward, outer, out))
                wanted.append((outward.terms, None, None))
        sent = [w[0][0] for w in wanted]
        work = [k for k, w in enumerate(wanted) if len(w[0]) > 1 or w[1] is not None]
        if work:
            for k, value in zip(work, turn(net, [wanted[k] for k in work])):
                sent[k] = value
        self.moving = [(*m[:3], v, lax.ppermute(v, "seq", m[3])) for m, v in zip(moves, sent)]

    def collect(self, values, *new):
        values, news, got = fence((values, [c.value for c in new], [(m[3], m[4]) for m in self.moving]))
        for c, value in zip(new, news):
            c.terms = [value]
        n = self.net.n_s
        for (inward, outward, outer, _, _), (sent, arrived) in zip(self.moving, got):
            if inward is not None:
                middle = inward.step == n // 2 - 1
                inward.terms = [sent, arrived] if middle else [*inward.terms, arrived]
                inward.step += 1
            if outward is not None:
                outward.terms = [take_if(outer, arrived, sent, outward.value.shape[0])]
                outward.step += 1
        self.queue = [c for c in self.queue if c.step < n - 1] + list(new)
        self.start()
        return values


def write_layer(net, layer, layers, before, down, proj, up, qkv):
    n_p = net.n_p
    rows = up[0].shape[0]
    cw, fw = D // n_p, FF // n_p
    split = isinstance(qkv[0], tuple)
    flat = [v for pair in qkv for v in pair] if split else list(qkv)
    n_in = 3 + n_p + len(flat)
    skip = 0 if before is None else 4
    steps = min(4, rows // 16)
    part = rows // steps
    down_rows = down[0].shape[0]
    down_part = down_rows // steps

    def body(place, *refs):
        p = place[0]
        downs, proj_ref = refs[:2], refs[2]
        ups, qkvs = refs[3 : 3 + n_p], refs[3 + n_p : n_in]
        qkv_out, proj_out, up_out, down_out = refs[n_in + skip :]
        proj_out[0] = proj_ref[...].astype(F32)
        for k in range(2):
            down_out[0, :, k * (D // 2) : (k + 1) * (D // 2)] = downs[k][...].astype(F32)
        for j in range(n_p):
            up_out[0, :, tile(p ^ j, fw)] = ups[j][...].astype(F32)
            for i in range(3):
                to = tile(i * n_p + (p ^ j), cw)
                ref, at = (qkvs[2 * j + i // 2], i % 2) if split else (qkvs[j], i)
                qkv_out[0, :, to] = ref[:, at * cw : (at + 1) * cw].astype(F32)

    def of_rows(v, size):
        return pl.BlockSpec((size, v.shape[1]), lambda i: (i, 0))

    ins = [*down, proj, *up, *flat]
    specs = [IN_SMEM] + [of_rows(v, down_part) for v in down] + [of_rows(v, part) for v in [proj, *up, *flat]]
    aliases = {}
    if before is not None:
        aliases = {1 + n_in + k: k for k in range(4)}
        specs += [IN_ANY] * 4
        ins = ins + list(before)
    shapes = [(rows, 3 * D), (rows, D), (rows, FF), (down_rows, D)]
    sizes = [part, part, part, down_part]
    return pl.pallas_call(
        body,
        grid=(steps,),
        out_shape=[jax.ShapeDtypeStruct((layers, *shape), F32) for shape in shapes],
        in_specs=specs,
        out_specs=[
            pl.BlockSpec((1, size, shape[1]), lambda i: (layer, i, 0)) for size, shape in zip(sizes, shapes)
        ],
        input_output_aliases=aliases,
        compiler_params=pltpu.CompilerParams(vmem_limit_bytes=16 << 20),
        name="write_layer",
    )(net.place, *ins)


def on_device(
    tokens,
    scene_ids,
    token_kind,
    out_grad,
    first_gain,
    first_shift,
    qkv_weight,
    qv_bias,
    proj_weight,
    proj_bias,
    second_gain,
    second_shift,
    up_weight,
    up_bias,
    down_weight,
    down_bias,
):
    net = Net()
    n_p = net.n_p
    layers = qkv_weight.shape[0]
    rows = tokens.shape[1]
    pair_groups = [[2 * i, 2 * i + 1] for i in range(n_p)]

    def fetch(weight, layer, groups):
        pieces = cut_columns(net, weight, layer, groups)
        return stack_halves([net.chip(v, j) for j, v in enumerate(pieces, 1)])

    def complete(mine, theirs, weight, groups, more, layer):
        own, rest = stack_rows(net, mine, theirs, weight, groups, more, layer)
        return (own, net.core(own)), (rest, net.core(rest))

    def swap_cores(both):
        return lax.all_to_all(both, "fsdp", 0, 0, axis_index_groups=pair_groups)

    small_in = [first_gain, first_shift, qv_bias, proj_bias, second_gain, second_shift, up_bias, down_bias]
    sizes = [v.shape[1] for v in small_in]
    tok = net.to_place(pack_tokens(tokens, scene_ids, token_kind))
    qkv_half = fetch(qkv_weight, 0, 3)
    small = pack_small(small_in)
    small_other = net.core(small)
    later = (qkv_weight, proj_weight, up_weight, down_weight, out_grad)
    tok, qkv_half, small, small_other, later = fence((tok, qkv_half, small, small_other, later))
    qkv_weight, proj_weight, up_weight, down_weight, out_grad = later
    tokg = net.gather(put_small(tok, small, small_other))
    qkv_next = net.next_plane(qkv_half)
    tokg, qkv_half, qkv_next = fence((tokg, qkv_half, qkv_next))

    weights = []
    kept = []
    dm = None
    codes = None
    hidden = None
    for layer in range(layers):
        last = layer == layers - 1
        a1g = tokg if layer == 0 else net.gather(a1)
        qkv_w, proj_w = complete(qkv_half, qkv_next, qkv_weight, 3, proj_weight, layer)
        a1g, qkv_w, proj_w, up_weight = fence((a1g, qkv_w, proj_w, up_weight))
        if layer == 0:
            tokg = a1g
            hidden = tokg[0]
            vectors = join_vectors(net, layers, tokg, sizes, rows)
            gain1, shift1, qv_b, proj_b, gain2, shift2, up_b, down_b = vectors
        norm = (gain1, shift1) if layer == 0 else None
        y, qkv, og, codes, a1g = attend(net, layer, rows, a1g, norm, qkv_w, qv_b, codes, proj_w)
        up_half = fetch(up_weight, layer, 1)
        y, up_half, down_weight = fence((y, up_half, down_weight))
        parts = net.exchange(y)
        up_next = net.next_plane(up_half)
        parts, up_next = fence((parts, up_next))
        h2, a2 = add_and_norm(net, layer, hidden, parts, proj_b, (layer, gain2, shift2))
        a2g = net.gather(a2)
        up_w, down_w = complete(up_half, up_next, up_weight, 1, down_weight, layer)
        a2g, up_w, down_w, qkv_weight, out_grad = fence((a2g, up_w, down_w, qkv_weight, out_grad))
        y, z, slope = feed_forward(net, layer, a2g, up_w, up_b, down_w)
        kept.append((hidden, a1g, qkv, og, h2, a2g, z, slope))
        weights.append((qkv_w, proj_w, up_w, down_w))
        if last:
            dmg = net.gather(dm)
            last_y, z, slope, dmg = fence((y, z, slope, dmg))
            break
        qkv_half = fetch(qkv_weight, layer + 1, 3)
        if layer == layers - 2:
            dm = net.to_chip(out_grad[0])
        y, qkv_half, proj_weight, dm = fence((y, qkv_half, proj_weight, dm))
        parts = net.exchange(y)
        qkv_next = net.next_plane(qkv_half)
        if layer == layers - 2:
            dm = net.to_plane(dm)
        parts, qkv_next, dm = fence((parts, qkv_next, dm))
        hidden, a1 = add_and_norm(net, layer, h2, parts, down_b, (layer + 1, gain1, shift1))

    flow = Flow(net)
    small_grads = [None] * layers
    sums = [None] * layers
    out = None
    grad = dm
    down_b_grad = column_sums(dm)

    def chunks(halves):
        return [Chunk(v) for v in halves]

    for layer in reversed(range(layers)):
        last = layer == layers - 1
        qkv_w, proj_w, up_w, down_w = weights[layer]
        h1, a1g, qkv, og, h2, a2g, z, slope = kept[layer]
        keep, send = down_weight_grad(net, z, dmg)
        da2, du, up_b_grad = feed_back(net, dmg, down_w, slope, up_w)
        send = net.core(send)
        da2, du, keep, send = fence((da2, du, keep, send))
        down_g = chunks(add_halves(keep, send))
        da2 = flow.collect(da2, down_g[0])
        parts = net.exchange(da2)
        both = swap_cores(up_weight_grad(net, a2g, du))
        parts, both = flow.collect((parts, both), down_g[1])
        up_g = chunks(add_pair(both))
        dh2, dy, sums2 = norm_back(net, layer, grad, h2, parts, gain2)
        dyg = net.gather(dy)
        dyg = flow.collect(dyg, up_g[0])
        tokens_in = tokg if layer == 0 else []
        da1, dqkv, qkv_b_grad, norm_sums = attend_back(net, dyg, proj_w, qkv, codes, qkv_w, tokens_in)
        if last:
            last_parts = net.exchange(last_y)
            da1, dqkv, last_parts = flow.collect((da1, dqkv, last_parts), up_g[1])
            (sent_out,) = add_and_norm(net, layer, h2, last_parts, down_b, None)
        else:
            da1, dqkv = flow.collect((da1, dqkv), up_g[1])
        parts = net.exchange(da1)
        names = [None, None, "heads", None, None, None, "chip", None]
        of_layer = [None, None, qkv_b_grad, sums2[2:3], sums2[0:1], sums2[1:2], up_b_grad, down_b_grad]
        small = None
        if layer == 0:
            of_layer[0], of_layer[1] = norm_sums[0:1], norm_sums[1:2]
            names[0] = names[1] = "own"
            small_grads[layer] = list(zip(of_layer, names))
            small = (sizes, small_grads)
        both = swap_cores(attend_weight_grad(net, a1g, dqkv, og, dyg, small))
        parts, both = fence((parts, both))
        attend_g = chunks(add_pair(both))
        grad, dm, sums1 = norm_back(net, layer, dh2, h1, parts, gain1)
        sums[layer] = (down_g, up_g, attend_g)
        dm = flow.collect(dm, attend_g[0])
        if layer > 0:
            of_layer[0], of_layer[1] = sums1[0:1], sums1[1:2]
            small_grads[layer] = list(zip(of_layer, names))
            dmg = net.gather(dm)
            down_b_grad = sums1[2:3]
            dmg, grad = flow.collect((dmg, grad), attend_g[1])

    def to_owners(chunks, extra):
        *pieces, rest = [*cut_rows(net, *[c.value for c in chunks], extra), None][: n_p + 1]
        return net.exchange(pieces), rest

    up_pieces, _ = to_owners(sums[1][1], None)
    dm, up_pieces = flow.collect((dm, up_pieces), attend_g[1])
    qkv_pieces, proj_g = to_owners(sums[1][2], 0)
    dm, sent_out, qkv_pieces, proj_g = flow.collect((dm, sent_out, qkv_pieces, proj_g))
    both_out = jnp.concatenate([dm, sent_out], axis=0)
    up_last = None
    first_part = None
    while flow.queue:
        if up_last is None and not [c for c in flow.queue if c in sums[0][1]]:
            up_last, _ = to_owners(sums[0][1], None)
            both_out, up_last = flow.collect((both_out, up_last))
        elif up_last is not None and first_part is None and attend_g[0] not in flow.queue:
            first_part = net.exchange(cut_part(net, attend_g[0].value, 2))
            both_out = net.from_plane(both_out)
            both_out, first_part = flow.collect((both_out, first_part))
        else:
            both_out = flow.collect(both_out)
    both_out = net.from_chip(both_out).astype(F32)
    input_grad, sent_out = both_out[:rows], both_out[rows:]
    *pieces, proj_last = cut_part(net, attend_g[1].value, 1, 16)
    second_part = net.exchange(pieces)
    out = write_layer(net, 1, layers, None, [c.value for c in sums[1][0]], proj_g, up_pieces, qkv_pieces)
    small_out = sum_small(layers, first_part, second_part, sizes, D // net.n_f)
    qkv_pieces = list(zip(first_part, second_part))
    out = write_layer(net, 0, layers, out, [c.value for c in sums[0][0]], proj_last, up_last, qkv_pieces)
    return (
        sent_out.astype(F32)[None],
        input_grad.astype(F32)[None],
        small_out[0],
        small_out[1],
        out[0],
        small_out[2],
        out[1],
        small_out[3],
        small_out[4],
        small_out[5],
        out[2],
        small_out[6],
        out[3],
        small_out[7],
    )


def solution(mesh):
    tok = P("fsdp", "seq", None)
    lab = P("fsdp", "seq")
    vec = P(None, "fsdp")
    mat = P(None, "fsdp", None)
    return jax.shard_map(
        on_device,
        mesh=mesh,
        in_specs=(tok, lab, lab, tok, vec, vec, mat, vec, mat, vec, vec, vec, mat, vec, mat, vec),
        out_specs=(tok, tok, vec, vec, mat, vec, mat, vec, vec, vec, mat, vec, mat, vec),
        check_vma=False,
    )
```

```python
import jax
import jax.numpy as jnp
from jax import lax
from jax.experimental import pallas as pl
from jax.experimental.pallas import tpu as pltpu
from jax.sharding import PartitionSpec as P

D = 1024
HEAD_DIM = 64
FF = 4096
EPS = 1e-05
NEG = -1e30
SCALE = 0.125
BF = jnp.bfloat16
F32 = jnp.float32
LANES = 128


def xor_pairs(count, mask):
    return [(i, i ^ mask) for i in range(count)]


class Net:
    def __init__(self):
        self.n_s = lax.axis_size("seq")
        self.n_f = lax.axis_size("fsdp")
        self.n_p = self.n_f // 2
        self.s = lax.axis_index("seq")
        self.f = lax.axis_index("fsdp")
        self.p = self.f // 2
        self.c = self.f % 2
        self.place = jnp.stack([self.p, self.c, self.s % 2]).astype(jnp.int32)

    def moves(self):
        square = [[s ^ q for s in range(self.n_s)] for q in range(self.n_p)]
        if self.n_p == 4:
            square = [[0, 2, 1, 3], [1, 3, 2, 0], [2, 0, 3, 1], [3, 1, 0, 2]]
        return [(s, square[q][s], q) for s in range(self.n_s) for q in range(self.n_p)]

    def send(self, v, moves):
        n = self.n_f
        pairs = [(s * n + 2 * p + c, t * n + 2 * q + c) for s, p, t, q in moves for c in range(2)]
        return lax.ppermute(v, ("seq", "fsdp"), pairs)

    def to_place(self, v):
        return self.send(v, [(s, p, p, q) for s, p, q in self.moves()])

    def from_place(self, v):
        return self.send(v, [(p, q, s, p) for s, p, q in self.moves()])

    def to_chip(self, v):
        return self.send(v, [(s, p, s, q) for s, p, q in self.moves()])

    def to_plane(self, v):
        return self.send(v, [(s, q, p, q) for s, p, q in self.moves()])

    def from_plane(self, v):
        return self.send(v, [(p, q, s, q) for s, p, q in self.moves()])

    def from_chip(self, v):
        return self.send(v, [(s, q, s, p) for s, p, q in self.moves()])

    def chip(self, v, j):
        return lax.ppermute(v, "fsdp", xor_pairs(self.n_f, 2 * j))

    def core(self, v):
        return lax.ppermute(v, "fsdp", xor_pairs(self.n_f, 1))

    def next_plane(self, v):
        return lax.ppermute(v, "seq", xor_pairs(self.n_s, 1))

    def gather(self, v):
        return [v] + [self.chip(v, j) for j in range(1, self.n_p)]

    def exchange(self, blocks):
        return [blocks[0]] + [self.chip(blocks[j], j) for j in range(1, self.n_p)]


def fence(values):
    return lax.optimization_barrier(values)


def block(v, index, size, axis):
    return lax.dynamic_slice_in_dim(v, index * size, size, axis=axis)


IN_VMEM = pl.BlockSpec(memory_space=pltpu.VMEM)
IN_SMEM = pl.BlockSpec(memory_space=pltpu.SMEM)
IN_ANY = pl.BlockSpec(memory_space=pl.ANY)
IN_HBM = pl.BlockSpec(memory_space=pltpu.HBM)


def run(name, body, outs, ins, place=None, scratch=(), flops=0, ins_at=None):
    specs = [IN_VMEM] * len(ins) if ins_at is None else ins_at
    if place is not None:
        specs = [IN_SMEM] + specs
        ins = [place, *ins]
    moved = sum(v.size * v.dtype.itemsize for v in ins)
    return pl.pallas_call(
        body,
        out_shape=[jax.ShapeDtypeStruct(shape, dtype) for shape, dtype in outs],
        in_specs=specs,
        out_specs=[IN_VMEM] * len(outs),
        scratch_shapes=list(scratch),
        compiler_params=pltpu.CompilerParams(vmem_limit_bytes=16 << 20),
        cost_estimate=pl.CostEstimate(flops=flops, bytes_accessed=moved, transcendentals=0),
        name=name,
    )(*ins)


def dot(a, b):
    return jnp.dot(a, b, preferred_element_type=F32)


def dot_nt(a, b):
    return lax.dot_general(a, b, (((1,), (1,)), ((), ())), preferred_element_type=F32)


def dot_tn(a, b):
    return lax.dot_general(a, b, (((0,), (0,)), ((), ())), preferred_element_type=F32)


def tile(i, size):
    return pl.ds(pl.multiple_of(i * size, size), size)


def copy_all(pairs, sems):
    copies = [pltpu.make_async_copy(src, dst, sems.at[k]) for k, (src, dst) in enumerate(pairs)]
    for copy in copies:
        copy.start()
    return copies


def own_first(v, parts, c):
    rows = v.shape[-1] // (2 * parts)
    own, other = [], []
    for i in range(parts):
        even = v[:, 2 * i * rows : (2 * i + 1) * rows]
        odd = v[:, (2 * i + 1) * rows : (2 * i + 2) * rows]
        own.append(jnp.where(c == 0, even, odd))
        other.append(jnp.where(c == 0, odd, even))
    return jnp.concatenate(own, axis=1), jnp.concatenate(other, axis=1)


def model_order(v, parts, c):
    half = v.shape[-1] // 2
    rows = half // parts
    out = []
    for i in range(parts):
        own = v[:, i * rows : (i + 1) * rows]
        other = v[:, half + i * rows : half + (i + 1) * rows]
        out += [jnp.where(c == 0, own, other), jnp.where(c == 0, other, own)]
    return jnp.concatenate(out, axis=1)


def columns_of(net, weight, groups):
    return weight.shape[2] // (groups * net.n_p) if groups else weight.shape[2]


def cut_columns(net, layer, weights):
    n_p = net.n_p
    rows = weights[0][0].shape[1] // 2
    widths = [columns_of(net, w, groups) for w, groups in weights]
    count = sum(groups or 1 for _, groups in weights)
    total = sum(width * (groups or 1) for width, (_, groups) in zip(widths, weights))

    def body(place, *refs):
        p, half = place[0], place[2]
        outs, sems = refs[len(weights) : -1], refs[-1]
        pairs = []
        for j in range(1, n_p):
            at = 0
            for ref, width, (_, groups) in zip(refs, widths, weights):
                for i in range(groups or 1):
                    cols = tile(i * n_p + (p ^ j), width) if groups else slice(0, width)
                    pairs.append((ref.at[layer, tile(half, rows), cols], outs[j - 1].at[:, at : at + width]))
                    at += width
        for copy in copy_all(pairs, sems):
            copy.wait()

    outs = [((rows, total), BF)] * (n_p - 1)
    scratch = [pltpu.SemaphoreType.DMA((count * (n_p - 1),))]
    ins = [w for w, _ in weights]
    return run("cut_columns", body, outs, ins, net.place, scratch, ins_at=[IN_HBM] * len(ins))


def stack_halves(pieces):
    rows, width = pieces[0].shape
    count = len(pieces)

    def body(*refs):
        out, sems = refs[count:]
        pairs = [(refs[j], out.at[j * rows : (j + 1) * rows]) for j in range(count)]
        for copy in copy_all(pairs, sems):
            copy.wait()

    outs = [((count * rows, width), BF)]
    scratch = [pltpu.SemaphoreType.DMA((count,))]
    return run("stack_halves", body, outs, pieces, None, scratch, ins_at=[IN_ANY] * count)[0]


def stack_rows(net, mine, theirs, parts, more, layer):
    n_p = net.n_p
    half_rows = parts[0][0].shape[1] // 2
    rows = 2 * half_rows
    widths = [columns_of(net, w, groups) for w, groups, _ in parts]
    count = len(more) + sum((groups or 1) + 2 * (n_p - 1) for _, groups, _ in parts)

    def body(place, mine_ref, their_ref, *refs):
        p, half = place[0], place[2]
        ins, outs, sems = refs[: len(parts) + len(more)], refs[len(parts) + len(more) : -1], refs[-1]
        pairs = [(ref.at[layer], out) for ref, out in zip(ins[len(parts) :], outs[len(parts) :])]
        for ref, own, width, (_, groups, first) in zip(ins, outs, widths, parts):
            for i in range(groups or 1):
                to = own.at[tile(p, rows), i * width : (i + 1) * width]
                cols = tile(i * n_p + p, width) if groups else slice(0, width)
                pairs.append((ref.at[layer, :, cols], to))
            cols = slice(first, first + (groups or 1) * width)
            for j in range(1, n_p):
                here = slice((j - 1) * half_rows, j * half_rows)
                at = (p ^ j) * 2
                pairs.append((mine_ref.at[here, cols], own.at[tile(at + half, half_rows)]))
                pairs.append((their_ref.at[here, cols], own.at[tile(at + 1 - half, half_rows)]))
        for copy in copy_all(pairs, sems):
            copy.wait()

    outs = [((n_p * rows, (g or 1) * width), BF) for (_, g, _), width in zip(parts, widths)]
    outs += [(w.shape[1:], BF) for w in more]
    ins = [mine, theirs, *[w for w, _, _ in parts], *more]
    specs = [IN_ANY] * 2 + [IN_HBM] * (len(parts) + len(more))
    scratch = [pltpu.SemaphoreType.DMA((count,))]
    return run("stack_rows", body, outs, ins, net.place, scratch, ins_at=specs)


def pack_tokens(tokens, scene_ids, token_kind):
    rows = tokens.shape[1]
    code = (scene_ids * 2 + token_kind).astype(BF)
    return jnp.pad(tokens[0], ((0, 16), (0, 0))) + jnp.pad(code, ((rows, 15), (0, D - rows)))


def pack_small(vectors):
    sizes = [v.shape[1] for v in vectors]
    total = None
    for k, v in enumerate(vectors):
        at = sum(sizes[:k])
        put = jnp.pad(v, ((0, 0), (at, sum(sizes) - at - sizes[k])))
        total = put if total is None else total + put
    return total


def put_small(tokens, own, other):
    rows = tokens.shape[0] - 16
    width = own.shape[1] // 2

    def body(token_ref, own_ref, other_ref, out, lines):
        out[0:rows, :] = token_ref[0:rows, :]
        lines[...] = token_ref[rows:, :].astype(F32)
        row = 1
        for ref in (own_ref, other_ref):
            low = ref[...].astype(F32)
            for layer in range(own.shape[0]):
                for half in range(2):
                    lines[row : row + 1, 0:width] = low[layer : layer + 1, half * width : (half + 1) * width]
                    row += 1
        out[rows:, :] = lines[...].astype(BF)

    scratch = [pltpu.VMEM((16, D), F32)]
    return run("put_small", body, [(tokens.shape, BF)], [tokens, own, other], None, scratch)[0]


def join_vectors(net, layers, blocks, sizes, rows):
    n_p = net.n_p
    width = sum(sizes) // 2
    starts = [sum(sizes[:i]) for i in range(len(sizes))]

    def body(place, *refs):
        p, c = place[0], place[1]
        ins, outs = refs[:n_p], refs[n_p:]
        for j in range(n_p):
            low = ins[j][rows : rows + 16, 0:width].astype(F32)
            for layer in range(layers):
                for half in range(2):
                    row = 1 + layer * 2 + half
                    own = low[row : row + 1, :]
                    other = low[2 * layers + row : 2 * layers + row + 1, :]
                    first = jnp.where(c == 0, own, other)
                    second = jnp.where(c == 0, other, own)
                    for k, (at, size) in enumerate(zip(starts, sizes)):
                        if at // width != half:
                            continue
                        cols = slice(at - half * width, at - half * width + size)
                        both = jnp.concatenate([first[:, cols], second[:, cols]], axis=1)
                        outs[k][layer : layer + 1, tile(p ^ j, 2 * size)] = both

    outs = [((layers, 2 * n_p * size), F32) for size in sizes]
    return run("join_vectors", body, outs, blocks, net.place)


def norm_rows(hidden):
    centred = hidden - jnp.mean(hidden, axis=-1, keepdims=True)
    spread = jnp.mean(centred * centred, axis=-1, keepdims=True)
    inverse = lax.rsqrt(spread + EPS)
    return centred * inverse, inverse


def close_layer(net, layer, hidden, parts, bias):
    rows = parts[0].shape[0]
    count = len(parts)

    def body(hidden_ref, bias_ref, *refs):
        total = hidden_ref[...] + bias_ref[layer : layer + 1, :]
        for part in refs[:count]:
            total = total + part[...].astype(F32)
        refs[count][...] = total
        refs[count + 1][...] = total.astype(BF)

    outs = [((rows, D), F32), ((rows, D), BF)]
    return run("close_layer", body, outs, [hidden, bias, *parts])


def close_attention(net, layer, hidden, blocks, pieces, proj, bias, gain, shift):
    n_p = net.n_p
    tokens, cw = pieces[0].shape
    rows = tokens // n_p
    half = cw // 2

    def body(place, *refs):
        hiddens, os = refs[:n_p], refs[n_p : 2 * n_p]
        p_own, p_other, bias_ref, gain_ref, shift_ref, out, low, acc, o = refs[2 * n_p :]
        p, c = place[0], place[1]
        aligned = half % LANES == 0
        for j in range(n_p):
            for i in range(n_p):
                there, here = slice(i * rows, (i + 1) * rows), slice((i ^ j) * rows, ((i ^ j) + 1) * rows)
                first, second = os[j][there, :half], os[j][there, half:]
                own, other = jnp.where(c == 0, first, second), jnp.where(c == 0, second, first)
                if aligned:
                    o[here, tile(p ^ j, half)] = own
                    o[here, tile(n_p + (p ^ j), half)] = other
                    continue
                part = dot(own, p_own[tile(p ^ j, half), :]) + dot(other, p_other[tile(p ^ j, half), :])
                if j == 0:
                    acc[here, :] = part
                else:
                    acc[here, :] += part
        if aligned:
            acc[...] = dot(o[:, : D // 2], p_own[...]) + dot(o[:, D // 2 :], p_other[...])
        line = slice(layer, layer + 1)
        for j in range(n_p):
            here = slice(j * rows, (j + 1) * rows)
            total = acc[here, :] + hiddens[j][0:rows, :].astype(F32) + bias_ref[line, :]
            if j == 0:
                out[...] = total
            normed, _ = norm_rows(total)
            own, other = own_first(normed * gain_ref[line, :] + shift_ref[line, :], n_p, c)
            low[here, : D // 2] = own.astype(BF)
            low[here, D // 2 :] = other.astype(BF)

    outs = [((rows, D), F32), ((tokens, D), BF)]
    scratch = [pltpu.VMEM((tokens, D), F32), pltpu.VMEM((tokens, D), BF)]
    ins = [hidden, *blocks[1:], *pieces, *proj, bias, gain, shift]
    return run("close_attention", body, outs, ins, net.place, scratch, flops=2 * tokens * D * D)


def norm_back(net, layer, grad, hidden, parts, gain):
    rows = parts[0].shape[0]
    count = len(parts)

    def body(place, grad_ref, hidden_ref, gain_ref, *refs):
        total = refs[0][...].astype(F32)
        for part in refs[1:count]:
            total = total + part[...].astype(F32)
        total = model_order(total, net.n_p, place[1])
        out, low, sums = refs[count:]
        normed, inverse = norm_rows(hidden_ref[0:rows, :].astype(F32))
        scaled = total * gain_ref[layer : layer + 1, :]
        one = jnp.mean(scaled, axis=-1, keepdims=True)
        two = jnp.mean(scaled * normed, axis=-1, keepdims=True)
        result = grad_ref[...].astype(F32) + inverse * (scaled - one - normed * two)
        rounded = result.astype(BF)
        out[...] = result
        low[...] = rounded
        sums[0:1, :] = jnp.sum(total * normed, axis=0, keepdims=True)
        sums[1:2, :] = jnp.sum(total, axis=0, keepdims=True)
        sums[2:3, :] = jnp.sum(rounded.astype(F32), axis=0, keepdims=True)

    outs = [((rows, D), F32), ((rows, D), BF), ((3, D), F32)]
    return run("norm_back", body, outs, [grad, hidden, gain, *parts], net.place)


def column_sums(v):
    def body(ref, out):
        out[...] = jnp.sum(ref[...].astype(F32), axis=0, keepdims=True)

    return run("column_sums", body, [((1, v.shape[1]), F32)], [v])[0]


def gather_rows(blocks, scratch):
    rows = scratch.shape[0] // len(blocks)
    for j, ref in enumerate(blocks):
        scratch[j * rows : (j + 1) * rows, :] = ref[0:rows, :]


def allowed_pairs(code_col, code_row):
    same = (code_col >> 1) == (code_row >> 1)
    return same & (((code_col & 1) == 0) | ((code_row & 1) == 1))


def head_lanes(shape, head, axis):
    lane = lax.broadcasted_iota(jnp.int32, shape, axis)
    return (lane < HEAD_DIM) if head == 0 else (lane >= HEAD_DIM)


def keep_head(v, head, axis):
    return jnp.where(head_lanes(v.shape, head, axis), v, jnp.zeros_like(v))


def probs_by_key(k2, q2, allowed, head):
    scores = jnp.where(allowed, dot_nt(keep_head(k2, head, 1), q2), NEG)
    powers = jnp.exp(scores - jnp.max(scores, axis=0, keepdims=True))
    return powers * (1.0 / jnp.sum(powers, axis=0, keepdims=True))


Q_TILE = 256


def attend(net, layer, rows, blocks, gain, shift, weight, bias, codes):
    n_p = net.n_p
    tokens = n_p * rows
    cw = D // n_p
    n_c = 0 if codes is None else 2

    def body(place, *refs):
        bias_ref, w_own, w_other, gain_ref, shift_ref, row_ref, col_ref = refs[n_p : n_p + 7]
        a, qkv, attended, vt = refs[n_p + 7 :]
        p, c = place[0], place[1]
        eye = lax.broadcasted_iota(jnp.int32, (rows, rows), 0) == lax.broadcasted_iota(
            jnp.int32, (rows, rows), 1
        )
        line = slice(layer, layer + 1)
        for j in range(n_p):
            here = slice(j * rows, (j + 1) * rows)
            if codes is None:
                code = refs[j][rows : rows + 1, 0:rows].astype(F32)
                row_ref[:, here] = code.astype(jnp.int32)
                column = jnp.sum(jnp.where(eye, code, 0.0), axis=1, keepdims=True)
                col_ref[here, :] = column.astype(jnp.int32)
            normed, _ = norm_rows(refs[j][0:rows, :].astype(F32))
            own, other = own_first(normed * gain_ref[line, :] + shift_ref[line, :], n_p, c)
            a[here, : D // 2] = own.astype(BF)
            a[here, D // 2 :] = other.astype(BF)
        for i in range(3):
            cols = slice(i * cw, (i + 1) * cw)
            out = dot(a[:, : D // 2], w_own[:, cols]) + dot(a[:, D // 2 :], w_other[:, cols])
            if i == 0:
                out = out + bias_ref[line, tile(p, cw)]
            if i == 2:
                out = out + bias_ref[line, tile(p + n_p, cw)]
            qkv[:, cols] = out.astype(BF)
        vt[...] = jnp.transpose(qkv[:, 2 * cw : 3 * cw].astype(F32)).astype(BF)

        @pl.loop(0, tokens // Q_TILE)
        def _(t):
            here = tile(t, Q_TILE)
            allowed = allowed_pairs(col_ref[...], row_ref[:, here])
            for pair in range(cw // LANES):
                lanes = slice(pair * LANES, (pair + 1) * LANES)
                q2 = qkv[here, lanes]
                k2 = qkv[:, cw + pair * LANES : cw + (pair + 1) * LANES]
                total = None
                for head in range(2):
                    probs = probs_by_key(k2, q2 * BF(SCALE), allowed, head).astype(BF)
                    part = dot(keep_head(vt[lanes, :], head, 0), probs)
                    total = part if total is None else total + part
                attended[here, lanes] = jnp.transpose(total).astype(BF)

    outs = [((tokens, D), BF), ((tokens, 3 * cw), BF), ((tokens, cw), BF)]
    if codes is None:
        outs = [((1, tokens), jnp.int32), ((tokens, 1), jnp.int32)] + outs
    ins = [*blocks, bias, *weight, gain, shift] + list(codes or [])
    scratch = [pltpu.VMEM((cw, tokens), BF)]
    got = run("attend", body, outs, ins, net.place, scratch, flops=2 * tokens * D * 3 * cw)
    if codes is None:
        codes, got = got[:2], got[2:]
    return (*got, codes)


def attend_back(net, blocks, proj, qkv, codes, weight, tokens_in):
    n_p = net.n_p
    rows = blocks[0].shape[0]
    tokens = n_p * rows
    cw = D // n_p
    n_t = len(tokens_in)

    def body(place, *refs):
        p_own, p_other, qkv_ref, row_ref, col_ref, w_own, w_other = refs[n_p : n_p + 7]
        token_refs = refs[n_p + 7 : n_p + 7 + n_t]
        refs_out = refs[n_p + 7 + n_t :]
        outs = refs_out[:n_p]
        dqkv, sums, norm_sums, do, kt, dk, dv = refs_out[n_p:]
        c = place[1]
        mine = tile(place[0], cw // 2)
        for j in range(n_p):
            here = slice(j * rows, (j + 1) * rows)
            own, other = dot_nt(refs[j][...], p_own[mine, :]), dot_nt(refs[j][...], p_other[mine, :])
            do[here, : cw // 2] = jnp.where(c == 0, own, other).astype(BF)
            do[here, cw // 2 :] = jnp.where(c == 0, other, own).astype(BF)
        kt[...] = jnp.transpose(qkv_ref[:, cw : 2 * cw].astype(F32)).astype(BF)
        dk[...] = jnp.zeros_like(dk)
        dv[...] = jnp.zeros_like(dv)

        @pl.loop(0, tokens // Q_TILE)
        def _(t):
            here = tile(t, Q_TILE)
            allowed = allowed_pairs(col_ref[...], row_ref[:, here])
            for pair in range(cw // LANES):
                lanes = slice(pair * LANES, (pair + 1) * LANES)
                q2 = qkv_ref[here, lanes]
                k2 = qkv_ref[:, cw + pair * LANES : cw + (pair + 1) * LANES]
                v2 = qkv_ref[:, 2 * cw + pair * LANES : 2 * cw + (pair + 1) * LANES]
                do2 = do[here, lanes]
                total = None
                for head in range(2):
                    probs = probs_by_key(k2, q2 * BF(SCALE), allowed, head)
                    dp = dot_nt(keep_head(v2, head, 1), do2)
                    mean = jnp.sum(probs * dp, axis=0, keepdims=True)
                    ds = (probs * (dp - mean)).astype(BF)
                    dv[:, lanes] += dot(probs.astype(BF), keep_head(do2, head, 1))
                    dk[:, lanes] += dot(ds, keep_head(q2, head, 1))
                    part = dot(keep_head(kt[lanes, :], head, 0), ds)
                    total = part if total is None else total + part
                dqkv[here, lanes] = (jnp.transpose(total) * SCALE).astype(BF)

        dqkv[:, cw : 2 * cw] = (dk[...] * SCALE).astype(BF)
        dqkv[:, 2 * cw :] = dv[...].astype(BF)
        sums[...] = jnp.sum(dqkv[...].astype(F32), axis=0, keepdims=True)
        norm_sums[...] = jnp.zeros_like(norm_sums)
        for j in range(n_p):
            normed = None
            if n_t:
                normed = own_first(norm_rows(token_refs[j][0:rows, :].astype(F32))[0], n_p, c)
            for k, w in enumerate((w_own, w_other)):
                cols = slice(k * (D // 2), (k + 1) * (D // 2))
                da1 = dot_nt(dqkv[j * rows : (j + 1) * rows, :], w[...])
                outs[j][:, cols] = da1.astype(BF)
                if n_t:
                    norm_sums[0:1, cols] += jnp.sum(da1 * normed[k], axis=0, keepdims=True)
                    norm_sums[1:2, cols] += jnp.sum(da1, axis=0, keepdims=True)

    outs = [((rows, D), BF)] * n_p + [((tokens, 3 * cw), BF), ((1, 3 * cw), F32), ((2, D), F32)]
    scratch = [
        pltpu.VMEM((tokens, cw), BF),
        pltpu.VMEM((cw, tokens), BF),
        pltpu.VMEM((tokens, cw), F32),
        pltpu.VMEM((tokens, cw), F32),
    ]
    ins = [*blocks, *proj, qkv, *codes, *weight, *tokens_in]
    got = run("attend_back", body, outs, ins, net.place, scratch, flops=2 * tokens * D * 8 * cw)
    return got[:n_p], got[n_p], got[n_p + 1], got[n_p + 2]


F_TILE = 256


def feed_forward(net, layer, a2, up, bias, down):
    n_p = net.n_p
    tokens = a2.shape[0]
    rows = tokens // n_p
    fw = FF // n_p

    def body(place, a_ref, up_own, up_other, bias_ref, d_own, d_other, *refs):
        outs, z_ref, slope_ref = refs[:n_p], refs[n_p], refs[n_p + 1]
        p, c = place[0], place[1]

        @pl.loop(0, fw // F_TILE)
        def _(t):
            cols = tile(t, F_TILE)
            there = pl.ds(pl.multiple_of(p * fw + t * F_TILE, F_TILE), F_TILE)
            u = dot(a_ref[:, : D // 2], up_own[:, cols]) + dot(a_ref[:, D // 2 :], up_other[:, cols])
            u = u + bias_ref[layer : layer + 1, there]
            phi = 0.5 * (1.0 + lax.erf(u * 0.7071067811865476))
            z_ref[:, cols] = (u * phi).astype(BF)
            slope_ref[:, cols] = phi + u * (jnp.exp(-0.5 * u * u) * 0.3989422804014327)

        for j in range(n_p):
            here = slice(j * rows, (j + 1) * rows)
            own, other = z_ref[here, tile(c, fw // 2)], z_ref[here, tile(1 - c, fw // 2)]
            outs[j][...] = (dot(own, d_own[...]) + dot(other, d_other[...])).astype(BF)

    outs = [((rows, D), BF)] * n_p + [((tokens, fw), BF), ((tokens, fw), F32)]
    ins = [a2, *up, bias, *down]
    got = run("feed_forward", body, outs, ins, net.place, flops=4 * tokens * D * fw)
    return got[:n_p], got[n_p], got[n_p + 1]


def feed_back(net, blocks, down, slope, up):
    n_p = net.n_p
    rows = blocks[0].shape[0]
    tokens = n_p * rows
    fw = FF // n_p

    def body(place, *refs):
        d_own, d_other, slope_ref, up_own, up_other = refs[n_p : n_p + 5]
        outs = refs[n_p + 5 : 2 * n_p + 5]
        du_ref, sums, dm = refs[2 * n_p + 5 :]
        c = place[1]
        gather_rows(refs[:n_p], dm)
        for w, core in ((d_own, c), (d_other, 1 - c)):

            @pl.loop(0, fw // (2 * F_TILE))
            def _(t):
                start = core * (fw // 2) + t * F_TILE
                cols = pl.ds(pl.multiple_of(start, F_TILE), F_TILE)
                dz = dot_nt(dm[...], w[tile(t, F_TILE), :])
                du = (dz * slope_ref[:, cols]).astype(BF)
                du_ref[:, cols] = du
                sums[:, cols] = jnp.sum(du.astype(F32), axis=0, keepdims=True)

        for j in range(n_p):
            du = du_ref[j * rows : (j + 1) * rows, :]
            outs[j][:, : D // 2] = dot_nt(du, up_own[...]).astype(BF)
            outs[j][:, D // 2 :] = dot_nt(du, up_other[...]).astype(BF)

    outs = [((rows, D), BF)] * n_p + [((tokens, fw), BF), ((1, fw), F32)]
    scratch = [pltpu.VMEM((tokens, D), BF)]
    ins = [*blocks, *down, slope, *up]
    got = run("feed_back", body, outs, ins, net.place, scratch, flops=4 * tokens * D * fw)
    return got[:n_p], got[n_p], got[n_p + 1]


def down_weight_grad(net, z, dm):
    n_r = len(dm)
    tokens, m = z.shape
    half = m // 2

    def body(place, z_ref, *refs):
        keep, send, b = refs[n_r:]
        c = place[1]
        gather_rows(refs[:n_r], b)
        keep[...] = dot_tn(z_ref[:, tile(c, half)], b[...]).astype(BF)
        send[...] = dot_tn(z_ref[:, tile(1 - c, half)], b[...]).astype(BF)

    outs = [((half, D), BF)] * 2
    scratch = [pltpu.VMEM((tokens, D), BF)]
    return run("down_weight_grad", body, outs, [z, *dm], net.place, scratch, flops=2 * tokens * m * D)


def up_weight_grad(net, a2, du):
    n_l = len(a2)
    tokens, n = du.shape

    def body(place, *refs):
        du_ref, out, a = refs[n_l:]
        c = place[1]
        gather_rows(refs[:n_l], a)
        out[c] = dot_tn(a[:, : D // 2], du_ref[...]).astype(BF)
        out[1 - c] = dot_tn(a[:, D // 2 :], du_ref[...]).astype(BF)

    scratch = [pltpu.VMEM((tokens, D), BF)]
    outs = [((2, D // 2, n), BF)]
    return run("up_weight_grad", body, outs, [*a2, du], net.place, scratch, flops=2 * tokens * D * n)[0]


def attend_weight_grad(net, a1, dqkv, attended, dy, small):
    n_p = net.n_p
    n_a = len(a1)
    tokens, width = dqkv.shape
    cw = D // n_p
    rows = D // net.n_f
    extra = 16 if small else 0
    flat = [v for of_layer in small[1] for v in of_layer] if small else []
    sizes = small[0] if small else []
    starts = [sum(sizes[:i]) for i in range(len(sizes))]

    def put_small(place, refs, low):
        p, c = place[0], place[1]
        low[...] = jnp.zeros_like(low)
        for k, (ref, (_, kind)) in enumerate(zip(refs, flat)):
            layer, which = divmod(k, len(sizes))
            at, size = starts[which], sizes[which]
            half = at // width
            row = slice(2 * layer + half, 2 * layer + half + 1)
            cols = slice(at - half * width, at - half * width + size)
            if kind == "chip":
                low[0, p, row, cols] = ref[:, :size]
                low[1, p, row, cols] = ref[:, size:]
            elif kind == "heads":
                low[p % 2, p // 2, row, cols] = ref[:, :size]
                low[p % 2, p // 2 + n_p // 2, row, cols] = ref[:, 2 * size :]
            elif kind == "own":
                for i in range(n_p):
                    low[c, i, row, cols] = ref[:, i * size : (i + 1) * size]
                    low[1 - c, i, row, cols] = ref[:, D // 2 + i * size : D // 2 + (i + 1) * size]
            else:
                for i in range(n_p):
                    for core in range(2):
                        to = (2 * i + core) * size
                        low[core, i, row, cols] = ref[:, to : to + size]

    def body(place, *refs):
        dqkv_ref, attended_ref = refs[n_a : n_a + 2]
        smalls = refs[n_a + 2 + n_p : n_a + 2 + n_p + len(flat)]
        out, a, b, low, lines = refs[n_a + 2 + n_p + len(flat) :]
        c = place[1]
        gather_rows(refs[:n_a], a)
        for k, core in ((0, c), (1, 1 - c)):
            both = dot_tn(a[:, k * (D // 2) : (k + 1) * (D // 2)], dqkv_ref[...]).astype(BF)
            for i in range(n_p):
                out[core, i * (rows + extra) : i * (rows + extra) + rows, :width] = both[i * rows : (i + 1) * rows]
        gather_rows(refs[n_a + 2 : n_a + 2 + n_p], b)
        low[...] = dot_tn(attended_ref[...], b[...]).astype(BF)
        for core in range(2):
            for i in range(n_p):
                here = slice(i * (rows + extra), i * (rows + extra) + rows)
                out[core, here, width:] = low[core * rows : (core + 1) * rows, i * cw : (i + 1) * cw]
        if extra:
            put_small(place, smalls, lines)
            for core in range(2):
                for i in range(n_p):
                    here = slice(i * (rows + extra) + rows, (i + 1) * (rows + extra))
                    out[core, here, :width] = lines[core, i].astype(BF)
                    out[core, here, width:] = jnp.zeros((extra, cw), BF)

    outs = [((2, n_p * (rows + extra), width + cw), BF)]
    scratch = [pltpu.VMEM((tokens, D), BF), pltpu.VMEM((tokens, D), BF), pltpu.VMEM((cw, D), BF)]
    scratch.append(pltpu.VMEM((2, n_p, 16, width), F32))
    flops = 2 * tokens * D * (width + cw)
    ins = [*a1, dqkv, attended, *dy, *[v for v, _ in flat]]
    return run("attend_weight_grad", body, outs, ins, net.place, scratch, flops=flops)[0]


def add_halves(a, b):
    rows, width = a.shape
    half = width // 2

    def body(a_ref, b_ref, *outs):
        for k in range(2):
            cols = slice(k * half, (k + 1) * half)
            outs[k][...] = (a_ref[:, cols].astype(F32) + b_ref[:, cols].astype(F32)).astype(BF)

    return run("add_halves", body, [((rows, half), BF)] * 2, [a, b])


def add_pair(both):
    _, rows, width = both.shape
    half = width // 2

    def body(ref, *outs):
        for k in range(2):
            cols = slice(k * half, (k + 1) * half)
            outs[k][...] = (ref[0, :, cols].astype(F32) + ref[1, :, cols].astype(F32)).astype(BF)

    return run("add_pair", body, [((rows, half), BF)] * 2, [both])


def cut_rows(net, first, second, extra):
    n_p = net.n_p
    rows = first.shape[0] // n_p
    width, more = first.shape[1], second.shape[1]
    split = extra is not None
    taken = more // 2 if split else more

    def body(place, a, b, *outs):
        p = place[0]
        for j in range(n_p):
            here = tile(p ^ j, rows)
            outs[j][:, :width] = a[here, :]
            outs[j][:, width:] = b[here, :taken]
        if split:
            for i in range(n_p):
                outs[n_p][:, i * taken : (i + 1) * taken] = b[i * rows : (i + 1) * rows - extra, taken:]

    outs = [((rows, width + taken), BF)] * n_p
    if split:
        outs.append(((rows - extra, n_p * taken), BF))
    return run("cut_rows", body, outs, [first, second], net.place)


def cut_part(net, v, groups, extra=None):
    n_p = net.n_p
    rows = v.shape[0] // n_p
    taken = groups * (D // n_p)
    rest = v.shape[1] - taken

    def body(place, ref, *outs):
        p = place[0]
        for j in range(n_p):
            outs[j][...] = ref[tile(p ^ j, rows), :taken]
        if extra is not None:
            for i in range(n_p):
                outs[n_p][:, i * rest : (i + 1) * rest] = ref[i * rows : (i + 1) * rows - extra, taken:]

    outs = [((rows, taken), BF)] * n_p
    if extra is not None:
        outs.append(((rows - extra, n_p * rest), BF))
    return run("cut_part", body, outs, [v], net.place)


def sum_small(layers, first, second, sizes, rows):
    count = len(first)
    split = first[0].shape[1]
    width = split + second[0].shape[1]
    starts = [sum(sizes[:i]) for i in range(len(sizes))]

    def body(*refs):
        parts = []
        for group in (refs[:count], refs[count : 2 * count]):
            total = group[0][rows:, :].astype(F32)
            for ref in group[1:]:
                total = total + ref[rows:, :].astype(F32)
            parts.append(total)
        total = jnp.concatenate(parts, axis=1)
        for out, at, size in zip(refs[2 * count :], starts, sizes):
            half = at // width
            for layer in range(layers):
                row = 2 * layer + half
                out[layer : layer + 1, :] = total[row : row + 1, at - half * width : at - half * width + size]

    return run("sum_small", body, [((layers, size), F32) for size in sizes], [*first, *second])


def take_if(here, a, b, rows):
    def body(flag, a_ref, b_ref, out):
        @pl.when(flag[0] != 0)
        def _():
            count = min(rows, a.shape[0])
            out[0:count, :] = a_ref[0:count, :]

        @pl.when(flag[0] == 0)
        def _():
            count = min(rows, b.shape[0])
            out[0:count, :] = b_ref[0:count, :]

    return run("take_if", body, [((rows, a.shape[1]), BF)], [a, b], here.astype(jnp.int32).reshape(1))[0]


def turn(net, wanted):
    flat, flags, outs = [], [], []
    for one, two, outer in wanted:
        flat += one + (two or [])
        rows = max(one[0].shape[0], two[0].shape[0] if two else 0)
        outs.append(((rows, one[0].shape[1]), BF))
        flags.append(jnp.zeros((), jnp.int32) if outer is None else outer.astype(jnp.int32))

    def put(refs, out):
        rows = refs[0].shape[0]
        if len(refs) == 1:
            out[0:rows, :] = refs[0][...]
            return
        total = refs[0][...].astype(F32)
        for ref in refs[1:]:
            total = total + ref[0:rows, :].astype(F32)
        out[0:rows, :] = total.astype(BF)

    def body(flag, *refs):
        at = 0
        for k, (one, two, outer) in enumerate(wanted):
            out = refs[len(flat) + k]
            first = refs[at : at + len(one)]
            at += len(one)
            if outer is None:
                put(first, out)
                continue
            second = refs[at : at + len(two)]
            at += len(two)
            pl.when(flag[k] != 0)(lambda first=first, out=out: put(first, out))
            pl.when(flag[k] == 0)(lambda second=second, out=out: put(second, out))

    return run("turn", body, outs, flat, jnp.stack(flags))


class Chunk:
    def __init__(self, value):
        self.terms = [value]
        self.step = 0

    @property
    def value(self):
        return self.terms[0]


class Flow:
    def __init__(self, net):
        self.net = net
        self.queue = []
        self.moving = []

    def first(self, step):
        for chunk in self.queue:
            if chunk.step == step:
                return chunk
        return None

    def start(self):
        net = self.net
        n = net.n_s
        half = n // 2
        moves, wanted = [], []
        for k in range(half):
            inward = self.first(k)
            outward = None if k == half - 1 else self.first(n - 2 - k)
            into = [(k, k + 1), (n - 1 - k, n - 2 - k)]
            out = [(k + 1, k), (n - 2 - k, n - 1 - k)]
            outer = (net.s == k) | (net.s == n - 1 - k)
            both = inward is not None and outward is not None
            if both and inward.value.shape[1] == outward.value.shape[1]:
                moves.append((inward, outward, outer, into + out))
                wanted.append((inward.terms, outward.terms, outer))
                continue
            if inward is not None:
                moves.append((inward, None, outer, into))
                wanted.append((inward.terms, None, None))
            if outward is not None:
                moves.append((None, outward, outer, out))
                wanted.append((outward.terms, None, None))
        sent = [w[0][0] for w in wanted]
        work = [k for k, w in enumerate(wanted) if len(w[0]) > 1 or w[1] is not None]
        if work:
            for k, value in zip(work, turn(net, [wanted[k] for k in work])):
                sent[k] = value
        self.moving = [(*m[:3], v, lax.ppermute(v, "seq", m[3])) for m, v in zip(moves, sent)]

    def collect(self, values, *new):
        values, news, got = fence((values, [c.value for c in new], [(m[3], m[4]) for m in self.moving]))
        for c, value in zip(new, news):
            c.terms = [value]
        n = self.net.n_s
        for (inward, outward, outer, _, _), (sent, arrived) in zip(self.moving, got):
            if inward is not None:
                middle = inward.step == n // 2 - 1
                inward.terms = [sent, arrived] if middle else [*inward.terms, arrived]
                inward.step += 1
            if outward is not None:
                outward.terms = [take_if(outer, arrived, sent, outward.value.shape[0])]
                outward.step += 1
        self.queue = [c for c in self.queue if c.step < n - 1] + list(new)
        self.start()
        return values


def write_layer(net, layer, layers, before, down, proj, up, qkv):
    n_p = net.n_p
    rows = up[0].shape[0]
    cw, fw = D // n_p, FF // n_p
    split = isinstance(qkv[0], tuple)
    flat = [v for pair in qkv for v in pair] if split else list(qkv)
    n_in = 3 + n_p + len(flat)
    skip = 0 if before is None else 4
    steps = min(4, rows // 16)
    part = rows // steps
    down_rows = down[0].shape[0]
    down_part = down_rows // steps

    def body(place, *refs):
        p = place[0]
        downs, proj_ref = refs[:2], refs[2]
        ups, qkvs = refs[3 : 3 + n_p], refs[3 + n_p : n_in]
        qkv_out, proj_out, up_out, down_out = refs[n_in + skip :]
        proj_out[0] = proj_ref[...].astype(F32)
        for k in range(2):
            down_out[0, :, k * (D // 2) : (k + 1) * (D // 2)] = downs[k][...].astype(F32)
        for j in range(n_p):
            up_out[0, :, tile(p ^ j, fw)] = ups[j][...].astype(F32)
            for i in range(3):
                to = tile(i * n_p + (p ^ j), cw)
                ref, at = (qkvs[2 * j + i // 2], i % 2) if split else (qkvs[j], i)
                qkv_out[0, :, to] = ref[:, at * cw : (at + 1) * cw].astype(F32)

    def of_rows(v, size):
        return pl.BlockSpec((size, v.shape[1]), lambda i: (i, 0))

    ins = [*down, proj, *up, *flat]
    specs = [IN_SMEM] + [of_rows(v, down_part) for v in down] + [of_rows(v, part) for v in [proj, *up, *flat]]
    aliases = {}
    if before is not None:
        aliases = {1 + n_in + k: k for k in range(4)}
        specs += [IN_ANY] * 4
        ins = ins + list(before)
    shapes = [(rows, 3 * D), (rows, D), (rows, FF), (down_rows, D)]
    sizes = [part, part, part, down_part]
    return pl.pallas_call(
        body,
        grid=(steps,),
        out_shape=[jax.ShapeDtypeStruct((layers, *shape), F32) for shape in shapes],
        in_specs=specs,
        out_specs=[
            pl.BlockSpec((1, size, shape[1]), lambda i: (layer, i, 0)) for size, shape in zip(sizes, shapes)
        ],
        input_output_aliases=aliases,
        compiler_params=pltpu.CompilerParams(vmem_limit_bytes=16 << 20),
        name="write_layer",
    )(net.place, *ins)


def on_device(
    tokens,
    scene_ids,
    token_kind,
    out_grad,
    first_gain,
    first_shift,
    qkv_weight,
    qv_bias,
    proj_weight,
    proj_bias,
    second_gain,
    second_shift,
    up_weight,
    up_bias,
    down_weight,
    down_bias,
):
    net = Net()
    n_p = net.n_p
    layers = qkv_weight.shape[0]
    rows = tokens.shape[1]
    pair_groups = [[2 * i, 2 * i + 1] for i in range(n_p)]

    def fetch(layer, *weights):
        pieces = cut_columns(net, layer, weights)
        return stack_halves([net.chip(v, j) for j, v in enumerate(pieces, 1)])

    def complete(mine, theirs, parts, more, layer):
        own = stack_rows(net, mine, theirs, parts, more, layer)
        return [(v, net.core(v)) for v in own]

    def swap_cores(both):
        return lax.all_to_all(both, "fsdp", 0, 0, axis_index_groups=pair_groups)

    small_in = [first_gain, first_shift, qv_bias, proj_bias, second_gain, second_shift, up_bias, down_bias]
    sizes = [v.shape[1] for v in small_in]
    tok = net.to_place(pack_tokens(tokens, scene_ids, token_kind))
    mine = fetch(0, (qkv_weight, 3), (proj_weight, None))
    small = pack_small(small_in)
    small_other = net.core(small)
    later = (qkv_weight, proj_weight, up_weight, down_weight, out_grad)
    tok, mine, small, small_other, later = fence((tok, mine, small, small_other, later))
    qkv_weight, proj_weight, up_weight, down_weight, out_grad = later
    tokg = net.gather(put_small(tok, small, small_other))
    theirs = net.next_plane(mine)
    tokg, mine, theirs = fence((tokg, mine, theirs))

    weights = []
    kept = []
    dm = None
    codes = None
    qkv_cols = 3 * D // n_p
    for layer in range(layers):
        last = layer == layers - 1
        blocks = tokg if layer == 0 else net.gather(low)
        parts = [(qkv_weight, 3, 0), (proj_weight, None, qkv_cols)]
        qkv_w, proj_w = complete(mine, theirs, parts, [], layer)
        blocks, qkv_w, proj_w, up_weight, out_grad = fence((blocks, qkv_w, proj_w, up_weight, out_grad))
        if layer == 0:
            tokg = blocks
            hidden = tokg[0]
            vectors = join_vectors(net, layers, tokg, sizes, rows)
            gain1, shift1, qv_b, proj_b, gain2, shift2, up_b, down_b = vectors
        a1g, qkv, og, codes = attend(net, layer, rows, blocks, gain1, shift1, qkv_w, qv_b, codes)
        mine = fetch(layer, (up_weight, 1))
        if last:
            dm = net.to_chip(out_grad[0])
        a1g, qkv, og, mine, dm, down_weight = fence((a1g, qkv, og, mine, dm, down_weight))
        pieces = net.gather(og)
        theirs = net.next_plane(mine)
        if last:
            dm = net.to_plane(dm)
        pieces, theirs, dm = fence((pieces, theirs, dm))
        up_w, down_w = complete(mine, theirs, [(up_weight, 1, 0)], [down_weight], layer)
        h2, a2g = close_attention(net, layer, hidden, blocks, pieces, proj_w, proj_b, gain2, shift2)
        a2g, up_w, down_w, qkv_weight, proj_weight = fence((a2g, up_w, down_w, qkv_weight, proj_weight))
        y, z, slope = feed_forward(net, layer, a2g, up_w, up_b, down_w)
        kept.append((hidden, [a1g], qkv, og, h2, [a2g], z, slope))
        weights.append((qkv_w, proj_w, up_w, down_w))
        if last:
            dmg = net.gather(dm)
            last_y, z, slope, dmg = fence((y, z, slope, dmg))
            break
        mine = fetch(layer + 1, (qkv_weight, 3), (proj_weight, None))
        y, mine = fence((y, mine))
        parts = net.exchange(y)
        theirs = net.next_plane(mine)
        parts, theirs = fence((parts, theirs))
        hidden, low = close_layer(net, layer, h2, parts, down_b)

    flow = Flow(net)
    small_grads = [None] * layers
    sums = [None] * layers
    out = None
    grad = dm
    down_b_grad = column_sums(dm)

    def chunks(halves):
        return [Chunk(v) for v in halves]

    for layer in reversed(range(layers)):
        last = layer == layers - 1
        qkv_w, proj_w, up_w, down_w = weights[layer]
        h1, a1g, qkv, og, h2, a2g, z, slope = kept[layer]
        keep, send = down_weight_grad(net, z, dmg)
        da2, du, up_b_grad = feed_back(net, dmg, down_w, slope, up_w)
        send = net.core(send)
        da2, du, keep, send = fence((da2, du, keep, send))
        down_g = chunks(add_halves(keep, send))
        da2 = flow.collect(da2, down_g[0])
        parts = net.exchange(da2)
        both = swap_cores(up_weight_grad(net, a2g, du))
        parts, both = flow.collect((parts, both), down_g[1])
        up_g = chunks(add_pair(both))
        dh2, dy, sums2 = norm_back(net, layer, grad, h2, parts, gain2)
        dyg = net.gather(dy)
        dyg = flow.collect(dyg, up_g[0])
        tokens_in = tokg if layer == 0 else []
        da1, dqkv, qkv_b_grad, norm_sums = attend_back(net, dyg, proj_w, qkv, codes, qkv_w, tokens_in)
        if last:
            last_parts = net.exchange(last_y)
            da1, dqkv, last_parts = flow.collect((da1, dqkv, last_parts), up_g[1])
            _, sent_out = close_layer(net, layer, h2, last_parts, down_b)
        else:
            da1, dqkv = flow.collect((da1, dqkv), up_g[1])
        parts = net.exchange(da1)
        names = [None, None, "heads", None, None, None, "chip", None]
        of_layer = [None, None, qkv_b_grad, sums2[2:3], sums2[0:1], sums2[1:2], up_b_grad, down_b_grad]
        small = None
        if layer == 0:
            of_layer[0], of_layer[1] = norm_sums[0:1], norm_sums[1:2]
            names[0] = names[1] = "own"
            small_grads[layer] = list(zip(of_layer, names))
            small = (sizes, small_grads)
        both = swap_cores(attend_weight_grad(net, a1g, dqkv, og, dyg, small))
        parts, both = fence((parts, both))
        attend_g = chunks(add_pair(both))
        grad, dm, sums1 = norm_back(net, layer, dh2, h1, parts, gain1)
        sums[layer] = (down_g, up_g, attend_g)
        dm = flow.collect(dm, attend_g[0])
        if layer > 0:
            of_layer[0], of_layer[1] = sums1[0:1], sums1[1:2]
            small_grads[layer] = list(zip(of_layer, names))
            dmg = net.gather(dm)
            down_b_grad = sums1[2:3]
            dmg, grad = flow.collect((dmg, grad), attend_g[1])

    def to_owners(chunks, extra):
        *pieces, rest = [*cut_rows(net, *[c.value for c in chunks], extra), None][: n_p + 1]
        return net.exchange(pieces), rest

    up_pieces, _ = to_owners(sums[1][1], None)
    dm, up_pieces = flow.collect((dm, up_pieces), attend_g[1])
    qkv_pieces, proj_g = to_owners(sums[1][2], 0)
    dm, sent_out, qkv_pieces, proj_g = flow.collect((dm, sent_out, qkv_pieces, proj_g))
    both_out = jnp.concatenate([dm, sent_out], axis=0)
    up_last = None
    first_part = None
    while flow.queue:
        if up_last is None and not [c for c in flow.queue if c in sums[0][1]]:
            up_last, _ = to_owners(sums[0][1], None)
            both_out, up_last = flow.collect((both_out, up_last))
        elif up_last is not None and first_part is None and attend_g[0] not in flow.queue:
            first_part = net.exchange(cut_part(net, attend_g[0].value, 2))
            both_out = net.from_plane(both_out)
            both_out, first_part = flow.collect((both_out, first_part))
        else:
            both_out = flow.collect(both_out)
    both_out = net.from_chip(both_out).astype(F32)
    input_grad, sent_out = both_out[:rows], both_out[rows:]
    *pieces, proj_last = cut_part(net, attend_g[1].value, 1, 16)
    second_part = net.exchange(pieces)
    out = write_layer(net, 1, layers, None, [c.value for c in sums[1][0]], proj_g, up_pieces, qkv_pieces)
    small_out = sum_small(layers, first_part, second_part, sizes, D // net.n_f)
    qkv_pieces = list(zip(first_part, second_part))
    out = write_layer(net, 0, layers, out, [c.value for c in sums[0][0]], proj_last, up_last, qkv_pieces)
    return (
        sent_out[None],
        input_grad[None],
        small_out[0],
        small_out[1],
        out[0],
        small_out[2],
        out[1],
        small_out[3],
        small_out[4],
        small_out[5],
        out[2],
        small_out[6],
        out[3],
        small_out[7],
    )


def solution(mesh):
    tok = P("fsdp", "seq", None)
    lab = P("fsdp", "seq")
    vec = P(None, "fsdp")
    mat = P(None, "fsdp", None)
    return jax.shard_map(
        on_device,
        mesh=mesh,
        in_specs=(tok, lab, lab, tok, vec, vec, mat, vec, mat, vec, vec, vec, mat, vec, mat, vec),
        out_specs=(tok, tok, vec, vec, mat, vec, mat, vec, vec, vec, mat, vec, mat, vec),
        check_vma=False,
    )
```

```python
import jax
import jax.numpy as jnp
from jax import lax
from jax.experimental import pallas as pl
from jax.experimental.pallas import tpu as pltpu
from jax.sharding import PartitionSpec as P

D = 1024
HEAD_DIM = 64
FF = 4096
EPS = 1e-05
NEG = -1e30
SCALE = 0.125
BF = jnp.bfloat16
F32 = jnp.float32
LANES = 128


def xor_pairs(count, mask):
    return [(i, i ^ mask) for i in range(count)]


class Net:
    def __init__(self):
        self.n_s = lax.axis_size("seq")
        self.n_f = lax.axis_size("fsdp")
        self.n_p = self.n_f // 2
        self.s = lax.axis_index("seq")
        self.f = lax.axis_index("fsdp")
        self.p = self.f // 2
        self.c = self.f % 2
        self.place = jnp.stack([self.p, self.c, self.s % 2]).astype(jnp.int32)

    def moves(self):
        square = [[s ^ q for s in range(self.n_s)] for q in range(self.n_p)]
        if self.n_p == 4:
            square = [[0, 2, 1, 3], [1, 3, 2, 0], [2, 0, 3, 1], [3, 1, 0, 2]]
        return [(s, square[q][s], q) for s in range(self.n_s) for q in range(self.n_p)]

    def send(self, v, moves):
        n = self.n_f
        pairs = [(s * n + 2 * p + c, t * n + 2 * q + c) for s, p, t, q in moves for c in range(2)]
        return lax.ppermute(v, ("seq", "fsdp"), pairs)

    def to_place(self, v):
        return self.send(v, [(s, p, p, q) for s, p, q in self.moves()])

    def from_place(self, v):
        return self.send(v, [(p, q, s, p) for s, p, q in self.moves()])

    def to_chip(self, v):
        return self.send(v, [(s, p, s, q) for s, p, q in self.moves()])

    def to_plane(self, v):
        return self.send(v, [(s, q, p, q) for s, p, q in self.moves()])

    def chip(self, v, j):
        return lax.ppermute(v, "fsdp", xor_pairs(self.n_f, 2 * j))

    def core(self, v):
        return lax.ppermute(v, "fsdp", xor_pairs(self.n_f, 1))

    def next_plane(self, v):
        return lax.ppermute(v, "seq", xor_pairs(self.n_s, 1))

    def gather(self, v):
        return [v] + [self.chip(v, j) for j in range(1, self.n_p)]

    def exchange(self, blocks):
        return [blocks[0]] + [self.chip(blocks[j], j) for j in range(1, self.n_p)]


def fence(values):
    return lax.optimization_barrier(values)


def block(v, index, size, axis):
    return lax.dynamic_slice_in_dim(v, index * size, size, axis=axis)


IN_VMEM = pl.BlockSpec(memory_space=pltpu.VMEM)
IN_SMEM = pl.BlockSpec(memory_space=pltpu.SMEM)
IN_ANY = pl.BlockSpec(memory_space=pl.ANY)
IN_HBM = pl.BlockSpec(memory_space=pltpu.HBM)


def run(name, body, outs, ins, place=None, scratch=(), flops=0, ins_at=None):
    specs = [IN_VMEM] * len(ins) if ins_at is None else ins_at
    if place is not None:
        specs = [IN_SMEM] + specs
        ins = [place, *ins]
    moved = sum(v.size * v.dtype.itemsize for v in ins)
    return pl.pallas_call(
        body,
        out_shape=[jax.ShapeDtypeStruct(shape, dtype) for shape, dtype in outs],
        in_specs=specs,
        out_specs=[IN_VMEM] * len(outs),
        scratch_shapes=list(scratch),
        compiler_params=pltpu.CompilerParams(vmem_limit_bytes=16 << 20),
        cost_estimate=pl.CostEstimate(flops=flops, bytes_accessed=moved, transcendentals=0),
        name=name,
    )(*ins)


def dot(a, b):
    return jnp.dot(a, b, preferred_element_type=F32)


def dot_nt(a, b):
    return lax.dot_general(a, b, (((1,), (1,)), ((), ())), preferred_element_type=F32)


def dot_tn(a, b):
    return lax.dot_general(a, b, (((0,), (0,)), ((), ())), preferred_element_type=F32)


def tile(i, size):
    return pl.ds(pl.multiple_of(i * size, size), size)


def copy_all(pairs, sems):
    copies = [pltpu.make_async_copy(src, dst, sems.at[k]) for k, (src, dst) in enumerate(pairs)]
    for copy in copies:
        copy.start()
    return copies


def own_first(v, parts, c):
    rows = v.shape[-1] // (2 * parts)
    own, other = [], []
    for i in range(parts):
        even = v[:, 2 * i * rows : (2 * i + 1) * rows]
        odd = v[:, (2 * i + 1) * rows : (2 * i + 2) * rows]
        own.append(jnp.where(c == 0, even, odd))
        other.append(jnp.where(c == 0, odd, even))
    return jnp.concatenate(own, axis=1), jnp.concatenate(other, axis=1)


def model_order(v, parts, c):
    half = v.shape[-1] // 2
    rows = half // parts
    out = []
    for i in range(parts):
        own = v[:, i * rows : (i + 1) * rows]
        other = v[:, half + i * rows : half + (i + 1) * rows]
        out += [jnp.where(c == 0, own, other), jnp.where(c == 0, other, own)]
    return jnp.concatenate(out, axis=1)


def columns_of(net, weight, groups):
    return weight.shape[2] // (groups * net.n_p) if groups else weight.shape[2]


def cut_columns(net, layer, weights):
    n_p = net.n_p
    rows = weights[0][0].shape[1] // 2
    widths = [columns_of(net, w, groups) for w, groups in weights]
    count = sum(groups or 1 for _, groups in weights)
    total = sum(width * (groups or 1) for width, (_, groups) in zip(widths, weights))

    def body(place, *refs):
        p, half = place[0], place[2]
        outs, sems = refs[len(weights) : -1], refs[-1]
        pairs = []
        for j in range(1, n_p):
            at = 0
            for ref, width, (_, groups) in zip(refs, widths, weights):
                for i in range(groups or 1):
                    cols = tile(i * n_p + (p ^ j), width) if groups else slice(0, width)
                    pairs.append((ref.at[layer, tile(half, rows), cols], outs[j - 1].at[:, at : at + width]))
                    at += width
        for copy in copy_all(pairs, sems):
            copy.wait()

    outs = [((rows, total), BF)] * (n_p - 1)
    scratch = [pltpu.SemaphoreType.DMA((count * (n_p - 1),))]
    ins = [w for w, _ in weights]
    return run("cut_columns", body, outs, ins, net.place, scratch, ins_at=[IN_HBM] * len(ins))


def stack_halves(pieces):
    rows, width = pieces[0].shape
    count = len(pieces)

    def body(*refs):
        out, sems = refs[count:]
        pairs = [(refs[j], out.at[j * rows : (j + 1) * rows]) for j in range(count)]
        for copy in copy_all(pairs, sems):
            copy.wait()

    outs = [((count * rows, width), BF)]
    scratch = [pltpu.SemaphoreType.DMA((count,))]
    return run("stack_halves", body, outs, pieces, None, scratch, ins_at=[IN_ANY] * count)[0]


def stack_rows(net, mine, theirs, parts, more, layer):
    n_p = net.n_p
    half_rows = parts[0][0].shape[1] // 2
    rows = 2 * half_rows
    widths = [columns_of(net, w, groups) for w, groups, _ in parts]
    count = len(more) + sum((groups or 1) + 2 * (n_p - 1) for _, groups, _ in parts)

    def body(place, mine_ref, their_ref, *refs):
        p, half = place[0], place[2]
        ins, outs, sems = refs[: len(parts) + len(more)], refs[len(parts) + len(more) : -1], refs[-1]
        pairs = [(ref.at[layer], out) for ref, out in zip(ins[len(parts) :], outs[len(parts) :])]
        for ref, own, width, (_, groups, first) in zip(ins, outs, widths, parts):
            for i in range(groups or 1):
                to = own.at[tile(p, rows), i * width : (i + 1) * width]
                cols = tile(i * n_p + p, width) if groups else slice(0, width)
                pairs.append((ref.at[layer, :, cols], to))
            cols = slice(first, first + (groups or 1) * width)
            for j in range(1, n_p):
                here = slice((j - 1) * half_rows, j * half_rows)
                at = (p ^ j) * 2
                pairs.append((mine_ref.at[here, cols], own.at[tile(at + half, half_rows)]))
                pairs.append((their_ref.at[here, cols], own.at[tile(at + 1 - half, half_rows)]))
        for copy in copy_all(pairs, sems):
            copy.wait()

    outs = [((n_p * rows, (g or 1) * width), BF) for (_, g, _), width in zip(parts, widths)]
    outs += [(w.shape[1:], BF) for w in more]
    ins = [mine, theirs, *[w for w, _, _ in parts], *more]
    specs = [IN_ANY] * 2 + [IN_HBM] * (len(parts) + len(more))
    scratch = [pltpu.SemaphoreType.DMA((count,))]
    return run("stack_rows", body, outs, ins, net.place, scratch, ins_at=specs)


def pack_tokens(tokens, scene_ids, token_kind):
    half = tokens.shape[1] // 2
    code = (scene_ids * 2 + token_kind).astype(BF)
    code = jnp.pad(code, ((half, 15), (0, D - 2 * half)))
    return tokens[0, :half], jnp.pad(tokens[0, half:], ((0, 16), (0, 0))) + code


def pack_small(vectors):
    sizes = [v.shape[1] for v in vectors]
    total = None
    for k, v in enumerate(vectors):
        at = sum(sizes[:k])
        put = jnp.pad(v, ((0, 0), (at, sum(sizes) - at - sizes[k])))
        total = put if total is None else total + put
    return total


def put_small(first, second, own, other):
    mid = first.shape[0]
    rows = 2 * mid
    width = own.shape[1] // 2

    def body(first_ref, second_ref, own_ref, other_ref, out, lines):
        out[0:mid, :] = first_ref[...]
        out[mid:rows, :] = second_ref[0:mid, :]
        lines[...] = second_ref[mid:, :].astype(F32)
        row = 1
        for ref in (own_ref, other_ref):
            low = ref[...].astype(F32)
            for layer in range(own.shape[0]):
                for half in range(2):
                    lines[row : row + 1, 0:width] = low[layer : layer + 1, half * width : (half + 1) * width]
                    row += 1
        out[rows:, :] = lines[...].astype(BF)

    scratch = [pltpu.VMEM((16, D), F32)]
    outs = [((rows + 16, D), BF)]
    return run("put_small", body, outs, [first, second, own, other], None, scratch)[0]


def join_vectors(net, layers, blocks, sizes, rows):
    n_p = net.n_p
    width = sum(sizes) // 2
    starts = [sum(sizes[:i]) for i in range(len(sizes))]

    def body(place, *refs):
        p, c = place[0], place[1]
        ins, outs = refs[:n_p], refs[n_p:]
        for j in range(n_p):
            low = ins[j][rows : rows + 16, 0:width].astype(F32)
            for layer in range(layers):
                for half in range(2):
                    row = 1 + layer * 2 + half
                    own = low[row : row + 1, :]
                    other = low[2 * layers + row : 2 * layers + row + 1, :]
                    first = jnp.where(c == 0, own, other)
                    second = jnp.where(c == 0, other, own)
                    for k, (at, size) in enumerate(zip(starts, sizes)):
                        if at // width != half:
                            continue
                        cols = slice(at - half * width, at - half * width + size)
                        both = jnp.concatenate([first[:, cols], second[:, cols]], axis=1)
                        outs[k][layer : layer + 1, tile(p ^ j, 2 * size)] = both

    outs = [((layers, 2 * n_p * size), F32) for size in sizes]
    return run("join_vectors", body, outs, blocks, net.place)


def norm_rows(hidden):
    centred = hidden - jnp.mean(hidden, axis=-1, keepdims=True)
    spread = jnp.mean(centred * centred, axis=-1, keepdims=True)
    inverse = lax.rsqrt(spread + EPS)
    return centred * inverse, inverse


def close_layer(net, layer, hidden, parts, bias):
    rows = parts[0].shape[0]
    count = len(parts)

    def body(hidden_ref, bias_ref, *refs):
        total = hidden_ref[...] + bias_ref[layer : layer + 1, :]
        for part in refs[:count]:
            total = total + part[...].astype(F32)
        refs[count][...] = total
        refs[count + 1][...] = total.astype(BF)

    outs = [((rows, D), F32), ((rows, D), BF)]
    return run("close_layer", body, outs, [hidden, bias, *parts])


def close_attention(net, layer, hidden, blocks, pieces, proj, bias, gain, shift):
    n_p = net.n_p
    tokens, cw = pieces[0].shape
    rows = tokens // n_p
    half = cw // 2

    def body(place, *refs):
        hiddens, os = refs[:n_p], refs[n_p : 2 * n_p]
        p_own, p_other, bias_ref, gain_ref, shift_ref, out, low, acc, o = refs[2 * n_p :]
        p, c = place[0], place[1]
        aligned = half % LANES == 0
        for j in range(n_p):
            for i in range(n_p):
                there, here = slice(i * rows, (i + 1) * rows), slice((i ^ j) * rows, ((i ^ j) + 1) * rows)
                first, second = os[j][there, :half], os[j][there, half:]
                own, other = jnp.where(c == 0, first, second), jnp.where(c == 0, second, first)
                if aligned:
                    o[here, tile(p ^ j, half)] = own
                    o[here, tile(n_p + (p ^ j), half)] = other
                    continue
                part = dot(own, p_own[tile(p ^ j, half), :]) + dot(other, p_other[tile(p ^ j, half), :])
                if j == 0:
                    acc[here, :] = part
                else:
                    acc[here, :] += part
        if aligned:
            acc[...] = dot(o[:, : D // 2], p_own[...]) + dot(o[:, D // 2 :], p_other[...])
        line = slice(layer, layer + 1)
        for j in range(n_p):
            here = slice(j * rows, (j + 1) * rows)
            total = acc[here, :] + hiddens[j][0:rows, :].astype(F32) + bias_ref[line, :]
            if j == 0:
                out[...] = total
            normed, _ = norm_rows(total)
            own, other = own_first(normed * gain_ref[line, :] + shift_ref[line, :], n_p, c)
            low[here, : D // 2] = own.astype(BF)
            low[here, D // 2 :] = other.astype(BF)

    outs = [((rows, D), F32), ((tokens, D), BF)]
    scratch = [pltpu.VMEM((tokens, D), F32), pltpu.VMEM((tokens, D), BF)]
    ins = [hidden, *blocks[1:], *pieces, *proj, bias, gain, shift]
    return run("close_attention", body, outs, ins, net.place, scratch, flops=2 * tokens * D * D)


def norm_back(net, layer, grad, hidden, parts, gain):
    rows = parts[0].shape[0]
    count = len(parts)

    def body(place, grad_ref, hidden_ref, gain_ref, *refs):
        total = refs[0][...].astype(F32)
        for part in refs[1:count]:
            total = total + part[...].astype(F32)
        total = model_order(total, net.n_p, place[1])
        out, low, sums = refs[count:]
        normed, inverse = norm_rows(hidden_ref[0:rows, :].astype(F32))
        scaled = total * gain_ref[layer : layer + 1, :]
        one = jnp.mean(scaled, axis=-1, keepdims=True)
        two = jnp.mean(scaled * normed, axis=-1, keepdims=True)
        result = grad_ref[...].astype(F32) + inverse * (scaled - one - normed * two)
        rounded = result.astype(BF)
        out[...] = result
        low[...] = rounded
        sums[0:1, :] = jnp.sum(total * normed, axis=0, keepdims=True)
        sums[1:2, :] = jnp.sum(total, axis=0, keepdims=True)
        sums[2:3, :] = jnp.sum(rounded.astype(F32), axis=0, keepdims=True)

    outs = [((rows, D), F32), ((rows, D), BF), ((3, D), F32)]
    return run("norm_back", body, outs, [grad, hidden, gain, *parts], net.place)


def column_sums(v):
    def body(ref, out):
        out[...] = jnp.sum(ref[...].astype(F32), axis=0, keepdims=True)

    return run("column_sums", body, [((1, v.shape[1]), F32)], [v])[0]


def gather_rows(blocks, scratch):
    rows = scratch.shape[0] // len(blocks)
    for j, ref in enumerate(blocks):
        scratch[j * rows : (j + 1) * rows, :] = ref[0:rows, :]


def allowed_pairs(code_col, code_row):
    same = (code_col >> 1) == (code_row >> 1)
    return same & (((code_col & 1) == 0) | ((code_row & 1) == 1))


def head_lanes(shape, head, axis):
    lane = lax.broadcasted_iota(jnp.int32, shape, axis)
    return (lane < HEAD_DIM) if head == 0 else (lane >= HEAD_DIM)


def keep_head(v, head, axis):
    return jnp.where(head_lanes(v.shape, head, axis), v, jnp.zeros_like(v))


def probs_by_key(k2, q2, allowed, head):
    scores = jnp.where(allowed, dot_nt(keep_head(k2, head, 1), q2), NEG)
    powers = jnp.exp(scores - jnp.max(scores, axis=0, keepdims=True))
    return powers * (1.0 / jnp.sum(powers, axis=0, keepdims=True))


Q_TILE = 256


def attend(net, layer, rows, blocks, gain, shift, weight, bias, codes):
    n_p = net.n_p
    tokens = n_p * rows
    cw = D // n_p
    n_c = 0 if codes is None else 2

    def body(place, *refs):
        bias_ref, w_own, w_other, gain_ref, shift_ref, row_ref, col_ref = refs[n_p : n_p + 7]
        a, qkv, attended, vt = refs[n_p + 7 :]
        p, c = place[0], place[1]
        eye = lax.broadcasted_iota(jnp.int32, (rows, rows), 0) == lax.broadcasted_iota(
            jnp.int32, (rows, rows), 1
        )
        line = slice(layer, layer + 1)
        for j in range(n_p):
            here = slice(j * rows, (j + 1) * rows)
            if codes is None:
                code = refs[j][rows : rows + 1, 0:rows].astype(F32)
                row_ref[:, here] = code.astype(jnp.int32)
                column = jnp.sum(jnp.where(eye, code, 0.0), axis=1, keepdims=True)
                col_ref[here, :] = column.astype(jnp.int32)
            normed, _ = norm_rows(refs[j][0:rows, :].astype(F32))
            own, other = own_first(normed * gain_ref[line, :] + shift_ref[line, :], n_p, c)
            a[here, : D // 2] = own.astype(BF)
            a[here, D // 2 :] = other.astype(BF)
        for i in range(3):
            cols = slice(i * cw, (i + 1) * cw)
            out = dot(a[:, : D // 2], w_own[:, cols]) + dot(a[:, D // 2 :], w_other[:, cols])
            if i == 0:
                out = out + bias_ref[line, tile(p, cw)]
            if i == 2:
                out = out + bias_ref[line, tile(p + n_p, cw)]
            qkv[:, cols] = out.astype(BF)
        vt[...] = jnp.transpose(qkv[:, 2 * cw : 3 * cw].astype(F32)).astype(BF)

        @pl.loop(0, tokens // Q_TILE)
        def _(t):
            here = tile(t, Q_TILE)
            allowed = allowed_pairs(col_ref[...], row_ref[:, here])
            for pair in range(cw // LANES):
                lanes = slice(pair * LANES, (pair + 1) * LANES)
                q2 = qkv[here, lanes]
                k2 = qkv[:, cw + pair * LANES : cw + (pair + 1) * LANES]
                total = None
                for head in range(2):
                    probs = probs_by_key(k2, q2 * BF(SCALE), allowed, head).astype(BF)
                    part = dot(keep_head(vt[lanes, :], head, 0), probs)
                    total = part if total is None else total + part
                attended[here, lanes] = jnp.transpose(total).astype(BF)

    outs = [((tokens, D), BF), ((tokens, 3 * cw), BF), ((tokens, cw), BF)]
    if codes is None:
        outs = [((1, tokens), jnp.int32), ((tokens, 1), jnp.int32)] + outs
    ins = [*blocks, bias, *weight, gain, shift] + list(codes or [])
    scratch = [pltpu.VMEM((cw, tokens), BF)]
    got = run("attend", body, outs, ins, net.place, scratch, flops=2 * tokens * D * 3 * cw)
    if codes is None:
        codes, got = got[:2], got[2:]
    return (*got, codes)


def attend_back(net, blocks, proj, qkv, codes, weight, tokens_in):
    n_p = net.n_p
    rows = blocks[0].shape[0]
    tokens = n_p * rows
    cw = D // n_p
    n_t = len(tokens_in)

    def body(place, *refs):
        p_own, p_other, qkv_ref, row_ref, col_ref, w_own, w_other = refs[n_p : n_p + 7]
        token_refs = refs[n_p + 7 : n_p + 7 + n_t]
        refs_out = refs[n_p + 7 + n_t :]
        outs = refs_out[:n_p]
        dqkv, sums, norm_sums, do, kt, dk, dv = refs_out[n_p:]
        c = place[1]
        mine = tile(place[0], cw // 2)
        for j in range(n_p):
            here = slice(j * rows, (j + 1) * rows)
            own, other = dot_nt(refs[j][...], p_own[mine, :]), dot_nt(refs[j][...], p_other[mine, :])
            do[here, : cw // 2] = jnp.where(c == 0, own, other).astype(BF)
            do[here, cw // 2 :] = jnp.where(c == 0, other, own).astype(BF)
        kt[...] = jnp.transpose(qkv_ref[:, cw : 2 * cw].astype(F32)).astype(BF)
        dk[...] = jnp.zeros_like(dk)
        dv[...] = jnp.zeros_like(dv)

        @pl.loop(0, tokens // Q_TILE)
        def _(t):
            here = tile(t, Q_TILE)
            allowed = allowed_pairs(col_ref[...], row_ref[:, here])
            for pair in range(cw // LANES):
                lanes = slice(pair * LANES, (pair + 1) * LANES)
                q2 = qkv_ref[here, lanes]
                k2 = qkv_ref[:, cw + pair * LANES : cw + (pair + 1) * LANES]
                v2 = qkv_ref[:, 2 * cw + pair * LANES : 2 * cw + (pair + 1) * LANES]
                do2 = do[here, lanes]
                total = None
                for head in range(2):
                    probs = probs_by_key(k2, q2 * BF(SCALE), allowed, head)
                    dp = dot_nt(keep_head(v2, head, 1), do2)
                    mean = jnp.sum(probs * dp, axis=0, keepdims=True)
                    ds = (probs * (dp - mean)).astype(BF)
                    dv[:, lanes] += dot(probs.astype(BF), keep_head(do2, head, 1))
                    dk[:, lanes] += dot(ds, keep_head(q2, head, 1))
                    part = dot(keep_head(kt[lanes, :], head, 0), ds)
                    total = part if total is None else total + part
                dqkv[here, lanes] = (jnp.transpose(total) * SCALE).astype(BF)

        dqkv[:, cw : 2 * cw] = (dk[...] * SCALE).astype(BF)
        dqkv[:, 2 * cw :] = dv[...].astype(BF)
        sums[...] = jnp.sum(dqkv[...].astype(F32), axis=0, keepdims=True)
        norm_sums[...] = jnp.zeros_like(norm_sums)
        for j in range(n_p):
            normed = None
            if n_t:
                normed = own_first(norm_rows(token_refs[j][0:rows, :].astype(F32))[0], n_p, c)
            for k, w in enumerate((w_own, w_other)):
                cols = slice(k * (D // 2), (k + 1) * (D // 2))
                da1 = dot_nt(dqkv[j * rows : (j + 1) * rows, :], w[...])
                outs[j][:, cols] = da1.astype(BF)
                if n_t:
                    norm_sums[0:1, cols] += jnp.sum(da1 * normed[k], axis=0, keepdims=True)
                    norm_sums[1:2, cols] += jnp.sum(da1, axis=0, keepdims=True)

    outs = [((rows, D), BF)] * n_p + [((tokens, 3 * cw), BF), ((1, 3 * cw), F32), ((2, D), F32)]
    scratch = [
        pltpu.VMEM((tokens, cw), BF),
        pltpu.VMEM((cw, tokens), BF),
        pltpu.VMEM((tokens, cw), F32),
        pltpu.VMEM((tokens, cw), F32),
    ]
    ins = [*blocks, *proj, qkv, *codes, *weight, *tokens_in]
    got = run("attend_back", body, outs, ins, net.place, scratch, flops=2 * tokens * D * 8 * cw)
    return got[:n_p], got[n_p], got[n_p + 1], got[n_p + 2]


F_TILE = 256


def feed_forward(net, layer, a2, up, bias, down):
    n_p = net.n_p
    tokens = a2.shape[0]
    rows = tokens // n_p
    fw = FF // n_p

    def body(place, a_ref, up_own, up_other, bias_ref, d_own, d_other, *refs):
        outs, z_ref, slope_ref = refs[:n_p], refs[n_p], refs[n_p + 1]
        p, c = place[0], place[1]

        @pl.loop(0, fw // F_TILE)
        def _(t):
            cols = tile(t, F_TILE)
            there = pl.ds(pl.multiple_of(p * fw + t * F_TILE, F_TILE), F_TILE)
            u = dot(a_ref[:, : D // 2], up_own[:, cols]) + dot(a_ref[:, D // 2 :], up_other[:, cols])
            u = u + bias_ref[layer : layer + 1, there]
            phi = 0.5 * (1.0 + lax.erf(u * 0.7071067811865476))
            z_ref[:, cols] = (u * phi).astype(BF)
            slope_ref[:, cols] = phi + u * (jnp.exp(-0.5 * u * u) * 0.3989422804014327)

        for j in range(n_p):
            here = slice(j * rows, (j + 1) * rows)
            own, other = z_ref[here, tile(c, fw // 2)], z_ref[here, tile(1 - c, fw // 2)]
            outs[j][...] = (dot(own, d_own[...]) + dot(other, d_other[...])).astype(BF)

    outs = [((rows, D), BF)] * n_p + [((tokens, fw), BF), ((tokens, fw), F32)]
    ins = [a2, *up, bias, *down]
    got = run("feed_forward", body, outs, ins, net.place, flops=4 * tokens * D * fw)
    return got[:n_p], got[n_p], got[n_p + 1]


def feed_back(net, blocks, down, slope, up):
    n_p = net.n_p
    rows = blocks[0].shape[0]
    tokens = n_p * rows
    fw = FF // n_p

    def body(place, *refs):
        d_own, d_other, slope_ref, up_own, up_other = refs[n_p : n_p + 5]
        outs = refs[n_p + 5 : 2 * n_p + 5]
        du_ref, sums, dm = refs[2 * n_p + 5 :]
        c = place[1]
        gather_rows(refs[:n_p], dm)
        for w, core in ((d_own, c), (d_other, 1 - c)):

            @pl.loop(0, fw // (2 * F_TILE))
            def _(t):
                start = core * (fw // 2) + t * F_TILE
                cols = pl.ds(pl.multiple_of(start, F_TILE), F_TILE)
                dz = dot_nt(dm[...], w[tile(t, F_TILE), :])
                du = (dz * slope_ref[:, cols]).astype(BF)
                du_ref[:, cols] = du
                sums[:, cols] = jnp.sum(du.astype(F32), axis=0, keepdims=True)

        for j in range(n_p):
            du = du_ref[j * rows : (j + 1) * rows, :]
            outs[j][:, : D // 2] = dot_nt(du, up_own[...]).astype(BF)
            outs[j][:, D // 2 :] = dot_nt(du, up_other[...]).astype(BF)

    outs = [((rows, D), BF)] * n_p + [((tokens, fw), BF), ((1, fw), F32)]
    scratch = [pltpu.VMEM((tokens, D), BF)]
    ins = [*blocks, *down, slope, *up]
    got = run("feed_back", body, outs, ins, net.place, scratch, flops=4 * tokens * D * fw)
    return got[:n_p], got[n_p], got[n_p + 1]


def down_weight_grad(net, z, dm):
    n_r = len(dm)
    tokens, m = z.shape
    half = m // 2

    def body(place, z_ref, *refs):
        keep, send, b = refs[n_r:]
        c = place[1]
        gather_rows(refs[:n_r], b)
        keep[...] = dot_tn(z_ref[:, tile(c, half)], b[...]).astype(BF)
        send[...] = dot_tn(z_ref[:, tile(1 - c, half)], b[...]).astype(BF)

    outs = [((half, D), BF)] * 2
    scratch = [pltpu.VMEM((tokens, D), BF)]
    return run("down_weight_grad", body, outs, [z, *dm], net.place, scratch, flops=2 * tokens * m * D)


def up_weight_grad(net, a2, du):
    n_l = len(a2)
    tokens, n = du.shape

    def body(place, *refs):
        du_ref, out, a = refs[n_l:]
        c = place[1]
        gather_rows(refs[:n_l], a)
        out[c] = dot_tn(a[:, : D // 2], du_ref[...]).astype(BF)
        out[1 - c] = dot_tn(a[:, D // 2 :], du_ref[...]).astype(BF)

    scratch = [pltpu.VMEM((tokens, D), BF)]
    outs = [((2, D // 2, n), BF)]
    return run("up_weight_grad", body, outs, [*a2, du], net.place, scratch, flops=2 * tokens * D * n)[0]


def attend_weight_grad(net, a1, dqkv, attended, dy, small):
    n_p = net.n_p
    n_a = len(a1)
    tokens, width = dqkv.shape
    cw = D // n_p
    rows = D // net.n_f
    lines_each = 2 * len(small[1]) if small else 0
    extra = n_p * lines_each
    flat = [v for of_layer in small[1] for v in of_layer] if small else []
    sizes = small[0] if small else []
    starts = [sum(sizes[:i]) for i in range(len(sizes))]

    def put_small(place, refs, low):
        p, c = place[0], place[1]
        low[...] = jnp.zeros_like(low)
        for k, (ref, (_, kind)) in enumerate(zip(refs, flat)):
            layer, which = divmod(k, len(sizes))
            at, size = starts[which], sizes[which]
            half = at // width
            row = slice(2 * layer + half, 2 * layer + half + 1)
            cols = slice(at - half * width, at - half * width + size)
            if kind == "chip":
                low[0, p, row, cols] = ref[:, :size]
                low[1, p, row, cols] = ref[:, size:]
            elif kind == "heads":
                low[p % 2, p // 2, row, cols] = ref[:, :size]
                low[p % 2, p // 2 + n_p // 2, row, cols] = ref[:, 2 * size :]
            elif kind == "own":
                for i in range(n_p):
                    low[c, i, row, cols] = ref[:, i * size : (i + 1) * size]
                    low[1 - c, i, row, cols] = ref[:, D // 2 + i * size : D // 2 + (i + 1) * size]
            else:
                for i in range(n_p):
                    for core in range(2):
                        to = (2 * i + core) * size
                        low[core, i, row, cols] = ref[:, to : to + size]

    def body(place, *refs):
        dqkv_ref, attended_ref = refs[n_a : n_a + 2]
        smalls = refs[n_a + 2 + n_p : n_a + 2 + n_p + len(flat)]
        out, a, b, low, lines, under = refs[n_a + 2 + n_p + len(flat) :]
        c = place[1]
        gather_rows(refs[:n_a], a)
        for k, core in ((0, c), (1, 1 - c)):
            both = dot_tn(a[:, k * (D // 2) : (k + 1) * (D // 2)], dqkv_ref[...]).astype(BF)
            for i in range(n_p):
                out[core, i * rows : (i + 1) * rows, :width] = both[i * rows : (i + 1) * rows]
        gather_rows(refs[n_a + 2 : n_a + 2 + n_p], b)
        low[...] = dot_tn(attended_ref[...], b[...]).astype(BF)
        for core in range(2):
            for i in range(n_p):
                here = slice(i * rows, (i + 1) * rows)
                out[core, here, width:] = low[core * rows : (core + 1) * rows, i * cw : (i + 1) * cw]
        if extra:
            put_small(place, smalls, lines)
            for core in range(2):
                for i in range(n_p):
                    for r in range(lines_each):
                        under[i * lines_each + r : i * lines_each + r + 1, :] = lines[core, i, r : r + 1, :]
                out[core, n_p * rows :, :width] = under[...].astype(BF)
                out[core, n_p * rows :, width:] = jnp.zeros((extra, cw), BF)

    outs = [((2, n_p * rows + extra, width + cw), BF)]
    scratch = [pltpu.VMEM((tokens, D), BF), pltpu.VMEM((tokens, D), BF), pltpu.VMEM((cw, D), BF)]
    scratch += [pltpu.VMEM((2, n_p, 8, width), F32), pltpu.VMEM((max(extra, 8), width), F32)]
    flops = 2 * tokens * D * (width + cw)
    ins = [*a1, dqkv, attended, *dy, *[v for v, _ in flat]]
    return run("attend_weight_grad", body, outs, ins, net.place, scratch, flops=flops)[0]


def add_halves(a, b):
    rows, width = a.shape
    half = width // 2

    def body(a_ref, b_ref, *outs):
        for k in range(2):
            cols = slice(k * half, (k + 1) * half)
            outs[k][...] = (a_ref[:, cols].astype(F32) + b_ref[:, cols].astype(F32)).astype(BF)

    return run("add_halves", body, [((rows, half), BF)] * 2, [a, b])


def add_pair(both):
    _, rows, width = both.shape
    half = width // 2

    def body(ref, *outs):
        for k in range(2):
            cols = slice(k * half, (k + 1) * half)
            outs[k][...] = (ref[0, :, cols].astype(F32) + ref[1, :, cols].astype(F32)).astype(BF)

    return run("add_pair", body, [((rows, half), BF)] * 2, [both])


def cut_rows(net, first, second, extra):
    n_p = net.n_p
    split = extra is not None
    under = extra or 0
    rows = (first.shape[0] - under) // n_p
    width, more = first.shape[1], second.shape[1]
    taken = more // 2 if split else more

    def body(place, a, b, *outs):
        p = place[0]
        for j in range(n_p):
            here = tile(p ^ j, rows)
            outs[j][0:rows, :width] = a[here, :]
            outs[j][0:rows, width:] = b[here, :taken]
            if under:
                outs[j][rows:, :width] = a[n_p * rows :, :]
                outs[j][rows:, width:] = b[n_p * rows :, :taken]
        if split:
            for i in range(n_p):
                outs[n_p][:, i * taken : (i + 1) * taken] = b[i * rows : (i + 1) * rows, taken:]

    outs = [((rows + under, width + taken), BF)] * n_p
    if split:
        outs.append(((rows, n_p * taken), BF))
    return run("cut_rows", body, outs, [first, second], net.place)


def sum_small(net, layers, pieces, sizes, rows, more):
    width = pieces[0].shape[1]
    count = len(pieces)
    starts = [sum(sizes[:i]) for i in range(len(sizes))]

    def body(place, *refs):
        every = refs[0][rows:, :].astype(F32)
        for ref in refs[1:count]:
            every = every + ref[rows:, :].astype(F32)
        total = jnp.zeros((2 * layers, width), F32)
        for i in range(net.n_p):
            total = jnp.where(place[0] == i, every[i * 2 * layers : (i + 1) * 2 * layers], total)
        outs = refs[count + len(more) :]
        for out, at, size in zip(outs, starts, sizes):
            half = at // width
            for layer in range(layers):
                row = 2 * layer + half
                out[layer : layer + 1, :] = total[row : row + 1, at - half * width : at - half * width + size]
        for ref, out in zip(refs[count : count + len(more)], outs[len(sizes) :]):
            out[...] = ref[...].astype(F32)

    outs = [((layers, size), F32) for size in sizes] + [(v.shape, F32) for v in more]
    return run("sum_small", body, outs, [*pieces, *more], net.place)


def take_if(here, a, b, rows):
    def body(flag, a_ref, b_ref, out):
        @pl.when(flag[0] != 0)
        def _():
            count = min(rows, a.shape[0])
            out[0:count, :] = a_ref[0:count, :]

        @pl.when(flag[0] == 0)
        def _():
            count = min(rows, b.shape[0])
            out[0:count, :] = b_ref[0:count, :]

    return run("take_if", body, [((rows, a.shape[1]), BF)], [a, b], here.astype(jnp.int32).reshape(1))[0]


def turn(net, wanted):
    flat, flags, outs = [], [], []
    for one, two, outer in wanted:
        flat += one + (two or [])
        rows = max(one[0].shape[0], two[0].shape[0] if two else 0)
        outs.append(((rows, one[0].shape[1]), BF))
        flags.append(jnp.zeros((), jnp.int32) if outer is None else outer.astype(jnp.int32))

    def put(refs, out):
        rows = refs[0].shape[0]
        if len(refs) == 1:
            out[0:rows, :] = refs[0][...]
            return
        total = refs[0][...].astype(F32)
        for ref in refs[1:]:
            total = total + ref[0:rows, :].astype(F32)
        out[0:rows, :] = total.astype(BF)

    def body(flag, *refs):
        at = 0
        for k, (one, two, outer) in enumerate(wanted):
            out = refs[len(flat) + k]
            first = refs[at : at + len(one)]
            at += len(one)
            if outer is None:
                put(first, out)
                continue
            second = refs[at : at + len(two)]
            at += len(two)
            pl.when(flag[k] != 0)(lambda first=first, out=out: put(first, out))
            pl.when(flag[k] == 0)(lambda second=second, out=out: put(second, out))

    return run("turn", body, outs, flat, jnp.stack(flags))


class Chunk:
    def __init__(self, value):
        self.terms = [value]
        self.step = 0

    @property
    def value(self):
        return self.terms[0]


class Flow:
    def __init__(self, net):
        self.net = net
        self.queue = []
        self.moving = []

    def first(self, step):
        for chunk in self.queue:
            if chunk.step == step:
                return chunk
        return None

    def start(self):
        net = self.net
        n = net.n_s
        half = n // 2
        moves, wanted = [], []
        for k in range(half):
            inward = self.first(k)
            outward = None if k == half - 1 else self.first(n - 2 - k)
            into = [(k, k + 1), (n - 1 - k, n - 2 - k)]
            out = [(k + 1, k), (n - 2 - k, n - 1 - k)]
            outer = (net.s == k) | (net.s == n - 1 - k)
            both = inward is not None and outward is not None
            if both and inward.value.shape[1] == outward.value.shape[1]:
                moves.append((inward, outward, outer, into + out))
                wanted.append((inward.terms, outward.terms, outer))
                continue
            if inward is not None:
                moves.append((inward, None, outer, into))
                wanted.append((inward.terms, None, None))
            if outward is not None:
                moves.append((None, outward, outer, out))
                wanted.append((outward.terms, None, None))
        sent = [w[0][0] for w in wanted]
        work = [k for k, w in enumerate(wanted) if len(w[0]) > 1 or w[1] is not None]
        if work:
            for k, value in zip(work, turn(net, [wanted[k] for k in work])):
                sent[k] = value
        self.moving = [(*m[:3], v, lax.ppermute(v, "seq", m[3])) for m, v in zip(moves, sent)]

    def collect(self, values, *new):
        values, news, got = fence((values, [c.value for c in new], [(m[3], m[4]) for m in self.moving]))
        for c, value in zip(new, news):
            c.terms = [value]
        n = self.net.n_s
        for (inward, outward, outer, _, _), (sent, arrived) in zip(self.moving, got):
            if inward is not None:
                middle = inward.step == n // 2 - 1
                inward.terms = [sent, arrived] if middle else [*inward.terms, arrived]
                inward.step += 1
            if outward is not None:
                outward.terms = [take_if(outer, arrived, sent, outward.value.shape[0])]
                outward.step += 1
        self.queue = [c for c in self.queue if c.step < n - 1] + list(new)
        self.start()
        return values


def write_layer(net, layer, layers, before, down, proj, up, qkv):
    n_p = net.n_p
    rows = up[0].shape[0]
    cw, fw = D // n_p, FF // n_p
    split = isinstance(qkv[0], tuple)
    flat = [v for pair in qkv for v in pair] if split else list(qkv)
    n_in = 3 + n_p + len(flat)
    skip = 0 if before is None else 4
    steps = min(4, rows // 16)
    part = rows // steps
    down_rows = down[0].shape[0]
    down_part = down_rows // steps

    def body(place, *refs):
        p = place[0]
        downs, proj_ref = refs[:2], refs[2]
        ups, qkvs = refs[3 : 3 + n_p], refs[3 + n_p : n_in]
        qkv_out, proj_out, up_out, down_out = refs[n_in + skip :]
        proj_out[0] = proj_ref[...].astype(F32)
        for k in range(2):
            down_out[0, :, k * (D // 2) : (k + 1) * (D // 2)] = downs[k][...].astype(F32)
        for j in range(n_p):
            up_out[0, :, tile(p ^ j, fw)] = ups[j][...].astype(F32)
            for i in range(3):
                to = tile(i * n_p + (p ^ j), cw)
                ref, at = (qkvs[2 * j + i // 2], i % 2) if split else (qkvs[j], i)
                qkv_out[0, :, to] = ref[:, at * cw : (at + 1) * cw].astype(F32)

    def of_rows(v, size):
        return pl.BlockSpec((size, v.shape[1]), lambda i: (i, 0))

    ins = [*down, proj, *up, *flat]
    specs = [IN_SMEM] + [of_rows(v, down_part) for v in down] + [of_rows(v, part) for v in [proj, *up, *flat]]
    aliases = {}
    if before is not None:
        aliases = {1 + n_in + k: k for k in range(4)}
        specs += [IN_ANY] * 4
        ins = ins + list(before)
    shapes = [(rows, 3 * D), (rows, D), (rows, FF), (down_rows, D)]
    sizes = [part, part, part, down_part]
    moved = 6 * sum(a * b for a, b in shapes)
    return pl.pallas_call(
        body,
        grid=(steps,),
        out_shape=[jax.ShapeDtypeStruct((layers, *shape), F32) for shape in shapes],
        in_specs=specs,
        out_specs=[
            pl.BlockSpec((1, size, shape[1]), lambda i: (layer, i, 0)) for size, shape in zip(sizes, shapes)
        ],
        input_output_aliases=aliases,
        compiler_params=pltpu.CompilerParams(vmem_limit_bytes=16 << 20),
        cost_estimate=pl.CostEstimate(flops=0, bytes_accessed=moved, transcendentals=0),
        name="write_layer",
    )(net.place, *ins)


def on_device(
    tokens,
    scene_ids,
    token_kind,
    out_grad,
    first_gain,
    first_shift,
    qkv_weight,
    qv_bias,
    proj_weight,
    proj_bias,
    second_gain,
    second_shift,
    up_weight,
    up_bias,
    down_weight,
    down_bias,
):
    net = Net()
    n_p = net.n_p
    layers = qkv_weight.shape[0]
    rows = tokens.shape[1]
    pair_groups = [[2 * i, 2 * i + 1] for i in range(n_p)]

    def fetch(layer, *weights):
        pieces = cut_columns(net, layer, weights)
        return stack_halves([net.chip(v, j) for j, v in enumerate(pieces, 1)])

    def complete(mine, theirs, parts, more, layer):
        own = stack_rows(net, mine, theirs, parts, more, layer)
        return [(v, net.core(v)) for v in own]

    def swap_cores(both):
        return lax.all_to_all(both, "fsdp", 0, 0, axis_index_groups=pair_groups)

    small_in = [first_gain, first_shift, qv_bias, proj_bias, second_gain, second_shift, up_bias, down_bias]
    sizes = [v.shape[1] for v in small_in]
    tok, tok_rest = pack_tokens(tokens, scene_ids, token_kind)
    tok, tok_rest = net.to_plane(net.to_chip(tok)), net.to_place(tok_rest)
    mine = fetch(0, (qkv_weight, 3), (proj_weight, None))
    small = pack_small(small_in)
    small_other = net.core(small)
    later = (qkv_weight, proj_weight, up_weight, down_weight, out_grad)
    tok, tok_rest, mine, small, small_other, later = fence((tok, tok_rest, mine, small, small_other, later))
    qkv_weight, proj_weight, up_weight, down_weight, out_grad = later
    tokg = net.gather(put_small(tok, tok_rest, small, small_other))
    theirs = net.next_plane(mine)
    tokg, mine, theirs = fence((tokg, mine, theirs))

    weights = []
    kept = []
    dm = None
    codes = None
    qkv_cols = 3 * D // n_p
    for layer in range(layers):
        last = layer == layers - 1
        blocks = tokg if layer == 0 else net.gather(low)
        parts = [(qkv_weight, 3, 0), (proj_weight, None, qkv_cols)]
        qkv_w, proj_w = complete(mine, theirs, parts, [], layer)
        blocks, qkv_w, proj_w, up_weight, out_grad = fence((blocks, qkv_w, proj_w, up_weight, out_grad))
        if layer == 0:
            tokg = blocks
            hidden = tokg[0]
            vectors = join_vectors(net, layers, tokg, sizes, rows)
            gain1, shift1, qv_b, proj_b, gain2, shift2, up_b, down_b = vectors
        a1g, qkv, og, codes = attend(net, layer, rows, blocks, gain1, shift1, qkv_w, qv_b, codes)
        mine = fetch(layer, (up_weight, 1))
        if last:
            dm = net.to_chip(out_grad[0])
        a1g, qkv, og, mine, dm, down_weight = fence((a1g, qkv, og, mine, dm, down_weight))
        pieces = net.gather(og)
        theirs = net.next_plane(mine)
        if last:
            dm = net.to_plane(dm)
        pieces, theirs, dm = fence((pieces, theirs, dm))
        up_w, down_w = complete(mine, theirs, [(up_weight, 1, 0)], [down_weight], layer)
        h2, a2g = close_attention(net, layer, hidden, blocks, pieces, proj_w, proj_b, gain2, shift2)
        a2g, up_w, down_w, qkv_weight, proj_weight = fence((a2g, up_w, down_w, qkv_weight, proj_weight))
        y, z, slope = feed_forward(net, layer, a2g, up_w, up_b, down_w)
        kept.append((hidden, [a1g], qkv, og, h2, [a2g], z, slope))
        weights.append((qkv_w, proj_w, up_w, down_w))
        if last:
            dmg = net.gather(dm)
            last_y, z, slope, dmg = fence((y, z, slope, dmg))
            break
        mine = fetch(layer + 1, (qkv_weight, 3), (proj_weight, None))
        y, mine = fence((y, mine))
        parts = net.exchange(y)
        theirs = net.next_plane(mine)
        parts, theirs = fence((parts, theirs))
        hidden, low = close_layer(net, layer, h2, parts, down_b)

    flow = Flow(net)
    small_grads = [None] * layers
    sums = [None] * layers
    out = None
    grad = dm
    down_b_grad = column_sums(dm)

    def chunks(halves):
        return [Chunk(v) for v in halves]

    for layer in reversed(range(layers)):
        last = layer == layers - 1
        qkv_w, proj_w, up_w, down_w = weights[layer]
        h1, a1g, qkv, og, h2, a2g, z, slope = kept[layer]
        keep, send = down_weight_grad(net, z, dmg)
        da2, du, up_b_grad = feed_back(net, dmg, down_w, slope, up_w)
        send = net.core(send)
        da2, du, keep, send = fence((da2, du, keep, send))
        down_g = chunks(add_halves(keep, send))
        da2 = flow.collect(da2, down_g[0])
        parts = net.exchange(da2)
        both = swap_cores(up_weight_grad(net, a2g, du))
        parts, both = flow.collect((parts, both), down_g[1])
        up_g = chunks(add_pair(both))
        dh2, dy, sums2 = norm_back(net, layer, grad, h2, parts, gain2)
        dyg = net.gather(dy)
        dyg = flow.collect(dyg, up_g[0])
        tokens_in = tokg if layer == 0 else []
        da1, dqkv, qkv_b_grad, norm_sums = attend_back(net, dyg, proj_w, qkv, codes, qkv_w, tokens_in)
        da1, dqkv = flow.collect((da1, dqkv), up_g[1])
        parts = net.exchange(da1)
        names = [None, None, "heads", None, None, None, "chip", None]
        of_layer = [None, None, qkv_b_grad, sums2[2:3], sums2[0:1], sums2[1:2], up_b_grad, down_b_grad]
        small = None
        if layer == 0:
            of_layer[0], of_layer[1] = norm_sums[0:1], norm_sums[1:2]
            names[0] = names[1] = "own"
            small_grads[layer] = list(zip(of_layer, names))
            small = (sizes, small_grads)
        both = swap_cores(attend_weight_grad(net, a1g, dqkv, og, dyg, small))
        parts, both = fence((parts, both))
        attend_g = chunks(add_pair(both))
        grad, dm, sums1 = norm_back(net, layer, dh2, h1, parts, gain1)
        sums[layer] = (down_g, up_g, attend_g)
        dm = flow.collect(dm, attend_g[0])
        if layer > 0:
            of_layer[0], of_layer[1] = sums1[0:1], sums1[1:2]
            small_grads[layer] = list(zip(of_layer, names))
            dmg = net.gather(dm)
            down_b_grad = sums1[2:3]
            dmg, grad = flow.collect((dmg, grad), attend_g[1])

    def to_owners(chunks, extra):
        *pieces, rest = [*cut_rows(net, *[c.value for c in chunks], extra), None][: n_p + 1]
        return net.exchange(pieces), rest

    last_parts = net.exchange(last_y)
    dm, last_parts = flow.collect((dm, last_parts), attend_g[1])
    _, sent_out = close_layer(net, layers - 1, kept[-1][4], last_parts, down_b)
    up_pieces, _ = to_owners(sums[1][1], None)
    dm, up_pieces = flow.collect((dm, up_pieces))
    qkv_pieces, proj_g = to_owners(sums[1][2], 0)
    dm, sent_out, qkv_pieces, proj_g = flow.collect((dm, sent_out, qkv_pieces, proj_g))
    while [c for c in flow.queue if c in sums[0][1]]:
        dm = flow.collect(dm)
    up_last, _ = to_owners(sums[0][1], None)
    dm, sent_out, up_last = flow.collect((dm, sent_out, up_last))
    while flow.queue:
        dm = flow.collect(dm)
    pieces, proj_last = to_owners(sums[0][2], 2 * layers * n_p)
    dm, sent_out = net.from_place(dm), net.from_place(sent_out)
    out = write_layer(net, 1, layers, None, [c.value for c in sums[1][0]], proj_g, up_pieces, qkv_pieces)
    *small_out, input_grad, sent_out = sum_small(net, layers, pieces, sizes, D // net.n_f, [dm, sent_out])
    out = write_layer(net, 0, layers, out, [c.value for c in sums[0][0]], proj_last, up_last, pieces)
    return (
        sent_out[None],
        input_grad[None],
        small_out[0],
        small_out[1],
        out[0],
        small_out[2],
        out[1],
        small_out[3],
        small_out[4],
        small_out[5],
        out[2],
        small_out[6],
        out[3],
        small_out[7],
    )


def solution(mesh):
    tok = P("fsdp", "seq", None)
    lab = P("fsdp", "seq")
    vec = P(None, "fsdp")
    mat = P(None, "fsdp", None)
    return jax.shard_map(
        on_device,
        mesh=mesh,
        in_specs=(tok, lab, lab, tok, vec, vec, mat, vec, mat, vec, vec, vec, mat, vec, mat, vec),
        out_specs=(tok, tok, vec, vec, mat, vec, mat, vec, vec, vec, mat, vec, mat, vec),
        check_vma=False,
    )
```

```python
import jax
import jax.numpy as jnp
from jax import lax
from jax.experimental import pallas as pl
from jax.experimental.pallas import tpu as pltpu
from jax.sharding import PartitionSpec as P

D = 1024
HEAD_DIM = 64
FF = 4096
EPS = 1e-05
NEG = -1e30
SCALE = 0.125
BF = jnp.bfloat16
F32 = jnp.float32
LANES = 128


def xor_pairs(count, mask):
    return [(i, i ^ mask) for i in range(count)]


class Net:
    def __init__(self):
        self.n_s = lax.axis_size("seq")
        self.n_f = lax.axis_size("fsdp")
        self.n_p = self.n_f // 2
        self.s = lax.axis_index("seq")
        self.f = lax.axis_index("fsdp")
        self.p = self.f // 2
        self.c = self.f % 2
        self.place = jnp.stack([self.p, self.c, self.s % 2]).astype(jnp.int32)

    def moves(self):
        square = [[s ^ q for s in range(self.n_s)] for q in range(self.n_p)]
        if self.n_p == 4:
            square = [[0, 2, 1, 3], [1, 3, 2, 0], [2, 0, 3, 1], [3, 1, 0, 2]]
        return [(s, square[q][s], q) for s in range(self.n_s) for q in range(self.n_p)]

    def send(self, v, moves):
        n = self.n_f
        pairs = [(s * n + 2 * p + c, t * n + 2 * q + c) for s, p, t, q in moves for c in range(2)]
        return lax.ppermute(v, ("seq", "fsdp"), pairs)

    def to_place(self, v):
        return self.send(v, [(s, p, p, q) for s, p, q in self.moves()])

    def from_place(self, v):
        return self.send(v, [(p, q, s, p) for s, p, q in self.moves()])

    def to_chip(self, v):
        return self.send(v, [(s, p, s, q) for s, p, q in self.moves()])

    def to_plane(self, v):
        return self.send(v, [(s, q, p, q) for s, p, q in self.moves()])

    def chip(self, v, j):
        return lax.ppermute(v, "fsdp", xor_pairs(self.n_f, 2 * j))

    def core(self, v):
        return lax.ppermute(v, "fsdp", xor_pairs(self.n_f, 1))

    def next_plane(self, v):
        return lax.ppermute(v, "seq", xor_pairs(self.n_s, 1))

    def gather(self, v):
        return [v] + [self.chip(v, j) for j in range(1, self.n_p)]

    def exchange(self, blocks):
        return [blocks[0]] + [self.chip(blocks[j], j) for j in range(1, self.n_p)]


def fence(values):
    return lax.optimization_barrier(values)


def block(v, index, size, axis):
    return lax.dynamic_slice_in_dim(v, index * size, size, axis=axis)


IN_VMEM = pl.BlockSpec(memory_space=pltpu.VMEM)
IN_SMEM = pl.BlockSpec(memory_space=pltpu.SMEM)
IN_ANY = pl.BlockSpec(memory_space=pl.ANY)
IN_HBM = pl.BlockSpec(memory_space=pltpu.HBM)


def run(name, body, outs, ins, place=None, scratch=(), flops=0, ins_at=None):
    specs = [IN_VMEM] * len(ins) if ins_at is None else ins_at
    if place is not None:
        specs = [IN_SMEM] + specs
        ins = [place, *ins]
    moved = sum(v.size * v.dtype.itemsize for v in ins)
    return pl.pallas_call(
        body,
        out_shape=[jax.ShapeDtypeStruct(shape, dtype) for shape, dtype in outs],
        in_specs=specs,
        out_specs=[IN_VMEM] * len(outs),
        scratch_shapes=list(scratch),
        compiler_params=pltpu.CompilerParams(vmem_limit_bytes=16 << 20),
        cost_estimate=pl.CostEstimate(flops=flops, bytes_accessed=moved, transcendentals=0),
        name=name,
    )(*ins)


def dot(a, b):
    return jnp.dot(a, b, preferred_element_type=F32)


def dot_nt(a, b):
    return lax.dot_general(a, b, (((1,), (1,)), ((), ())), preferred_element_type=F32)


def dot_tn(a, b):
    return lax.dot_general(a, b, (((0,), (0,)), ((), ())), preferred_element_type=F32)


def tile(i, size):
    return pl.ds(pl.multiple_of(i * size, size), size)


def copy_all(pairs, sems):
    copies = [pltpu.make_async_copy(src, dst, sems.at[k]) for k, (src, dst) in enumerate(pairs)]
    for copy in copies:
        copy.start()
    return copies


def own_first(v, parts, c):
    rows = v.shape[-1] // (2 * parts)
    own, other = [], []
    for i in range(parts):
        even = v[:, 2 * i * rows : (2 * i + 1) * rows]
        odd = v[:, (2 * i + 1) * rows : (2 * i + 2) * rows]
        own.append(jnp.where(c == 0, even, odd))
        other.append(jnp.where(c == 0, odd, even))
    return jnp.concatenate(own, axis=1), jnp.concatenate(other, axis=1)


def model_order(v, parts, c):
    half = v.shape[-1] // 2
    rows = half // parts
    out = []
    for i in range(parts):
        own = v[:, i * rows : (i + 1) * rows]
        other = v[:, half + i * rows : half + (i + 1) * rows]
        out += [jnp.where(c == 0, own, other), jnp.where(c == 0, other, own)]
    return jnp.concatenate(out, axis=1)


def columns_of(net, weight, groups):
    return weight.shape[2] // (groups * net.n_p) if groups else weight.shape[2]


def cut_columns(net, layer, weights):
    n_p = net.n_p
    rows = weights[0][0].shape[1] // 2
    widths = [columns_of(net, w, groups) for w, groups in weights]
    count = sum(groups or 1 for _, groups in weights)
    total = sum(width * (groups or 1) for width, (_, groups) in zip(widths, weights))

    def body(place, *refs):
        p, half = place[0], place[2]
        outs, sems = refs[len(weights) : -1], refs[-1]
        pairs = []
        for j in range(1, n_p):
            at = 0
            for ref, width, (_, groups) in zip(refs, widths, weights):
                for i in range(groups or 1):
                    cols = tile(i * n_p + (p ^ j), width) if groups else slice(0, width)
                    pairs.append((ref.at[layer, tile(half, rows), cols], outs[j - 1].at[:, at : at + width]))
                    at += width
        for copy in copy_all(pairs, sems):
            copy.wait()

    outs = [((rows, total), BF)] * (n_p - 1)
    scratch = [pltpu.SemaphoreType.DMA((count * (n_p - 1),))]
    ins = [w for w, _ in weights]
    return run("cut_columns", body, outs, ins, net.place, scratch, ins_at=[IN_HBM] * len(ins))


def stack_halves(pieces):
    rows, width = pieces[0].shape
    count = len(pieces)

    def body(*refs):
        out, sems = refs[count:]
        pairs = [(refs[j], out.at[j * rows : (j + 1) * rows]) for j in range(count)]
        for copy in copy_all(pairs, sems):
            copy.wait()

    outs = [((count * rows, width), BF)]
    scratch = [pltpu.SemaphoreType.DMA((count,))]
    return run("stack_halves", body, outs, pieces, None, scratch, ins_at=[IN_ANY] * count)[0]


def stack_rows(net, mine, theirs, parts, more, layer):
    n_p = net.n_p
    half_rows = parts[0][0].shape[1] // 2
    rows = 2 * half_rows
    widths = [columns_of(net, w, groups) for w, groups, _ in parts]
    count = len(more) + sum((groups or 1) + 2 * (n_p - 1) for _, groups, _ in parts)

    def body(place, mine_ref, their_ref, *refs):
        p, half = place[0], place[2]
        ins, outs, sems = refs[: len(parts) + len(more)], refs[len(parts) + len(more) : -1], refs[-1]
        pairs = [(ref.at[layer], out) for ref, out in zip(ins[len(parts) :], outs[len(parts) :])]
        for ref, own, width, (_, groups, first) in zip(ins, outs, widths, parts):
            for i in range(groups or 1):
                to = own.at[tile(p, rows), i * width : (i + 1) * width]
                cols = tile(i * n_p + p, width) if groups else slice(0, width)
                pairs.append((ref.at[layer, :, cols], to))
            cols = slice(first, first + (groups or 1) * width)
            for j in range(1, n_p):
                here = slice((j - 1) * half_rows, j * half_rows)
                at = (p ^ j) * 2
                pairs.append((mine_ref.at[here, cols], own.at[tile(at + half, half_rows)]))
                pairs.append((their_ref.at[here, cols], own.at[tile(at + 1 - half, half_rows)]))
        for copy in copy_all(pairs, sems):
            copy.wait()

    outs = [((n_p * rows, (g or 1) * width), BF) for (_, g, _), width in zip(parts, widths)]
    outs += [(w.shape[1:], BF) for w in more]
    ins = [mine, theirs, *[w for w, _, _ in parts], *more]
    specs = [IN_ANY] * 2 + [IN_HBM] * (len(parts) + len(more))
    scratch = [pltpu.SemaphoreType.DMA((count,))]
    return run("stack_rows", body, outs, ins, net.place, scratch, ins_at=specs)


def pack_tokens(tokens, scene_ids, token_kind):
    half = tokens.shape[1] // 2
    code = (scene_ids * 2 + token_kind).astype(BF)
    code = jnp.pad(code, ((half, 15), (0, D - 2 * half)))
    return tokens[0, :half], jnp.pad(tokens[0, half:], ((0, 16), (0, 0))) + code


def pack_small(vectors):
    sizes = [v.shape[1] for v in vectors]
    total = None
    for k, v in enumerate(vectors):
        at = sum(sizes[:k])
        put = jnp.pad(v, ((0, 0), (at, sum(sizes) - at - sizes[k])))
        total = put if total is None else total + put
    return total


def put_small(first, second, own, other):
    mid = first.shape[0]
    rows = 2 * mid
    width = own.shape[1] // 2

    def body(first_ref, second_ref, own_ref, other_ref, out, lines):
        out[0:mid, :] = first_ref[...]
        out[mid:rows, :] = second_ref[0:mid, :]
        lines[...] = second_ref[mid:, :].astype(F32)
        row = 1
        for ref in (own_ref, other_ref):
            low = ref[...].astype(F32)
            for layer in range(own.shape[0]):
                for half in range(2):
                    lines[row : row + 1, 0:width] = low[layer : layer + 1, half * width : (half + 1) * width]
                    row += 1
        out[rows:, :] = lines[...].astype(BF)

    scratch = [pltpu.VMEM((16, D), F32)]
    outs = [((rows + 16, D), BF)]
    return run("put_small", body, outs, [first, second, own, other], None, scratch)[0]


def join_vectors(net, layers, blocks, sizes, rows):
    n_p = net.n_p
    width = sum(sizes) // 2
    starts = [sum(sizes[:i]) for i in range(len(sizes))]

    def body(place, *refs):
        p, c = place[0], place[1]
        ins, outs = refs[:n_p], refs[n_p:]
        for j in range(n_p):
            low = ins[j][rows : rows + 16, 0:width].astype(F32)
            for layer in range(layers):
                for half in range(2):
                    row = 1 + layer * 2 + half
                    own = low[row : row + 1, :]
                    other = low[2 * layers + row : 2 * layers + row + 1, :]
                    first = jnp.where(c == 0, own, other)
                    second = jnp.where(c == 0, other, own)
                    for k, (at, size) in enumerate(zip(starts, sizes)):
                        if at // width != half:
                            continue
                        cols = slice(at - half * width, at - half * width + size)
                        both = jnp.concatenate([first[:, cols], second[:, cols]], axis=1)
                        outs[k][layer : layer + 1, tile(p ^ j, 2 * size)] = both

    outs = [((layers, 2 * n_p * size), F32) for size in sizes]
    return run("join_vectors", body, outs, blocks, net.place)


def norm_rows(hidden):
    centred = hidden - jnp.mean(hidden, axis=-1, keepdims=True)
    spread = jnp.mean(centred * centred, axis=-1, keepdims=True)
    inverse = lax.rsqrt(spread + EPS)
    return centred * inverse, inverse


def close_layer(net, layer, hidden, parts, bias):
    rows = parts[0].shape[0]
    count = len(parts)

    def body(hidden_ref, bias_ref, *refs):
        total = hidden_ref[...] + bias_ref[layer : layer + 1, :]
        for part in refs[:count]:
            total = total + part[...].astype(F32)
        refs[count][...] = total
        refs[count + 1][...] = total.astype(BF)

    outs = [((rows, D), F32), ((rows, D), BF)]
    return run("close_layer", body, outs, [hidden, bias, *parts])


def close_attention(net, layer, hidden, blocks, pieces, proj, bias, gain, shift):
    n_p = net.n_p
    tokens, cw = pieces[0].shape
    rows = tokens // n_p
    half = cw // 2

    def body(place, *refs):
        hiddens, os = refs[:n_p], refs[n_p : 2 * n_p]
        p_own, p_other, bias_ref, gain_ref, shift_ref, out, low, acc, o = refs[2 * n_p :]
        p, c = place[0], place[1]
        aligned = half % LANES == 0
        for j in range(n_p):
            for i in range(n_p):
                there, here = slice(i * rows, (i + 1) * rows), slice((i ^ j) * rows, ((i ^ j) + 1) * rows)
                first, second = os[j][there, :half], os[j][there, half:]
                own, other = jnp.where(c == 0, first, second), jnp.where(c == 0, second, first)
                if aligned:
                    o[here, tile(p ^ j, half)] = own
                    o[here, tile(n_p + (p ^ j), half)] = other
                    continue
                part = dot(own, p_own[tile(p ^ j, half), :]) + dot(other, p_other[tile(p ^ j, half), :])
                if j == 0:
                    acc[here, :] = part
                else:
                    acc[here, :] += part
        if aligned:
            acc[...] = dot(o[:, : D // 2], p_own[...]) + dot(o[:, D // 2 :], p_other[...])
        line = slice(layer, layer + 1)
        for j in range(n_p):
            here = slice(j * rows, (j + 1) * rows)
            total = acc[here, :] + hiddens[j][0:rows, :].astype(F32) + bias_ref[line, :]
            if j == 0:
                out[...] = total
            normed, _ = norm_rows(total)
            own, other = own_first(normed * gain_ref[line, :] + shift_ref[line, :], n_p, c)
            low[here, : D // 2] = own.astype(BF)
            low[here, D // 2 :] = other.astype(BF)

    outs = [((rows, D), F32), ((tokens, D), BF)]
    scratch = [pltpu.VMEM((tokens, D), F32), pltpu.VMEM((tokens, D), BF)]
    ins = [hidden, *blocks[1:], *pieces, *proj, bias, gain, shift]
    return run("close_attention", body, outs, ins, net.place, scratch, flops=2 * tokens * D * D)


def norm_back(net, layer, grad, hidden, parts, gain):
    rows = parts[0].shape[0]
    count = len(parts)

    def body(place, grad_ref, hidden_ref, gain_ref, *refs):
        total = refs[0][...].astype(F32)
        for part in refs[1:count]:
            total = total + part[...].astype(F32)
        total = model_order(total, net.n_p, place[1])
        out, low, sums = refs[count:]
        normed, inverse = norm_rows(hidden_ref[0:rows, :].astype(F32))
        scaled = total * gain_ref[layer : layer + 1, :]
        one = jnp.mean(scaled, axis=-1, keepdims=True)
        two = jnp.mean(scaled * normed, axis=-1, keepdims=True)
        result = grad_ref[...].astype(F32) + inverse * (scaled - one - normed * two)
        rounded = result.astype(BF)
        out[...] = result
        low[...] = rounded
        sums[0:1, :] = jnp.sum(total * normed, axis=0, keepdims=True)
        sums[1:2, :] = jnp.sum(total, axis=0, keepdims=True)
        sums[2:3, :] = jnp.sum(rounded.astype(F32), axis=0, keepdims=True)

    outs = [((rows, D), F32), ((rows, D), BF), ((3, D), F32)]
    return run("norm_back", body, outs, [grad, hidden, gain, *parts], net.place)


def column_sums(v):
    def body(ref, out):
        out[...] = jnp.sum(ref[...].astype(F32), axis=0, keepdims=True)

    return run("column_sums", body, [((1, v.shape[1]), F32)], [v])[0]


def gather_rows(blocks, scratch):
    rows = scratch.shape[0] // len(blocks)
    for j, ref in enumerate(blocks):
        scratch[j * rows : (j + 1) * rows, :] = ref[0:rows, :]


def allowed_pairs(code_col, code_row):
    same = (code_col >> 1) == (code_row >> 1)
    return same & (((code_col & 1) == 0) | ((code_row & 1) == 1))


def head_lanes(shape, head, axis):
    lane = lax.broadcasted_iota(jnp.int32, shape, axis)
    return (lane < HEAD_DIM) if head == 0 else (lane >= HEAD_DIM)


def keep_head(v, head, axis):
    return jnp.where(head_lanes(v.shape, head, axis), v, jnp.zeros_like(v))


def probs_by_key(k2, q2, allowed, head):
    scores = jnp.where(allowed, dot_nt(keep_head(k2, head, 1), q2), NEG)
    powers = jnp.exp(scores - jnp.max(scores, axis=0, keepdims=True))
    return powers * (1.0 / jnp.sum(powers, axis=0, keepdims=True))


Q_TILE = 256


def attend(net, layer, rows, blocks, gain, shift, weight, bias, codes):
    n_p = net.n_p
    tokens = n_p * rows
    cw = D // n_p
    n_c = 0 if codes is None else 2

    def body(place, *refs):
        bias_ref, w_own, w_other, gain_ref, shift_ref, row_ref, col_ref = refs[n_p : n_p + 7]
        a, qkv, attended, vt = refs[n_p + 7 :]
        p, c = place[0], place[1]
        eye = lax.broadcasted_iota(jnp.int32, (rows, rows), 0) == lax.broadcasted_iota(
            jnp.int32, (rows, rows), 1
        )
        line = slice(layer, layer + 1)
        for j in range(n_p):
            here = slice(j * rows, (j + 1) * rows)
            if codes is None:
                code = refs[j][rows : rows + 1, 0:rows].astype(F32)
                row_ref[:, here] = code.astype(jnp.int32)
                column = jnp.sum(jnp.where(eye, code, 0.0), axis=1, keepdims=True)
                col_ref[here, :] = column.astype(jnp.int32)
            normed, _ = norm_rows(refs[j][0:rows, :].astype(F32))
            own, other = own_first(normed * gain_ref[line, :] + shift_ref[line, :], n_p, c)
            a[here, : D // 2] = own.astype(BF)
            a[here, D // 2 :] = other.astype(BF)
        for i in range(3):
            cols = slice(i * cw, (i + 1) * cw)
            out = dot(a[:, : D // 2], w_own[:, cols]) + dot(a[:, D // 2 :], w_other[:, cols])
            if i == 0:
                out = out + bias_ref[line, tile(p, cw)]
            if i == 2:
                out = out + bias_ref[line, tile(p + n_p, cw)]
            qkv[:, cols] = out.astype(BF)
        vt[...] = jnp.transpose(qkv[:, 2 * cw : 3 * cw].astype(F32)).astype(BF)

        @pl.loop(0, tokens // Q_TILE)
        def _(t):
            here = tile(t, Q_TILE)
            allowed = allowed_pairs(col_ref[...], row_ref[:, here])
            for pair in range(cw // LANES):
                lanes = slice(pair * LANES, (pair + 1) * LANES)
                q2 = qkv[here, lanes]
                k2 = qkv[:, cw + pair * LANES : cw + (pair + 1) * LANES]
                total = None
                for head in range(2):
                    probs = probs_by_key(k2, q2 * BF(SCALE), allowed, head).astype(BF)
                    part = dot(keep_head(vt[lanes, :], head, 0), probs)
                    total = part if total is None else total + part
                attended[here, lanes] = jnp.transpose(total).astype(BF)

    outs = [((tokens, D), BF), ((tokens, 3 * cw), BF), ((tokens, cw), BF)]
    if codes is None:
        outs = [((1, tokens), jnp.int32), ((tokens, 1), jnp.int32)] + outs
    ins = [*blocks, bias, *weight, gain, shift] + list(codes or [])
    scratch = [pltpu.VMEM((cw, tokens), BF)]
    got = run("attend", body, outs, ins, net.place, scratch, flops=2 * tokens * D * 3 * cw)
    if codes is None:
        codes, got = got[:2], got[2:]
    return (*got, codes)


def attend_back(net, blocks, proj, qkv, codes, weight, tokens_in):
    n_p = net.n_p
    rows = blocks[0].shape[0]
    tokens = n_p * rows
    cw = D // n_p
    n_t = len(tokens_in)

    def body(place, *refs):
        p_own, p_other, qkv_ref, row_ref, col_ref, w_own, w_other = refs[n_p : n_p + 7]
        token_refs = refs[n_p + 7 : n_p + 7 + n_t]
        refs_out = refs[n_p + 7 + n_t :]
        outs = refs_out[:n_p]
        dqkv, sums, norm_sums, do, kt, dk, dv = refs_out[n_p:]
        c = place[1]
        mine = tile(place[0], cw // 2)
        for j in range(n_p):
            here = slice(j * rows, (j + 1) * rows)
            own, other = dot_nt(refs[j][...], p_own[mine, :]), dot_nt(refs[j][...], p_other[mine, :])
            do[here, : cw // 2] = jnp.where(c == 0, own, other).astype(BF)
            do[here, cw // 2 :] = jnp.where(c == 0, other, own).astype(BF)
        kt[...] = jnp.transpose(qkv_ref[:, cw : 2 * cw].astype(F32)).astype(BF)
        dk[...] = jnp.zeros_like(dk)
        dv[...] = jnp.zeros_like(dv)

        @pl.loop(0, tokens // Q_TILE)
        def _(t):
            here = tile(t, Q_TILE)
            allowed = allowed_pairs(col_ref[...], row_ref[:, here])
            for pair in range(cw // LANES):
                lanes = slice(pair * LANES, (pair + 1) * LANES)
                q2 = qkv_ref[here, lanes]
                k2 = qkv_ref[:, cw + pair * LANES : cw + (pair + 1) * LANES]
                v2 = qkv_ref[:, 2 * cw + pair * LANES : 2 * cw + (pair + 1) * LANES]
                do2 = do[here, lanes]
                total = None
                for head in range(2):
                    probs = probs_by_key(k2, q2 * BF(SCALE), allowed, head)
                    dp = dot_nt(keep_head(v2, head, 1), do2)
                    mean = jnp.sum(probs * dp, axis=0, keepdims=True)
                    ds = (probs * (dp - mean)).astype(BF)
                    dv[:, lanes] += dot(probs.astype(BF), keep_head(do2, head, 1))
                    dk[:, lanes] += dot(ds, keep_head(q2, head, 1))
                    part = dot(keep_head(kt[lanes, :], head, 0), ds)
                    total = part if total is None else total + part
                dqkv[here, lanes] = (jnp.transpose(total) * SCALE).astype(BF)

        dqkv[:, cw : 2 * cw] = (dk[...] * SCALE).astype(BF)
        dqkv[:, 2 * cw :] = dv[...].astype(BF)
        sums[...] = jnp.sum(dqkv[...].astype(F32), axis=0, keepdims=True)
        norm_sums[...] = jnp.zeros_like(norm_sums)
        for j in range(n_p):
            normed = None
            if n_t:
                normed = own_first(norm_rows(token_refs[j][0:rows, :].astype(F32))[0], n_p, c)
            for k, w in enumerate((w_own, w_other)):
                cols = slice(k * (D // 2), (k + 1) * (D // 2))
                da1 = dot_nt(dqkv[j * rows : (j + 1) * rows, :], w[...])
                outs[j][:, cols] = da1.astype(BF)
                if n_t:
                    norm_sums[0:1, cols] += jnp.sum(da1 * normed[k], axis=0, keepdims=True)
                    norm_sums[1:2, cols] += jnp.sum(da1, axis=0, keepdims=True)

    outs = [((rows, D), BF)] * n_p + [((tokens, 3 * cw), BF), ((1, 3 * cw), F32), ((2, D), F32)]
    scratch = [
        pltpu.VMEM((tokens, cw), BF),
        pltpu.VMEM((cw, tokens), BF),
        pltpu.VMEM((tokens, cw), F32),
        pltpu.VMEM((tokens, cw), F32),
    ]
    ins = [*blocks, *proj, qkv, *codes, *weight, *tokens_in]
    got = run("attend_back", body, outs, ins, net.place, scratch, flops=2 * tokens * D * 8 * cw)
    return got[:n_p], got[n_p], got[n_p + 1], got[n_p + 2]


F_TILE = 256


def feed_forward(net, layer, a2, up, bias, down):
    n_p = net.n_p
    tokens = a2.shape[0]
    rows = tokens // n_p
    fw = FF // n_p

    def body(place, a_ref, up_own, up_other, bias_ref, d_own, d_other, *refs):
        outs, z_ref, slope_ref = refs[:n_p], refs[n_p], refs[n_p + 1]
        p, c = place[0], place[1]

        @pl.loop(0, fw // F_TILE)
        def _(t):
            cols = tile(t, F_TILE)
            there = pl.ds(pl.multiple_of(p * fw + t * F_TILE, F_TILE), F_TILE)
            u = dot(a_ref[:, : D // 2], up_own[:, cols]) + dot(a_ref[:, D // 2 :], up_other[:, cols])
            u = u + bias_ref[layer : layer + 1, there]
            phi = 0.5 * (1.0 + lax.erf(u * 0.7071067811865476))
            z_ref[:, cols] = (u * phi).astype(BF)
            slope_ref[:, cols] = phi + u * (jnp.exp(-0.5 * u * u) * 0.3989422804014327)

        for j in range(n_p):
            here = slice(j * rows, (j + 1) * rows)
            own, other = z_ref[here, tile(c, fw // 2)], z_ref[here, tile(1 - c, fw // 2)]
            outs[j][...] = (dot(own, d_own[...]) + dot(other, d_other[...])).astype(BF)

    outs = [((rows, D), BF)] * n_p + [((tokens, fw), BF), ((tokens, fw), F32)]
    ins = [a2, *up, bias, *down]
    got = run("feed_forward", body, outs, ins, net.place, flops=4 * tokens * D * fw)
    return got[:n_p], got[n_p], got[n_p + 1]


def feed_back(net, blocks, down, slope, up):
    n_p = net.n_p
    rows = blocks[0].shape[0]
    tokens = n_p * rows
    fw = FF // n_p

    def body(place, *refs):
        d_own, d_other, slope_ref, up_own, up_other = refs[n_p : n_p + 5]
        outs = refs[n_p + 5 : 2 * n_p + 5]
        du_ref, sums, dm = refs[2 * n_p + 5 :]
        c = place[1]
        gather_rows(refs[:n_p], dm)
        for w, core in ((d_own, c), (d_other, 1 - c)):

            @pl.loop(0, fw // (2 * F_TILE))
            def _(t):
                start = core * (fw // 2) + t * F_TILE
                cols = pl.ds(pl.multiple_of(start, F_TILE), F_TILE)
                dz = dot_nt(dm[...], w[tile(t, F_TILE), :])
                du = (dz * slope_ref[:, cols]).astype(BF)
                du_ref[:, cols] = du
                sums[:, cols] = jnp.sum(du.astype(F32), axis=0, keepdims=True)

        for j in range(n_p):
            du = du_ref[j * rows : (j + 1) * rows, :]
            outs[j][:, : D // 2] = dot_nt(du, up_own[...]).astype(BF)
            outs[j][:, D // 2 :] = dot_nt(du, up_other[...]).astype(BF)

    outs = [((rows, D), BF)] * n_p + [((tokens, fw), BF), ((1, fw), F32)]
    scratch = [pltpu.VMEM((tokens, D), BF)]
    ins = [*blocks, *down, slope, *up]
    got = run("feed_back", body, outs, ins, net.place, scratch, flops=4 * tokens * D * fw)
    return got[:n_p], got[n_p], got[n_p + 1]


def down_weight_grad(net, z, dm):
    n_r = len(dm)
    tokens, m = z.shape
    half = m // 2

    def body(place, z_ref, *refs):
        keep, send, b = refs[n_r:]
        c = place[1]
        gather_rows(refs[:n_r], b)
        keep[...] = dot_tn(z_ref[:, tile(c, half)], b[...]).astype(BF)
        send[...] = dot_tn(z_ref[:, tile(1 - c, half)], b[...]).astype(BF)

    outs = [((half, D), BF)] * 2
    scratch = [pltpu.VMEM((tokens, D), BF)]
    return run("down_weight_grad", body, outs, [z, *dm], net.place, scratch, flops=2 * tokens * m * D)


def up_weight_grad(net, a2, du):
    n_l = len(a2)
    tokens, n = du.shape

    def body(place, *refs):
        du_ref, out, a = refs[n_l:]
        c = place[1]
        gather_rows(refs[:n_l], a)
        out[c] = dot_tn(a[:, : D // 2], du_ref[...]).astype(BF)
        out[1 - c] = dot_tn(a[:, D // 2 :], du_ref[...]).astype(BF)

    scratch = [pltpu.VMEM((tokens, D), BF)]
    outs = [((2, D // 2, n), BF)]
    return run("up_weight_grad", body, outs, [*a2, du], net.place, scratch, flops=2 * tokens * D * n)[0]


def attend_weight_grad(net, a1, dqkv, attended, dy, small):
    n_p = net.n_p
    n_a = len(a1)
    tokens, width = dqkv.shape
    cw = D // n_p
    rows = D // net.n_f
    lines_each = 2 * len(small[1]) if small else 0
    extra = n_p * lines_each
    flat = [v for of_layer in small[1] for v in of_layer] if small else []
    sizes = small[0] if small else []
    starts = [sum(sizes[:i]) for i in range(len(sizes))]

    def put_small(place, refs, low):
        p, c = place[0], place[1]
        low[...] = jnp.zeros_like(low)
        for k, (ref, (_, kind)) in enumerate(zip(refs, flat)):
            layer, which = divmod(k, len(sizes))
            at, size = starts[which], sizes[which]
            half = at // width
            row = slice(2 * layer + half, 2 * layer + half + 1)
            cols = slice(at - half * width, at - half * width + size)
            if kind == "chip":
                low[0, p, row, cols] = ref[:, :size]
                low[1, p, row, cols] = ref[:, size:]
            elif kind == "heads":
                low[p % 2, p // 2, row, cols] = ref[:, :size]
                low[p % 2, p // 2 + n_p // 2, row, cols] = ref[:, 2 * size :]
            elif kind == "own":
                for i in range(n_p):
                    low[c, i, row, cols] = ref[:, i * size : (i + 1) * size]
                    low[1 - c, i, row, cols] = ref[:, D // 2 + i * size : D // 2 + (i + 1) * size]
            else:
                for i in range(n_p):
                    for core in range(2):
                        to = (2 * i + core) * size
                        low[core, i, row, cols] = ref[:, to : to + size]

    def body(place, *refs):
        dqkv_ref, attended_ref = refs[n_a : n_a + 2]
        smalls = refs[n_a + 2 + n_p : n_a + 2 + n_p + len(flat)]
        out, a, b, low, lines, under = refs[n_a + 2 + n_p + len(flat) :]
        c = place[1]
        gather_rows(refs[:n_a], a)
        for k, core in ((0, c), (1, 1 - c)):
            both = dot_tn(a[:, k * (D // 2) : (k + 1) * (D // 2)], dqkv_ref[...]).astype(BF)
            for i in range(n_p):
                out[core, i * rows : (i + 1) * rows, :width] = both[i * rows : (i + 1) * rows]
        gather_rows(refs[n_a + 2 : n_a + 2 + n_p], b)
        low[...] = dot_tn(attended_ref[...], b[...]).astype(BF)
        for core in range(2):
            for i in range(n_p):
                here = slice(i * rows, (i + 1) * rows)
                out[core, here, width:] = low[core * rows : (core + 1) * rows, i * cw : (i + 1) * cw]
        if extra:
            put_small(place, smalls, lines)
            for core in range(2):
                for i in range(n_p):
                    for r in range(lines_each):
                        under[i * lines_each + r : i * lines_each + r + 1, :] = lines[core, i, r : r + 1, :]
                out[core, n_p * rows :, :width] = under[...].astype(BF)
                out[core, n_p * rows :, width:] = jnp.zeros((extra, cw), BF)

    outs = [((2, n_p * rows + extra, width + cw), BF)]
    scratch = [pltpu.VMEM((tokens, D), BF), pltpu.VMEM((tokens, D), BF), pltpu.VMEM((cw, D), BF)]
    scratch += [pltpu.VMEM((2, n_p, 8, width), F32), pltpu.VMEM((max(extra, 8), width), F32)]
    flops = 2 * tokens * D * (width + cw)
    ins = [*a1, dqkv, attended, *dy, *[v for v, _ in flat]]
    return run("attend_weight_grad", body, outs, ins, net.place, scratch, flops=flops)[0]


def add_halves(a, b):
    rows, width = a.shape
    half = width // 2

    def body(a_ref, b_ref, *outs):
        for k in range(2):
            cols = slice(k * half, (k + 1) * half)
            outs[k][...] = (a_ref[:, cols].astype(F32) + b_ref[:, cols].astype(F32)).astype(BF)

    return run("add_halves", body, [((rows, half), BF)] * 2, [a, b])


def add_pair(both):
    _, rows, width = both.shape
    half = width // 2

    def body(ref, *outs):
        for k in range(2):
            cols = slice(k * half, (k + 1) * half)
            outs[k][...] = (ref[0, :, cols].astype(F32) + ref[1, :, cols].astype(F32)).astype(BF)

    return run("add_pair", body, [((rows, half), BF)] * 2, [both])


def cut_rows(net, first, second, extra):
    n_p = net.n_p
    split = extra is not None
    under = extra or 0
    rows = (first.shape[0] - under) // n_p
    width, more = first.shape[1], second.shape[1]
    taken = more // 2 if split else more

    def body(place, a, b, *outs):
        p = place[0]
        for j in range(n_p):
            here = tile(p ^ j, rows)
            outs[j][0:rows, :width] = a[here, :]
            outs[j][0:rows, width:] = b[here, :taken]
            for k in range(3 if under else 0):
                at = slice(rows + k * under, rows + (k + 1) * under)
                outs[j][at, :width] = a[n_p * rows :, :]
                outs[j][at, width:] = b[n_p * rows :, :taken]
        if split:
            for i in range(n_p):
                outs[n_p][:, i * taken : (i + 1) * taken] = b[i * rows : (i + 1) * rows, taken:]

    outs = [((rows + 3 * under, width + taken), BF)] * n_p
    if split:
        outs.append(((rows, n_p * taken), BF))
    return run("cut_rows", body, outs, [first, second], net.place)


def sum_small(net, layers, pieces, sizes, rows, more):
    width = pieces[0].shape[1]
    count = len(pieces)
    starts = [sum(sizes[:i]) for i in range(len(sizes))]

    def body(place, *refs):
        lines = slice(rows, rows + 2 * layers * net.n_p)
        every = refs[0][lines, :].astype(F32)
        for ref in refs[1:count]:
            every = every + ref[lines, :].astype(F32)
        total = jnp.zeros((2 * layers, width), F32)
        for i in range(net.n_p):
            total = jnp.where(place[0] == i, every[i * 2 * layers : (i + 1) * 2 * layers], total)
        outs = refs[count + len(more) :]
        for out, at, size in zip(outs, starts, sizes):
            half = at // width
            for layer in range(layers):
                row = 2 * layer + half
                out[layer : layer + 1, :] = total[row : row + 1, at - half * width : at - half * width + size]
        for ref, out in zip(refs[count : count + len(more)], outs[len(sizes) :]):
            out[...] = ref[...].astype(F32)

    outs = [((layers, size), F32) for size in sizes] + [(v.shape, F32) for v in more]
    return run("sum_small", body, outs, [*pieces, *more], net.place)


def take_if(here, a, b, rows):
    def body(flag, a_ref, b_ref, out):
        @pl.when(flag[0] != 0)
        def _():
            count = min(rows, a.shape[0])
            out[0:count, :] = a_ref[0:count, :]

        @pl.when(flag[0] == 0)
        def _():
            count = min(rows, b.shape[0])
            out[0:count, :] = b_ref[0:count, :]

    return run("take_if", body, [((rows, a.shape[1]), BF)], [a, b], here.astype(jnp.int32).reshape(1))[0]


def turn(net, wanted):
    flat, flags, outs = [], [], []
    for one, two, outer in wanted:
        flat += one + (two or [])
        rows = max(one[0].shape[0], two[0].shape[0] if two else 0)
        outs.append(((rows, one[0].shape[1]), BF))
        flags.append(jnp.zeros((), jnp.int32) if outer is None else outer.astype(jnp.int32))

    def put(refs, out):
        rows = refs[0].shape[0]
        if len(refs) == 1:
            out[0:rows, :] = refs[0][...]
            return
        total = refs[0][...].astype(F32)
        for ref in refs[1:]:
            total = total + ref[0:rows, :].astype(F32)
        out[0:rows, :] = total.astype(BF)

    def body(flag, *refs):
        at = 0
        for k, (one, two, outer) in enumerate(wanted):
            out = refs[len(flat) + k]
            first = refs[at : at + len(one)]
            at += len(one)
            if outer is None:
                put(first, out)
                continue
            second = refs[at : at + len(two)]
            at += len(two)
            pl.when(flag[k] != 0)(lambda first=first, out=out: put(first, out))
            pl.when(flag[k] == 0)(lambda second=second, out=out: put(second, out))

    return run("turn", body, outs, flat, jnp.stack(flags))


class Chunk:
    def __init__(self, value):
        self.terms = [value]
        self.step = 0

    @property
    def value(self):
        return self.terms[0]


class Flow:
    def __init__(self, net):
        self.net = net
        self.queue = []
        self.moving = []

    def first(self, step):
        for chunk in self.queue:
            if chunk.step == step:
                return chunk
        return None

    def start(self):
        net = self.net
        n = net.n_s
        half = n // 2
        moves, wanted = [], []
        for k in range(half):
            inward = self.first(k)
            outward = None if k == half - 1 else self.first(n - 2 - k)
            into = [(k, k + 1), (n - 1 - k, n - 2 - k)]
            out = [(k + 1, k), (n - 2 - k, n - 1 - k)]
            outer = (net.s == k) | (net.s == n - 1 - k)
            both = inward is not None and outward is not None
            if both and inward.value.shape[1] == outward.value.shape[1]:
                moves.append((inward, outward, outer, into + out))
                wanted.append((inward.terms, outward.terms, outer))
                continue
            if inward is not None:
                moves.append((inward, None, outer, into))
                wanted.append((inward.terms, None, None))
            if outward is not None:
                moves.append((None, outward, outer, out))
                wanted.append((outward.terms, None, None))
        sent = [w[0][0] for w in wanted]
        work = [k for k, w in enumerate(wanted) if len(w[0]) > 1 or w[1] is not None]
        if work:
            for k, value in zip(work, turn(net, [wanted[k] for k in work])):
                sent[k] = value
        self.moving = [(*m[:3], v, lax.ppermute(v, "seq", m[3])) for m, v in zip(moves, sent)]

    def collect(self, values, *new):
        values, news, got = fence((values, [c.value for c in new], [(m[3], m[4]) for m in self.moving]))
        for c, value in zip(new, news):
            c.terms = [value]
        n = self.net.n_s
        for (inward, outward, outer, _, _), (sent, arrived) in zip(self.moving, got):
            if inward is not None:
                middle = inward.step == n // 2 - 1
                inward.terms = [sent, arrived] if middle else [*inward.terms, arrived]
                inward.step += 1
            if outward is not None:
                outward.terms = [take_if(outer, arrived, sent, outward.value.shape[0])]
                outward.step += 1
        self.queue = [c for c in self.queue if c.step < n - 1] + list(new)
        self.start()
        return values


def write_layer(net, layer, layers, before, down, proj, up, qkv):
    n_p = net.n_p
    rows = up[0].shape[0]
    cw, fw = D // n_p, FF // n_p
    split = isinstance(qkv[0], tuple)
    flat = [v for pair in qkv for v in pair] if split else list(qkv)
    n_in = 3 + n_p + len(flat)
    skip = 0 if before is None else 4
    steps = min(4, rows // 16)
    part = rows // steps
    down_rows = down[0].shape[0]
    down_part = down_rows // steps

    def body(place, *refs):
        p = place[0]
        downs, proj_ref = refs[:2], refs[2]
        ups, qkvs = refs[3 : 3 + n_p], refs[3 + n_p : n_in]
        qkv_out, proj_out, up_out, down_out = refs[n_in + skip :]
        proj_out[0] = proj_ref[...].astype(F32)
        for k in range(2):
            down_out[0, :, k * (D // 2) : (k + 1) * (D // 2)] = downs[k][...].astype(F32)
        for j in range(n_p):
            up_out[0, :, tile(p ^ j, fw)] = ups[j][...].astype(F32)
            for i in range(3):
                to = tile(i * n_p + (p ^ j), cw)
                ref, at = (qkvs[2 * j + i // 2], i % 2) if split else (qkvs[j], i)
                qkv_out[0, :, to] = ref[:, at * cw : (at + 1) * cw].astype(F32)

    def of_rows(v, size):
        return pl.BlockSpec((size, v.shape[1]), lambda i: (i, 0))

    ins = [*down, proj, *up, *flat]
    specs = [IN_SMEM] + [of_rows(v, down_part) for v in down] + [of_rows(v, part) for v in [proj, *up, *flat]]
    aliases = {}
    if before is not None:
        aliases = {1 + n_in + k: k for k in range(4)}
        specs += [IN_ANY] * 4
        ins = ins + list(before)
    shapes = [(rows, 3 * D), (rows, D), (rows, FF), (down_rows, D)]
    sizes = [part, part, part, down_part]
    moved = 6 * sum(a * b for a, b in shapes)
    return pl.pallas_call(
        body,
        grid=(steps,),
        out_shape=[jax.ShapeDtypeStruct((layers, *shape), F32) for shape in shapes],
        in_specs=specs,
        out_specs=[
            pl.BlockSpec((1, size, shape[1]), lambda i: (layer, i, 0)) for size, shape in zip(sizes, shapes)
        ],
        input_output_aliases=aliases,
        compiler_params=pltpu.CompilerParams(vmem_limit_bytes=16 << 20),
        cost_estimate=pl.CostEstimate(flops=0, bytes_accessed=moved, transcendentals=0),
        name="write_layer",
    )(net.place, *ins)


def on_device(
    tokens,
    scene_ids,
    token_kind,
    out_grad,
    first_gain,
    first_shift,
    qkv_weight,
    qv_bias,
    proj_weight,
    proj_bias,
    second_gain,
    second_shift,
    up_weight,
    up_bias,
    down_weight,
    down_bias,
):
    net = Net()
    n_p = net.n_p
    layers = qkv_weight.shape[0]
    rows = tokens.shape[1]
    pair_groups = [[2 * i, 2 * i + 1] for i in range(n_p)]

    def fetch(layer, *weights):
        pieces = cut_columns(net, layer, weights)
        return stack_halves([net.chip(v, j) for j, v in enumerate(pieces, 1)])

    def complete(mine, theirs, parts, more, layer):
        own = stack_rows(net, mine, theirs, parts, more, layer)
        return [(v, net.core(v)) for v in own]

    def swap_cores(both):
        return lax.all_to_all(both, "fsdp", 0, 0, axis_index_groups=pair_groups)

    small_in = [first_gain, first_shift, qv_bias, proj_bias, second_gain, second_shift, up_bias, down_bias]
    sizes = [v.shape[1] for v in small_in]
    tok, tok_rest = pack_tokens(tokens, scene_ids, token_kind)
    tok, tok_rest = net.to_plane(net.to_chip(tok)), net.to_place(tok_rest)
    mine = fetch(0, (qkv_weight, 3), (proj_weight, None))
    small = pack_small(small_in)
    small_other = net.core(small)
    later = (qkv_weight, proj_weight, up_weight, down_weight, out_grad)
    tok, tok_rest, mine, small, small_other, later = fence((tok, tok_rest, mine, small, small_other, later))
    qkv_weight, proj_weight, up_weight, down_weight, out_grad = later
    tokg = net.gather(put_small(tok, tok_rest, small, small_other))
    theirs = net.next_plane(mine)
    tokg, mine, theirs = fence((tokg, mine, theirs))

    weights = []
    kept = []
    dm = None
    codes = None
    qkv_cols = 3 * D // n_p
    for layer in range(layers):
        last = layer == layers - 1
        blocks = tokg if layer == 0 else net.gather(low)
        parts = [(qkv_weight, 3, 0), (proj_weight, None, qkv_cols)]
        qkv_w, proj_w = complete(mine, theirs, parts, [], layer)
        blocks, qkv_w, proj_w, up_weight, out_grad = fence((blocks, qkv_w, proj_w, up_weight, out_grad))
        if layer == 0:
            tokg = blocks
            hidden = tokg[0]
            vectors = join_vectors(net, layers, tokg, sizes, rows)
            gain1, shift1, qv_b, proj_b, gain2, shift2, up_b, down_b = vectors
        a1g, qkv, og, codes = attend(net, layer, rows, blocks, gain1, shift1, qkv_w, qv_b, codes)
        mine = fetch(layer, (up_weight, 1))
        if last:
            dm = net.to_chip(out_grad[0])
        a1g, qkv, og, mine, dm, down_weight = fence((a1g, qkv, og, mine, dm, down_weight))
        pieces = net.gather(og)
        theirs = net.next_plane(mine)
        if last:
            dm = net.to_plane(dm)
        pieces, theirs, dm = fence((pieces, theirs, dm))
        up_w, down_w = complete(mine, theirs, [(up_weight, 1, 0)], [down_weight], layer)
        h2, a2g = close_attention(net, layer, hidden, blocks, pieces, proj_w, proj_b, gain2, shift2)
        a2g, up_w, down_w, qkv_weight, proj_weight = fence((a2g, up_w, down_w, qkv_weight, proj_weight))
        y, z, slope = feed_forward(net, layer, a2g, up_w, up_b, down_w)
        kept.append((hidden, [a1g], qkv, og, h2, [a2g], z, slope))
        weights.append((qkv_w, proj_w, up_w, down_w))
        if last:
            dmg = net.gather(dm)
            last_y, z, slope, dmg = fence((y, z, slope, dmg))
            break
        mine = fetch(layer + 1, (qkv_weight, 3), (proj_weight, None))
        y, mine = fence((y, mine))
        parts = net.exchange(y)
        theirs = net.next_plane(mine)
        parts, theirs = fence((parts, theirs))
        hidden, low = close_layer(net, layer, h2, parts, down_b)

    flow = Flow(net)
    small_grads = [None] * layers
    sums = [None] * layers
    out = None
    grad = dm
    down_b_grad = column_sums(dm)

    def chunks(halves):
        return [Chunk(v) for v in halves]

    for layer in reversed(range(layers)):
        last = layer == layers - 1
        qkv_w, proj_w, up_w, down_w = weights[layer]
        h1, a1g, qkv, og, h2, a2g, z, slope = kept[layer]
        keep, send = down_weight_grad(net, z, dmg)
        da2, du, up_b_grad = feed_back(net, dmg, down_w, slope, up_w)
        send = net.core(send)
        da2, du, keep, send = fence((da2, du, keep, send))
        down_g = chunks(add_halves(keep, send))
        da2 = flow.collect(da2, down_g[0])
        parts = net.exchange(da2)
        both = swap_cores(up_weight_grad(net, a2g, du))
        parts, both = flow.collect((parts, both), down_g[1])
        up_g = chunks(add_pair(both))
        dh2, dy, sums2 = norm_back(net, layer, grad, h2, parts, gain2)
        dyg = net.gather(dy)
        dyg = flow.collect(dyg, up_g[0])
        tokens_in = tokg if layer == 0 else []
        da1, dqkv, qkv_b_grad, norm_sums = attend_back(net, dyg, proj_w, qkv, codes, qkv_w, tokens_in)
        da1, dqkv = flow.collect((da1, dqkv), up_g[1])
        parts = net.exchange(da1)
        names = [None, None, "heads", None, None, None, "chip", None]
        of_layer = [None, None, qkv_b_grad, sums2[2:3], sums2[0:1], sums2[1:2], up_b_grad, down_b_grad]
        small = None
        if layer == 0:
            of_layer[0], of_layer[1] = norm_sums[0:1], norm_sums[1:2]
            names[0] = names[1] = "own"
            small_grads[layer] = list(zip(of_layer, names))
            small = (sizes, small_grads)
        both = swap_cores(attend_weight_grad(net, a1g, dqkv, og, dyg, small))
        parts, both = fence((parts, both))
        attend_g = chunks(add_pair(both))
        grad, dm, sums1 = norm_back(net, layer, dh2, h1, parts, gain1)
        sums[layer] = (down_g, up_g, attend_g)
        dm = flow.collect(dm, attend_g[0])
        if layer > 0:
            of_layer[0], of_layer[1] = sums1[0:1], sums1[1:2]
            small_grads[layer] = list(zip(of_layer, names))
            dmg = net.gather(dm)
            down_b_grad = sums1[2:3]
            dmg, grad = flow.collect((dmg, grad), attend_g[1])

    def to_owners(chunks, extra):
        *pieces, rest = [*cut_rows(net, *[c.value for c in chunks], extra), None][: n_p + 1]
        return net.exchange(pieces), rest

    last_parts = net.exchange(last_y)
    dm, last_parts = flow.collect((dm, last_parts), attend_g[1])
    _, sent_out = close_layer(net, layers - 1, kept[-1][4], last_parts, down_b)
    up_pieces, _ = to_owners(sums[1][1], None)
    dm, up_pieces = flow.collect((dm, up_pieces))
    qkv_pieces, proj_g = to_owners(sums[1][2], 0)
    dm, sent_out, qkv_pieces, proj_g = flow.collect((dm, sent_out, qkv_pieces, proj_g))
    while [c for c in flow.queue if c in sums[0][1]]:
        dm = flow.collect(dm)
    up_last, _ = to_owners(sums[0][1], None)
    dm, sent_out, up_last = flow.collect((dm, sent_out, up_last))
    while flow.queue:
        dm = flow.collect(dm)
    pieces, proj_last = to_owners(sums[0][2], 2 * layers * n_p)
    dm, sent_out = net.from_place(dm), net.from_place(sent_out)
    out = write_layer(net, 1, layers, None, [c.value for c in sums[1][0]], proj_g, up_pieces, qkv_pieces)
    *small_out, input_grad, sent_out = sum_small(net, layers, pieces, sizes, D // net.n_f, [dm, sent_out])
    out = write_layer(net, 0, layers, out, [c.value for c in sums[0][0]], proj_last, up_last, pieces)
    return (
        sent_out[None],
        input_grad[None],
        small_out[0],
        small_out[1],
        out[0],
        small_out[2],
        out[1],
        small_out[3],
        small_out[4],
        small_out[5],
        out[2],
        small_out[6],
        out[3],
        small_out[7],
    )


def solution(mesh):
    tok = P("fsdp", "seq", None)
    lab = P("fsdp", "seq")
    vec = P(None, "fsdp")
    mat = P(None, "fsdp", None)
    return jax.shard_map(
        on_device,
        mesh=mesh,
        in_specs=(tok, lab, lab, tok, vec, vec, mat, vec, mat, vec, vec, vec, mat, vec, mat, vec),
        out_specs=(tok, tok, vec, vec, mat, vec, mat, vec, vec, vec, mat, vec, mat, vec),
        check_vma=False,
    )
```

```python
import jax
import jax.numpy as jnp
from jax import lax
from jax.experimental import pallas as pl
from jax.experimental.pallas import tpu as pltpu
from jax.sharding import PartitionSpec as P

D = 1024
HEAD_DIM = 64
FF = 4096
EPS = 1e-05
NEG = -1e30
SCALE = 0.125
BF = jnp.bfloat16
F32 = jnp.float32
LANES = 128


def xor_pairs(count, mask):
    return [(i, i ^ mask) for i in range(count)]


class Net:
    def __init__(self):
        self.n_s = lax.axis_size("seq")
        self.n_f = lax.axis_size("fsdp")
        self.n_p = self.n_f // 2
        self.s = lax.axis_index("seq")
        self.f = lax.axis_index("fsdp")
        self.p = self.f // 2
        self.c = self.f % 2
        self.place = jnp.stack([self.p, self.c, self.s % 2]).astype(jnp.int32)

    def moves(self):
        square = [[s ^ q for s in range(self.n_s)] for q in range(self.n_p)]
        if self.n_p == 4:
            square = [[0, 2, 1, 3], [1, 3, 2, 0], [2, 0, 3, 1], [3, 1, 0, 2]]
        return [(s, square[q][s], q) for s in range(self.n_s) for q in range(self.n_p)]

    def send(self, v, moves):
        n = self.n_f
        pairs = [(s * n + 2 * p + c, t * n + 2 * q + c) for s, p, t, q in moves for c in range(2)]
        return lax.ppermute(v, ("seq", "fsdp"), pairs)

    def to_place(self, v):
        return self.send(v, [(s, p, p, q) for s, p, q in self.moves()])

    def from_place(self, v):
        return self.send(v, [(p, q, s, p) for s, p, q in self.moves()])

    def to_chip(self, v):
        return self.send(v, [(s, p, s, q) for s, p, q in self.moves()])

    def to_plane(self, v):
        return self.send(v, [(s, q, p, q) for s, p, q in self.moves()])

    def chip(self, v, j):
        return lax.ppermute(v, "fsdp", xor_pairs(self.n_f, 2 * j))

    def core(self, v):
        return lax.ppermute(v, "fsdp", xor_pairs(self.n_f, 1))

    def next_plane(self, v):
        return lax.ppermute(v, "seq", xor_pairs(self.n_s, 1))

    def gather(self, v):
        return [v] + [self.chip(v, j) for j in range(1, self.n_p)]

    def exchange(self, blocks):
        return [blocks[0]] + [self.chip(blocks[j], j) for j in range(1, self.n_p)]


def fence(values):
    return lax.optimization_barrier(values)


def block(v, index, size, axis):
    return lax.dynamic_slice_in_dim(v, index * size, size, axis=axis)


IN_VMEM = pl.BlockSpec(memory_space=pltpu.VMEM)
IN_SMEM = pl.BlockSpec(memory_space=pltpu.SMEM)
IN_ANY = pl.BlockSpec(memory_space=pl.ANY)
IN_HBM = pl.BlockSpec(memory_space=pltpu.HBM)


def run(name, body, outs, ins, place=None, scratch=(), flops=0, ins_at=None):
    specs = [IN_VMEM] * len(ins) if ins_at is None else ins_at
    if place is not None:
        specs = [IN_SMEM] + specs
        ins = [place, *ins]
    moved = sum(v.size * v.dtype.itemsize for v in ins)
    return pl.pallas_call(
        body,
        out_shape=[jax.ShapeDtypeStruct(shape, dtype) for shape, dtype in outs],
        in_specs=specs,
        out_specs=[IN_VMEM] * len(outs),
        scratch_shapes=list(scratch),
        compiler_params=pltpu.CompilerParams(vmem_limit_bytes=16 << 20),
        cost_estimate=pl.CostEstimate(flops=flops, bytes_accessed=moved, transcendentals=0),
        name=name,
    )(*ins)


def dot(a, b):
    return jnp.dot(a, b, preferred_element_type=F32)


def dot_nt(a, b):
    return lax.dot_general(a, b, (((1,), (1,)), ((), ())), preferred_element_type=F32)


def dot_tn(a, b):
    return lax.dot_general(a, b, (((0,), (0,)), ((), ())), preferred_element_type=F32)


def tile(i, size):
    return pl.ds(pl.multiple_of(i * size, size), size)


def copy_all(pairs, sems):
    copies = [pltpu.make_async_copy(src, dst, sems.at[k]) for k, (src, dst) in enumerate(pairs)]
    for copy in copies:
        copy.start()
    return copies


def own_first(v, parts, c):
    rows = v.shape[-1] // (2 * parts)
    own, other = [], []
    for i in range(parts):
        even = v[:, 2 * i * rows : (2 * i + 1) * rows]
        odd = v[:, (2 * i + 1) * rows : (2 * i + 2) * rows]
        own.append(jnp.where(c == 0, even, odd))
        other.append(jnp.where(c == 0, odd, even))
    return jnp.concatenate(own, axis=1), jnp.concatenate(other, axis=1)


def model_order(v, parts, c):
    half = v.shape[-1] // 2
    rows = half // parts
    out = []
    for i in range(parts):
        own = v[:, i * rows : (i + 1) * rows]
        other = v[:, half + i * rows : half + (i + 1) * rows]
        out += [jnp.where(c == 0, own, other), jnp.where(c == 0, other, own)]
    return jnp.concatenate(out, axis=1)


def columns_of(net, weight, groups):
    return weight.shape[2] // (groups * net.n_p) if groups else weight.shape[2]


def cut_columns(net, layer, weights):
    n_p = net.n_p
    rows = weights[0][0].shape[1] // 2
    widths = [columns_of(net, w, groups) for w, groups in weights]
    count = sum(groups or 1 for _, groups in weights)
    total = sum(width * (groups or 1) for width, (_, groups) in zip(widths, weights))

    def body(place, *refs):
        p, half = place[0], place[2]
        outs, sems = refs[len(weights) : -1], refs[-1]
        pairs = []
        for j in range(1, n_p):
            at = 0
            for ref, width, (_, groups) in zip(refs, widths, weights):
                for i in range(groups or 1):
                    cols = tile(i * n_p + (p ^ j), width) if groups else slice(0, width)
                    pairs.append((ref.at[layer, tile(half, rows), cols], outs[j - 1].at[:, at : at + width]))
                    at += width
        for copy in copy_all(pairs, sems):
            copy.wait()

    outs = [((rows, total), BF)] * (n_p - 1)
    scratch = [pltpu.SemaphoreType.DMA((count * (n_p - 1),))]
    ins = [w for w, _ in weights]
    return run("cut_columns", body, outs, ins, net.place, scratch, ins_at=[IN_HBM] * len(ins))


def stack_halves(pieces):
    rows, width = pieces[0].shape
    count = len(pieces)

    def body(*refs):
        out, sems = refs[count:]
        pairs = [(refs[j], out.at[j * rows : (j + 1) * rows]) for j in range(count)]
        for copy in copy_all(pairs, sems):
            copy.wait()

    outs = [((count * rows, width), BF)]
    scratch = [pltpu.SemaphoreType.DMA((count,))]
    return run("stack_halves", body, outs, pieces, None, scratch, ins_at=[IN_ANY] * count)[0]


def stack_rows(net, mine, theirs, parts, more, layer):
    n_p = net.n_p
    half_rows = parts[0][0].shape[1] // 2
    rows = 2 * half_rows
    widths = [columns_of(net, w, groups) for w, groups, _ in parts]
    count = len(more) + sum((groups or 1) + 2 * (n_p - 1) for _, groups, _ in parts)

    def body(place, mine_ref, their_ref, *refs):
        p, half = place[0], place[2]
        ins, outs, sems = refs[: len(parts) + len(more)], refs[len(parts) + len(more) : -1], refs[-1]
        pairs = [(ref.at[layer], out) for ref, out in zip(ins[len(parts) :], outs[len(parts) :])]
        for ref, own, width, (_, groups, first) in zip(ins, outs, widths, parts):
            for i in range(groups or 1):
                to = own.at[tile(p, rows), i * width : (i + 1) * width]
                cols = tile(i * n_p + p, width) if groups else slice(0, width)
                pairs.append((ref.at[layer, :, cols], to))
            cols = slice(first, first + (groups or 1) * width)
            for j in range(1, n_p):
                here = slice((j - 1) * half_rows, j * half_rows)
                at = (p ^ j) * 2
                pairs.append((mine_ref.at[here, cols], own.at[tile(at + half, half_rows)]))
                pairs.append((their_ref.at[here, cols], own.at[tile(at + 1 - half, half_rows)]))
        for copy in copy_all(pairs, sems):
            copy.wait()

    outs = [((n_p * rows, (g or 1) * width), BF) for (_, g, _), width in zip(parts, widths)]
    outs += [(w.shape[1:], BF) for w in more]
    ins = [mine, theirs, *[w for w, _, _ in parts], *more]
    specs = [IN_ANY] * 2 + [IN_HBM] * (len(parts) + len(more))
    scratch = [pltpu.SemaphoreType.DMA((count,))]
    return run("stack_rows", body, outs, ins, net.place, scratch, ins_at=specs)


def pack_tokens(tokens, scene_ids, token_kind):
    half = tokens.shape[1] // 2
    code = (scene_ids * 2 + token_kind).astype(BF)
    code = jnp.pad(code, ((half, 15), (0, D - 2 * half)))
    return tokens[0, :half], jnp.pad(tokens[0, half:], ((0, 16), (0, 0))) + code


def pack_small(vectors):
    sizes = [v.shape[1] for v in vectors]
    total = None
    for k, v in enumerate(vectors):
        at = sum(sizes[:k])
        put = jnp.pad(v, ((0, 0), (at, sum(sizes) - at - sizes[k])))
        total = put if total is None else total + put
    return total


def put_small(first, second, own, other):
    mid = first.shape[0]
    rows = 2 * mid
    width = own.shape[1] // 2

    def body(first_ref, second_ref, own_ref, other_ref, out, lines):
        out[0:mid, :] = first_ref[...]
        out[mid:rows, :] = second_ref[0:mid, :]
        lines[...] = second_ref[mid:, :].astype(F32)
        row = 1
        for ref in (own_ref, other_ref):
            low = ref[...].astype(F32)
            for layer in range(own.shape[0]):
                for half in range(2):
                    lines[row : row + 1, 0:width] = low[layer : layer + 1, half * width : (half + 1) * width]
                    row += 1
        out[rows:, :] = lines[...].astype(BF)

    scratch = [pltpu.VMEM((16, D), F32)]
    outs = [((rows + 16, D), BF)]
    return run("put_small", body, outs, [first, second, own, other], None, scratch)[0]


def join_vectors(net, layers, blocks, sizes, rows):
    n_p = net.n_p
    width = sum(sizes) // 2
    starts = [sum(sizes[:i]) for i in range(len(sizes))]

    def body(place, *refs):
        p, c = place[0], place[1]
        ins, outs = refs[:n_p], refs[n_p:]
        for j in range(n_p):
            low = ins[j][rows : rows + 16, 0:width].astype(F32)
            for layer in range(layers):
                for half in range(2):
                    row = 1 + layer * 2 + half
                    own = low[row : row + 1, :]
                    other = low[2 * layers + row : 2 * layers + row + 1, :]
                    first = jnp.where(c == 0, own, other)
                    second = jnp.where(c == 0, other, own)
                    for k, (at, size) in enumerate(zip(starts, sizes)):
                        if at // width != half:
                            continue
                        cols = slice(at - half * width, at - half * width + size)
                        both = jnp.concatenate([first[:, cols], second[:, cols]], axis=1)
                        outs[k][layer : layer + 1, tile(p ^ j, 2 * size)] = both

    outs = [((layers, 2 * n_p * size), F32) for size in sizes]
    return run("join_vectors", body, outs, blocks, net.place)


def norm_rows(hidden):
    centred = hidden - jnp.mean(hidden, axis=-1, keepdims=True)
    spread = jnp.mean(centred * centred, axis=-1, keepdims=True)
    inverse = lax.rsqrt(spread + EPS)
    return centred * inverse, inverse


def close_layer(net, layer, hidden, parts, bias):
    rows = parts[0].shape[0]
    count = len(parts)

    def body(hidden_ref, bias_ref, *refs):
        total = hidden_ref[...] + bias_ref[layer : layer + 1, :]
        for part in refs[:count]:
            total = total + part[...].astype(F32)
        refs[count][...] = total
        refs[count + 1][...] = total.astype(BF)

    outs = [((rows, D), F32), ((rows, D), BF)]
    return run("close_layer", body, outs, [hidden, bias, *parts])


def close_attention(net, layer, hidden, blocks, pieces, proj, bias, gain, shift):
    n_p = net.n_p
    tokens, cw = pieces[0].shape
    rows = tokens // n_p
    half = cw // 2

    def body(place, *refs):
        hiddens, os = refs[:n_p], refs[n_p : 2 * n_p]
        p_own, p_other, bias_ref, gain_ref, shift_ref, out, low, acc, o = refs[2 * n_p :]
        p, c = place[0], place[1]
        aligned = half % LANES == 0
        for j in range(n_p):
            for i in range(n_p):
                there, here = slice(i * rows, (i + 1) * rows), slice((i ^ j) * rows, ((i ^ j) + 1) * rows)
                first, second = os[j][there, :half], os[j][there, half:]
                own, other = jnp.where(c == 0, first, second), jnp.where(c == 0, second, first)
                if aligned:
                    o[here, tile(p ^ j, half)] = own
                    o[here, tile(n_p + (p ^ j), half)] = other
                    continue
                part = dot(own, p_own[tile(p ^ j, half), :]) + dot(other, p_other[tile(p ^ j, half), :])
                if j == 0:
                    acc[here, :] = part
                else:
                    acc[here, :] += part
        if aligned:
            acc[...] = dot(o[:, : D // 2], p_own[...]) + dot(o[:, D // 2 :], p_other[...])
        line = slice(layer, layer + 1)
        for j in range(n_p):
            here = slice(j * rows, (j + 1) * rows)
            total = acc[here, :] + hiddens[j][0:rows, :].astype(F32) + bias_ref[line, :]
            if j == 0:
                out[...] = total
            normed, _ = norm_rows(total)
            own, other = own_first(normed * gain_ref[line, :] + shift_ref[line, :], n_p, c)
            low[here, : D // 2] = own.astype(BF)
            low[here, D // 2 :] = other.astype(BF)

    outs = [((rows, D), F32), ((tokens, D), BF)]
    scratch = [pltpu.VMEM((tokens, D), F32), pltpu.VMEM((tokens, D), BF)]
    ins = [hidden, *blocks[1:], *pieces, *proj, bias, gain, shift]
    return run("close_attention", body, outs, ins, net.place, scratch, flops=2 * tokens * D * D)


def norm_back(net, layer, grad, hidden, parts, gain):
    rows = parts[0].shape[0]
    count = len(parts)

    def body(place, grad_ref, hidden_ref, gain_ref, *refs):
        total = refs[0][...].astype(F32)
        for part in refs[1:count]:
            total = total + part[...].astype(F32)
        total = model_order(total, net.n_p, place[1])
        out, low, sums = refs[count:]
        normed, inverse = norm_rows(hidden_ref[0:rows, :].astype(F32))
        scaled = total * gain_ref[layer : layer + 1, :]
        one = jnp.mean(scaled, axis=-1, keepdims=True)
        two = jnp.mean(scaled * normed, axis=-1, keepdims=True)
        result = grad_ref[...].astype(F32) + inverse * (scaled - one - normed * two)
        rounded = result.astype(BF)
        out[...] = result
        low[...] = rounded
        sums[0:1, :] = jnp.sum(total * normed, axis=0, keepdims=True)
        sums[1:2, :] = jnp.sum(total, axis=0, keepdims=True)
        sums[2:3, :] = jnp.sum(rounded.astype(F32), axis=0, keepdims=True)

    outs = [((rows, D), F32), ((rows, D), BF), ((3, D), F32)]
    return run("norm_back", body, outs, [grad, hidden, gain, *parts], net.place)


def column_sums(v):
    def body(ref, out):
        out[...] = jnp.sum(ref[...].astype(F32), axis=0, keepdims=True)

    return run("column_sums", body, [((1, v.shape[1]), F32)], [v])[0]


def gather_rows(blocks, scratch):
    rows = scratch.shape[0] // len(blocks)
    for j, ref in enumerate(blocks):
        scratch[j * rows : (j + 1) * rows, :] = ref[0:rows, :]


def allowed_pairs(code_col, code_row):
    same = (code_col >> 1) == (code_row >> 1)
    return same & (((code_col & 1) == 0) | ((code_row & 1) == 1))


def head_lanes(shape, head, axis):
    lane = lax.broadcasted_iota(jnp.int32, shape, axis)
    return (lane < HEAD_DIM) if head == 0 else (lane >= HEAD_DIM)


def keep_head(v, head, axis):
    return jnp.where(head_lanes(v.shape, head, axis), v, jnp.zeros_like(v))


def probs_by_key(k2, q2, allowed, head):
    scores = jnp.where(allowed, dot_nt(keep_head(k2, head, 1), q2), NEG)
    powers = jnp.exp(scores - jnp.max(scores, axis=0, keepdims=True))
    return powers * (1.0 / jnp.sum(powers, axis=0, keepdims=True))


Q_TILE = 256


def attend(net, layer, rows, blocks, gain, shift, weight, bias, codes):
    n_p = net.n_p
    tokens = n_p * rows
    cw = D // n_p
    n_c = 0 if codes is None else 2

    def body(place, *refs):
        bias_ref, w_own, w_other, gain_ref, shift_ref, row_ref, col_ref = refs[n_p : n_p + 7]
        a, qkv, attended, vt = refs[n_p + 7 :]
        p, c = place[0], place[1]
        eye = lax.broadcasted_iota(jnp.int32, (rows, rows), 0) == lax.broadcasted_iota(
            jnp.int32, (rows, rows), 1
        )
        line = slice(layer, layer + 1)
        for j in range(n_p):
            here = slice(j * rows, (j + 1) * rows)
            if codes is None:
                code = refs[j][rows : rows + 1, 0:rows].astype(F32)
                row_ref[:, here] = code.astype(jnp.int32)
                column = jnp.sum(jnp.where(eye, code, 0.0), axis=1, keepdims=True)
                col_ref[here, :] = column.astype(jnp.int32)
            normed, _ = norm_rows(refs[j][0:rows, :].astype(F32))
            own, other = own_first(normed * gain_ref[line, :] + shift_ref[line, :], n_p, c)
            a[here, : D // 2] = own.astype(BF)
            a[here, D // 2 :] = other.astype(BF)
        for i in range(3):
            cols = slice(i * cw, (i + 1) * cw)
            out = dot(a[:, : D // 2], w_own[:, cols]) + dot(a[:, D // 2 :], w_other[:, cols])
            if i == 0:
                out = out + bias_ref[line, tile(p, cw)]
            if i == 2:
                out = out + bias_ref[line, tile(p + n_p, cw)]
            qkv[:, cols] = out.astype(BF)
        vt[...] = jnp.transpose(qkv[:, 2 * cw : 3 * cw].astype(F32)).astype(BF)

        @pl.loop(0, tokens // Q_TILE)
        def _(t):
            here = tile(t, Q_TILE)
            allowed = allowed_pairs(col_ref[...], row_ref[:, here])
            for pair in range(cw // LANES):
                lanes = slice(pair * LANES, (pair + 1) * LANES)
                q2 = qkv[here, lanes]
                k2 = qkv[:, cw + pair * LANES : cw + (pair + 1) * LANES]
                total = None
                for head in range(2):
                    probs = probs_by_key(k2, q2 * BF(SCALE), allowed, head).astype(BF)
                    part = dot(keep_head(vt[lanes, :], head, 0), probs)
                    total = part if total is None else total + part
                attended[here, lanes] = jnp.transpose(total).astype(BF)

    outs = [((tokens, D), BF), ((tokens, 3 * cw), BF), ((tokens, cw), BF)]
    if codes is None:
        outs = [((1, tokens), jnp.int32), ((tokens, 1), jnp.int32)] + outs
    ins = [*blocks, bias, *weight, gain, shift] + list(codes or [])
    scratch = [pltpu.VMEM((cw, tokens), BF)]
    got = run("attend", body, outs, ins, net.place, scratch, flops=2 * tokens * D * 3 * cw)
    if codes is None:
        codes, got = got[:2], got[2:]
    return (*got, codes)


def attend_back(net, blocks, proj, qkv, codes, weight, tokens_in):
    n_p = net.n_p
    rows = blocks[0].shape[0]
    tokens = n_p * rows
    cw = D // n_p
    n_t = len(tokens_in)

    def body(place, *refs):
        p_own, p_other, qkv_ref, row_ref, col_ref, w_own, w_other = refs[n_p : n_p + 7]
        token_refs = refs[n_p + 7 : n_p + 7 + n_t]
        refs_out = refs[n_p + 7 + n_t :]
        outs = refs_out[:n_p]
        dqkv, sums, norm_sums, do, kt, dk, dv = refs_out[n_p:]
        c = place[1]
        mine = tile(place[0], cw // 2)
        for j in range(n_p):
            here = slice(j * rows, (j + 1) * rows)
            own, other = dot_nt(refs[j][...], p_own[mine, :]), dot_nt(refs[j][...], p_other[mine, :])
            do[here, : cw // 2] = jnp.where(c == 0, own, other).astype(BF)
            do[here, cw // 2 :] = jnp.where(c == 0, other, own).astype(BF)
        kt[...] = jnp.transpose(qkv_ref[:, cw : 2 * cw].astype(F32)).astype(BF)
        dk[...] = jnp.zeros_like(dk)
        dv[...] = jnp.zeros_like(dv)

        @pl.loop(0, tokens // Q_TILE)
        def _(t):
            here = tile(t, Q_TILE)
            allowed = allowed_pairs(col_ref[...], row_ref[:, here])
            for pair in range(cw // LANES):
                lanes = slice(pair * LANES, (pair + 1) * LANES)
                q2 = qkv_ref[here, lanes]
                k2 = qkv_ref[:, cw + pair * LANES : cw + (pair + 1) * LANES]
                v2 = qkv_ref[:, 2 * cw + pair * LANES : 2 * cw + (pair + 1) * LANES]
                do2 = do[here, lanes]
                total = None
                for head in range(2):
                    probs = probs_by_key(k2, q2 * BF(SCALE), allowed, head)
                    dp = dot_nt(keep_head(v2, head, 1), do2)
                    mean = jnp.sum(probs * dp, axis=0, keepdims=True)
                    ds = (probs * (dp - mean)).astype(BF)
                    dv[:, lanes] += dot(probs.astype(BF), keep_head(do2, head, 1))
                    dk[:, lanes] += dot(ds, keep_head(q2, head, 1))
                    part = dot(keep_head(kt[lanes, :], head, 0), ds)
                    total = part if total is None else total + part
                dqkv[here, lanes] = (jnp.transpose(total) * SCALE).astype(BF)

        dqkv[:, cw : 2 * cw] = (dk[...] * SCALE).astype(BF)
        dqkv[:, 2 * cw :] = dv[...].astype(BF)
        sums[...] = jnp.sum(dqkv[...].astype(F32), axis=0, keepdims=True)
        norm_sums[...] = jnp.zeros_like(norm_sums)
        for j in range(n_p):
            normed = None
            if n_t:
                normed = own_first(norm_rows(token_refs[j][0:rows, :].astype(F32))[0], n_p, c)
            for k, w in enumerate((w_own, w_other)):
                cols = slice(k * (D // 2), (k + 1) * (D // 2))
                da1 = dot_nt(dqkv[j * rows : (j + 1) * rows, :], w[...])
                outs[j][:, cols] = da1.astype(BF)
                if n_t:
                    norm_sums[0:1, cols] += jnp.sum(da1 * normed[k], axis=0, keepdims=True)
                    norm_sums[1:2, cols] += jnp.sum(da1, axis=0, keepdims=True)

    outs = [((rows, D), BF)] * n_p + [((tokens, 3 * cw), BF), ((1, 3 * cw), F32), ((2, D), F32)]
    scratch = [
        pltpu.VMEM((tokens, cw), BF),
        pltpu.VMEM((cw, tokens), BF),
        pltpu.VMEM((tokens, cw), F32),
        pltpu.VMEM((tokens, cw), F32),
    ]
    ins = [*blocks, *proj, qkv, *codes, *weight, *tokens_in]
    got = run("attend_back", body, outs, ins, net.place, scratch, flops=2 * tokens * D * 8 * cw)
    return got[:n_p], got[n_p], got[n_p + 1], got[n_p + 2]


F_TILE = 256


def feed_forward(net, layer, a2, up, bias, down):
    n_p = net.n_p
    tokens = a2.shape[0]
    rows = tokens // n_p
    fw = FF // n_p

    def body(place, a_ref, up_own, up_other, bias_ref, d_own, d_other, *refs):
        outs, z_ref, slope_ref = refs[:n_p], refs[n_p], refs[n_p + 1]
        p, c = place[0], place[1]

        @pl.loop(0, fw // F_TILE)
        def _(t):
            cols = tile(t, F_TILE)
            there = pl.ds(pl.multiple_of(p * fw + t * F_TILE, F_TILE), F_TILE)
            u = dot(a_ref[:, : D // 2], up_own[:, cols]) + dot(a_ref[:, D // 2 :], up_other[:, cols])
            u = u + bias_ref[layer : layer + 1, there]
            phi = 0.5 * (1.0 + lax.erf(u * 0.7071067811865476))
            z_ref[:, cols] = (u * phi).astype(BF)
            slope_ref[:, cols] = phi + u * (jnp.exp(-0.5 * u * u) * 0.3989422804014327)

        for j in range(n_p):
            here = slice(j * rows, (j + 1) * rows)
            own, other = z_ref[here, tile(c, fw // 2)], z_ref[here, tile(1 - c, fw // 2)]
            outs[j][...] = (dot(own, d_own[...]) + dot(other, d_other[...])).astype(BF)

    outs = [((rows, D), BF)] * n_p + [((tokens, fw), BF), ((tokens, fw), F32)]
    ins = [a2, *up, bias, *down]
    got = run("feed_forward", body, outs, ins, net.place, flops=4 * tokens * D * fw)
    return got[:n_p], got[n_p], got[n_p + 1]


def feed_back(net, blocks, down, slope, up):
    n_p = net.n_p
    rows = blocks[0].shape[0]
    tokens = n_p * rows
    fw = FF // n_p

    def body(place, *refs):
        d_own, d_other, slope_ref, up_own, up_other = refs[n_p : n_p + 5]
        outs = refs[n_p + 5 : 2 * n_p + 5]
        du_ref, sums, dm = refs[2 * n_p + 5 :]
        c = place[1]
        gather_rows(refs[:n_p], dm)
        for w, core in ((d_own, c), (d_other, 1 - c)):

            @pl.loop(0, fw // (2 * F_TILE))
            def _(t):
                start = core * (fw // 2) + t * F_TILE
                cols = pl.ds(pl.multiple_of(start, F_TILE), F_TILE)
                dz = dot_nt(dm[...], w[tile(t, F_TILE), :])
                du = (dz * slope_ref[:, cols]).astype(BF)
                du_ref[:, cols] = du
                sums[:, cols] = jnp.sum(du.astype(F32), axis=0, keepdims=True)

        for j in range(n_p):
            du = du_ref[j * rows : (j + 1) * rows, :]
            outs[j][:, : D // 2] = dot_nt(du, up_own[...]).astype(BF)
            outs[j][:, D // 2 :] = dot_nt(du, up_other[...]).astype(BF)

    outs = [((rows, D), BF)] * n_p + [((tokens, fw), BF), ((1, fw), F32)]
    scratch = [pltpu.VMEM((tokens, D), BF)]
    ins = [*blocks, *down, slope, *up]
    got = run("feed_back", body, outs, ins, net.place, scratch, flops=4 * tokens * D * fw)
    return got[:n_p], got[n_p], got[n_p + 1]


def down_weight_grad(net, z, dm):
    n_r = len(dm)
    tokens, m = z.shape
    half = m // 2

    def body(place, z_ref, *refs):
        keep, send, b = refs[n_r:]
        c = place[1]
        gather_rows(refs[:n_r], b)
        keep[...] = dot_tn(z_ref[:, tile(c, half)], b[...]).astype(BF)
        send[...] = dot_tn(z_ref[:, tile(1 - c, half)], b[...]).astype(BF)

    outs = [((half, D), BF)] * 2
    scratch = [pltpu.VMEM((tokens, D), BF)]
    return run("down_weight_grad", body, outs, [z, *dm], net.place, scratch, flops=2 * tokens * m * D)


def up_weight_grad(net, a2, du):
    n_l = len(a2)
    tokens, n = du.shape

    def body(place, *refs):
        du_ref, out, a = refs[n_l:]
        c = place[1]
        gather_rows(refs[:n_l], a)
        out[c] = dot_tn(a[:, : D // 2], du_ref[...]).astype(BF)
        out[1 - c] = dot_tn(a[:, D // 2 :], du_ref[...]).astype(BF)

    scratch = [pltpu.VMEM((tokens, D), BF)]
    outs = [((2, D // 2, n), BF)]
    return run("up_weight_grad", body, outs, [*a2, du], net.place, scratch, flops=2 * tokens * D * n)[0]


def attend_weight_grad(net, a1, dqkv, attended, dy, small):
    n_p = net.n_p
    n_a = len(a1)
    tokens, width = dqkv.shape
    cw = D // n_p
    rows = D // net.n_f
    lines_each = 2 * len(small[1]) if small else 0
    extra = n_p * lines_each
    flat = [v for of_layer in small[1] for v in of_layer] if small else []
    sizes = small[0] if small else []
    starts = [sum(sizes[:i]) for i in range(len(sizes))]

    def put_small(place, refs, low):
        p, c = place[0], place[1]
        low[...] = jnp.zeros_like(low)
        for k, (ref, (_, kind)) in enumerate(zip(refs, flat)):
            layer, which = divmod(k, len(sizes))
            at, size = starts[which], sizes[which]
            half = at // width
            row = slice(2 * layer + half, 2 * layer + half + 1)
            cols = slice(at - half * width, at - half * width + size)
            if kind == "chip":
                low[0, p, row, cols] = ref[:, :size]
                low[1, p, row, cols] = ref[:, size:]
            elif kind == "heads":
                low[p % 2, p // 2, row, cols] = ref[:, :size]
                low[p % 2, p // 2 + n_p // 2, row, cols] = ref[:, 2 * size :]
            elif kind == "own":
                for i in range(n_p):
                    low[c, i, row, cols] = ref[:, i * size : (i + 1) * size]
                    low[1 - c, i, row, cols] = ref[:, D // 2 + i * size : D // 2 + (i + 1) * size]
            else:
                for i in range(n_p):
                    for core in range(2):
                        to = (2 * i + core) * size
                        low[core, i, row, cols] = ref[:, to : to + size]

    def body(place, *refs):
        dqkv_ref, attended_ref = refs[n_a : n_a + 2]
        smalls = refs[n_a + 2 + n_p : n_a + 2 + n_p + len(flat)]
        out, a, b, low, lines, under = refs[n_a + 2 + n_p + len(flat) :]
        c = place[1]
        gather_rows(refs[:n_a], a)
        for k, core in ((0, c), (1, 1 - c)):
            both = dot_tn(a[:, k * (D // 2) : (k + 1) * (D // 2)], dqkv_ref[...]).astype(BF)
            for i in range(n_p):
                out[core, i * rows : (i + 1) * rows, :width] = both[i * rows : (i + 1) * rows]
        gather_rows(refs[n_a + 2 : n_a + 2 + n_p], b)
        low[...] = dot_tn(attended_ref[...], b[...]).astype(BF)
        for core in range(2):
            for i in range(n_p):
                here = slice(i * rows, (i + 1) * rows)
                out[core, here, width:] = low[core * rows : (core + 1) * rows, i * cw : (i + 1) * cw]
        if extra:
            put_small(place, smalls, lines)
            for core in range(2):
                for i in range(n_p):
                    for r in range(lines_each):
                        under[i * lines_each + r : i * lines_each + r + 1, :] = lines[core, i, r : r + 1, :]
                out[core, n_p * rows :, :width] = under[...].astype(BF)
                out[core, n_p * rows :, width:] = jnp.zeros((extra, cw), BF)

    outs = [((2, n_p * rows + extra, width + cw), BF)]
    scratch = [pltpu.VMEM((tokens, D), BF), pltpu.VMEM((tokens, D), BF), pltpu.VMEM((cw, D), BF)]
    scratch += [pltpu.VMEM((2, n_p, 8, width), F32), pltpu.VMEM((max(extra, 8), width), F32)]
    flops = 2 * tokens * D * (width + cw)
    ins = [*a1, dqkv, attended, *dy, *[v for v, _ in flat]]
    return run("attend_weight_grad", body, outs, ins, net.place, scratch, flops=flops)[0]


def add_halves(a, b):
    rows, width = a.shape
    half = width // 2

    def body(a_ref, b_ref, *outs):
        for k in range(2):
            cols = slice(k * half, (k + 1) * half)
            outs[k][...] = (a_ref[:, cols].astype(F32) + b_ref[:, cols].astype(F32)).astype(BF)

    return run("add_halves", body, [((rows, half), BF)] * 2, [a, b])


def add_pair(both):
    _, rows, width = both.shape
    half = width // 2

    def body(ref, *outs):
        for k in range(2):
            cols = slice(k * half, (k + 1) * half)
            outs[k][...] = (ref[0, :, cols].astype(F32) + ref[1, :, cols].astype(F32)).astype(BF)

    return run("add_pair", body, [((rows, half), BF)] * 2, [both])


def cut_rows(net, first, second, extra):
    n_p = net.n_p
    split = extra is not None
    under = extra or 0
    rows = (first.shape[0] - under) // n_p
    width, more = first.shape[1], second.shape[1]
    taken = more // 2 if split else more

    def body(place, a, b, *outs):
        p = place[0]
        for j in range(n_p):
            here = tile(p ^ j, rows)
            outs[j][0:rows, :width] = a[here, :]
            outs[j][0:rows, width:] = b[here, :taken]
            for k in range(3 if under else 0):
                at = slice(rows + k * under, rows + (k + 1) * under)
                outs[j][at, :width] = a[n_p * rows :, :]
                outs[j][at, width:] = b[n_p * rows :, :taken]
        if split:
            for i in range(n_p):
                outs[n_p][:, i * taken : (i + 1) * taken] = b[i * rows : (i + 1) * rows, taken:]

    outs = [((rows + 3 * under, width + taken), BF)] * n_p
    if split:
        outs.append(((rows, n_p * taken), BF))
    return run("cut_rows", body, outs, [first, second], net.place)


def sum_small(net, layers, pieces, sizes, rows, more):
    width = pieces[0].shape[1]
    count = len(pieces)
    starts = [sum(sizes[:i]) for i in range(len(sizes))]

    def body(place, *refs):
        lines = slice(rows, rows + 2 * layers * net.n_p)
        every = refs[0][lines, :].astype(F32)
        for ref in refs[1:count]:
            every = every + ref[lines, :].astype(F32)
        total = jnp.zeros((2 * layers, width), F32)
        for i in range(net.n_p):
            total = jnp.where(place[0] == i, every[i * 2 * layers : (i + 1) * 2 * layers], total)
        outs = refs[count + len(more) :]
        for out, at, size in zip(outs, starts, sizes):
            half = at // width
            for layer in range(layers):
                row = 2 * layer + half
                out[layer : layer + 1, :] = total[row : row + 1, at - half * width : at - half * width + size]
        for ref, out in zip(refs[count : count + len(more)], outs[len(sizes) :]):
            out[...] = ref[...].astype(F32)

    outs = [((layers, size), F32) for size in sizes] + [(v.shape, F32) for v in more]
    return run("sum_small", body, outs, [*pieces, *more], net.place)


def take_if(here, a, b, rows):
    def body(flag, a_ref, b_ref, out):
        @pl.when(flag[0] != 0)
        def _():
            count = min(rows, a.shape[0])
            out[0:count, :] = a_ref[0:count, :]

        @pl.when(flag[0] == 0)
        def _():
            count = min(rows, b.shape[0])
            out[0:count, :] = b_ref[0:count, :]

    return run("take_if", body, [((rows, a.shape[1]), BF)], [a, b], here.astype(jnp.int32).reshape(1))[0]


def turn(net, wanted):
    flat, flags, outs = [], [], []
    for one, two, outer in wanted:
        flat += one + (two or [])
        rows = max(one[0].shape[0], two[0].shape[0] if two else 0)
        outs.append(((rows, one[0].shape[1]), BF))
        flags.append(jnp.zeros((), jnp.int32) if outer is None else outer.astype(jnp.int32))

    def put(refs, out):
        rows = refs[0].shape[0]
        if len(refs) == 1:
            out[0:rows, :] = refs[0][...]
            return
        total = refs[0][...].astype(F32)
        for ref in refs[1:]:
            total = total + ref[0:rows, :].astype(F32)
        out[0:rows, :] = total.astype(BF)

    def body(flag, *refs):
        at = 0
        for k, (one, two, outer) in enumerate(wanted):
            out = refs[len(flat) + k]
            first = refs[at : at + len(one)]
            at += len(one)
            if outer is None:
                put(first, out)
                continue
            second = refs[at : at + len(two)]
            at += len(two)
            pl.when(flag[k] != 0)(lambda first=first, out=out: put(first, out))
            pl.when(flag[k] == 0)(lambda second=second, out=out: put(second, out))

    return run("turn", body, outs, flat, jnp.stack(flags))


class Chunk:
    def __init__(self, value):
        self.terms = [value]
        self.step = 0

    @property
    def value(self):
        return self.terms[0]


class Flow:
    def __init__(self, net):
        self.net = net
        self.queue = []
        self.moving = []

    def first(self, step):
        for chunk in self.queue:
            if chunk.step == step:
                return chunk
        return None

    def start(self):
        net = self.net
        n = net.n_s
        half = n // 2
        moves, wanted = [], []
        for k in range(half):
            inward = self.first(k)
            outward = None if k == half - 1 else self.first(n - 2 - k)
            into = [(k, k + 1), (n - 1 - k, n - 2 - k)]
            out = [(k + 1, k), (n - 2 - k, n - 1 - k)]
            outer = (net.s == k) | (net.s == n - 1 - k)
            both = inward is not None and outward is not None
            if both and inward.value.shape[1] == outward.value.shape[1]:
                moves.append((inward, outward, outer, into + out))
                wanted.append((inward.terms, outward.terms, outer))
                continue
            if inward is not None:
                moves.append((inward, None, outer, into))
                wanted.append((inward.terms, None, None))
            if outward is not None:
                moves.append((None, outward, outer, out))
                wanted.append((outward.terms, None, None))
        sent = [w[0][0] for w in wanted]
        work = [k for k, w in enumerate(wanted) if len(w[0]) > 1 or w[1] is not None]
        if work:
            for k, value in zip(work, turn(net, [wanted[k] for k in work])):
                sent[k] = value
        self.moving = [(*m[:3], v, lax.ppermute(v, "seq", m[3])) for m, v in zip(moves, sent)]

    def collect(self, values, *new):
        values, news, got = fence((values, [c.value for c in new], [(m[3], m[4]) for m in self.moving]))
        for c, value in zip(new, news):
            c.terms = [value]
        n = self.net.n_s
        for (inward, outward, outer, _, _), (sent, arrived) in zip(self.moving, got):
            if inward is not None:
                middle = inward.step == n // 2 - 1
                inward.terms = [sent, arrived] if middle else [*inward.terms, arrived]
                inward.step += 1
            if outward is not None:
                outward.terms = [take_if(outer, arrived, sent, outward.value.shape[0])]
                outward.step += 1
        self.queue = [c for c in self.queue if c.step < n - 1] + list(new)
        self.start()
        return values


def write_layer(net, layer, layers, before, attention, feed):
    n_p = net.n_p
    cw, fw = D // n_p, FF // n_p
    proj, qkv = attention or (None, [])
    up, down = feed or ([], [])
    rows = (up[0] if feed else proj).shape[0]
    split = len(qkv) > 0 and isinstance(qkv[0], tuple)
    flat = [v for pair in qkv for v in pair] if split else list(qkv)
    steps = min(4, rows // 16)
    which = [0, 1] * (attention is not None) + [2, 3] * (feed is not None)
    ins = [proj] * (attention is not None) + [*flat, *up, *down]
    n_in = len(ins)
    skip = 0 if before is None else len(which)

    def body(place, *refs):
        p = place[0]
        outs = refs[n_in + skip :]
        taken = 0
        if attention is not None:
            qkvs = refs[1 : 1 + len(flat)]
            taken = 1 + len(flat)
            qkv_out, proj_out, *outs = outs
            proj_out[0] = refs[0][...].astype(F32)
            for j in range(n_p):
                for i in range(3):
                    to = tile(i * n_p + (p ^ j), cw)
                    ref, at = (qkvs[2 * j + i // 2], i % 2) if split else (qkvs[j], i)
                    qkv_out[0, :, to] = ref[:, at * cw : (at + 1) * cw].astype(F32)
        if feed is not None:
            ups, downs = refs[taken : taken + n_p], refs[taken + n_p : n_in]
            up_out, down_out = outs
            for k in range(2):
                down_out[0, :, k * (D // 2) : (k + 1) * (D // 2)] = downs[k][...].astype(F32)
            for j in range(n_p):
                up_out[0, :, tile(p ^ j, fw)] = ups[j][...].astype(F32)

    down_rows = down[0].shape[0] if feed else 0
    all_shapes = [(rows, 3 * D), (rows, D), (rows, FF), (down_rows, D)]
    shapes = [all_shapes[k] for k in which]
    specs = [IN_SMEM] + [pl.BlockSpec((rows // steps, v.shape[1]), lambda i: (i, 0)) for v in ins[: n_in - len(down)]]
    specs += [pl.BlockSpec((down_rows // steps, v.shape[1]), lambda i: (i, 0)) for v in down]
    aliases = {}
    if before is not None:
        aliases = {1 + n_in + k: k for k in range(skip)}
        specs += [IN_ANY] * skip
        ins = ins + [before[k] for k in which]
    moved = 6 * sum(a * b for a, b in shapes)
    new = pl.pallas_call(
        body,
        grid=(steps,),
        out_shape=[jax.ShapeDtypeStruct((layers, *shape), F32) for shape in shapes],
        in_specs=specs,
        out_specs=[pl.BlockSpec((1, shape[0] // steps, shape[1]), lambda i: (layer, i, 0)) for shape in shapes],
        input_output_aliases=aliases,
        compiler_params=pltpu.CompilerParams(vmem_limit_bytes=16 << 20),
        cost_estimate=pl.CostEstimate(flops=0, bytes_accessed=moved, transcendentals=0),
        name="write_layer",
    )(net.place, *ins)
    out = [None] * 4 if before is None else list(before)
    for k, v in zip(which, new):
        out[k] = v
    return out


def on_device(
    tokens,
    scene_ids,
    token_kind,
    out_grad,
    first_gain,
    first_shift,
    qkv_weight,
    qv_bias,
    proj_weight,
    proj_bias,
    second_gain,
    second_shift,
    up_weight,
    up_bias,
    down_weight,
    down_bias,
):
    net = Net()
    n_p = net.n_p
    layers = qkv_weight.shape[0]
    rows = tokens.shape[1]
    pair_groups = [[2 * i, 2 * i + 1] for i in range(n_p)]

    def fetch(layer, *weights):
        pieces = cut_columns(net, layer, weights)
        return stack_halves([net.chip(v, j) for j, v in enumerate(pieces, 1)])

    def complete(mine, theirs, parts, more, layer):
        own = stack_rows(net, mine, theirs, parts, more, layer)
        return [(v, net.core(v)) for v in own]

    def swap_cores(both):
        return lax.all_to_all(both, "fsdp", 0, 0, axis_index_groups=pair_groups)

    small_in = [first_gain, first_shift, qv_bias, proj_bias, second_gain, second_shift, up_bias, down_bias]
    sizes = [v.shape[1] for v in small_in]
    tok, tok_rest = pack_tokens(tokens, scene_ids, token_kind)
    tok, tok_rest = net.to_plane(net.to_chip(tok)), net.to_place(tok_rest)
    mine = fetch(0, (qkv_weight, 3), (proj_weight, None))
    small = pack_small(small_in)
    small_other = net.core(small)
    later = (qkv_weight, proj_weight, up_weight, down_weight, out_grad)
    tok, tok_rest, mine, small, small_other, later = fence((tok, tok_rest, mine, small, small_other, later))
    qkv_weight, proj_weight, up_weight, down_weight, out_grad = later
    tokg = net.gather(put_small(tok, tok_rest, small, small_other))
    theirs = net.next_plane(mine)
    tokg, mine, theirs = fence((tokg, mine, theirs))

    weights = []
    kept = []
    dm = None
    codes = None
    qkv_cols = 3 * D // n_p
    for layer in range(layers):
        last = layer == layers - 1
        blocks = tokg if layer == 0 else net.gather(low)
        parts = [(qkv_weight, 3, 0), (proj_weight, None, qkv_cols)]
        qkv_w, proj_w = complete(mine, theirs, parts, [], layer)
        blocks, qkv_w, proj_w, up_weight, out_grad = fence((blocks, qkv_w, proj_w, up_weight, out_grad))
        if layer == 0:
            tokg = blocks
            hidden = tokg[0]
            vectors = join_vectors(net, layers, tokg, sizes, rows)
            gain1, shift1, qv_b, proj_b, gain2, shift2, up_b, down_b = vectors
        a1g, qkv, og, codes = attend(net, layer, rows, blocks, gain1, shift1, qkv_w, qv_b, codes)
        mine = fetch(layer, (up_weight, 1))
        if last:
            dm = net.to_chip(out_grad[0])
        a1g, qkv, og, mine, dm, down_weight = fence((a1g, qkv, og, mine, dm, down_weight))
        pieces = net.gather(og)
        theirs = net.next_plane(mine)
        if last:
            dm = net.to_plane(dm)
        pieces, theirs, dm = fence((pieces, theirs, dm))
        up_w, down_w = complete(mine, theirs, [(up_weight, 1, 0)], [down_weight], layer)
        h2, a2g = close_attention(net, layer, hidden, blocks, pieces, proj_w, proj_b, gain2, shift2)
        a2g, up_w, down_w, qkv_weight, proj_weight = fence((a2g, up_w, down_w, qkv_weight, proj_weight))
        y, z, slope = feed_forward(net, layer, a2g, up_w, up_b, down_w)
        kept.append((hidden, [a1g], qkv, og, h2, [a2g], z, slope))
        weights.append((qkv_w, proj_w, up_w, down_w))
        if last:
            dmg = net.gather(dm)
            last_y, z, slope, dmg = fence((y, z, slope, dmg))
            break
        mine = fetch(layer + 1, (qkv_weight, 3), (proj_weight, None))
        y, mine = fence((y, mine))
        parts = net.exchange(y)
        theirs = net.next_plane(mine)
        parts, theirs = fence((parts, theirs))
        hidden, low = close_layer(net, layer, h2, parts, down_b)

    flow = Flow(net)
    small_grads = [None] * layers
    sums = [None] * layers
    out = None
    grad = dm
    down_b_grad = column_sums(dm)

    def chunks(halves):
        return [Chunk(v) for v in halves]

    for layer in reversed(range(layers)):
        last = layer == layers - 1
        qkv_w, proj_w, up_w, down_w = weights[layer]
        h1, a1g, qkv, og, h2, a2g, z, slope = kept[layer]
        keep, send = down_weight_grad(net, z, dmg)
        da2, du, up_b_grad = feed_back(net, dmg, down_w, slope, up_w)
        send = net.core(send)
        da2, du, keep, send = fence((da2, du, keep, send))
        down_g = chunks(add_halves(keep, send))
        da2 = flow.collect(da2, down_g[0])
        parts = net.exchange(da2)
        both = swap_cores(up_weight_grad(net, a2g, du))
        parts, both = flow.collect((parts, both), down_g[1])
        up_g = chunks(add_pair(both))
        dh2, dy, sums2 = norm_back(net, layer, grad, h2, parts, gain2)
        dyg = net.gather(dy)
        dyg = flow.collect(dyg, up_g[0])
        tokens_in = tokg if layer == 0 else []
        da1, dqkv, qkv_b_grad, norm_sums = attend_back(net, dyg, proj_w, qkv, codes, qkv_w, tokens_in)
        da1, dqkv = flow.collect((da1, dqkv), up_g[1])
        parts = net.exchange(da1)
        names = [None, None, "heads", None, None, None, "chip", None]
        of_layer = [None, None, qkv_b_grad, sums2[2:3], sums2[0:1], sums2[1:2], up_b_grad, down_b_grad]
        small = None
        if layer == 0:
            of_layer[0], of_layer[1] = norm_sums[0:1], norm_sums[1:2]
            names[0] = names[1] = "own"
            small_grads[layer] = list(zip(of_layer, names))
            small = (sizes, small_grads)
        both = swap_cores(attend_weight_grad(net, a1g, dqkv, og, dyg, small))
        parts, both = fence((parts, both))
        attend_g = chunks(add_pair(both))
        grad, dm, sums1 = norm_back(net, layer, dh2, h1, parts, gain1)
        sums[layer] = (down_g, up_g, attend_g)
        dm = flow.collect(dm, attend_g[0])
        if layer > 0:
            of_layer[0], of_layer[1] = sums1[0:1], sums1[1:2]
            small_grads[layer] = list(zip(of_layer, names))
            dmg = net.gather(dm)
            down_b_grad = sums1[2:3]
            dmg, grad = flow.collect((dmg, grad), attend_g[1])

    def to_owners(chunks, extra):
        *pieces, rest = [*cut_rows(net, *[c.value for c in chunks], extra), None][: n_p + 1]
        return net.exchange(pieces), rest

    last_parts = net.exchange(last_y)
    dm, last_parts = flow.collect((dm, last_parts), attend_g[1])
    _, sent_out = close_layer(net, layers - 1, kept[-1][4], last_parts, down_b)
    up_pieces, _ = to_owners(sums[1][1], None)
    dm, up_pieces = flow.collect((dm, up_pieces))
    qkv_pieces, proj_g = to_owners(sums[1][2], 0)
    dm, sent_out, qkv_pieces, proj_g = flow.collect((dm, sent_out, qkv_pieces, proj_g))
    while [c for c in flow.queue if c in sums[0][1]]:
        dm = flow.collect(dm)
    up_last, _ = to_owners(sums[0][1], None)
    dm, sent_out, up_last = flow.collect((dm, sent_out, up_last))
    while flow.queue:
        dm = flow.collect(dm)
    pieces, proj_last = to_owners(sums[0][2], 2 * layers * n_p)
    dm, sent_out = net.from_place(dm), net.from_place(sent_out)
    downs = [[c.value for c in sums[layer][0]] for layer in range(layers)]
    out = write_layer(net, 1, layers, None, (proj_g, qkv_pieces), (up_pieces, downs[1]))
    out = write_layer(net, 0, layers, out, None, (up_last, downs[0]))
    *small_out, input_grad, sent_out = sum_small(net, layers, pieces, sizes, D // net.n_f, [dm, sent_out])
    out = write_layer(net, 0, layers, out, (proj_last, pieces), None)
    return (
        sent_out[None],
        input_grad[None],
        small_out[0],
        small_out[1],
        out[0],
        small_out[2],
        out[1],
        small_out[3],
        small_out[4],
        small_out[5],
        out[2],
        small_out[6],
        out[3],
        small_out[7],
    )


def solution(mesh):
    tok = P("fsdp", "seq", None)
    lab = P("fsdp", "seq")
    vec = P(None, "fsdp")
    mat = P(None, "fsdp", None)
    return jax.shard_map(
        on_device,
        mesh=mesh,
        in_specs=(tok, lab, lab, tok, vec, vec, mat, vec, mat, vec, vec, vec, mat, vec, mat, vec),
        out_specs=(tok, tok, vec, vec, mat, vec, mat, vec, vec, vec, mat, vec, mat, vec),
        check_vma=False,
    )
```

```python
import jax
import jax.numpy as jnp
from jax import lax
from jax.experimental import pallas as pl
from jax.experimental.pallas import tpu as pltpu
from jax.sharding import PartitionSpec as P

D = 1024
HEAD_DIM = 64
FF = 4096
EPS = 1e-05
NEG = -1e30
SCALE = 0.125
BF = jnp.bfloat16
F32 = jnp.float32
LANES = 128


def xor_pairs(count, mask):
    return [(i, i ^ mask) for i in range(count)]


class Net:
    def __init__(self):
        self.n_s = lax.axis_size("seq")
        self.n_f = lax.axis_size("fsdp")
        self.n_p = self.n_f // 2
        self.s = lax.axis_index("seq")
        self.f = lax.axis_index("fsdp")
        self.p = self.f // 2
        self.c = self.f % 2
        self.place = jnp.stack([self.p, self.c, self.s % 2]).astype(jnp.int32)

    def moves(self):
        square = [[s ^ q for s in range(self.n_s)] for q in range(self.n_p)]
        if self.n_p == 4:
            square = [[0, 2, 1, 3], [1, 3, 2, 0], [2, 0, 3, 1], [3, 1, 0, 2]]
        return [(s, square[q][s], q) for s in range(self.n_s) for q in range(self.n_p)]

    def send(self, v, moves):
        n = self.n_f
        pairs = [(s * n + 2 * p + c, t * n + 2 * q + c) for s, p, t, q in moves for c in range(2)]
        return lax.ppermute(v, ("seq", "fsdp"), pairs)

    def to_place(self, v):
        return self.send(v, [(s, p, p, q) for s, p, q in self.moves()])

    def from_place(self, v):
        return self.send(v, [(p, q, s, p) for s, p, q in self.moves()])

    def to_chip(self, v):
        return self.send(v, [(s, p, s, q) for s, p, q in self.moves()])

    def to_plane(self, v):
        return self.send(v, [(s, q, p, q) for s, p, q in self.moves()])

    def chip(self, v, j):
        return lax.ppermute(v, "fsdp", xor_pairs(self.n_f, 2 * j))

    def core(self, v):
        return lax.ppermute(v, "fsdp", xor_pairs(self.n_f, 1))

    def next_plane(self, v):
        return lax.ppermute(v, "seq", xor_pairs(self.n_s, 1))

    def gather(self, v):
        return [v] + [self.chip(v, j) for j in range(1, self.n_p)]

    def exchange(self, blocks):
        return [blocks[0]] + [self.chip(blocks[j], j) for j in range(1, self.n_p)]


def fence(values):
    return lax.optimization_barrier(values)


def block(v, index, size, axis):
    return lax.dynamic_slice_in_dim(v, index * size, size, axis=axis)


IN_VMEM = pl.BlockSpec(memory_space=pltpu.VMEM)
IN_SMEM = pl.BlockSpec(memory_space=pltpu.SMEM)
IN_ANY = pl.BlockSpec(memory_space=pl.ANY)
IN_HBM = pl.BlockSpec(memory_space=pltpu.HBM)


def run(name, body, outs, ins, place=None, scratch=(), flops=0, ins_at=None):
    specs = [IN_VMEM] * len(ins) if ins_at is None else ins_at
    if place is not None:
        specs = [IN_SMEM] + specs
        ins = [place, *ins]
    moved = sum(v.size * v.dtype.itemsize for v in ins)
    return pl.pallas_call(
        body,
        out_shape=[jax.ShapeDtypeStruct(shape, dtype) for shape, dtype in outs],
        in_specs=specs,
        out_specs=[IN_VMEM] * len(outs),
        scratch_shapes=list(scratch),
        compiler_params=pltpu.CompilerParams(vmem_limit_bytes=16 << 20),
        cost_estimate=pl.CostEstimate(flops=flops, bytes_accessed=moved, transcendentals=0),
        name=name,
    )(*ins)


def dot(a, b):
    return jnp.dot(a, b, preferred_element_type=F32)


def dot_nt(a, b):
    return lax.dot_general(a, b, (((1,), (1,)), ((), ())), preferred_element_type=F32)


def dot_tn(a, b):
    return lax.dot_general(a, b, (((0,), (0,)), ((), ())), preferred_element_type=F32)


def tile(i, size):
    return pl.ds(pl.multiple_of(i * size, size), size)


def copy_all(pairs, sems):
    copies = [pltpu.make_async_copy(src, dst, sems.at[k]) for k, (src, dst) in enumerate(pairs)]
    for copy in copies:
        copy.start()
    return copies


def own_first(v, parts, c):
    rows = v.shape[-1] // (2 * parts)
    own, other = [], []
    for i in range(parts):
        even = v[:, 2 * i * rows : (2 * i + 1) * rows]
        odd = v[:, (2 * i + 1) * rows : (2 * i + 2) * rows]
        own.append(jnp.where(c == 0, even, odd))
        other.append(jnp.where(c == 0, odd, even))
    return jnp.concatenate(own, axis=1), jnp.concatenate(other, axis=1)


def model_order(v, parts, c):
    half = v.shape[-1] // 2
    rows = half // parts
    out = []
    for i in range(parts):
        own = v[:, i * rows : (i + 1) * rows]
        other = v[:, half + i * rows : half + (i + 1) * rows]
        out += [jnp.where(c == 0, own, other), jnp.where(c == 0, other, own)]
    return jnp.concatenate(out, axis=1)


def columns_of(net, weight, groups):
    return weight.shape[2] // (groups * net.n_p) if groups else weight.shape[2]


def cut_columns(net, layer, weights):
    n_p = net.n_p
    rows = weights[0][0].shape[1] // 2
    widths = [columns_of(net, w, groups) for w, groups in weights]
    count = sum(groups or 1 for _, groups in weights)
    total = sum(width * (groups or 1) for width, (_, groups) in zip(widths, weights))

    def body(place, *refs):
        p, half = place[0], place[2]
        outs, sems = refs[len(weights) : -1], refs[-1]
        pairs = []
        for j in range(1, n_p):
            at = 0
            for ref, width, (_, groups) in zip(refs, widths, weights):
                for i in range(groups or 1):
                    cols = tile(i * n_p + (p ^ j), width) if groups else slice(0, width)
                    pairs.append((ref.at[layer, tile(half, rows), cols], outs[j - 1].at[:, at : at + width]))
                    at += width
        for copy in copy_all(pairs, sems):
            copy.wait()

    outs = [((rows, total), BF)] * (n_p - 1)
    scratch = [pltpu.SemaphoreType.DMA((count * (n_p - 1),))]
    ins = [w for w, _ in weights]
    return run("cut_columns", body, outs, ins, net.place, scratch, ins_at=[IN_HBM] * len(ins))


def stack_halves(pieces):
    rows, width = pieces[0].shape
    count = len(pieces)

    def body(*refs):
        out, sems = refs[count:]
        pairs = [(refs[j], out.at[j * rows : (j + 1) * rows]) for j in range(count)]
        for copy in copy_all(pairs, sems):
            copy.wait()

    outs = [((count * rows, width), BF)]
    scratch = [pltpu.SemaphoreType.DMA((count,))]
    return run("stack_halves", body, outs, pieces, None, scratch, ins_at=[IN_ANY] * count)[0]


def stack_rows(net, mine, theirs, parts, more, layer):
    n_p = net.n_p
    half_rows = parts[0][0].shape[1] // 2
    rows = 2 * half_rows
    widths = [columns_of(net, w, groups) for w, groups, _ in parts]
    count = len(more) + sum((groups or 1) + 2 * (n_p - 1) for _, groups, _ in parts)

    def body(place, mine_ref, their_ref, *refs):
        p, half = place[0], place[2]
        ins, outs, sems = refs[: len(parts) + len(more)], refs[len(parts) + len(more) : -1], refs[-1]
        pairs = [(ref.at[layer], out) for ref, out in zip(ins[len(parts) :], outs[len(parts) :])]
        for ref, own, width, (_, groups, first) in zip(ins, outs, widths, parts):
            for i in range(groups or 1):
                to = own.at[tile(p, rows), i * width : (i + 1) * width]
                cols = tile(i * n_p + p, width) if groups else slice(0, width)
                pairs.append((ref.at[layer, :, cols], to))
            cols = slice(first, first + (groups or 1) * width)
            for j in range(1, n_p):
                here = slice((j - 1) * half_rows, j * half_rows)
                at = (p ^ j) * 2
                pairs.append((mine_ref.at[here, cols], own.at[tile(at + half, half_rows)]))
                pairs.append((their_ref.at[here, cols], own.at[tile(at + 1 - half, half_rows)]))
        for copy in copy_all(pairs, sems):
            copy.wait()

    outs = [((n_p * rows, (g or 1) * width), BF) for (_, g, _), width in zip(parts, widths)]
    outs += [(w.shape[1:], BF) for w in more]
    ins = [mine, theirs, *[w for w, _, _ in parts], *more]
    specs = [IN_ANY] * 2 + [IN_HBM] * (len(parts) + len(more))
    scratch = [pltpu.SemaphoreType.DMA((count,))]
    return run("stack_rows", body, outs, ins, net.place, scratch, ins_at=specs)


def pack_tokens(tokens, scene_ids, token_kind):
    half = tokens.shape[1] // 2
    code = (scene_ids * 2 + token_kind).astype(BF)
    code = jnp.pad(code, ((half, 15), (0, D - 2 * half)))
    return tokens[0, :half], jnp.pad(tokens[0, half:], ((0, 16), (0, 0))) + code


def pack_small(vectors):
    sizes = [v.shape[1] for v in vectors]
    total = None
    for k, v in enumerate(vectors):
        at = sum(sizes[:k])
        put = jnp.pad(v, ((0, 0), (at, sum(sizes) - at - sizes[k])))
        total = put if total is None else total + put
    return total


def put_small(first, second, own, other):
    mid = first.shape[0]
    rows = 2 * mid
    width = own.shape[1] // 2

    def body(first_ref, second_ref, own_ref, other_ref, out, lines):
        out[0:mid, :] = first_ref[...]
        out[mid:rows, :] = second_ref[0:mid, :]
        lines[...] = second_ref[mid:, :].astype(F32)
        row = 1
        for ref in (own_ref, other_ref):
            low = ref[...].astype(F32)
            for layer in range(own.shape[0]):
                for half in range(2):
                    lines[row : row + 1, 0:width] = low[layer : layer + 1, half * width : (half + 1) * width]
                    row += 1
        out[rows:, :] = lines[...].astype(BF)

    scratch = [pltpu.VMEM((16, D), F32)]
    outs = [((rows + 16, D), BF)]
    return run("put_small", body, outs, [first, second, own, other], None, scratch)[0]


def join_vectors(net, layers, blocks, sizes, rows):
    n_p = net.n_p
    width = sum(sizes) // 2
    starts = [sum(sizes[:i]) for i in range(len(sizes))]

    def body(place, *refs):
        p, c = place[0], place[1]
        ins, outs = refs[:n_p], refs[n_p:]
        for j in range(n_p):
            low = ins[j][rows : rows + 16, 0:width].astype(F32)
            for layer in range(layers):
                for half in range(2):
                    row = 1 + layer * 2 + half
                    own = low[row : row + 1, :]
                    other = low[2 * layers + row : 2 * layers + row + 1, :]
                    first = jnp.where(c == 0, own, other)
                    second = jnp.where(c == 0, other, own)
                    for k, (at, size) in enumerate(zip(starts, sizes)):
                        if at // width != half:
                            continue
                        cols = slice(at - half * width, at - half * width + size)
                        both = jnp.concatenate([first[:, cols], second[:, cols]], axis=1)
                        outs[k][layer : layer + 1, tile(p ^ j, 2 * size)] = both

    outs = [((layers, 2 * n_p * size), F32) for size in sizes]
    return run("join_vectors", body, outs, blocks, net.place)


def norm_rows(hidden):
    centred = hidden - jnp.mean(hidden, axis=-1, keepdims=True)
    spread = jnp.mean(centred * centred, axis=-1, keepdims=True)
    inverse = lax.rsqrt(spread + EPS)
    return centred * inverse, inverse


def close_layer(net, layer, hidden, parts, bias):
    rows = parts[0].shape[0]
    count = len(parts)

    def body(hidden_ref, bias_ref, *refs):
        total = hidden_ref[...] + bias_ref[layer : layer + 1, :]
        for part in refs[:count]:
            total = total + part[...].astype(F32)
        refs[count][...] = total
        refs[count + 1][...] = total.astype(BF)

    outs = [((rows, D), F32), ((rows, D), BF)]
    return run("close_layer", body, outs, [hidden, bias, *parts])


def close_attention(net, layer, hidden, blocks, pieces, proj, bias, gain, shift):
    n_p = net.n_p
    tokens, cw = pieces[0].shape
    rows = tokens // n_p
    half = cw // 2

    def body(place, *refs):
        hiddens, os = refs[:n_p], refs[n_p : 2 * n_p]
        p_own, p_other, bias_ref, gain_ref, shift_ref, out, low, acc, o = refs[2 * n_p :]
        p, c = place[0], place[1]
        aligned = half % LANES == 0
        for j in range(n_p):
            for i in range(n_p):
                there, here = slice(i * rows, (i + 1) * rows), slice((i ^ j) * rows, ((i ^ j) + 1) * rows)
                first, second = os[j][there, :half], os[j][there, half:]
                own, other = jnp.where(c == 0, first, second), jnp.where(c == 0, second, first)
                if aligned:
                    o[here, tile(p ^ j, half)] = own
                    o[here, tile(n_p + (p ^ j), half)] = other
                    continue
                part = dot(own, p_own[tile(p ^ j, half), :]) + dot(other, p_other[tile(p ^ j, half), :])
                if j == 0:
                    acc[here, :] = part
                else:
                    acc[here, :] += part
        if aligned:
            acc[...] = dot(o[:, : D // 2], p_own[...]) + dot(o[:, D // 2 :], p_other[...])
        line = slice(layer, layer + 1)
        for j in range(n_p):
            here = slice(j * rows, (j + 1) * rows)
            total = acc[here, :] + hiddens[j][0:rows, :].astype(F32) + bias_ref[line, :]
            if j == 0:
                out[...] = total
            normed, _ = norm_rows(total)
            own, other = own_first(normed * gain_ref[line, :] + shift_ref[line, :], n_p, c)
            low[here, : D // 2] = own.astype(BF)
            low[here, D // 2 :] = other.astype(BF)

    outs = [((rows, D), F32), ((tokens, D), BF)]
    scratch = [pltpu.VMEM((tokens, D), F32), pltpu.VMEM((tokens, D), BF)]
    ins = [hidden, *blocks[1:], *pieces, *proj, bias, gain, shift]
    return run("close_attention", body, outs, ins, net.place, scratch, flops=2 * tokens * D * D)


def norm_back(net, layer, grad, hidden, parts, gain):
    rows = parts[0].shape[0]
    count = len(parts)

    def body(place, grad_ref, hidden_ref, gain_ref, *refs):
        total = refs[0][...].astype(F32)
        for part in refs[1:count]:
            total = total + part[...].astype(F32)
        total = model_order(total, net.n_p, place[1])
        out, low, sums = refs[count:]
        normed, inverse = norm_rows(hidden_ref[0:rows, :].astype(F32))
        scaled = total * gain_ref[layer : layer + 1, :]
        one = jnp.mean(scaled, axis=-1, keepdims=True)
        two = jnp.mean(scaled * normed, axis=-1, keepdims=True)
        result = grad_ref[...].astype(F32) + inverse * (scaled - one - normed * two)
        rounded = result.astype(BF)
        out[...] = result
        low[...] = rounded
        sums[0:1, :] = jnp.sum(total * normed, axis=0, keepdims=True)
        sums[1:2, :] = jnp.sum(total, axis=0, keepdims=True)
        sums[2:3, :] = jnp.sum(rounded.astype(F32), axis=0, keepdims=True)

    outs = [((rows, D), F32), ((rows, D), BF), ((3, D), F32)]
    return run("norm_back", body, outs, [grad, hidden, gain, *parts], net.place)


def column_sums(v):
    def body(ref, out):
        out[...] = jnp.sum(ref[...].astype(F32), axis=0, keepdims=True)

    return run("column_sums", body, [((1, v.shape[1]), F32)], [v])[0]


def gather_rows(blocks, scratch):
    rows = scratch.shape[0] // len(blocks)
    for j, ref in enumerate(blocks):
        scratch[j * rows : (j + 1) * rows, :] = ref[0:rows, :]


def allowed_pairs(code_col, code_row):
    same = (code_col >> 1) == (code_row >> 1)
    return same & (((code_col & 1) == 0) | ((code_row & 1) == 1))


def head_lanes(shape, head, axis):
    lane = lax.broadcasted_iota(jnp.int32, shape, axis)
    return (lane < HEAD_DIM) if head == 0 else (lane >= HEAD_DIM)


def keep_head(v, head, axis):
    return jnp.where(head_lanes(v.shape, head, axis), v, jnp.zeros_like(v))


def probs_by_key(k2, q2, allowed, head):
    scores = jnp.where(allowed, dot_nt(keep_head(k2, head, 1), q2), NEG)
    powers = jnp.exp(scores - jnp.max(scores, axis=0, keepdims=True))
    return powers * (1.0 / jnp.sum(powers, axis=0, keepdims=True))


Q_TILE = 256


def attend(net, layer, rows, blocks, gain, shift, weight, bias, codes):
    n_p = net.n_p
    tokens = n_p * rows
    cw = D // n_p
    n_c = 0 if codes is None else 2

    def body(place, *refs):
        bias_ref, w_own, w_other, gain_ref, shift_ref, row_ref, col_ref = refs[n_p : n_p + 7]
        a, qkv, attended, vt = refs[n_p + 7 :]
        p, c = place[0], place[1]
        eye = lax.broadcasted_iota(jnp.int32, (rows, rows), 0) == lax.broadcasted_iota(
            jnp.int32, (rows, rows), 1
        )
        line = slice(layer, layer + 1)
        for j in range(n_p):
            here = slice(j * rows, (j + 1) * rows)
            if codes is None:
                code = refs[j][rows : rows + 1, 0:rows].astype(F32)
                row_ref[:, here] = code.astype(jnp.int32)
                column = jnp.sum(jnp.where(eye, code, 0.0), axis=1, keepdims=True)
                col_ref[here, :] = column.astype(jnp.int32)
            normed, _ = norm_rows(refs[j][0:rows, :].astype(F32))
            own, other = own_first(normed * gain_ref[line, :] + shift_ref[line, :], n_p, c)
            a[here, : D // 2] = own.astype(BF)
            a[here, D // 2 :] = other.astype(BF)
        for i in range(3):
            cols = slice(i * cw, (i + 1) * cw)
            out = dot(a[:, : D // 2], w_own[:, cols]) + dot(a[:, D // 2 :], w_other[:, cols])
            if i == 0:
                out = out + bias_ref[line, tile(p, cw)]
            if i == 2:
                out = out + bias_ref[line, tile(p + n_p, cw)]
            qkv[:, cols] = out.astype(BF)
        vt[...] = jnp.transpose(qkv[:, 2 * cw : 3 * cw].astype(F32)).astype(BF)

        @pl.loop(0, tokens // Q_TILE)
        def _(t):
            here = tile(t, Q_TILE)
            allowed = allowed_pairs(col_ref[...], row_ref[:, here])
            for pair in range(cw // LANES):
                lanes = slice(pair * LANES, (pair + 1) * LANES)
                q2 = qkv[here, lanes]
                k2 = qkv[:, cw + pair * LANES : cw + (pair + 1) * LANES]
                total = None
                for head in range(2):
                    probs = probs_by_key(k2, q2 * BF(SCALE), allowed, head).astype(BF)
                    part = dot(keep_head(vt[lanes, :], head, 0), probs)
                    total = part if total is None else total + part
                attended[here, lanes] = jnp.transpose(total).astype(BF)

    outs = [((tokens, D), BF), ((tokens, 3 * cw), BF), ((tokens, cw), BF)]
    if codes is None:
        outs = [((1, tokens), jnp.int32), ((tokens, 1), jnp.int32)] + outs
    ins = [*blocks, bias, *weight, gain, shift] + list(codes or [])
    scratch = [pltpu.VMEM((cw, tokens), BF)]
    got = run("attend", body, outs, ins, net.place, scratch, flops=2 * tokens * D * 3 * cw)
    if codes is None:
        codes, got = got[:2], got[2:]
    return (*got, codes)


def attend_back(net, blocks, proj, qkv, codes, weight, tokens_in):
    n_p = net.n_p
    rows = blocks[0].shape[0]
    tokens = n_p * rows
    cw = D // n_p
    n_t = len(tokens_in)

    def body(place, *refs):
        p_own, p_other, qkv_ref, row_ref, col_ref, w_own, w_other = refs[n_p : n_p + 7]
        token_refs = refs[n_p + 7 : n_p + 7 + n_t]
        refs_out = refs[n_p + 7 + n_t :]
        outs = refs_out[:n_p]
        dqkv, sums, norm_sums, do, kt, dk, dv = refs_out[n_p:]
        c = place[1]
        mine = tile(place[0], cw // 2)
        for j in range(n_p):
            here = slice(j * rows, (j + 1) * rows)
            own, other = dot_nt(refs[j][...], p_own[mine, :]), dot_nt(refs[j][...], p_other[mine, :])
            do[here, : cw // 2] = jnp.where(c == 0, own, other).astype(BF)
            do[here, cw // 2 :] = jnp.where(c == 0, other, own).astype(BF)
        kt[...] = jnp.transpose(qkv_ref[:, cw : 2 * cw].astype(F32)).astype(BF)
        dk[...] = jnp.zeros_like(dk)
        dv[...] = jnp.zeros_like(dv)

        @pl.loop(0, tokens // Q_TILE)
        def _(t):
            here = tile(t, Q_TILE)
            allowed = allowed_pairs(col_ref[...], row_ref[:, here])
            for pair in range(cw // LANES):
                lanes = slice(pair * LANES, (pair + 1) * LANES)
                q2 = qkv_ref[here, lanes]
                k2 = qkv_ref[:, cw + pair * LANES : cw + (pair + 1) * LANES]
                v2 = qkv_ref[:, 2 * cw + pair * LANES : 2 * cw + (pair + 1) * LANES]
                do2 = do[here, lanes]
                total = None
                for head in range(2):
                    probs = probs_by_key(k2, q2 * BF(SCALE), allowed, head)
                    dp = dot_nt(keep_head(v2, head, 1), do2)
                    mean = jnp.sum(probs * dp, axis=0, keepdims=True)
                    ds = (probs * (dp - mean)).astype(BF)
                    dv[:, lanes] += dot(probs.astype(BF), keep_head(do2, head, 1))
                    dk[:, lanes] += dot(ds, keep_head(q2, head, 1))
                    part = dot(keep_head(kt[lanes, :], head, 0), ds)
                    total = part if total is None else total + part
                dqkv[here, lanes] = (jnp.transpose(total) * SCALE).astype(BF)

        dqkv[:, cw : 2 * cw] = (dk[...] * SCALE).astype(BF)
        dqkv[:, 2 * cw :] = dv[...].astype(BF)
        sums[...] = jnp.sum(dqkv[...].astype(F32), axis=0, keepdims=True)
        norm_sums[...] = jnp.zeros_like(norm_sums)
        for j in range(n_p):
            normed = None
            if n_t:
                normed = own_first(norm_rows(token_refs[j][0:rows, :].astype(F32))[0], n_p, c)
            for k, w in enumerate((w_own, w_other)):
                cols = slice(k * (D // 2), (k + 1) * (D // 2))
                da1 = dot_nt(dqkv[j * rows : (j + 1) * rows, :], w[...])
                outs[j][:, cols] = da1.astype(BF)
                if n_t:
                    norm_sums[0:1, cols] += jnp.sum(da1 * normed[k], axis=0, keepdims=True)
                    norm_sums[1:2, cols] += jnp.sum(da1, axis=0, keepdims=True)

    outs = [((rows, D), BF)] * n_p + [((tokens, 3 * cw), BF), ((1, 3 * cw), F32), ((2, D), F32)]
    scratch = [
        pltpu.VMEM((tokens, cw), BF),
        pltpu.VMEM((cw, tokens), BF),
        pltpu.VMEM((tokens, cw), F32),
        pltpu.VMEM((tokens, cw), F32),
    ]
    ins = [*blocks, *proj, qkv, *codes, *weight, *tokens_in]
    got = run("attend_back", body, outs, ins, net.place, scratch, flops=2 * tokens * D * 8 * cw)
    return got[:n_p], got[n_p], got[n_p + 1], got[n_p + 2]


F_TILE = 256


def feed_forward(net, layer, a2, up, bias, down):
    n_p = net.n_p
    tokens = a2.shape[0]
    rows = tokens // n_p
    fw = FF // n_p

    def body(place, a_ref, up_own, up_other, bias_ref, d_own, d_other, *refs):
        outs, z_ref, slope_ref = refs[:n_p], refs[n_p], refs[n_p + 1]
        p, c = place[0], place[1]

        @pl.loop(0, fw // F_TILE)
        def _(t):
            cols = tile(t, F_TILE)
            there = pl.ds(pl.multiple_of(p * fw + t * F_TILE, F_TILE), F_TILE)
            u = dot(a_ref[:, : D // 2], up_own[:, cols]) + dot(a_ref[:, D // 2 :], up_other[:, cols])
            u = u + bias_ref[layer : layer + 1, there]
            phi = 0.5 * (1.0 + lax.erf(u * 0.7071067811865476))
            z_ref[:, cols] = (u * phi).astype(BF)
            slope_ref[:, cols] = phi + u * (jnp.exp(-0.5 * u * u) * 0.3989422804014327)

        for j in range(n_p):
            here = slice(j * rows, (j + 1) * rows)
            own, other = z_ref[here, tile(c, fw // 2)], z_ref[here, tile(1 - c, fw // 2)]
            outs[j][...] = (dot(own, d_own[...]) + dot(other, d_other[...])).astype(BF)

    outs = [((rows, D), BF)] * n_p + [((tokens, fw), BF), ((tokens, fw), F32)]
    ins = [a2, *up, bias, *down]
    got = run("feed_forward", body, outs, ins, net.place, flops=4 * tokens * D * fw)
    return got[:n_p], got[n_p], got[n_p + 1]


def feed_back(net, blocks, down, slope, up):
    n_p = net.n_p
    rows = blocks[0].shape[0]
    tokens = n_p * rows
    fw = FF // n_p

    def body(place, *refs):
        d_own, d_other, slope_ref, up_own, up_other = refs[n_p : n_p + 5]
        outs = refs[n_p + 5 : 2 * n_p + 5]
        du_ref, sums, dm = refs[2 * n_p + 5 :]
        c = place[1]
        gather_rows(refs[:n_p], dm)
        for w, core in ((d_own, c), (d_other, 1 - c)):

            @pl.loop(0, fw // (2 * F_TILE))
            def _(t):
                start = core * (fw // 2) + t * F_TILE
                cols = pl.ds(pl.multiple_of(start, F_TILE), F_TILE)
                dz = dot_nt(dm[...], w[tile(t, F_TILE), :])
                du = (dz * slope_ref[:, cols]).astype(BF)
                du_ref[:, cols] = du
                sums[:, cols] = jnp.sum(du.astype(F32), axis=0, keepdims=True)

        for j in range(n_p):
            du = du_ref[j * rows : (j + 1) * rows, :]
            outs[j][:, : D // 2] = dot_nt(du, up_own[...]).astype(BF)
            outs[j][:, D // 2 :] = dot_nt(du, up_other[...]).astype(BF)

    outs = [((rows, D), BF)] * n_p + [((tokens, fw), BF), ((1, fw), F32)]
    scratch = [pltpu.VMEM((tokens, D), BF)]
    ins = [*blocks, *down, slope, *up]
    got = run("feed_back", body, outs, ins, net.place, scratch, flops=4 * tokens * D * fw)
    return got[:n_p], got[n_p], got[n_p + 1]


def down_weight_grad(net, z, dm):
    n_r = len(dm)
    tokens, m = z.shape
    half = m // 2

    def body(place, z_ref, *refs):
        keep, send, b = refs[n_r:]
        c = place[1]
        gather_rows(refs[:n_r], b)
        keep[...] = dot_tn(z_ref[:, tile(c, half)], b[...]).astype(BF)
        send[...] = dot_tn(z_ref[:, tile(1 - c, half)], b[...]).astype(BF)

    outs = [((half, D), BF)] * 2
    scratch = [pltpu.VMEM((tokens, D), BF)]
    return run("down_weight_grad", body, outs, [z, *dm], net.place, scratch, flops=2 * tokens * m * D)


def up_weight_grad(net, a2, du):
    n_l = len(a2)
    tokens, n = du.shape

    def body(place, *refs):
        du_ref, out, a = refs[n_l:]
        c = place[1]
        gather_rows(refs[:n_l], a)
        out[c] = dot_tn(a[:, : D // 2], du_ref[...]).astype(BF)
        out[1 - c] = dot_tn(a[:, D // 2 :], du_ref[...]).astype(BF)

    scratch = [pltpu.VMEM((tokens, D), BF)]
    outs = [((2, D // 2, n), BF)]
    return run("up_weight_grad", body, outs, [*a2, du], net.place, scratch, flops=2 * tokens * D * n)[0]


def attend_weight_grad(net, a1, dqkv, attended, dy, small):
    n_p = net.n_p
    n_a = len(a1)
    tokens, width = dqkv.shape
    cw = D // n_p
    rows = D // net.n_f
    lines_each = 2 * len(small[1]) if small else 0
    extra = n_p * lines_each
    flat = [v for of_layer in small[1] for v in of_layer] if small else []
    sizes = small[0] if small else []
    starts = [sum(sizes[:i]) for i in range(len(sizes))]

    def put_small(place, refs, low):
        p, c = place[0], place[1]
        low[...] = jnp.zeros_like(low)
        for k, (ref, (_, kind)) in enumerate(zip(refs, flat)):
            layer, which = divmod(k, len(sizes))
            at, size = starts[which], sizes[which]
            half = at // width
            row = slice(2 * layer + half, 2 * layer + half + 1)
            cols = slice(at - half * width, at - half * width + size)
            if kind == "chip":
                low[0, p, row, cols] = ref[:, :size]
                low[1, p, row, cols] = ref[:, size:]
            elif kind == "heads":
                low[p % 2, p // 2, row, cols] = ref[:, :size]
                low[p % 2, p // 2 + n_p // 2, row, cols] = ref[:, 2 * size :]
            elif kind == "own":
                for i in range(n_p):
                    low[c, i, row, cols] = ref[:, i * size : (i + 1) * size]
                    low[1 - c, i, row, cols] = ref[:, D // 2 + i * size : D // 2 + (i + 1) * size]
            else:
                for i in range(n_p):
                    for core in range(2):
                        to = (2 * i + core) * size
                        low[core, i, row, cols] = ref[:, to : to + size]

    def body(place, *refs):
        dqkv_ref, attended_ref = refs[n_a : n_a + 2]
        smalls = refs[n_a + 2 + n_p : n_a + 2 + n_p + len(flat)]
        out, a, b, low, lines, under = refs[n_a + 2 + n_p + len(flat) :]
        c = place[1]
        gather_rows(refs[:n_a], a)
        for k, core in ((0, c), (1, 1 - c)):
            both = dot_tn(a[:, k * (D // 2) : (k + 1) * (D // 2)], dqkv_ref[...]).astype(BF)
            for i in range(n_p):
                out[core, i * rows : (i + 1) * rows, :width] = both[i * rows : (i + 1) * rows]
        gather_rows(refs[n_a + 2 : n_a + 2 + n_p], b)
        low[...] = dot_tn(attended_ref[...], b[...]).astype(BF)
        for core in range(2):
            for i in range(n_p):
                here = slice(i * rows, (i + 1) * rows)
                out[core, here, width:] = low[core * rows : (core + 1) * rows, i * cw : (i + 1) * cw]
        if extra:
            put_small(place, smalls, lines)
            for core in range(2):
                for i in range(n_p):
                    for r in range(lines_each):
                        under[i * lines_each + r : i * lines_each + r + 1, :] = lines[core, i, r : r + 1, :]
                out[core, n_p * rows :, :width] = under[...].astype(BF)
                out[core, n_p * rows :, width:] = jnp.zeros((extra, cw), BF)

    outs = [((2, n_p * rows + extra, width + cw), BF)]
    scratch = [pltpu.VMEM((tokens, D), BF), pltpu.VMEM((tokens, D), BF), pltpu.VMEM((cw, D), BF)]
    scratch += [pltpu.VMEM((2, n_p, 8, width), F32), pltpu.VMEM((max(extra, 8), width), F32)]
    flops = 2 * tokens * D * (width + cw)
    ins = [*a1, dqkv, attended, *dy, *[v for v, _ in flat]]
    return run("attend_weight_grad", body, outs, ins, net.place, scratch, flops=flops)[0]


def add_halves(a, b):
    rows, width = a.shape
    half = width // 2

    def body(a_ref, b_ref, *outs):
        for k in range(2):
            cols = slice(k * half, (k + 1) * half)
            outs[k][...] = (a_ref[:, cols].astype(F32) + b_ref[:, cols].astype(F32)).astype(BF)

    return run("add_halves", body, [((rows, half), BF)] * 2, [a, b])


def add_pair(both):
    _, rows, width = both.shape
    half = width // 2

    def body(ref, *outs):
        for k in range(2):
            cols = slice(k * half, (k + 1) * half)
            outs[k][...] = (ref[0, :, cols].astype(F32) + ref[1, :, cols].astype(F32)).astype(BF)

    return run("add_pair", body, [((rows, half), BF)] * 2, [both])


def cut_rows(net, first, second, extra):
    n_p = net.n_p
    split = extra is not None
    under = extra or 0
    rows = (first.shape[0] - under) // n_p
    width, more = first.shape[1], second.shape[1]
    taken = more // 2 if split else more

    def body(place, a, b, *outs):
        p = place[0]
        for j in range(n_p):
            here = tile(p ^ j, rows)
            outs[j][0:rows, :width] = a[here, :]
            outs[j][0:rows, width:] = b[here, :taken]
            for k in range(3 if under else 0):
                at = slice(rows + k * under, rows + (k + 1) * under)
                outs[j][at, :width] = a[n_p * rows :, :]
                outs[j][at, width:] = b[n_p * rows :, :taken]
        if split:
            for i in range(n_p):
                outs[n_p][:, i * taken : (i + 1) * taken] = b[i * rows : (i + 1) * rows, taken:]

    outs = [((rows + 3 * under, width + taken), BF)] * n_p
    if split:
        outs.append(((rows, n_p * taken), BF))
    return run("cut_rows", body, outs, [first, second], net.place)


def sum_small(net, layers, pieces, sizes, rows):
    width = pieces[0].shape[1]
    starts = [sum(sizes[:i]) for i in range(len(sizes))]
    lines = 2 * layers * net.n_p
    block = (lines, rows // lines) if rows % lines == 0 and lines % 16 == 0 else (pieces[0].shape[0], 0)
    first = 0 if block[1] else rows

    def body(place, *refs):
        here = slice(first, first + lines)
        every = refs[0][here, :].astype(F32)
        for ref in refs[1 : len(pieces)]:
            every = every + ref[here, :].astype(F32)
        total = jnp.zeros((2 * layers, width), F32)
        for i in range(net.n_p):
            total = jnp.where(place[0] == i, every[i * 2 * layers : (i + 1) * 2 * layers], total)
        for out, at, size in zip(refs[len(pieces) :], starts, sizes):
            half = at // width
            for layer in range(layers):
                row = 2 * layer + half
                out[layer : layer + 1, :] = total[row : row + 1, at - half * width : at - half * width + size]

    return pl.pallas_call(
        body,
        grid=(1,),
        out_shape=[jax.ShapeDtypeStruct((layers, size), F32) for size in sizes],
        in_specs=[IN_SMEM] + [pl.BlockSpec((block[0], width), lambda i: (block[1], 0))] * len(pieces),
        out_specs=[pl.BlockSpec((layers, size), lambda i: (0, 0)) for size in sizes],
        compiler_params=pltpu.CompilerParams(vmem_limit_bytes=16 << 20),
        name="sum_small",
    )(net.place, *pieces)


def widen(net, values):
    def body(place, *refs):
        for ref, out in zip(refs, refs[len(values) :]):
            out[...] = ref[...].astype(F32)

    return run("widen", body, [(v.shape, F32) for v in values], values, net.place)


def take_if(here, a, b, rows):
    def body(flag, a_ref, b_ref, out):
        @pl.when(flag[0] != 0)
        def _():
            count = min(rows, a.shape[0])
            out[0:count, :] = a_ref[0:count, :]

        @pl.when(flag[0] == 0)
        def _():
            count = min(rows, b.shape[0])
            out[0:count, :] = b_ref[0:count, :]

    return run("take_if", body, [((rows, a.shape[1]), BF)], [a, b], here.astype(jnp.int32).reshape(1))[0]


def turn(net, wanted):
    flat, flags, outs = [], [], []
    for one, two, outer in wanted:
        flat += one + (two or [])
        rows = max(one[0].shape[0], two[0].shape[0] if two else 0)
        outs.append(((rows, one[0].shape[1]), BF))
        flags.append(jnp.zeros((), jnp.int32) if outer is None else outer.astype(jnp.int32))

    def put(refs, out):
        rows = refs[0].shape[0]
        if len(refs) == 1:
            out[0:rows, :] = refs[0][...]
            return
        total = refs[0][...].astype(F32)
        for ref in refs[1:]:
            total = total + ref[0:rows, :].astype(F32)
        out[0:rows, :] = total.astype(BF)

    def body(flag, *refs):
        at = 0
        for k, (one, two, outer) in enumerate(wanted):
            out = refs[len(flat) + k]
            first = refs[at : at + len(one)]
            at += len(one)
            if outer is None:
                put(first, out)
                continue
            second = refs[at : at + len(two)]
            at += len(two)
            pl.when(flag[k] != 0)(lambda first=first, out=out: put(first, out))
            pl.when(flag[k] == 0)(lambda second=second, out=out: put(second, out))

    return run("turn", body, outs, flat, jnp.stack(flags))


class Chunk:
    def __init__(self, value):
        self.terms = [value]
        self.step = 0

    @property
    def value(self):
        return self.terms[0]


class Flow:
    def __init__(self, net):
        self.net = net
        self.queue = []
        self.moving = []

    def first(self, step):
        for chunk in self.queue:
            if chunk.step == step:
                return chunk
        return None

    def start(self):
        net = self.net
        n = net.n_s
        half = n // 2
        moves, wanted = [], []
        for k in range(half):
            inward = self.first(k)
            outward = None if k == half - 1 else self.first(n - 2 - k)
            into = [(k, k + 1), (n - 1 - k, n - 2 - k)]
            out = [(k + 1, k), (n - 2 - k, n - 1 - k)]
            outer = (net.s == k) | (net.s == n - 1 - k)
            both = inward is not None and outward is not None
            if both and inward.value.shape[1] == outward.value.shape[1]:
                moves.append((inward, outward, outer, into + out))
                wanted.append((inward.terms, outward.terms, outer))
                continue
            if inward is not None:
                moves.append((inward, None, outer, into))
                wanted.append((inward.terms, None, None))
            if outward is not None:
                moves.append((None, outward, outer, out))
                wanted.append((outward.terms, None, None))
        sent = [w[0][0] for w in wanted]
        work = [k for k, w in enumerate(wanted) if len(w[0]) > 1 or w[1] is not None]
        if work:
            for k, value in zip(work, turn(net, [wanted[k] for k in work])):
                sent[k] = value
        self.moving = [(*m[:3], v, lax.ppermute(v, "seq", m[3])) for m, v in zip(moves, sent)]

    def collect(self, values, *new):
        values, news, got = fence((values, [c.value for c in new], [(m[3], m[4]) for m in self.moving]))
        for c, value in zip(new, news):
            c.terms = [value]
        n = self.net.n_s
        for (inward, outward, outer, _, _), (sent, arrived) in zip(self.moving, got):
            if inward is not None:
                middle = inward.step == n // 2 - 1
                inward.terms = [sent, arrived] if middle else [*inward.terms, arrived]
                inward.step += 1
            if outward is not None:
                outward.terms = [take_if(outer, arrived, sent, outward.value.shape[0])]
                outward.step += 1
        self.queue = [c for c in self.queue if c.step < n - 1] + list(new)
        self.start()
        return values


def write_layer(net, layer, layers, before, attention, feed):
    n_p = net.n_p
    cw, fw = D // n_p, FF // n_p
    proj, qkv = attention or (None, [])
    up, down = feed or ([], [])
    rows = (up[0] if feed else proj).shape[0]
    split = len(qkv) > 0 and isinstance(qkv[0], tuple)
    flat = [v for pair in qkv for v in pair] if split else list(qkv)
    steps = min(4, rows // 16)
    which = [0, 1] * (attention is not None) + [2, 3] * (feed is not None)
    ins = [proj] * (attention is not None) + [*flat, *up, *down]
    n_in = len(ins)
    skip = 0 if before is None else len(which)

    def body(place, *refs):
        p = place[0]
        outs = refs[n_in + skip :]
        taken = 0
        if attention is not None:
            qkvs = refs[1 : 1 + len(flat)]
            taken = 1 + len(flat)
            qkv_out, proj_out, *outs = outs
            proj_out[0] = refs[0][...].astype(F32)
            for j in range(n_p):
                for i in range(3):
                    to = tile(i * n_p + (p ^ j), cw)
                    ref, at = (qkvs[2 * j + i // 2], i % 2) if split else (qkvs[j], i)
                    qkv_out[0, :, to] = ref[:, at * cw : (at + 1) * cw].astype(F32)
        if feed is not None:
            ups, downs = refs[taken : taken + n_p], refs[taken + n_p : n_in]
            up_out, down_out = outs
            for k in range(2):
                down_out[0, :, k * (D // 2) : (k + 1) * (D // 2)] = downs[k][...].astype(F32)
            for j in range(n_p):
                up_out[0, :, tile(p ^ j, fw)] = ups[j][...].astype(F32)

    down_rows = down[0].shape[0] if feed else 0
    all_shapes = [(rows, 3 * D), (rows, D), (rows, FF), (down_rows, D)]
    shapes = [all_shapes[k] for k in which]
    specs = [IN_SMEM] + [pl.BlockSpec((rows // steps, v.shape[1]), lambda i: (i, 0)) for v in ins[: n_in - len(down)]]
    specs += [pl.BlockSpec((down_rows // steps, v.shape[1]), lambda i: (i, 0)) for v in down]
    aliases = {}
    if before is not None:
        aliases = {1 + n_in + k: k for k in range(skip)}
        specs += [IN_ANY] * skip
        ins = ins + [before[k] for k in which]
    moved = 6 * sum(a * b for a, b in shapes)
    new = pl.pallas_call(
        body,
        grid=(steps,),
        out_shape=[jax.ShapeDtypeStruct((layers, *shape), F32) for shape in shapes],
        in_specs=specs,
        out_specs=[pl.BlockSpec((1, shape[0] // steps, shape[1]), lambda i: (layer, i, 0)) for shape in shapes],
        input_output_aliases=aliases,
        compiler_params=pltpu.CompilerParams(vmem_limit_bytes=16 << 20),
        cost_estimate=pl.CostEstimate(flops=0, bytes_accessed=moved, transcendentals=0),
        name="write_layer",
    )(net.place, *ins)
    out = [None] * 4 if before is None else list(before)
    for k, v in zip(which, new):
        out[k] = v
    return out


def on_device(
    tokens,
    scene_ids,
    token_kind,
    out_grad,
    first_gain,
    first_shift,
    qkv_weight,
    qv_bias,
    proj_weight,
    proj_bias,
    second_gain,
    second_shift,
    up_weight,
    up_bias,
    down_weight,
    down_bias,
):
    net = Net()
    n_p = net.n_p
    layers = qkv_weight.shape[0]
    rows = tokens.shape[1]
    pair_groups = [[2 * i, 2 * i + 1] for i in range(n_p)]

    def fetch(layer, *weights):
        pieces = cut_columns(net, layer, weights)
        return stack_halves([net.chip(v, j) for j, v in enumerate(pieces, 1)])

    def complete(mine, theirs, parts, more, layer):
        own = stack_rows(net, mine, theirs, parts, more, layer)
        return [(v, net.core(v)) for v in own]

    def swap_cores(both):
        return lax.all_to_all(both, "fsdp", 0, 0, axis_index_groups=pair_groups)

    small_in = [first_gain, first_shift, qv_bias, proj_bias, second_gain, second_shift, up_bias, down_bias]
    sizes = [v.shape[1] for v in small_in]
    tok, tok_rest = pack_tokens(tokens, scene_ids, token_kind)
    tok, tok_rest = net.to_plane(net.to_chip(tok)), net.to_place(tok_rest)
    mine = fetch(0, (qkv_weight, 3), (proj_weight, None))
    small = pack_small(small_in)
    small_other = net.core(small)
    later = (qkv_weight, proj_weight, up_weight, down_weight, out_grad)
    tok, tok_rest, mine, small, small_other, later = fence((tok, tok_rest, mine, small, small_other, later))
    qkv_weight, proj_weight, up_weight, down_weight, out_grad = later
    tokg = net.gather(put_small(tok, tok_rest, small, small_other))
    theirs = net.next_plane(mine)
    tokg, mine, theirs = fence((tokg, mine, theirs))

    weights = []
    kept = []
    dm = None
    codes = None
    qkv_cols = 3 * D // n_p
    for layer in range(layers):
        last = layer == layers - 1
        blocks = tokg if layer == 0 else net.gather(low)
        parts = [(qkv_weight, 3, 0), (proj_weight, None, qkv_cols)]
        qkv_w, proj_w = complete(mine, theirs, parts, [], layer)
        blocks, qkv_w, proj_w, up_weight, out_grad = fence((blocks, qkv_w, proj_w, up_weight, out_grad))
        if layer == 0:
            tokg = blocks
            hidden = tokg[0]
            vectors = join_vectors(net, layers, tokg, sizes, rows)
            gain1, shift1, qv_b, proj_b, gain2, shift2, up_b, down_b = vectors
        a1g, qkv, og, codes = attend(net, layer, rows, blocks, gain1, shift1, qkv_w, qv_b, codes)
        mine = fetch(layer, (up_weight, 1))
        if last:
            dm = net.to_chip(out_grad[0])
        a1g, qkv, og, mine, dm, down_weight = fence((a1g, qkv, og, mine, dm, down_weight))
        pieces = net.gather(og)
        theirs = net.next_plane(mine)
        if last:
            dm = net.to_plane(dm)
        pieces, theirs, dm = fence((pieces, theirs, dm))
        up_w, down_w = complete(mine, theirs, [(up_weight, 1, 0)], [down_weight], layer)
        h2, a2g = close_attention(net, layer, hidden, blocks, pieces, proj_w, proj_b, gain2, shift2)
        a2g, up_w, down_w, qkv_weight, proj_weight = fence((a2g, up_w, down_w, qkv_weight, proj_weight))
        y, z, slope = feed_forward(net, layer, a2g, up_w, up_b, down_w)
        kept.append((hidden, [a1g], qkv, og, h2, [a2g], z, slope))
        weights.append((qkv_w, proj_w, up_w, down_w))
        if last:
            dmg = net.gather(dm)
            last_y, z, slope, dmg = fence((y, z, slope, dmg))
            break
        mine = fetch(layer + 1, (qkv_weight, 3), (proj_weight, None))
        y, mine = fence((y, mine))
        parts = net.exchange(y)
        theirs = net.next_plane(mine)
        parts, theirs = fence((parts, theirs))
        hidden, low = close_layer(net, layer, h2, parts, down_b)

    flow = Flow(net)
    small_grads = [None] * layers
    sums = [None] * layers
    out = None
    grad = dm
    down_b_grad = column_sums(dm)

    def chunks(halves):
        return [Chunk(v) for v in halves]

    for layer in reversed(range(layers)):
        last = layer == layers - 1
        qkv_w, proj_w, up_w, down_w = weights[layer]
        h1, a1g, qkv, og, h2, a2g, z, slope = kept[layer]
        keep, send = down_weight_grad(net, z, dmg)
        da2, du, up_b_grad = feed_back(net, dmg, down_w, slope, up_w)
        send = net.core(send)
        da2, du, keep, send = fence((da2, du, keep, send))
        down_g = chunks(add_halves(keep, send))
        da2 = flow.collect(da2, down_g[0])
        parts = net.exchange(da2)
        both = swap_cores(up_weight_grad(net, a2g, du))
        parts, both = flow.collect((parts, both), down_g[1])
        up_g = chunks(add_pair(both))
        dh2, dy, sums2 = norm_back(net, layer, grad, h2, parts, gain2)
        dyg = net.gather(dy)
        dyg = flow.collect(dyg, up_g[0])
        tokens_in = tokg if layer == 0 else []
        da1, dqkv, qkv_b_grad, norm_sums = attend_back(net, dyg, proj_w, qkv, codes, qkv_w, tokens_in)
        da1, dqkv = flow.collect((da1, dqkv), up_g[1])
        parts = net.exchange(da1)
        names = [None, None, "heads", None, None, None, "chip", None]
        of_layer = [None, None, qkv_b_grad, sums2[2:3], sums2[0:1], sums2[1:2], up_b_grad, down_b_grad]
        small = None
        if layer == 0:
            of_layer[0], of_layer[1] = norm_sums[0:1], norm_sums[1:2]
            names[0] = names[1] = "own"
            small_grads[layer] = list(zip(of_layer, names))
            small = (sizes, small_grads)
        both = swap_cores(attend_weight_grad(net, a1g, dqkv, og, dyg, small))
        parts, both = fence((parts, both))
        attend_g = chunks(add_pair(both))
        grad, dm, sums1 = norm_back(net, layer, dh2, h1, parts, gain1)
        sums[layer] = (down_g, up_g, attend_g)
        dm = flow.collect(dm, attend_g[0])
        if layer > 0:
            of_layer[0], of_layer[1] = sums1[0:1], sums1[1:2]
            small_grads[layer] = list(zip(of_layer, names))
            dmg = net.gather(dm)
            down_b_grad = sums1[2:3]
            dmg, grad = flow.collect((dmg, grad), attend_g[1])

    def to_owners(chunks, extra):
        *pieces, rest = [*cut_rows(net, *[c.value for c in chunks], extra), None][: n_p + 1]
        return net.exchange(pieces), rest

    last_parts = net.exchange(last_y)
    dm, last_parts = flow.collect((dm, last_parts), attend_g[1])
    _, sent_out = close_layer(net, layers - 1, kept[-1][4], last_parts, down_b)
    up_pieces, _ = to_owners(sums[1][1], None)
    dm, up_pieces = flow.collect((dm, up_pieces))
    qkv_pieces, proj_g = to_owners(sums[1][2], 0)
    dm, sent_out, qkv_pieces, proj_g = flow.collect((dm, sent_out, qkv_pieces, proj_g))
    while [c for c in flow.queue if c in sums[0][1]]:
        dm = flow.collect(dm)
    up_last, _ = to_owners(sums[0][1], None)
    dm, sent_out, up_last = flow.collect((dm, sent_out, up_last))
    while flow.queue:
        dm = flow.collect(dm)
    pieces, proj_last = to_owners(sums[0][2], 2 * layers * n_p)
    dm, sent_out = net.from_place(dm), net.from_place(sent_out)
    downs = [[c.value for c in sums[layer][0]] for layer in range(layers)]
    out = write_layer(net, 1, layers, None, (proj_g, qkv_pieces), (up_pieces, downs[1]))
    out = write_layer(net, 0, layers, out, None, (up_last, downs[0]))
    input_grad, sent_out = widen(net, [dm, sent_out])
    small_out = sum_small(net, layers, pieces, sizes, D // net.n_f)
    out = write_layer(net, 0, layers, out, (proj_last, pieces), None)
    return (
        sent_out[None],
        input_grad[None],
        small_out[0],
        small_out[1],
        out[0],
        small_out[2],
        out[1],
        small_out[3],
        small_out[4],
        small_out[5],
        out[2],
        small_out[6],
        out[3],
        small_out[7],
    )


def solution(mesh):
    tok = P("fsdp", "seq", None)
    lab = P("fsdp", "seq")
    vec = P(None, "fsdp")
    mat = P(None, "fsdp", None)
    return jax.shard_map(
        on_device,
        mesh=mesh,
        in_specs=(tok, lab, lab, tok, vec, vec, mat, vec, mat, vec, vec, vec, mat, vec, mat, vec),
        out_specs=(tok, tok, vec, vec, mat, vec, mat, vec, vec, vec, mat, vec, mat, vec),
        check_vma=False,
    )
```
